32 devices in a mesh: box: 16 (over z, x, core), rhs: 2 (over y).
Axes of the slice: x: 2, y: 2, z: 4, core: 2. Of those that a mesh axis runs over, the one named last changes fastest.
Arguments:
- basis: float32 [8, 16, 131072], P(None, 'rhs', 'box')
- facet_centres: float32 [3, 131072], P(None, 'box'), as said below
- normals: float32 [3, 131072], P(None, 'box'), as said below
- areas: float32 [131072], P('box'), may hold values from 0.2 to 2
- contrast: float32 [131072], P('box'), may hold values from -0.9 to 0.9
- facet_counts: int32 [512], P('box'), may hold values from 64 to 256, as said below
- box_centres: float32 [3, 512], P(None, 'box'), as said below
- near_boxes: int32 [512, 27], P('box'), may hold values from -1 to 511, as said below
- far_boxes: int32 [512, 189], P('box'), may hold values from -1 to 511, as said below
Outputs:
- next_vector: float32 [16, 131072], P('rhs', 'box')
- hessenberg: float32 [9, 16], P(None, 'rhs')
The draws below stay inside these ranges and needn't reach their ends.
Inputs may be any that keep to these rules, and one draw needn't show every extreme that they name: Live facets of box b occupy its first facet_counts[b] slots; at least one box in five is full. `box_centres`: box b stands for the lattice code c(b) = 32 * (b div 32) + p(b mod 32), p a permutation of 0 to 31 drawn for each aligned block of 32 boxes. With l = c mod 64: x = bit 0 of l + 2 * bit 3 of l, y = bit 1 + 2 * bit 4, z = bit 2 + 2 * bit 5 + 4 * (c div 64); the lattice is 4 by 4 by 32 boxes. Box b's centre lies within 0.1 in each coordinate of its lattice point. `near_boxes`: row b holds b itself first, then the boxes at the 26 lattice points next to b's (Chebyshev distance 1) in an order drawn for each row, -1 where a neighbour lies outside the lattice. `far_boxes`: row b holds the octree interaction list of b: the boxes at the children of the neighbours of b's parent (lattice point divided by 2) that are not lattice neighbours of b, in an order drawn for each row, -1 where one lies outside the lattice. `facet_centres`: each facet lies within 0.45 in each coordinate of its box's centre. `normals`: unit vectors.
All inputs are finite; a program needn't handle non-finite values.
Results may differ from the reference program's by a relative error of at most 0.00034.
Values may be sent and summed in bfloat16 or wider, within the bound.
No kernel may reach another device: no remote copies, remote signals or barrier semaphores. Data moves between devices by JAX's collectives and lax.ppermute only.
A program may use at most 64 MiB of HBM per device.

```python
import math
import jax
import jax.numpy as jnp
import numpy as np
from jax import lax

SLOTS = 256
RHS = 16
KRYLOV = 8
NEAR = 27
FAR = 189
BOXES = 512
FACET_SLOTS_ALL = 131072


def block_orders(key):
    block_keys = jax.random.split(jax.random.fold_in(key, 5), BOXES // 32)
    return jax.vmap(lambda one_key: jax.random.permutation(one_key, 32))(block_keys).astype(jnp.int32)


def lattice_coords(key):
    orders = block_orders(key)
    box_index = jnp.arange(BOXES, dtype=jnp.int32)
    lattice_code = 32 * (box_index // 32) + orders.reshape(BOXES)
    local_code = lattice_code % 64
    coord_x = jnp.bitwise_and(local_code, 1) + 2 * jnp.bitwise_and(jnp.right_shift(local_code, 3), 1)
    coord_y = jnp.bitwise_and(jnp.right_shift(local_code, 1), 1) + 2 * jnp.bitwise_and(jnp.right_shift(local_code, 4), 1)
    coord_z = jnp.bitwise_and(jnp.right_shift(local_code, 2), 1) + 2 * jnp.bitwise_and(jnp.right_shift(local_code, 5), 1) + 4 * (lattice_code // 64)
    return (coord_x, coord_y, coord_z)


def lattice_rank(key, coord_x, coord_y, coord_z):
    inside = (coord_x >= 0) & (coord_x < 4) & (coord_y >= 0) & (coord_y < 4) & (coord_z >= 0) & (coord_z < BOXES // 16)
    safe_x = jnp.clip(coord_x, 0, 3)
    safe_y = jnp.clip(coord_y, 0, 3)
    safe_z = jnp.clip(coord_z, 0, BOXES // 16 - 1)
    code = jnp.bitwise_and(safe_x, 1) + 2 * jnp.bitwise_and(safe_y, 1) + 4 * jnp.bitwise_and(safe_z, 1)
    code = code + 8 * jnp.right_shift(safe_x, 1) + 16 * jnp.right_shift(safe_y, 1) + 32 * jnp.bitwise_and(jnp.right_shift(safe_z, 1), 1)
    code = code + 64 * jnp.right_shift(safe_z, 2)
    inverse = jnp.argsort(block_orders(key), axis=1, stable=True).astype(jnp.int32).reshape(BOXES)
    box_of_code = 32 * (code // 32) + jnp.take(inverse, code.astype(jnp.int32))
    return jnp.where(inside, box_of_code, -1).astype(jnp.int32)


def morton_centres(key):
    coord_x, coord_y, coord_z = lattice_coords(key)
    coords = jnp.stack([coord_x, coord_y, coord_z]).astype(jnp.float32)
    jitter = jax.random.uniform(jax.random.fold_in(key, 7), (3, BOXES), jnp.float32, -0.1, 0.1)
    return coords + jitter


def draw_box_centres(key, part):
    return morton_centres(key)


def draw_facet_centres(key, part):
    centres = morton_centres(key)
    spread = jax.random.uniform(jax.random.fold_in(key, 8), (3, BOXES, SLOTS), jnp.float32, -0.45, 0.45)
    return (centres[:, :, None] + spread).reshape(3, FACET_SLOTS_ALL)


def draw_normals(key, part):
    height = jax.random.uniform(jax.random.fold_in(key, 21), (FACET_SLOTS_ALL,), jnp.float32, -1.0, 1.0)
    turning = jax.random.uniform(jax.random.fold_in(key, 22), (FACET_SLOTS_ALL,), jnp.float32, -jnp.pi, jnp.pi)
    radial = jnp.sqrt(jnp.maximum(1.0 - height * height, 0.0))
    return jnp.stack([radial * jnp.cos(turning), radial * jnp.sin(turning), height])


def draw_basis(key, part):
    ramp = jnp.exp(jnp.log(3.0) * jnp.arange(FACET_SLOTS_ALL, dtype=jnp.float32) / FACET_SLOTS_ALL)
    return jax.random.uniform(jax.random.fold_in(key, 33), (KRYLOV, RHS, FACET_SLOTS_ALL), jnp.float32, -0.5, 1.5) * ramp


def draw_facet_counts(key, part):
    counts = jax.random.randint(jax.random.fold_in(key, 41), (BOXES,), SLOTS // 4, SLOTS + 1)
    box_index = jnp.arange(BOXES, dtype=jnp.int32)
    return jnp.where(box_index % 5 == 0, SLOTS, counts).astype(jnp.int32)


def draw_near_boxes(key, part):
    coord_x, coord_y, coord_z = lattice_coords(key)
    offset_table = np.array([[dx, dy, dz] for dx in (-1, 0, 1) for dy in (-1, 0, 1) for dz in (-1, 0, 1) if (dx, dy, dz) != (0, 0, 0)], dtype=np.int32)
    step_x = jnp.asarray(offset_table[:, 0])[None, :]
    step_y = jnp.asarray(offset_table[:, 1])[None, :]
    step_z = jnp.asarray(offset_table[:, 2])[None, :]
    neighbours = lattice_rank(key, coord_x[:, None] + step_x, coord_y[:, None] + step_y, coord_z[:, None] + step_z)
    row_keys = jax.random.split(jax.random.fold_in(key, 51), BOXES)
    orders = jax.vmap(lambda one_key: jax.random.permutation(one_key, 26))(row_keys).astype(jnp.int32)
    shuffled = jnp.take_along_axis(neighbours, orders, axis=1)
    box_index = jnp.arange(BOXES, dtype=jnp.int32)
    return jnp.concatenate([box_index[:, None], shuffled], 1).astype(jnp.int32)


def draw_far_boxes(key, part):
    coord_x, coord_y, coord_z = lattice_coords(key)
    child_table = np.array([[cx, cy, cz] for cx in range(-2, 4) for cy in range(-2, 4) for cz in range(-2, 4)], dtype=np.int32)
    base_x = (coord_x - jnp.bitwise_and(coord_x, 1))[:, None]
    base_y = (coord_y - jnp.bitwise_and(coord_y, 1))[:, None]
    base_z = (coord_z - jnp.bitwise_and(coord_z, 1))[:, None]
    cand_x = base_x + jnp.asarray(child_table[:, 0])[None, :]
    cand_y = base_y + jnp.asarray(child_table[:, 1])[None, :]
    cand_z = base_z + jnp.asarray(child_table[:, 2])[None, :]
    adjacent = (jnp.abs(cand_x - coord_x[:, None]) <= 1) & (jnp.abs(cand_y - coord_y[:, None]) <= 1) & (jnp.abs(cand_z - coord_z[:, None]) <= 1)
    ranks = lattice_rank(key, cand_x, cand_y, cand_z)
    row_keys = jax.random.split(jax.random.fold_in(key, 61), BOXES)
    orders = jax.vmap(lambda one_key: jax.random.permutation(one_key, 216))(row_keys).astype(jnp.int32)
    scores = orders + 1000 * adjacent.astype(jnp.int32)
    picked = jnp.argsort(scores, axis=1, stable=True)[:, :FAR].astype(jnp.int32)
    return jnp.take_along_axis(ranks, picked, axis=1).astype(jnp.int32)


def shard_levels(stream_key, extent, pieces, least, largest):
    factor_of, own = 1.0, jax.random.fold_in(stream_key, 6)
    for dim, blocks in pieces:
        heights = jnp.exp(jax.random.uniform(jax.random.fold_in(own, dim), (blocks,), jnp.float32, least / len(pieces), largest / len(pieces)))
        factor_of = factor_of * jnp.repeat(heights, extent[dim] // blocks).reshape([-1 if axis == dim else 1 for axis in range(len(extent))])
    return factor_of


def setup_inputs(seed: int = 0) -> dict:
    splits = jax.random.split(jax.random.key(seed), 10)
    basis = draw_basis(jax.random.fold_in(splits[9], 71), 0)
    facet_centres = draw_facet_centres(jax.random.fold_in(splits[9], 71), 0)
    normals = draw_normals(jax.random.fold_in(splits[9], 71), 0)
    areas = jnp.clip(jnp.exp(math.log(2.0) - 2.3025851 * jax.random.uniform(splits[3], (FACET_SLOTS_ALL,), jnp.float32) ** shard_levels(splits[3], (FACET_SLOTS_ALL,), ((0, 16),), -0.2, 0.2)), 0.2, 2.0)
    contrast = jnp.clip(jax.random.uniform(splits[4], (FACET_SLOTS_ALL,), jnp.float32, -0.9, 0.9) * shard_levels(splits[4], (FACET_SLOTS_ALL,), ((0, 16),), -0.4, 0.0), -0.9, 0.9)
    facet_counts = draw_facet_counts(jax.random.fold_in(splits[9], 71), 0)
    box_centres = draw_box_centres(jax.random.fold_in(splits[9], 71), 0)
    near_boxes = draw_near_boxes(jax.random.fold_in(splits[9], 71), 0)
    far_boxes = draw_far_boxes(jax.random.fold_in(splits[9], 71), 0)
    return {"basis": basis, "facet_centres": facet_centres, "normals": normals, "areas": areas, "contrast": contrast, "facet_counts": facet_counts, "box_centres": box_centres, "near_boxes": near_boxes, "far_boxes": far_boxes}


soften = 0.0025
epsilon = 1e-06
largest_index = lax.Precision.HIGHEST

def near_kernel(target_centres, target_normals, source_centres):
    diff_x = target_centres[0][:, :, None] - source_centres[0][:, None, :]
    diff_y = target_centres[1][:, :, None] - source_centres[1][:, None, :]
    diff_z = target_centres[2][:, :, None] - source_centres[2][:, None, :]
    normal_part = diff_x * target_normals[0][:, :, None] + diff_y * target_normals[1][:, :, None] + diff_z * target_normals[2][:, :, None]
    spread = diff_x * diff_x + diff_y * diff_y + diff_z * diff_z + soften
    return (normal_part / (spread * jnp.sqrt(spread))).astype(jnp.bfloat16)

def far_coeffs(target_centres, target_normals, centres_far):
    offsets = [target_centres[axis_number][:, None, :] - centres_far[axis_number][:, :, None] for axis_number in range(3)]
    distance = offsets[0] * offsets[0] + offsets[1] * offsets[1] + offsets[2] * offsets[2] + soften
    inverse_cube = 1.0 / (distance * jnp.sqrt(distance))
    normal_part = offsets[0] * target_normals[0][:, None, :] + offsets[1] * target_normals[1][:, None, :] + offsets[2] * target_normals[2][:, None, :]
    coeff_list = [normal_part * inverse_cube]
    for axis_number in range(3):
        coeff_list.append(3.0 * normal_part * offsets[axis_number] * inverse_cube / distance - target_normals[axis_number][:, None, :] * inverse_cube)
    return jnp.stack(coeff_list)

def reference(basis, facet_centres, normals, areas, contrast, facet_counts, box_centres, near_boxes, far_boxes):
    current = basis[KRYLOV - 1]
    slot_index = jnp.arange(SLOTS, dtype=jnp.int32)[None, :]
    live_mask = (slot_index < facet_counts[:, None]).astype(jnp.float32).reshape(FACET_SLOTS_ALL)
    weighted = current * (areas * live_mask / SLOTS)[None, :]
    charge_boxes = weighted.astype(jnp.bfloat16).reshape(RHS, BOXES, SLOTS)
    centre_boxes = facet_centres.reshape(3, BOXES, SLOTS)
    normal_boxes = normals.reshape(3, BOXES, SLOTS)
    weighted_boxes = weighted.reshape(RHS, BOXES, SLOTS)
    relative = centre_boxes - box_centres[:, :, None]
    monopole = lax.optimization_barrier(jnp.sum(weighted_boxes, axis=2))
    dipole = jnp.einsum('rbj,abj->arb', weighted_boxes, relative, precision=largest_index)
    moments = jnp.concatenate([monopole[None], dipole], 0)

    def one_box(box_number):
        target_centres = centre_boxes[:, box_number]
        target_normals = normal_boxes[:, box_number]
        near_ids = near_boxes[box_number]
        near_valid = near_ids >= 0
        near_safe = jnp.where(near_valid, near_ids, 0).astype(jnp.int32)
        source_centres = jnp.take(centre_boxes, near_safe, axis=1)
        source_charges = (jnp.take(charge_boxes, near_safe, axis=1) * near_valid[None, :, None].astype(jnp.bfloat16)).astype(jnp.float32)
        spread_centres = jnp.broadcast_to(target_centres[:, None, :], (3, NEAR, SLOTS))
        spread_normals = jnp.broadcast_to(target_normals[:, None, :], (3, NEAR, SLOTS))
        kernel = near_kernel(spread_centres, spread_normals, source_centres).astype(jnp.float32)
        near_part = jnp.einsum('kij,rkj->ri', kernel, source_charges, precision=largest_index)
        far_ids = far_boxes[box_number]
        far_valid = far_ids >= 0
        far_safe = jnp.where(far_valid, far_ids, 0).astype(jnp.int32)
        picked = jnp.take(moments, far_safe, axis=2) * far_valid[None, None, :].astype(jnp.float32)
        centres_far = jnp.take(box_centres, far_safe, axis=1)
        coeffs = far_coeffs(target_centres[:, None, :], target_normals[:, None, :], centres_far[:, None, :])
        far_part = jnp.einsum('mki,mrk->ri', coeffs[:, 0], picked, precision=largest_index)
        return near_part + far_part
    fields = lax.map(one_box, jnp.arange(BOXES, dtype=jnp.int32))
    field_flat = jnp.transpose(fields, (1, 0, 2)).reshape(RHS, FACET_SLOTS_ALL)
    image_vector = live_mask[None, :] * (current - 2.0 * contrast[None, :] * field_flat)
    basis_masked_rows = basis * live_mask[None, None, :]
    basis_projections = jnp.einsum('lbe,be->lb', basis_masked_rows, image_vector, precision=largest_index) / FACET_SLOTS_ALL
    residual_vector = image_vector - jnp.einsum('zo,zov->ov', basis_projections, basis_masked_rows, precision=largest_index)
    remaining = lax.optimization_barrier(jnp.sum(residual_vector * residual_vector, axis=1))
    norm_scale = jnp.sqrt(remaining / FACET_SLOTS_ALL + epsilon)
    next_vector = residual_vector / norm_scale[:, None]
    hessenberg = jnp.concatenate([basis_projections, norm_scale[None, :]], 0)
    return (next_vector, hessenberg)
```

```python
import functools

import jax
import jax.numpy as jnp
from jax import lax
from jax.experimental import pallas as pl
from jax.experimental.pallas import tpu as pltpu
from jax.sharding import PartitionSpec as P

soften = 0.0025
epsilon = 1e-06
f32 = jnp.float32
bf16 = jnp.bfloat16
box_rows = 24
plane_boxes = 16
tail = plane_boxes * box_rows
pack_rows = tail + 16
depth = 128


def lattice(centres_s, b):
    x = (centres_s[0, b] + 0.5).astype(jnp.int32)
    y = (centres_s[1, b] + 0.5).astype(jnp.int32)
    z = (centres_s[2, b] + 0.5).astype(jnp.int32)
    return x, y, z


def wide_row(ref, b):
    return jnp.concatenate([ref[pl.ds(2 * b, 1), :], ref[pl.ds(2 * b + 1, 1), :]], axis=1)


def live_row(counts_s, b, per_box):
    slots = lax.broadcasted_iota(jnp.int32, (1, per_box), 1)
    return (slots < counts_s[b]).astype(f32)


def prep_kernel(centres_s, counts_s, current_ref, facets_ref, areas_ref, low_ref, high_ref, packs):
    boxes = counts_s.shape[0]
    per_box = current_ref.shape[2] // boxes
    lane = lax.broadcasted_iota(jnp.int32, (8, 128), 1)
    row = lax.broadcasted_iota(jnp.int32, (8, 128), 0)

    def one_box(b, carry):
        moments, centres = carry
        x, y, z = lattice(centres_s, b)
        plane = z & 1
        place = y * 4 + x
        slot = plane * plane_boxes + place
        lanes = pl.ds(pl.multiple_of(b * per_box, per_box), per_box)
        facets = facets_ref[:, lanes]
        live = live_row(counts_s, b, per_box)
        weighted = current_ref[0, :, lanes] * (wide_row(areas_ref, b) * live / per_box)
        charges = weighted.astype(bf16).astype(f32)
        start = pl.multiple_of(plane * pack_rows + place * box_rows, 8)
        packs[pl.ds(start, 8), :] = charges[:, :128]
        packs[pl.ds(start + 8, 8), :] = charges[:, 128:]
        packs[pl.ds(start + 16, 8), :] = jnp.concatenate(
            [facets[:, :128], facets[:, 128:], jnp.zeros((2, 128), f32)], axis=0
        )
        moments += jnp.where(lane == slot, jnp.sum(weighted, axis=1, keepdims=True), 0.0)
        for a in range(3):
            dipole = jnp.sum(weighted * (facets[a : a + 1] - centres_s[a, b]), axis=1, keepdims=True)
            moments += jnp.where(lane == 32 * (a + 1) + slot, dipole, 0.0)
            centres += jnp.where((lane == slot) & (row == a), centres_s[a, b], 0.0)
        return moments, centres

    zeros = jnp.zeros((8, 128), f32)
    moments, centres = lax.fori_loop(0, boxes, one_box, (zeros, zeros), unroll=4)
    low_ref[:tail] = packs[:tail]
    high_ref[:tail] = packs[pack_rows : pack_rows + tail]
    for ref in (low_ref, high_ref):
        ref[tail : tail + 8] = moments
        ref[tail + 8 :] = centres


def thirds(x):
    high = x.astype(bf16).astype(f32)
    rest = x - high
    middle = rest.astype(bf16).astype(f32)
    return high, middle, (rest - middle).astype(bf16).astype(f32)


def stacked_rows(parts, width):
    zeros = jnp.zeros((depth - 8 * len(parts), width), f32)
    return jnp.concatenate([*parts, zeros], axis=0)


def local_facets(pack_ref, place, origin):
    start = pl.multiple_of(place * box_rows + 16, 8)
    tile = pack_ref[pl.ds(start, 8), :]
    both = jnp.concatenate([tile[0:3], tile[3:6]], axis=1)
    return jnp.concatenate([both - origin, jnp.zeros((5, 256), f32)], axis=0)


def field_kernel(
    centres_s, counts_s, prev_ref, low_ref, high_ref, next_ref, normals_ref, contrast_ref, basis_ref,
    image_ref, sums_ref, left, right, field, far_centres
):
    boxes = counts_s.shape[0]
    krylov = basis_ref.shape[0]
    per_box = image_ref.shape[1] // boxes
    packs = (prev_ref, low_ref, high_ref, next_ref)
    row = lax.broadcasted_iota(jnp.int32, (8, per_box), 0)
    _, _, z = lattice(centres_s, 0)
    base_z = (z - (z & 1)).astype(f32) + 0.5
    axis_row = lax.broadcasted_iota(jnp.int32, (3, 1), 0)
    origin = jnp.where(axis_row == 2, base_z, 1.5)

    for plane, pack in enumerate(packs):

        def source_features(place, _, plane=plane, pack=pack):
            local = local_facets(pack, place, origin)
            square = jnp.sum(local * local, axis=0, keepdims=True)
            features = jnp.where(row == 3, square, jnp.where(row == 4, 1.0, local))
            high, middle, low = thirds(features)
            columns = stacked_rows((high, high, high, middle, middle, low), per_box)
            start = pl.multiple_of((plane * plane_boxes + place) * per_box, per_box)
            left[pl.ds(start, per_box), :] = jnp.transpose(columns).astype(bf16)
            return 0

        lax.fori_loop(0, plane_boxes, source_features, 0, unroll=2)

    for group, pack in enumerate((prev_ref, low_ref, next_ref)):
        columns = jnp.transpose(pack[tail + 8 : tail + 16, :])[:32]
        for a in range(3):
            shift = base_z if a == 2 else 1.5
            far_centres[(group * 3 + a) * 32 : (group * 3 + a + 1) * 32, :] = jnp.broadcast_to(
                columns[:, a : a + 1] - shift, (32, 128)
            )
    far_moments = jnp.concatenate([pack[tail : tail + 8, :] for pack in (prev_ref, low_ref, next_ref)], axis=1)
    far_high = far_moments.astype(bf16).astype(f32)
    far_both = jnp.concatenate([far_high, far_moments - far_high], axis=0)
    far_lane = lax.broadcasted_iota(jnp.int32, (1, 384), 1)
    lane_x = far_lane & 3
    lane_y = (far_lane >> 2) & 3
    lane_z = 2 * (far_lane >> 7) - 2 + ((far_lane >> 4) & 1)

    def target(b, _):
        x, y, z = lattice(centres_s, b)
        plane = z & 1
        place = y * 4 + x
        slot = plane * plane_boxes + place
        lanes = pl.ds(pl.multiple_of(b * per_box, per_box), per_box)
        start = pl.multiple_of(place * box_rows + 16, 8)
        tile = jnp.where(plane == 0, low_ref[pl.ds(start, 8), :], high_ref[pl.ds(start, 8), :])
        local = jnp.concatenate([tile[0:3], tile[3:6]], axis=1) - origin
        normal = normals_ref[:, lanes]
        five = jnp.zeros((5, per_box), f32)
        local_8 = jnp.concatenate([local, five], axis=0)
        normal_8 = jnp.concatenate([normal, five], axis=0)
        square = jnp.sum(local_8 * local_8, axis=0, keepdims=True) + soften
        along = jnp.sum(local_8 * normal_8, axis=0, keepdims=True)
        distance = jnp.where(row == 3, 1.0, jnp.where(row == 4, square, -2.0 * local_8))
        slope = jnp.where(row == 4, along, -normal_8)
        both = jnp.concatenate([distance, slope], axis=1)
        high, middle, low = thirds(both)
        rows = stacked_rows((high, middle, low, high, middle, high), 2 * per_box)
        right[pl.ds(pl.multiple_of(slot * depth, depth), depth), :] = rows.astype(bf16)

        coefficients = []
        for group in range(3):
            d = []
            for a in range(3):
                centre = far_centres[(group * 3 + a) * 32 : (group * 3 + a + 1) * 32, :]
                d.append(local[a : a + 1] - jnp.concatenate([centre, centre], axis=1))
            q = d[0] * d[0] + d[1] * d[1] + d[2] * d[2] + soften
            inverse = lax.rsqrt(q)
            inverse_2 = inverse * inverse
            inverse_3 = inverse_2 * inverse
            t = d[0] * normal[0:1] + d[1] * normal[1:2] + d[2] * normal[2:3]
            single = t * inverse_3
            coefficients.append(single)
            steep = 3.0 * single * inverse_2
            for a in range(3):
                coefficients.append(steep * d[a] - normal[a : a + 1] * inverse_3)
        whole = jnp.concatenate(coefficients, axis=0)
        upper = whole.astype(bf16)
        lower = (whole - upper.astype(f32)).astype(bf16)
        near = (
            (jnp.abs(lane_x - x) <= 1) & (jnp.abs(lane_y - y) <= 1) & (jnp.abs(lane_z - plane) <= 1)
        )
        picked = jnp.where(near, 0.0, far_both).astype(bf16)
        first = jnp.dot(picked, upper, preferred_element_type=f32)
        second = jnp.dot(picked, lower, preferred_element_type=f32)
        field[pl.ds(pl.multiple_of(slot * 8, 8), 8), :] = first[:8] + first[8:] + second[:8]
        return 0

    lax.fori_loop(0, boxes, target, 0)

    for step in range(3):
        for plane in range(2):
            pack = packs[plane + step]

            def near_rows(item, _, plane=plane, step=step, pack=pack):
                target_y = (item + 1) // 3
                source_y = target_y + lax.rem(item + 1, 3) - 1
                source_start = pl.multiple_of((plane + step) * plane_boxes * per_box + source_y * 4 * per_box, per_box)
                charges = []
                for x in range(4):
                    start = pl.multiple_of((source_y * 4 + x) * box_rows, 8)
                    charges.append(
                        jnp.concatenate(
                            [pack[pl.ds(start, 8), :], pack[pl.ds(start + 8, 8), :]], axis=1
                        ).astype(bf16)
                    )
                for x in range(4):
                    slot = plane * plane_boxes + target_y * 4 + x
                    weights = right[pl.ds(pl.multiple_of(slot * depth, depth), depth), :]
                    total = None
                    for source_x in range(max(x - 1, 0), min(x + 2, 4)):
                        facets = left[pl.ds(source_start + source_x * per_box, per_box), :]
                        geometry = jnp.dot(facets, weights, preferred_element_type=f32)
                        inverse = lax.rsqrt(geometry[:, :per_box])
                        kernel = (geometry[:, per_box:] * inverse) * (inverse * inverse)
                        part = jnp.dot(charges[source_x], kernel.astype(bf16), preferred_element_type=f32)
                        total = part if total is None else total + part
                    field[pl.ds(pl.multiple_of(slot * 8, 8), 8), :] += total
                return 0

            lax.fori_loop(0, 10, near_rows, 0)

    def image_box(b, carry):
        x, y, z = lattice(centres_s, b)
        slot = (z & 1) * plane_boxes + y * 4 + x
        lanes = pl.ds(pl.multiple_of(b * per_box, per_box), per_box)
        live = live_row(counts_s, b, per_box)
        current = basis_ref[krylov - 1, :, lanes]
        part = field[pl.ds(pl.multiple_of(slot * 8, 8), 8), :]
        image = live * (current - 2.0 * wide_row(contrast_ref, b) * part)
        image_ref[:, lanes] = image
        sums = []
        for m in range(krylov + 1):
            product = image * (basis_ref[m, :, lanes] if m < krylov else image)
            sums.append(carry[m] + product[:, :128] + product[:, 128:])
        return tuple(sums)

    zeros = jnp.zeros((8, 128), f32)
    sums = lax.fori_loop(0, boxes, image_box, (zeros,) * (krylov + 1))
    pairs = [(m, n) for m in range(krylov) for n in range(m + 1)]

    def gram_box(b, carry):
        lanes = pl.ds(pl.multiple_of(b * per_box, per_box), per_box)
        live = live_row(counts_s, b, per_box)
        rows = [basis_ref[m, :, lanes] * live for m in range(krylov)]
        out = []
        for k, (m, n) in enumerate(pairs):
            product = rows[m] * rows[n]
            out.append(carry[k] + product[:, :128] + product[:, 128:])
        return tuple(out)

    gram = lax.fori_loop(0, boxes, gram_box, (zeros,) * len(pairs))
    lane = lax.broadcasted_iota(jnp.int32, (8, 128), 1)
    total = zeros
    for k, value in enumerate([*sums, *gram]):
        total = jnp.where(lane == k, jnp.sum(value, axis=1, keepdims=True), total)
    sums_ref[...] = total


def two_sum(a, b):
    s = a + b
    c = s - a
    return s, (a - (s - c)) + (b - c)


def halves(a):
    c = a * 4097.0
    high = c - (c - a)
    return high, a - high


def two_product(a, b):
    p = a * b
    a_high, a_low = halves(a)
    b_high, b_low = halves(b)
    return p, ((a_high * b_high - p) + a_high * b_low + a_low * b_high) + a_low * b_low


def finish_kernel(total_facets, counts_s, sums_ref, rest_ref, image_ref, basis_ref, next_ref, hessenberg_ref):
    boxes = counts_s.shape[0]
    krylov = basis_ref.shape[0]
    per_box = image_ref.shape[1] // boxes
    lane = lax.broadcasted_iota(jnp.int32, (8, 128), 1)
    sums = sums_ref[...]
    rest = rest_ref[...]
    exact = sums + rest
    projections = [exact[:, m : m + 1] / total_facets for m in range(krylov)]
    pairs = [(m, n) for m in range(krylov) for n in range(m + 1)]
    first = jnp.where(lane == krylov, 1.0, 0.0)
    second = jnp.where(lane <= krylov, 1.0, 0.0)
    for m in range(krylov):
        first = jnp.where(lane == m, -2.0 * projections[m], first)
    for k, (m, n) in enumerate(pairs):
        at = lane == krylov + 1 + k
        scale = 1.0 if m == n else 2.0
        first = jnp.where(at, scale * projections[m], first)
        second = jnp.where(at, projections[n], second)
    factor, factor_rest = two_product(first, second)
    value, value_rest = two_product(factor, sums)
    value_rest = value_rest + (factor * rest + factor_rest * sums)
    for shift in (64, 32, 16, 8, 4, 2, 1):
        other = pltpu.roll(value, shift, 1)
        other_rest = pltpu.roll(value_rest, shift, 1)
        value, error = two_sum(value, other)
        value_rest = (value_rest + other_rest) + error
    remaining = jnp.maximum(value + value_rest, 0.0)
    norm = jnp.sqrt(remaining / total_facets + epsilon)
    heads = jnp.where(lane == krylov, norm, 0.0)
    for m in range(krylov):
        heads = jnp.where(lane == m, projections[m], heads)
    hessenberg_ref[...] = jnp.transpose(heads)[: krylov + 1]
    wide = [jnp.broadcast_to(p, (8, per_box)) for p in projections]
    scale = jnp.concatenate([1.0 / norm] * (per_box // 128), axis=1)

    def one_box(b, _):
        lanes = pl.ds(pl.multiple_of(b * per_box, per_box), per_box)
        live = live_row(counts_s, b, per_box)
        sent = wide[0] * basis_ref[0, :, lanes]
        for m in range(1, krylov):
            sent += wide[m] * basis_ref[m, :, lanes]
        next_ref[:, lanes] = (image_ref[:, lanes] - sent * live) * scale
        return 0

    lax.fori_loop(0, boxes, one_box, 0, unroll=4)


smem = pl.BlockSpec(memory_space=pltpu.SMEM)
vmem = pl.BlockSpec(memory_space=pltpu.VMEM)


def summed(value, axis):
    count = lax.axis_size(axis)
    rest = jnp.zeros_like(value)
    step = 1
    while step < count:
        pairs = [(i, i ^ step) for i in range(count)]
        if step == 1:
            value, rest = two_sum(value, lax.ppermute(value, axis, pairs))
        else:
            other = lax.ppermute(jnp.stack([value, rest]), axis, pairs)
            value, error = two_sum(value, other[0])
            rest = (rest + other[1]) + error
        step *= 2
    return value, rest


def on_device(
    basis, facet_centres, normals, areas, contrast, facet_counts, box_centres, near_boxes, far_boxes
):
    krylov, rhs_local, facet_local = basis.shape
    boxes = facet_counts.shape[0]
    per_box = facet_local // boxes
    count = lax.axis_size("box")
    total_facets = count * facet_local
    areas = areas.reshape(-1, 128)
    contrast = contrast.reshape(-1, 128)
    pack = jax.ShapeDtypeStruct((pack_rows, 128), f32)
    low, high = pl.pallas_call(
        prep_kernel,
        grid=(1,),
        out_shape=(pack, pack),
        in_specs=[
            smem,
            smem,
            pl.BlockSpec((1, rhs_local, facet_local), lambda i: (krylov - 1, 0, 0)),
            vmem,
            vmem,
        ],
        out_specs=(vmem, vmem),
        scratch_shapes=[pltpu.VMEM((2 * pack_rows, 128), f32)],
        name="prepare",
    )(box_centres, facet_counts, basis, facet_centres, areas)
    below = lax.ppermute(high, "box", [(i, i + 1) for i in range(count - 1)])
    above = lax.ppermute(low, "box", [(i + 1, i) for i in range(count - 1)])
    image, sums = pl.pallas_call(
        field_kernel,
        out_shape=(
            jax.ShapeDtypeStruct((rhs_local, facet_local), f32),
            jax.ShapeDtypeStruct((8, 128), f32),
        ),
        in_specs=[smem, smem] + [vmem] * 7,
        out_specs=(vmem, vmem),
        scratch_shapes=[
            pltpu.VMEM((4 * plane_boxes * per_box, depth), bf16),
            pltpu.VMEM((boxes * depth, 2 * per_box), bf16),
            pltpu.VMEM((boxes * 8, per_box), f32),
            pltpu.VMEM((9 * 32, 128), f32),
        ],
        compiler_params=pltpu.CompilerParams(vmem_limit_bytes=48 * 1024 * 1024),
        name="fields",
    )(box_centres, facet_counts, below, low, high, above, normals, contrast, basis)
    value, rest = summed(sums, "box")
    return tuple(
        pl.pallas_call(
            functools.partial(finish_kernel, total_facets),
            out_shape=(
                jax.ShapeDtypeStruct((rhs_local, facet_local), f32),
                jax.ShapeDtypeStruct((krylov + 1, rhs_local), f32),
            ),
            in_specs=[smem] + [vmem] * 4,
            out_specs=(vmem, vmem),
            compiler_params=pltpu.CompilerParams(vmem_limit_bytes=16 * 1024 * 1024),
            name="finish",
        )(facet_counts, value, rest, image, basis)
    )


def solution(mesh):
    return jax.shard_map(
        on_device,
        mesh=mesh,
        in_specs=(
            P(None, "rhs", "box"),
            P(None, "box"),
            P(None, "box"),
            P("box"),
            P("box"),
            P("box"),
            P(None, "box"),
            P("box", None),
            P("box", None),
        ),
        out_specs=(P("rhs", "box"), P(None, "rhs")),
        check_vma=False,
    )
```

```python
import functools

import jax
import jax.numpy as jnp
from jax import lax
from jax.experimental import pallas as pl
from jax.experimental.pallas import tpu as pltpu
from jax.sharding import PartitionSpec as P

soften = 0.0025
epsilon = 1e-06
f32 = jnp.float32
bf16 = jnp.bfloat16
box_rows = 24
plane_boxes = 16
per_box = 256
tail = plane_boxes * box_rows
pack_rows = tail + 16
depth = 128


def lattice(centres_s, b):
    x = (centres_s[0, b] + 0.5).astype(jnp.int32)
    y = (centres_s[1, b] + 0.5).astype(jnp.int32)
    z = (centres_s[2, b] + 0.5).astype(jnp.int32)
    return x, y, z


def wide_row(ref, b):
    return jnp.concatenate([ref[pl.ds(2 * b, 1), :], ref[pl.ds(2 * b + 1, 1), :]], axis=1)


def live_row(counts_s, b):
    slots = lax.broadcasted_iota(jnp.int32, (1, per_box), 1)
    return (slots < counts_s[b]).astype(f32)


def prep_kernel(centres_s, counts_s, current_ref, facets_ref, areas_ref, low_ref, high_ref, packs):
    boxes = counts_s.shape[0]
    lane = lax.broadcasted_iota(jnp.int32, (8, 128), 1)
    row = lax.broadcasted_iota(jnp.int32, (8, 128), 0)

    def one_box(b, carry):
        moments, centres = carry
        x, y, z = lattice(centres_s, b)
        plane = z & 1
        place = y * 4 + x
        slot = plane * plane_boxes + place
        lanes = pl.ds(pl.multiple_of(b * per_box, per_box), per_box)
        facets = facets_ref[:, lanes]
        live = live_row(counts_s, b)
        weighted = current_ref[0, :, lanes] * (wide_row(areas_ref, b) * live / per_box)
        charges = weighted.astype(bf16).astype(f32)
        start = pl.multiple_of(plane * pack_rows + place * box_rows, 8)
        packs[pl.ds(start, 8), :] = charges[:, :128]
        packs[pl.ds(start + 8, 8), :] = charges[:, 128:]
        packs[pl.ds(start + 16, 8), :] = jnp.concatenate(
            [facets[:, :128], facets[:, 128:], jnp.zeros((2, 128), f32)], axis=0
        )
        moments += jnp.where(lane == slot, jnp.sum(weighted, axis=1, keepdims=True), 0.0)
        for a in range(3):
            dipole = jnp.sum(weighted * (facets[a : a + 1] - centres_s[a, b]), axis=1, keepdims=True)
            moments += jnp.where(lane == 32 * (a + 1) + slot, dipole, 0.0)
            centres += jnp.where((lane == slot) & (row == a), centres_s[a, b], 0.0)
        return moments, centres

    zeros = jnp.zeros((8, 128), f32)
    moments, centres = lax.fori_loop(0, boxes, one_box, (zeros, zeros), unroll=4)
    low_ref[:tail] = packs[:tail]
    high_ref[:tail] = packs[pack_rows : pack_rows + tail]
    for ref in (low_ref, high_ref):
        ref[tail : tail + 8] = moments
        ref[tail + 8 :] = centres


def thirds(x):
    high = x.astype(bf16).astype(f32)
    rest = x - high
    middle = rest.astype(bf16).astype(f32)
    return high, middle, (rest - middle).astype(bf16).astype(f32)


def stacked_rows(parts, width):
    zeros = jnp.zeros((depth - 8 * len(parts), width), f32)
    return jnp.concatenate([*parts, zeros], axis=0)


def local_facets(pack_ref, place, origin):
    start = pl.multiple_of(place * box_rows + 16, 8)
    tile = pack_ref[pl.ds(start, 8), :]
    both = jnp.concatenate([tile[0:3], tile[3:6]], axis=1)
    return jnp.concatenate([both - origin, jnp.zeros((5, 256), f32)], axis=0)


def slab_origin(centres_s):
    _, _, z = lattice(centres_s, 0)
    base_z = (z - (z & 1)).astype(f32) + 0.5
    axis_row = lax.broadcasted_iota(jnp.int32, (3, 1), 0)
    return jnp.where(axis_row == 2, base_z, 1.5), base_z


def store_source_features(pack, origin, left, first):
    row = lax.broadcasted_iota(jnp.int32, (8, per_box), 0)

    def one_box(place, _):
        local = local_facets(pack, place, origin)
        square = jnp.sum(local * local, axis=0, keepdims=True)
        features = jnp.where(row == 3, square, jnp.where(row == 4, 1.0, local))
        high, middle, low = thirds(features)
        columns = stacked_rows((high, high, high, middle, middle, low), per_box)
        start = pl.multiple_of(first + place * per_box, per_box)
        left[pl.ds(start, per_box), :] = jnp.transpose(columns).astype(bf16)
        return 0

    lax.fori_loop(0, plane_boxes, one_box, 0, unroll=2)


def target_place(centres_s, b):
    x, y, z = lattice(centres_s, b)
    plane = z & 1
    place = y * 4 + x
    return x, y, plane, place, plane * plane_boxes + place


def facets_at(low_ref, high_ref, plane, place, origin):
    start = pl.multiple_of(place * box_rows + 16, 8)
    tile = jnp.where(plane == 0, low_ref[pl.ds(start, 8), :], high_ref[pl.ds(start, 8), :])
    return jnp.concatenate([tile[0:3], tile[3:6]], axis=1) - origin


def feature_kernel(centres_s, low_ref, high_ref, normals_ref, left, right):
    boxes = centres_s.shape[1]
    row = lax.broadcasted_iota(jnp.int32, (8, per_box), 0)
    origin, _ = slab_origin(centres_s)
    store_source_features(low_ref, origin, left, 0)
    store_source_features(high_ref, origin, left, plane_boxes * per_box)

    def target(b, _):
        _, _, plane, place, slot = target_place(centres_s, b)
        local = facets_at(low_ref, high_ref, plane, place, origin)
        normal = normals_ref[:, pl.ds(pl.multiple_of(b * per_box, per_box), per_box)]
        five = jnp.zeros((5, per_box), f32)
        local_8 = jnp.concatenate([local, five], axis=0)
        normal_8 = jnp.concatenate([normal, five], axis=0)
        square = jnp.sum(local_8 * local_8, axis=0, keepdims=True) + soften
        along = jnp.sum(local_8 * normal_8, axis=0, keepdims=True)
        distance = jnp.where(row == 3, 1.0, jnp.where(row == 4, square, -2.0 * local_8))
        slope = jnp.where(row == 4, along, -normal_8)
        both = jnp.concatenate([distance, slope], axis=1)
        high, middle, low = thirds(both)
        rows = stacked_rows((high, middle, low, high, middle, high), 2 * per_box)
        right[pl.ds(pl.multiple_of(slot * depth, depth), depth), :] = rows.astype(bf16)
        return 0

    lax.fori_loop(0, boxes, target, 0, unroll=2)


def near_plane(pack, left, first, right, plane, field):
    def near_rows(item, _):
        target_y = (item + 1) // 3
        source_y = target_y + lax.rem(item + 1, 3) - 1
        source_start = pl.multiple_of(first + source_y * 4 * per_box, per_box)
        charges = []
        for x in range(4):
            start = pl.multiple_of((source_y * 4 + x) * box_rows, 8)
            charges.append(
                jnp.concatenate([pack[pl.ds(start, 8), :], pack[pl.ds(start + 8, 8), :]], axis=1).astype(bf16)
            )
        for x in range(4):
            slot = plane * plane_boxes + target_y * 4 + x
            weights = right[pl.ds(pl.multiple_of(slot * depth, depth), depth), :]
            low, high = max(x - 1, 0), min(x + 2, 4)
            facets = left[pl.ds(source_start + low * per_box, (high - low) * per_box), :]
            geometry = jnp.dot(facets, weights, preferred_element_type=f32)
            inverse = lax.rsqrt(geometry[:, :per_box])
            kernel = ((geometry[:, per_box:] * inverse) * (inverse * inverse)).astype(bf16)
            row_charges = jnp.concatenate(charges[low:high], axis=1)
            total = jnp.dot(row_charges, kernel, preferred_element_type=f32)
            field[pl.ds(pl.multiple_of(slot * 8, 8), 8), :] += total
        return 0

    lax.fori_loop(0, 10, near_rows, 0)


def own_kernel(low_ref, high_ref, left, right, field):
    field[...] = jnp.zeros_like(field)
    for plane in range(2):
        near_plane(low_ref, left, 0, right, plane, field)
        near_plane(high_ref, left, plane_boxes * per_box, right, plane, field)


def halo_kernel(
    centres_s, counts_s, prev_ref, low_ref, high_ref, next_ref, normals_ref, contrast_ref, basis_ref, right,
    own_field, image_ref, sums_ref, left, field, far_centres
):
    boxes = counts_s.shape[0]
    krylov = basis_ref.shape[0]
    origin, base_z = slab_origin(centres_s)
    field[...] = own_field[...]
    store_source_features(prev_ref, origin, left, 0)
    store_source_features(next_ref, origin, left, plane_boxes * per_box)
    near_plane(prev_ref, left, 0, right, 0, field)
    near_plane(next_ref, left, plane_boxes * per_box, right, 1, field)

    for group, pack in enumerate((prev_ref, low_ref, next_ref)):
        columns = jnp.transpose(pack[tail + 8 : tail + 16, :])[:32]
        for a in range(3):
            shift = base_z if a == 2 else 1.5
            far_centres[(group * 3 + a) * 32 : (group * 3 + a + 1) * 32, :] = jnp.broadcast_to(
                columns[:, a : a + 1] - shift, (32, 128)
            )
    far_moments = jnp.concatenate([pack[tail : tail + 8, :] for pack in (prev_ref, low_ref, next_ref)], axis=1)
    far_high = far_moments.astype(bf16).astype(f32)
    far_both = jnp.concatenate([far_high, far_moments - far_high], axis=0)
    far_lane = lax.broadcasted_iota(jnp.int32, (1, 384), 1)
    lane_x = far_lane & 3
    lane_y = (far_lane >> 2) & 3
    lane_z = 2 * (far_lane >> 7) - 2 + ((far_lane >> 4) & 1)

    def far_box(b, _):
        x, y, plane, place, slot = target_place(centres_s, b)
        local = facets_at(low_ref, high_ref, plane, place, origin)
        normal = normals_ref[:, pl.ds(pl.multiple_of(b * per_box, per_box), per_box)]
        coefficients = []
        for group in range(3):
            d = []
            for a in range(3):
                centre = far_centres[(group * 3 + a) * 32 : (group * 3 + a + 1) * 32, :]
                d.append(local[a : a + 1] - jnp.concatenate([centre, centre], axis=1))
            q = d[0] * d[0] + d[1] * d[1] + d[2] * d[2] + soften
            inverse = lax.rsqrt(q)
            inverse_2 = inverse * inverse
            inverse_3 = inverse_2 * inverse
            t = d[0] * normal[0:1] + d[1] * normal[1:2] + d[2] * normal[2:3]
            single = t * inverse_3
            coefficients.append(single)
            steep = 3.0 * single * inverse_2
            for a in range(3):
                coefficients.append(steep * d[a] - normal[a : a + 1] * inverse_3)
        whole = jnp.concatenate(coefficients, axis=0)
        upper = whole.astype(bf16)
        lower = (whole - upper.astype(f32)).astype(bf16)
        near = (jnp.abs(lane_x - x) <= 1) & (jnp.abs(lane_y - y) <= 1) & (jnp.abs(lane_z - plane) <= 1)
        picked = jnp.where(near, 0.0, far_both).astype(bf16)
        first = jnp.dot(picked, upper, preferred_element_type=f32)
        second = jnp.dot(picked, lower, preferred_element_type=f32)
        field[pl.ds(pl.multiple_of(slot * 8, 8), 8), :] += first[:8] + first[8:] + second[:8]
        return 0

    lax.fori_loop(0, boxes, far_box, 0)

    def image_box(b, carry):
        _, _, _, _, slot = target_place(centres_s, b)
        lanes = pl.ds(pl.multiple_of(b * per_box, per_box), per_box)
        live = live_row(counts_s, b)
        current = basis_ref[krylov - 1, :, lanes]
        part = field[pl.ds(pl.multiple_of(slot * 8, 8), 8), :]
        image = live * (current - 2.0 * wide_row(contrast_ref, b) * part)
        image_ref[:, lanes] = image
        sums = []
        for m in range(krylov + 1):
            product = image * (basis_ref[m, :, lanes] if m < krylov else image)
            sums.append(carry[m] + product[:, :128] + product[:, 128:])
        return tuple(sums)

    zeros = jnp.zeros((8, 128), f32)
    sums = lax.fori_loop(0, boxes, image_box, (zeros,) * (krylov + 1), unroll=2)
    pairs = [(m, n) for m in range(krylov) for n in range(m + 1)]

    def gram_box(b, carry):
        lanes = pl.ds(pl.multiple_of(b * per_box, per_box), per_box)
        live = live_row(counts_s, b)
        rows = [basis_ref[m, :, lanes] * live for m in range(krylov)]
        out = []
        for k, (m, n) in enumerate(pairs):
            product = rows[m] * rows[n]
            out.append(carry[k] + product[:, :128] + product[:, 128:])
        return tuple(out)

    gram = lax.fori_loop(0, boxes, gram_box, (zeros,) * len(pairs))
    lane = lax.broadcasted_iota(jnp.int32, (8, 128), 1)
    total = zeros
    for k, value in enumerate([*sums, *gram]):
        total = jnp.where(lane == k, jnp.sum(value, axis=1, keepdims=True), total)
    sums_ref[...] = jnp.broadcast_to(total[None], sums_ref.shape)


def two_sum(a, b):
    s = a + b
    c = s - a
    return s, (a - (s - c)) + (b - c)


def halves(a):
    c = a * 4097.0
    high = c - (c - a)
    return high, a - high


def two_product(a, b):
    p = a * b
    a_high, a_low = halves(a)
    b_high, b_low = halves(b)
    return p, ((a_high * b_high - p) + a_high * b_low + a_low * b_high) + a_low * b_low


def finish_kernel(total_facets, counts_s, tiles_ref, image_ref, basis_ref, next_ref, hessenberg_ref):
    boxes = counts_s.shape[0]
    krylov = basis_ref.shape[0]
    lane = lax.broadcasted_iota(jnp.int32, (8, 128), 1)

    def add_tile(i, carry):
        value, error = two_sum(carry[0], tiles_ref[i])
        return value, carry[1] + error

    sums, rest = lax.fori_loop(0, tiles_ref.shape[0], add_tile, (jnp.zeros((8, 128), f32),) * 2, unroll=8)
    exact = sums + rest
    projections = [exact[:, m : m + 1] / total_facets for m in range(krylov)]
    pairs = [(m, n) for m in range(krylov) for n in range(m + 1)]
    first = jnp.where(lane == krylov, 1.0, 0.0)
    second = jnp.where(lane <= krylov, 1.0, 0.0)
    for m in range(krylov):
        first = jnp.where(lane == m, -2.0 * projections[m], first)
    for k, (m, n) in enumerate(pairs):
        at = lane == krylov + 1 + k
        scale = 1.0 if m == n else 2.0
        first = jnp.where(at, scale * projections[m], first)
        second = jnp.where(at, projections[n], second)
    factor, factor_rest = two_product(first, second)
    value, value_rest = two_product(factor, sums)
    value_rest = value_rest + (factor * rest + factor_rest * sums)
    for shift in (64, 32, 16, 8, 4, 2, 1):
        other = pltpu.roll(value, shift, 1)
        other_rest = pltpu.roll(value_rest, shift, 1)
        value, error = two_sum(value, other)
        value_rest = (value_rest + other_rest) + error
    remaining = jnp.maximum(value + value_rest, 0.0)
    norm = jnp.sqrt(remaining / total_facets + epsilon)
    heads = jnp.where(lane == krylov, norm, 0.0)
    for m in range(krylov):
        heads = jnp.where(lane == m, projections[m], heads)
    hessenberg_ref[...] = heads[:, : krylov + 1]
    wide = [jnp.broadcast_to(p, (8, per_box)) for p in projections]
    scale = jnp.concatenate([1.0 / norm] * (per_box // 128), axis=1)

    def one_box(b, _):
        lanes = pl.ds(pl.multiple_of(b * per_box, per_box), per_box)
        live = live_row(counts_s, b)
        sent = wide[0] * basis_ref[0, :, lanes]
        for m in range(1, krylov):
            sent += wide[m] * basis_ref[m, :, lanes]
        next_ref[:, lanes] = (image_ref[:, lanes] - sent * live) * scale
        return 0

    lax.fori_loop(0, boxes, one_box, 0, unroll=4)


smem = pl.BlockSpec(memory_space=pltpu.SMEM)
vmem = pl.BlockSpec(memory_space=pltpu.VMEM)


def on_device(
    basis, facet_centres, normals, areas, contrast, facet_counts, box_centres, near_boxes, far_boxes
):
    krylov, rhs_local, facet_local = basis.shape
    boxes = facet_counts.shape[0]
    count = lax.axis_size("box")
    total_facets = count * facet_local
    areas = areas.reshape(-1, 128)
    contrast = contrast.reshape(-1, 128)
    pack = jax.ShapeDtypeStruct((pack_rows, 128), f32)
    low, high = pl.pallas_call(
        prep_kernel,
        grid=(1,),
        out_shape=(pack, pack),
        in_specs=[
            smem,
            smem,
            pl.BlockSpec((1, rhs_local, facet_local), lambda i: (krylov - 1, 0, 0)),
            vmem,
            vmem,
        ],
        out_specs=(vmem, vmem),
        scratch_shapes=[pltpu.VMEM((2 * pack_rows, 128), f32)],
        name="prepare",
    )(box_centres, facet_counts, basis, facet_centres, areas)
    below = lax.ppermute(high, "box", [(i, i + 1) for i in range(count - 1)])
    above = lax.ppermute(low, "box", [(i + 1, i) for i in range(count - 1)])
    slots = boxes * per_box
    left, right = pl.pallas_call(
        feature_kernel,
        out_shape=(
            jax.ShapeDtypeStruct((slots, depth), bf16),
            jax.ShapeDtypeStruct((boxes * depth, 2 * per_box), bf16),
        ),
        in_specs=[smem] + [vmem] * 3,
        out_specs=(vmem, vmem),
        compiler_params=pltpu.CompilerParams(vmem_limit_bytes=16 * 1024 * 1024),
        name="features",
    )(box_centres, low, high, normals)
    own_field = pl.pallas_call(
        own_kernel,
        out_shape=jax.ShapeDtypeStruct((boxes * 8, per_box), f32),
        in_specs=[vmem] * 4,
        out_specs=vmem,
        compiler_params=pltpu.CompilerParams(vmem_limit_bytes=24 * 1024 * 1024),
        name="own",
    )(low, high, left, right)
    image, tiles = pl.pallas_call(
        halo_kernel,
        out_shape=(
            jax.ShapeDtypeStruct((rhs_local, facet_local), f32),
            jax.ShapeDtypeStruct((count, 8, 128), f32),
        ),
        in_specs=[smem, smem] + [vmem] * 9,
        out_specs=(vmem, vmem),
        scratch_shapes=[
            pltpu.VMEM((slots, depth), bf16),
            pltpu.VMEM((boxes * 8, per_box), f32),
            pltpu.VMEM((9 * 32, 128), f32),
        ],
        compiler_params=pltpu.CompilerParams(vmem_limit_bytes=32 * 1024 * 1024),
        name="halo",
    )(box_centres, facet_counts, below, low, high, above, normals, contrast, basis, right, own_field)
    tiles = lax.all_to_all(tiles, "box", 0, 0, tiled=True)
    next_vector, hessenberg = pl.pallas_call(
        functools.partial(finish_kernel, total_facets),
        out_shape=(
            jax.ShapeDtypeStruct((rhs_local, facet_local), f32),
            jax.ShapeDtypeStruct((rhs_local, krylov + 1), f32),
        ),
        in_specs=[smem] + [vmem] * 3,
        out_specs=(vmem, vmem),
        compiler_params=pltpu.CompilerParams(vmem_limit_bytes=16 * 1024 * 1024),
        name="finish",
    )(facet_counts, tiles, image, basis)
    return next_vector, hessenberg.T


def solution(mesh):
    return jax.shard_map(
        on_device,
        mesh=mesh,
        in_specs=(
            P(None, "rhs", "box"),
            P(None, "box"),
            P(None, "box"),
            P("box"),
            P("box"),
            P("box"),
            P(None, "box"),
            P("box", None),
            P("box", None),
        ),
        out_specs=(P("rhs", "box"), P(None, "rhs")),
        check_vma=False,
    )
```

```python
import functools

import jax
import jax.numpy as jnp
from jax import lax
from jax.experimental import pallas as pl
from jax.experimental.pallas import tpu as pltpu
from jax.sharding import PartitionSpec as P

soften = 0.0025
epsilon = 1e-06
f32 = jnp.float32
bf16 = jnp.bfloat16
box_rows = 24
plane_boxes = 16
per_box = 256
tail = plane_boxes * box_rows
pack_rows = tail + 16
depth = 128


def lattice(centres_s, b):
    x = (centres_s[0, b] + 0.5).astype(jnp.int32)
    y = (centres_s[1, b] + 0.5).astype(jnp.int32)
    z = (centres_s[2, b] + 0.5).astype(jnp.int32)
    return x, y, z


def wide_row(ref, b):
    return jnp.concatenate([ref[pl.ds(2 * b, 1), :], ref[pl.ds(2 * b + 1, 1), :]], axis=1)


def live_row(counts_s, b):
    slots = lax.broadcasted_iota(jnp.int32, (1, per_box), 1)
    return (slots < counts_s[b]).astype(f32)


def prep_kernel(centres_s, counts_s, current_ref, facets_ref, areas_ref, low_ref, high_ref, own_low, own_high, packs):
    boxes = counts_s.shape[0]
    lane = lax.broadcasted_iota(jnp.int32, (8, 128), 1)
    row = lax.broadcasted_iota(jnp.int32, (8, 128), 0)

    def one_box(b, carry):
        moments, centres = carry
        x, y, z = lattice(centres_s, b)
        plane = z & 1
        place = y * 4 + x
        slot = plane * plane_boxes + place
        lanes = pl.ds(pl.multiple_of(b * per_box, per_box), per_box)
        facets = facets_ref[:, lanes]
        live = live_row(counts_s, b)
        weighted = current_ref[0, :, lanes] * (wide_row(areas_ref, b) * live / per_box)
        charges = weighted.astype(bf16).astype(f32)
        start = pl.multiple_of(plane * pack_rows + place * box_rows, 8)
        packs[pl.ds(start, 8), :] = charges[:, :128]
        packs[pl.ds(start + 8, 8), :] = charges[:, 128:]
        packs[pl.ds(start + 16, 8), :] = jnp.concatenate(
            [facets[:, :128], facets[:, 128:], jnp.zeros((2, 128), f32)], axis=0
        )
        moments += jnp.where(lane == slot, jnp.sum(weighted, axis=1, keepdims=True), 0.0)
        for a in range(3):
            dipole = jnp.sum(weighted * (facets[a : a + 1] - centres_s[a, b]), axis=1, keepdims=True)
            moments += jnp.where(lane == 32 * (a + 1) + slot, dipole, 0.0)
            centres += jnp.where((lane == slot) & (row == a), centres_s[a, b], 0.0)
        return moments, centres

    zeros = jnp.zeros((8, 128), f32)
    moments, centres = lax.fori_loop(0, boxes, one_box, (zeros, zeros), unroll=4)
    for ref, first in ((low_ref, 0), (high_ref, pack_rows), (own_low, 0), (own_high, pack_rows)):
        ref[:tail] = packs[first : first + tail]
        ref[tail : tail + 8] = moments
        ref[tail + 8 :] = centres


def thirds(x):
    high = x.astype(bf16).astype(f32)
    rest = x - high
    middle = rest.astype(bf16).astype(f32)
    return high, middle, (rest - middle).astype(bf16).astype(f32)


def stacked_rows(parts, width):
    zeros = jnp.zeros((depth - 8 * len(parts), width), f32)
    return jnp.concatenate([*parts, zeros], axis=0)


def local_facets(pack_ref, place, origin):
    start = pl.multiple_of(place * box_rows + 16, 8)
    tile = pack_ref[pl.ds(start, 8), :]
    both = jnp.concatenate([tile[0:3], tile[3:6]], axis=1)
    return jnp.concatenate([both - origin, jnp.zeros((5, 256), f32)], axis=0)


def slab_origin(centres_s):
    _, _, z = lattice(centres_s, 0)
    base_z = (z - (z & 1)).astype(f32) + 0.5
    axis_row = lax.broadcasted_iota(jnp.int32, (3, 1), 0)
    return jnp.where(axis_row == 2, base_z, 1.5), base_z


def store_source_features(pack, origin, left, columns, first):
    row = lax.broadcasted_iota(jnp.int32, (8, per_box), 0)

    def one_box(place, _):
        local = local_facets(pack, place, origin)
        square = jnp.sum(local * local, axis=0, keepdims=True)
        features = jnp.where(row == 3, square, jnp.where(row == 4, 1.0, local))
        high, middle, low = thirds(features)
        rows = stacked_rows((high, high, high, middle, middle, low, features), per_box)
        start = pl.multiple_of(first + place * per_box, per_box)
        turned = jnp.transpose(rows)
        left[pl.ds(start, per_box), :] = turned.astype(bf16)
        columns[pl.ds(start, per_box), :] = turned
        return 0

    lax.fori_loop(0, plane_boxes, one_box, 0, unroll=2)


def target_place(centres_s, b):
    x, y, z = lattice(centres_s, b)
    plane = z & 1
    place = y * 4 + x
    return x, y, plane, place, plane * plane_boxes + place


def facets_at(low_ref, high_ref, plane, place, origin):
    start = pl.multiple_of(place * box_rows + 16, 8)
    tile = jnp.where(plane == 0, low_ref[pl.ds(start, 8), :], high_ref[pl.ds(start, 8), :])
    return jnp.concatenate([tile[0:3], tile[3:6]], axis=1) - origin


def own_kernel(centres_s, low_ref, high_ref, normals_ref, right, planes, field, left, columns):
    boxes = centres_s.shape[1]
    row = lax.broadcasted_iota(jnp.int32, (8, per_box), 0)
    origin, _ = slab_origin(centres_s)
    store_source_features(low_ref, origin, left, columns, 0)
    store_source_features(high_ref, origin, left, columns, plane_boxes * per_box)

    def target(b, _):
        _, _, plane, place, slot = target_place(centres_s, b)
        local = facets_at(low_ref, high_ref, plane, place, origin)
        normal = normals_ref[:, pl.ds(pl.multiple_of(b * per_box, per_box), per_box)]
        five = jnp.zeros((5, per_box), f32)
        local_8 = jnp.concatenate([local, five], axis=0)
        normal_8 = jnp.concatenate([normal, five], axis=0)
        square = jnp.sum(local_8 * local_8, axis=0, keepdims=True) + soften
        along = jnp.sum(local_8 * normal_8, axis=0, keepdims=True)
        distance = jnp.where(row == 3, 1.0, jnp.where(row == 4, square, -2.0 * local_8))
        high, middle, low = thirds(distance)
        rows = stacked_rows((high, middle, low, high, middle, high), per_box)
        right[pl.ds(pl.multiple_of(slot * depth, depth), depth), :] = rows.astype(bf16)
        planes[pl.ds(pl.multiple_of(slot * 8, 8), 8), :] = jnp.where(row == 3, along, normal_8)
        return 0

    lax.fori_loop(0, boxes, target, 0, unroll=2)
    field[...] = jnp.zeros_like(field)
    for plane in range(2):
        near_plane(low_ref, left, columns, 0, right, planes, plane, field)
        near_plane(high_ref, left, columns, plane_boxes * per_box, right, planes, plane, field)


def near_plane(pack, left, columns, first, right, planes, plane, field):
    def near_rows(item, _):
        target_y = (item + 1) // 3
        source_y = target_y + lax.rem(item + 1, 3) - 1
        source_start = pl.multiple_of(first + source_y * 4 * per_box, per_box)
        charges = []
        spread = []
        for x in range(4):
            start = pl.multiple_of((source_y * 4 + x) * box_rows, 8)
            charges.append(
                jnp.concatenate([pack[pl.ds(start, 8), :], pack[pl.ds(start + 8, 8), :]], axis=1).astype(bf16)
            )
            column = columns[pl.ds(source_start + x * per_box, per_box), :]
            spread.append([jnp.broadcast_to(column[:, 48 + a : 49 + a], (per_box, 128)) for a in range(3)])
        for x in range(4):
            slot = plane * plane_boxes + target_y * 4 + x
            weights = right[pl.ds(pl.multiple_of(slot * depth, depth), depth), :]
            side = planes[pl.ds(pl.multiple_of(slot * 8, 8), 8), :]
            low, high = max(x - 1, 0), min(x + 2, 4)
            facets = left[pl.ds(source_start + low * per_box, (high - low) * per_box), :]
            distance = jnp.dot(facets, weights, preferred_element_type=f32)
            kernels = []
            for source_x in range(low, high):
                begin = (source_x - low) * per_box
                halves_of = []
                for lanes in (slice(0, 128), slice(128, 256)):
                    inverse = lax.rsqrt(distance[begin : begin + per_box, lanes])
                    slope = side[3:4, lanes] - spread[source_x][0] * side[0:1, lanes]
                    slope = slope - spread[source_x][1] * side[1:2, lanes]
                    slope = slope - spread[source_x][2] * side[2:3, lanes]
                    halves_of.append(((slope * inverse) * (inverse * inverse)).astype(bf16))
                kernels.append(jnp.concatenate(halves_of, axis=1))
            row_charges = jnp.concatenate(charges[low:high], axis=1)
            total = jnp.dot(row_charges, jnp.concatenate(kernels, axis=0), preferred_element_type=f32)
            field[pl.ds(pl.multiple_of(slot * 8, 8), 8), :] += total
        return 0

    lax.fori_loop(0, 10, near_rows, 0)


def halo_kernel(
    centres_s, counts_s, prev_ref, low_ref, high_ref, next_ref, normals_ref, contrast_ref, basis_ref, right,
    planes, own_field, image_ref, sums_ref, left, columns, field, far_centres
):
    boxes = counts_s.shape[0]
    krylov = basis_ref.shape[0]
    origin, base_z = slab_origin(centres_s)
    field[...] = own_field[...]
    store_source_features(prev_ref, origin, left, columns, 0)
    store_source_features(next_ref, origin, left, columns, plane_boxes * per_box)
    near_plane(prev_ref, left, columns, 0, right, planes, 0, field)
    near_plane(next_ref, left, columns, plane_boxes * per_box, right, planes, 1, field)

    for group, pack in enumerate((prev_ref, low_ref, next_ref)):
        columns = jnp.transpose(pack[tail + 8 : tail + 16, :])[:32]
        for a in range(3):
            shift = base_z if a == 2 else 1.5
            far_centres[(group * 3 + a) * 32 : (group * 3 + a + 1) * 32, :] = jnp.broadcast_to(
                columns[:, a : a + 1] - shift, (32, 128)
            )
    far_moments = jnp.concatenate([pack[tail : tail + 8, :] for pack in (prev_ref, low_ref, next_ref)], axis=1)
    far_high = far_moments.astype(bf16).astype(f32)
    far_both = jnp.concatenate([far_high, far_moments - far_high], axis=0)
    far_lane = lax.broadcasted_iota(jnp.int32, (1, 384), 1)
    lane_x = far_lane & 3
    lane_y = (far_lane >> 2) & 3
    lane_z = 2 * (far_lane >> 7) - 2 + ((far_lane >> 4) & 1)

    def far_box(b, _):
        x, y, plane, place, slot = target_place(centres_s, b)
        local = facets_at(low_ref, high_ref, plane, place, origin)
        normal = normals_ref[:, pl.ds(pl.multiple_of(b * per_box, per_box), per_box)]
        coefficients = []
        for group in range(3):
            d = []
            for a in range(3):
                centre = far_centres[(group * 3 + a) * 32 : (group * 3 + a + 1) * 32, :]
                d.append(local[a : a + 1] - jnp.concatenate([centre, centre], axis=1))
            q = d[0] * d[0] + d[1] * d[1] + d[2] * d[2] + soften
            inverse = lax.rsqrt(q)
            inverse_2 = inverse * inverse
            inverse_3 = inverse_2 * inverse
            t = d[0] * normal[0:1] + d[1] * normal[1:2] + d[2] * normal[2:3]
            single = t * inverse_3
            coefficients.append(single)
            steep = 3.0 * single * inverse_2
            for a in range(3):
                coefficients.append(steep * d[a] - normal[a : a + 1] * inverse_3)
        whole = jnp.concatenate(coefficients, axis=0)
        upper = whole.astype(bf16)
        lower = (whole - upper.astype(f32)).astype(bf16)
        near = (jnp.abs(lane_x - x) <= 1) & (jnp.abs(lane_y - y) <= 1) & (jnp.abs(lane_z - plane) <= 1)
        picked = jnp.where(near, 0.0, far_both).astype(bf16)
        first = jnp.dot(picked, upper, preferred_element_type=f32)
        second = jnp.dot(picked, lower, preferred_element_type=f32)
        field[pl.ds(pl.multiple_of(slot * 8, 8), 8), :] += first[:8] + first[8:] + second[:8]
        return 0

    lax.fori_loop(0, boxes, far_box, 0)

    def image_box(b, carry):
        _, _, _, _, slot = target_place(centres_s, b)
        lanes = pl.ds(pl.multiple_of(b * per_box, per_box), per_box)
        live = live_row(counts_s, b)
        current = basis_ref[krylov - 1, :, lanes]
        part = field[pl.ds(pl.multiple_of(slot * 8, 8), 8), :]
        image = live * (current - 2.0 * wide_row(contrast_ref, b) * part)
        image_ref[:, lanes] = image
        sums = []
        for m in range(krylov + 1):
            product = image * (basis_ref[m, :, lanes] if m < krylov else image)
            sums.append(carry[m] + product[:, :128] + product[:, 128:])
        return tuple(sums)

    zeros = jnp.zeros((8, 128), f32)
    sums = lax.fori_loop(0, boxes, image_box, (zeros,) * (krylov + 1), unroll=2)
    pairs = [(m, n) for m in range(krylov) for n in range(m + 1)]

    def gram_box(b, carry):
        lanes = pl.ds(pl.multiple_of(b * per_box, per_box), per_box)
        live = live_row(counts_s, b)
        rows = [basis_ref[m, :, lanes] * live for m in range(krylov)]
        out = []
        for k, (m, n) in enumerate(pairs):
            product = rows[m] * rows[n]
            out.append(carry[k] + product[:, :128] + product[:, 128:])
        return tuple(out)

    gram = lax.fori_loop(0, boxes, gram_box, (zeros,) * len(pairs))
    lane = lax.broadcasted_iota(jnp.int32, (8, 128), 1)
    total = zeros
    for k, value in enumerate([*sums, *gram]):
        total = jnp.where(lane == k, jnp.sum(value, axis=1, keepdims=True), total)
    sums_ref[...] = jnp.broadcast_to(total[None], sums_ref.shape)


def two_sum(a, b):
    s = a + b
    c = s - a
    return s, (a - (s - c)) + (b - c)


def halves(a):
    c = a * 4097.0
    high = c - (c - a)
    return high, a - high


def two_product(a, b):
    p = a * b
    a_high, a_low = halves(a)
    b_high, b_low = halves(b)
    return p, ((a_high * b_high - p) + a_high * b_low + a_low * b_high) + a_low * b_low


def finish_kernel(total_facets, counts_s, tiles_ref, image_ref, basis_ref, next_ref, hessenberg_ref):
    boxes = counts_s.shape[0]
    krylov = basis_ref.shape[0]
    lane = lax.broadcasted_iota(jnp.int32, (8, 128), 1)

    def add_tile(i, carry):
        value, error = two_sum(carry[0], tiles_ref[i])
        return value, carry[1] + error

    sums, rest = lax.fori_loop(0, tiles_ref.shape[0], add_tile, (jnp.zeros((8, 128), f32),) * 2, unroll=8)
    exact = sums + rest
    projections = [exact[:, m : m + 1] / total_facets for m in range(krylov)]
    pairs = [(m, n) for m in range(krylov) for n in range(m + 1)]
    first = jnp.where(lane == krylov, 1.0, 0.0)
    second = jnp.where(lane <= krylov, 1.0, 0.0)
    for m in range(krylov):
        first = jnp.where(lane == m, -2.0 * projections[m], first)
    for k, (m, n) in enumerate(pairs):
        at = lane == krylov + 1 + k
        scale = 1.0 if m == n else 2.0
        first = jnp.where(at, scale * projections[m], first)
        second = jnp.where(at, projections[n], second)
    factor, factor_rest = two_product(first, second)
    value, value_rest = two_product(factor, sums)
    value_rest = value_rest + (factor * rest + factor_rest * sums)
    for shift in (64, 32, 16, 8, 4, 2, 1):
        other = pltpu.roll(value, shift, 1)
        other_rest = pltpu.roll(value_rest, shift, 1)
        value, error = two_sum(value, other)
        value_rest = (value_rest + other_rest) + error
    remaining = jnp.maximum(value + value_rest, 0.0)
    norm = jnp.sqrt(remaining / total_facets + epsilon)
    heads = jnp.where(lane == krylov, norm, 0.0)
    for m in range(krylov):
        heads = jnp.where(lane == m, projections[m], heads)
    hessenberg_ref[...] = heads[:, : krylov + 1]
    wide = [jnp.broadcast_to(p, (8, per_box)) for p in projections]
    scale = jnp.concatenate([1.0 / norm] * (per_box // 128), axis=1)

    def one_box(b, _):
        lanes = pl.ds(pl.multiple_of(b * per_box, per_box), per_box)
        live = live_row(counts_s, b)
        sent = wide[0] * basis_ref[0, :, lanes]
        for m in range(1, krylov):
            sent += wide[m] * basis_ref[m, :, lanes]
        next_ref[:, lanes] = (image_ref[:, lanes] - sent * live) * scale
        return 0

    lax.fori_loop(0, boxes, one_box, 0, unroll=4)


smem = pl.BlockSpec(memory_space=pltpu.SMEM)
vmem = pl.BlockSpec(memory_space=pltpu.VMEM)


def on_device(
    basis, facet_centres, normals, areas, contrast, facet_counts, box_centres, near_boxes, far_boxes
):
    krylov, rhs_local, facet_local = basis.shape
    boxes = facet_counts.shape[0]
    count = lax.axis_size("box")
    total_facets = count * facet_local
    areas = areas.reshape(-1, 128)
    contrast = contrast.reshape(-1, 128)
    pack = jax.ShapeDtypeStruct((pack_rows, 128), f32)
    sent_low, sent_high, low, high = pl.pallas_call(
        prep_kernel,
        grid=(1,),
        out_shape=(pack,) * 4,
        in_specs=[
            smem,
            smem,
            pl.BlockSpec((1, rhs_local, facet_local), lambda i: (krylov - 1, 0, 0)),
            vmem,
            vmem,
        ],
        out_specs=(vmem,) * 4,
        scratch_shapes=[pltpu.VMEM((2 * pack_rows, 128), f32)],
        name="prepare",
    )(box_centres, facet_counts, basis, facet_centres, areas)
    below = lax.ppermute(sent_high, "box", [(i, i + 1) for i in range(count - 1)])
    above = lax.ppermute(sent_low, "box", [(i + 1, i) for i in range(count - 1)])
    slots = boxes * per_box
    right, planes, own_field = pl.pallas_call(
        own_kernel,
        out_shape=(
            jax.ShapeDtypeStruct((boxes * depth, per_box), bf16),
            jax.ShapeDtypeStruct((boxes * 8, per_box), f32),
            jax.ShapeDtypeStruct((boxes * 8, per_box), f32),
        ),
        in_specs=[smem] + [vmem] * 3,
        out_specs=(vmem,) * 3,
        scratch_shapes=[pltpu.VMEM((slots, depth), bf16), pltpu.VMEM((slots, depth), f32)],
        compiler_params=pltpu.CompilerParams(vmem_limit_bytes=32 * 1024 * 1024),
        name="own",
    )(box_centres, low, high, normals)
    image, tiles = pl.pallas_call(
        halo_kernel,
        out_shape=(
            jax.ShapeDtypeStruct((rhs_local, facet_local), f32),
            jax.ShapeDtypeStruct((count, 8, 128), f32),
        ),
        in_specs=[smem, smem] + [vmem] * 10,
        out_specs=(vmem, vmem),
        scratch_shapes=[
            pltpu.VMEM((slots, depth), bf16),
            pltpu.VMEM((slots, depth), f32),
            pltpu.VMEM((boxes * 8, per_box), f32),
            pltpu.VMEM((9 * 32, 128), f32),
        ],
        compiler_params=pltpu.CompilerParams(vmem_limit_bytes=32 * 1024 * 1024),
        name="halo",
    )(box_centres, facet_counts, below, low, high, above, normals, contrast, basis, right, planes, own_field)
    tiles = lax.all_to_all(tiles, "box", 0, 0, tiled=True)
    next_vector, hessenberg = pl.pallas_call(
        functools.partial(finish_kernel, total_facets),
        out_shape=(
            jax.ShapeDtypeStruct((rhs_local, facet_local), f32),
            jax.ShapeDtypeStruct((rhs_local, krylov + 1), f32),
        ),
        in_specs=[smem] + [vmem] * 3,
        out_specs=(vmem, vmem),
        compiler_params=pltpu.CompilerParams(vmem_limit_bytes=16 * 1024 * 1024),
        name="finish",
    )(facet_counts, tiles, image, basis)
    return next_vector, hessenberg.T


def solution(mesh):
    return jax.shard_map(
        on_device,
        mesh=mesh,
        in_specs=(
            P(None, "rhs", "box"),
            P(None, "box"),
            P(None, "box"),
            P("box"),
            P("box"),
            P("box"),
            P(None, "box"),
            P("box", None),
            P("box", None),
        ),
        out_specs=(P("rhs", "box"), P(None, "rhs")),
        check_vma=False,
    )
```

```python
import functools

import jax
import jax.numpy as jnp
from jax import lax
from jax.experimental import pallas as pl
from jax.experimental.pallas import tpu as pltpu
from jax.sharding import PartitionSpec as P

soften = 0.0025
epsilon = 1e-06
f32 = jnp.float32
bf16 = jnp.bfloat16
box_rows = 24
plane_boxes = 16
per_box = 256
tail = plane_boxes * box_rows
pack_rows = tail + 16
depth = 128


def lattice(centres_s, b):
    x = (centres_s[0, b] + 0.5).astype(jnp.int32)
    y = (centres_s[1, b] + 0.5).astype(jnp.int32)
    z = (centres_s[2, b] + 0.5).astype(jnp.int32)
    return x, y, z


def wide_row(ref, b):
    return jnp.concatenate([ref[pl.ds(2 * b, 1), :], ref[pl.ds(2 * b + 1, 1), :]], axis=1)


def live_row(counts_s, b):
    slots = lax.broadcasted_iota(jnp.int32, (1, per_box), 1)
    return (slots < counts_s[b]).astype(f32)


def prep_kernel(centres_s, counts_s, current_ref, facets_ref, areas_ref, low_ref, high_ref, own_low, own_high, packs):
    boxes = counts_s.shape[0]
    lane = lax.broadcasted_iota(jnp.int32, (8, 128), 1)
    row = lax.broadcasted_iota(jnp.int32, (8, 128), 0)

    def one_box(b, carry):
        moments, centres = carry
        x, y, z = lattice(centres_s, b)
        plane = z & 1
        place = y * 4 + x
        slot = plane * plane_boxes + place
        lanes = pl.ds(pl.multiple_of(b * per_box, per_box), per_box)
        facets = facets_ref[:, lanes]
        live = live_row(counts_s, b)
        weighted = current_ref[0, :, lanes] * (wide_row(areas_ref, b) * live / per_box)
        charges = weighted.astype(bf16).astype(f32)
        start = pl.multiple_of(plane * pack_rows + place * box_rows, 8)
        packs[pl.ds(start, 8), :] = charges[:, :128]
        packs[pl.ds(start + 8, 8), :] = charges[:, 128:]
        packs[pl.ds(start + 16, 8), :] = jnp.concatenate(
            [facets[:, :128], facets[:, 128:], jnp.zeros((2, 128), f32)], axis=0
        )
        moments += jnp.where(lane == slot, jnp.sum(weighted, axis=1, keepdims=True), 0.0)
        for a in range(3):
            dipole = jnp.sum(weighted * (facets[a : a + 1] - centres_s[a, b]), axis=1, keepdims=True)
            moments += jnp.where(lane == 32 * (a + 1) + slot, dipole, 0.0)
            centres += jnp.where((lane == slot) & (row == a), centres_s[a, b], 0.0)
        return moments, centres

    zeros = jnp.zeros((8, 128), f32)
    moments, centres = lax.fori_loop(0, boxes, one_box, (zeros, zeros), unroll=4)
    for ref, first in ((low_ref, 0), (high_ref, pack_rows), (own_low, 0), (own_high, pack_rows)):
        ref[:tail] = packs[first : first + tail]
        ref[tail : tail + 8] = moments
        ref[tail + 8 :] = centres


def thirds(x):
    high = x.astype(bf16).astype(f32)
    rest = x - high
    middle = rest.astype(bf16).astype(f32)
    return high, middle, (rest - middle).astype(bf16).astype(f32)


def stacked_rows(parts, width):
    zeros = jnp.zeros((depth - 8 * len(parts), width), f32)
    return jnp.concatenate([*parts, zeros], axis=0)


def local_facets(pack_ref, place, origin):
    start = pl.multiple_of(place * box_rows + 16, 8)
    tile = pack_ref[pl.ds(start, 8), :]
    both = jnp.concatenate([tile[0:3], tile[3:6]], axis=1)
    return jnp.concatenate([both - origin, jnp.zeros((5, 256), f32)], axis=0)


def slab_origin(centres_s):
    _, _, z = lattice(centres_s, 0)
    base_z = (z - (z & 1)).astype(f32) + 0.5
    axis_row = lax.broadcasted_iota(jnp.int32, (3, 1), 0)
    return jnp.where(axis_row == 2, base_z, 1.5), base_z


def store_source_features(pack, origin, geometry, strengths, first):
    row = lax.broadcasted_iota(jnp.int32, (8, per_box), 0)

    def one_box(place, _):
        local = local_facets(pack, place, origin)
        square = jnp.sum(local * local, axis=0, keepdims=True)
        features = jnp.where(row == 3, square, jnp.where(row == 4, 1.0, local))
        high, middle, low = thirds(features)
        rows = stacked_rows((high, high, high, middle, middle, low), per_box)
        geometry[pl.ds(pl.multiple_of((first + place) * depth, depth), depth), :] = rows.astype(bf16)
        start = pl.multiple_of(place * box_rows, 8)
        charges = jnp.concatenate([pack[pl.ds(start, 8), :], pack[pl.ds(start + 8, 8), :]], axis=1)
        products = jnp.concatenate([charges] + [charges * local[a : a + 1] for a in range(3)], axis=0)
        rows = jnp.concatenate([*thirds(products), jnp.zeros((32, per_box), f32)], axis=0)
        strengths[pl.ds(pl.multiple_of((first + place) * per_box, per_box), per_box), :] = jnp.transpose(rows).astype(bf16)
        return 0

    lax.fori_loop(0, plane_boxes, one_box, 0, unroll=2)


def target_place(centres_s, b):
    x, y, z = lattice(centres_s, b)
    plane = z & 1
    place = y * 4 + x
    return x, y, plane, place, plane * plane_boxes + place


def facets_at(low_ref, high_ref, plane, place, origin):
    start = pl.multiple_of(place * box_rows + 16, 8)
    tile = jnp.where(plane == 0, low_ref[pl.ds(start, 8), :], high_ref[pl.ds(start, 8), :])
    return jnp.concatenate([tile[0:3], tile[3:6]], axis=1) - origin


def own_kernel(centres_s, low_ref, high_ref, normals_ref, right, planes, field, left, columns):
    boxes = centres_s.shape[1]
    row = lax.broadcasted_iota(jnp.int32, (8, per_box), 0)
    origin, _ = slab_origin(centres_s)
    store_source_features(low_ref, origin, left, columns, 0)
    store_source_features(high_ref, origin, left, columns, plane_boxes * per_box)

    def target(b, _):
        _, _, plane, place, slot = target_place(centres_s, b)
        local = facets_at(low_ref, high_ref, plane, place, origin)
        normal = normals_ref[:, pl.ds(pl.multiple_of(b * per_box, per_box), per_box)]
        five = jnp.zeros((5, per_box), f32)
        local_8 = jnp.concatenate([local, five], axis=0)
        normal_8 = jnp.concatenate([normal, five], axis=0)
        square = jnp.sum(local_8 * local_8, axis=0, keepdims=True) + soften
        along = jnp.sum(local_8 * normal_8, axis=0, keepdims=True)
        distance = jnp.where(row == 3, 1.0, jnp.where(row == 4, square, -2.0 * local_8))
        high, middle, low = thirds(distance)
        rows = stacked_rows((high, middle, low, high, middle, high), per_box)
        right[pl.ds(pl.multiple_of(slot * depth, depth), depth), :] = rows.astype(bf16)
        planes[pl.ds(pl.multiple_of(slot * 8, 8), 8), :] = jnp.where(row == 3, along, normal_8)
        return 0

    lax.fori_loop(0, boxes, target, 0, unroll=2)
    field[...] = jnp.zeros_like(field)
    for plane in range(2):
        near_plane(low_ref, left, columns, 0, right, planes, plane, field)
        near_plane(high_ref, left, columns, plane_boxes * per_box, right, planes, plane, field)


def near_planes(sources, geometry, strengths, targets, total):
    def near_rows(item, _):
        target_y = (item + 1) // 3
        source_y = target_y + lax.rem(item + 1, 3) - 1
        for first, planes in sources:
            for x in range(4):
                box = first + source_y * 4 + x
                low, high = max(x - 1, 0), min(x + 2, 4)
                size = (high - low) * per_box
                starts = [
                    pl.multiple_of((plane * plane_boxes + target_y * 4 + low) * per_box, per_box) for plane in planes
                ]
                facets = jnp.concatenate([targets[pl.ds(start, size), :] for start in starts], axis=0)
                weights = geometry[pl.ds(pl.multiple_of(box * depth, depth), depth), :]
                inverse = lax.rsqrt(jnp.dot(facets, weights, preferred_element_type=f32))
                cubed = (inverse * inverse * inverse).astype(bf16)
                given = strengths[pl.ds(pl.multiple_of(box * per_box, per_box), per_box), :]
                part = jnp.dot(cubed, given, preferred_element_type=f32)
                for k, start in enumerate(starts):
                    total[pl.ds(start, size), :] += part[k * size : (k + 1) * size]
        return 0

    lax.fori_loop(0, 10, near_rows, 0)


def own_kernel(centres_s, low_ref, high_ref, normals_ref, targets, planes, total, geometry, strengths):
    boxes = centres_s.shape[1]
    row = lax.broadcasted_iota(jnp.int32, (8, per_box), 0)
    origin, _ = slab_origin(centres_s)
    store_source_features(low_ref, origin, geometry, strengths, 0)
    store_source_features(high_ref, origin, geometry, strengths, plane_boxes)

    def target(b, _):
        _, _, plane, place, slot = target_place(centres_s, b)
        local = facets_at(low_ref, high_ref, plane, place, origin)
        normal = normals_ref[:, pl.ds(pl.multiple_of(b * per_box, per_box), per_box)]
        five = jnp.zeros((5, per_box), f32)
        local_8 = jnp.concatenate([local, five], axis=0)
        normal_8 = jnp.concatenate([normal, five], axis=0)
        square = jnp.sum(local_8 * local_8, axis=0, keepdims=True) + soften
        along = jnp.sum(local_8 * normal_8, axis=0, keepdims=True)
        distance = jnp.where(row == 3, 1.0, jnp.where(row == 4, square, -2.0 * local_8))
        high, middle, low = thirds(distance)
        rows = stacked_rows((high, middle, low, high, middle, high), per_box)
        start = pl.multiple_of(slot * per_box, per_box)
        targets[pl.ds(start, per_box), :] = jnp.transpose(rows).astype(bf16)
        planes[pl.ds(pl.multiple_of(slot * 8, 8), 8), :] = jnp.where(row == 3, along, normal_8)
        return 0

    lax.fori_loop(0, boxes, target, 0, unroll=2)
    total[...] = jnp.zeros_like(total)
    near_planes(((0, (0, 1)), (plane_boxes, (0, 1))), geometry, strengths, targets, total)


def halo_kernel(
    centres_s, counts_s, prev_ref, low_ref, high_ref, next_ref, normals_ref, contrast_ref, basis_ref, targets,
    planes, own_total, image_ref, sums_ref, geometry, strengths, total, field, far_centres
):
    boxes = counts_s.shape[0]
    krylov = basis_ref.shape[0]
    origin, base_z = slab_origin(centres_s)
    store_source_features(prev_ref, origin, geometry, strengths, 0)
    store_source_features(next_ref, origin, geometry, strengths, plane_boxes)
    total[...] = jnp.zeros_like(total)
    near_planes(((0, (0,)), (plane_boxes, (1,))), geometry, strengths, targets, total)

    def near_field(slot, _):
        rows = pl.ds(pl.multiple_of(slot * per_box, per_box), per_box)
        turned = jnp.transpose(total[rows, :] + own_total[rows, :])
        sums = turned[:32] + (turned[32:64] + turned[64:96])
        side = planes[pl.ds(pl.multiple_of(slot * 8, 8), 8), :]
        value = side[3:4] * sums[:8] - side[0:1] * sums[8:16]
        value = value - side[1:2] * sums[16:24] - side[2:3] * sums[24:32]
        field[pl.ds(pl.multiple_of(slot * 8, 8), 8), :] = value
        return 0

    lax.fori_loop(0, boxes, near_field, 0, unroll=2)

    for group, pack in enumerate((prev_ref, low_ref, next_ref)):
        columns = jnp.transpose(pack[tail + 8 : tail + 16, :])[:32]
        for a in range(3):
            shift = base_z if a == 2 else 1.5
            far_centres[(group * 3 + a) * 32 : (group * 3 + a + 1) * 32, :] = jnp.broadcast_to(
                columns[:, a : a + 1] - shift, (32, 128)
            )
    far_moments = jnp.concatenate([pack[tail : tail + 8, :] for pack in (prev_ref, low_ref, next_ref)], axis=1)
    far_high = far_moments.astype(bf16).astype(f32)
    far_both = jnp.concatenate([far_high, far_moments - far_high], axis=0)
    far_lane = lax.broadcasted_iota(jnp.int32, (1, 384), 1)
    lane_x = far_lane & 3
    lane_y = (far_lane >> 2) & 3
    lane_z = 2 * (far_lane >> 7) - 2 + ((far_lane >> 4) & 1)

    def far_box(b, _):
        x, y, plane, place, slot = target_place(centres_s, b)
        local = facets_at(low_ref, high_ref, plane, place, origin)
        normal = normals_ref[:, pl.ds(pl.multiple_of(b * per_box, per_box), per_box)]
        coefficients = []
        for group in range(3):
            d = []
            for a in range(3):
                centre = far_centres[(group * 3 + a) * 32 : (group * 3 + a + 1) * 32, :]
                d.append(local[a : a + 1] - jnp.concatenate([centre, centre], axis=1))
            q = d[0] * d[0] + d[1] * d[1] + d[2] * d[2] + soften
            inverse = lax.rsqrt(q)
            inverse_2 = inverse * inverse
            inverse_3 = inverse_2 * inverse
            t = d[0] * normal[0:1] + d[1] * normal[1:2] + d[2] * normal[2:3]
            single = t * inverse_3
            coefficients.append(single)
            steep = 3.0 * single * inverse_2
            for a in range(3):
                coefficients.append(steep * d[a] - normal[a : a + 1] * inverse_3)
        whole = jnp.concatenate(coefficients, axis=0)
        upper = whole.astype(bf16)
        lower = (whole - upper.astype(f32)).astype(bf16)
        near = (jnp.abs(lane_x - x) <= 1) & (jnp.abs(lane_y - y) <= 1) & (jnp.abs(lane_z - plane) <= 1)
        picked = jnp.where(near, 0.0, far_both).astype(bf16)
        first = jnp.dot(picked, upper, preferred_element_type=f32)
        second = jnp.dot(picked, lower, preferred_element_type=f32)
        field[pl.ds(pl.multiple_of(slot * 8, 8), 8), :] += first[:8] + first[8:] + second[:8]
        return 0

    lax.fori_loop(0, boxes, far_box, 0)

    def image_box(b, carry):
        _, _, _, _, slot = target_place(centres_s, b)
        lanes = pl.ds(pl.multiple_of(b * per_box, per_box), per_box)
        live = live_row(counts_s, b)
        current = basis_ref[krylov - 1, :, lanes]
        part = field[pl.ds(pl.multiple_of(slot * 8, 8), 8), :]
        image = live * (current - 2.0 * wide_row(contrast_ref, b) * part)
        image_ref[:, lanes] = image
        sums = []
        for m in range(krylov + 1):
            product = image * (basis_ref[m, :, lanes] if m < krylov else image)
            sums.append(carry[m] + product[:, :128] + product[:, 128:])
        return tuple(sums)

    zeros = jnp.zeros((8, 128), f32)
    sums = lax.fori_loop(0, boxes, image_box, (zeros,) * (krylov + 1), unroll=2)
    pairs = [(m, n) for m in range(krylov) for n in range(m + 1)]

    def gram_box(b, carry):
        lanes = pl.ds(pl.multiple_of(b * per_box, per_box), per_box)
        live = live_row(counts_s, b)
        rows = [basis_ref[m, :, lanes] * live for m in range(krylov)]
        out = []
        for k, (m, n) in enumerate(pairs):
            product = rows[m] * rows[n]
            out.append(carry[k] + product[:, :128] + product[:, 128:])
        return tuple(out)

    gram = lax.fori_loop(0, boxes, gram_box, (zeros,) * len(pairs))
    lane = lax.broadcasted_iota(jnp.int32, (8, 128), 1)
    total = zeros
    for k, value in enumerate([*sums, *gram]):
        total = jnp.where(lane == k, jnp.sum(value, axis=1, keepdims=True), total)
    sums_ref[...] = jnp.broadcast_to(total[None], sums_ref.shape)


def two_sum(a, b):
    s = a + b
    c = s - a
    return s, (a - (s - c)) + (b - c)


def halves(a):
    c = a * 4097.0
    high = c - (c - a)
    return high, a - high


def two_product(a, b):
    p = a * b
    a_high, a_low = halves(a)
    b_high, b_low = halves(b)
    return p, ((a_high * b_high - p) + a_high * b_low + a_low * b_high) + a_low * b_low


def finish_kernel(total_facets, counts_s, tiles_ref, image_ref, basis_ref, next_ref, hessenberg_ref):
    boxes = counts_s.shape[0]
    krylov = basis_ref.shape[0]
    lane = lax.broadcasted_iota(jnp.int32, (8, 128), 1)

    def add_tile(i, carry):
        value, error = two_sum(carry[0], tiles_ref[i])
        return value, carry[1] + error

    sums, rest = lax.fori_loop(0, tiles_ref.shape[0], add_tile, (jnp.zeros((8, 128), f32),) * 2, unroll=8)
    exact = sums + rest
    projections = [exact[:, m : m + 1] / total_facets for m in range(krylov)]
    pairs = [(m, n) for m in range(krylov) for n in range(m + 1)]
    first = jnp.where(lane == krylov, 1.0, 0.0)
    second = jnp.where(lane <= krylov, 1.0, 0.0)
    for m in range(krylov):
        first = jnp.where(lane == m, -2.0 * projections[m], first)
    for k, (m, n) in enumerate(pairs):
        at = lane == krylov + 1 + k
        scale = 1.0 if m == n else 2.0
        first = jnp.where(at, scale * projections[m], first)
        second = jnp.where(at, projections[n], second)
    factor, factor_rest = two_product(first, second)
    value, value_rest = two_product(factor, sums)
    value_rest = value_rest + (factor * rest + factor_rest * sums)
    for shift in (64, 32, 16, 8, 4, 2, 1):
        other = pltpu.roll(value, shift, 1)
        other_rest = pltpu.roll(value_rest, shift, 1)
        value, error = two_sum(value, other)
        value_rest = (value_rest + other_rest) + error
    remaining = jnp.maximum(value + value_rest, 0.0)
    norm = jnp.sqrt(remaining / total_facets + epsilon)
    heads = jnp.where(lane == krylov, norm, 0.0)
    for m in range(krylov):
        heads = jnp.where(lane == m, projections[m], heads)
    hessenberg_ref[...] = heads[:, : krylov + 1]
    wide = [jnp.broadcast_to(p, (8, per_box)) for p in projections]
    scale = jnp.concatenate([1.0 / norm] * (per_box // 128), axis=1)

    def one_box(b, _):
        lanes = pl.ds(pl.multiple_of(b * per_box, per_box), per_box)
        live = live_row(counts_s, b)
        sent = wide[0] * basis_ref[0, :, lanes]
        for m in range(1, krylov):
            sent += wide[m] * basis_ref[m, :, lanes]
        next_ref[:, lanes] = (image_ref[:, lanes] - sent * live) * scale
        return 0

    lax.fori_loop(0, boxes, one_box, 0, unroll=4)


smem = pl.BlockSpec(memory_space=pltpu.SMEM)
vmem = pl.BlockSpec(memory_space=pltpu.VMEM)


def on_device(
    basis, facet_centres, normals, areas, contrast, facet_counts, box_centres, near_boxes, far_boxes
):
    krylov, rhs_local, facet_local = basis.shape
    boxes = facet_counts.shape[0]
    count = lax.axis_size("box")
    total_facets = count * facet_local
    areas = areas.reshape(-1, 128)
    contrast = contrast.reshape(-1, 128)
    pack = jax.ShapeDtypeStruct((pack_rows, 128), f32)
    sent_low, sent_high, low, high = pl.pallas_call(
        prep_kernel,
        grid=(1,),
        out_shape=(pack,) * 4,
        in_specs=[
            smem,
            smem,
            pl.BlockSpec((1, rhs_local, facet_local), lambda i: (krylov - 1, 0, 0)),
            vmem,
            vmem,
        ],
        out_specs=(vmem,) * 4,
        scratch_shapes=[pltpu.VMEM((2 * pack_rows, 128), f32)],
        name="prepare",
    )(box_centres, facet_counts, basis, facet_centres, areas)
    below = lax.ppermute(sent_high, "box", [(i, i + 1) for i in range(count - 1)])
    above = lax.ppermute(sent_low, "box", [(i + 1, i) for i in range(count - 1)])
    slots = boxes * per_box
    targets, planes, own_total = pl.pallas_call(
        own_kernel,
        out_shape=(
            jax.ShapeDtypeStruct((slots, depth), bf16),
            jax.ShapeDtypeStruct((boxes * 8, per_box), f32),
            jax.ShapeDtypeStruct((slots, 128), f32),
        ),
        in_specs=[smem] + [vmem] * 3,
        out_specs=(vmem,) * 3,
        scratch_shapes=[pltpu.VMEM((boxes * depth, per_box), bf16), pltpu.VMEM((slots, 128), bf16)],
        compiler_params=pltpu.CompilerParams(vmem_limit_bytes=24 * 1024 * 1024),
        name="own",
    )(box_centres, low, high, normals)
    image, tiles = pl.pallas_call(
        halo_kernel,
        out_shape=(
            jax.ShapeDtypeStruct((rhs_local, facet_local), f32),
            jax.ShapeDtypeStruct((count, 8, 128), f32),
        ),
        in_specs=[smem, smem] + [vmem] * 10,
        out_specs=(vmem, vmem),
        scratch_shapes=[
            pltpu.VMEM((boxes * depth, per_box), bf16),
            pltpu.VMEM((slots, 128), bf16),
            pltpu.VMEM((slots, 128), f32),
            pltpu.VMEM((boxes * 8, per_box), f32),
            pltpu.VMEM((9 * 32, 128), f32),
        ],
        compiler_params=pltpu.CompilerParams(vmem_limit_bytes=32 * 1024 * 1024),
        name="halo",
    )(box_centres, facet_counts, below, low, high, above, normals, contrast, basis, targets, planes, own_total)
    tiles = lax.all_to_all(tiles, "box", 0, 0, tiled=True)
    next_vector, hessenberg = pl.pallas_call(
        functools.partial(finish_kernel, total_facets),
        out_shape=(
            jax.ShapeDtypeStruct((rhs_local, facet_local), f32),
            jax.ShapeDtypeStruct((rhs_local, krylov + 1), f32),
        ),
        in_specs=[smem] + [vmem] * 3,
        out_specs=(vmem, vmem),
        compiler_params=pltpu.CompilerParams(vmem_limit_bytes=16 * 1024 * 1024),
        name="finish",
    )(facet_counts, tiles, image, basis)
    return next_vector, hessenberg.T


def solution(mesh):
    return jax.shard_map(
        on_device,
        mesh=mesh,
        in_specs=(
            P(None, "rhs", "box"),
            P(None, "box"),
            P(None, "box"),
            P("box"),
            P("box"),
            P("box"),
            P(None, "box"),
            P("box", None),
            P("box", None),
        ),
        out_specs=(P("rhs", "box"), P(None, "rhs")),
        check_vma=False,
    )
```

```python
import functools

import jax
import jax.numpy as jnp
from jax import lax
from jax.experimental import pallas as pl
from jax.experimental.pallas import tpu as pltpu
from jax.sharding import PartitionSpec as P

soften = 0.0025
epsilon = 1e-06
f32 = jnp.float32
bf16 = jnp.bfloat16
box_rows = 24
plane_boxes = 16
per_box = 256
tail = plane_boxes * box_rows
pack_rows = tail + 16
depth = 128


def lattice(centres_s, b):
    x = (centres_s[0, b] + 0.5).astype(jnp.int32)
    y = (centres_s[1, b] + 0.5).astype(jnp.int32)
    z = (centres_s[2, b] + 0.5).astype(jnp.int32)
    return x, y, z


def wide_row(ref, b):
    return jnp.concatenate([ref[pl.ds(2 * b, 1), :], ref[pl.ds(2 * b + 1, 1), :]], axis=1)


def live_row(counts_s, b):
    slots = lax.broadcasted_iota(jnp.int32, (1, per_box), 1)
    return (slots < counts_s[b]).astype(f32)


def prep_kernel(centres_s, counts_s, current_ref, facets_ref, areas_ref, low_ref, high_ref, packs):
    boxes = counts_s.shape[0]
    lane = lax.broadcasted_iota(jnp.int32, (8, 128), 1)
    row = lax.broadcasted_iota(jnp.int32, (8, 128), 0)

    def one_box(b, carry):
        moments, centres = carry
        x, y, z = lattice(centres_s, b)
        plane = z & 1
        place = y * 4 + x
        slot = plane * plane_boxes + place
        lanes = pl.ds(pl.multiple_of(b * per_box, per_box), per_box)
        facets = facets_ref[:, lanes]
        live = live_row(counts_s, b)
        weighted = current_ref[0, :, lanes] * (wide_row(areas_ref, b) * live / per_box)
        charges = weighted.astype(bf16).astype(f32)
        start = pl.multiple_of(plane * pack_rows + place * box_rows, 8)
        packs[pl.ds(start, 8), :] = charges[:, :128]
        packs[pl.ds(start + 8, 8), :] = charges[:, 128:]
        packs[pl.ds(start + 16, 8), :] = jnp.concatenate(
            [facets[:, :128], facets[:, 128:], jnp.zeros((2, 128), f32)], axis=0
        )
        moments += jnp.where(lane == slot, jnp.sum(weighted, axis=1, keepdims=True), 0.0)
        for a in range(3):
            dipole = jnp.sum(weighted * (facets[a : a + 1] - centres_s[a, b]), axis=1, keepdims=True)
            moments += jnp.where(lane == 32 * (a + 1) + slot, dipole, 0.0)
            centres += jnp.where((lane == slot) & (row == a), centres_s[a, b], 0.0)
        return moments, centres

    zeros = jnp.zeros((8, 128), f32)
    moments, centres = lax.fori_loop(0, boxes, one_box, (zeros, zeros), unroll=4)
    for ref, first in ((low_ref, 0), (high_ref, pack_rows)):
        ref[:tail] = packs[first : first + tail]
        ref[tail : tail + 8] = moments
        ref[tail + 8 :] = centres


def thirds(x):
    high = x.astype(bf16).astype(f32)
    rest = x - high
    middle = rest.astype(bf16).astype(f32)
    return high, middle, (rest - middle).astype(bf16).astype(f32)


def stacked_rows(parts, width):
    zeros = jnp.zeros((depth - 8 * len(parts), width), f32)
    return jnp.concatenate([*parts, zeros], axis=0)


def local_facets(pack_ref, place, origin):
    start = pl.multiple_of(place * box_rows + 16, 8)
    tile = pack_ref[pl.ds(start, 8), :]
    both = jnp.concatenate([tile[0:3], tile[3:6]], axis=1)
    return jnp.concatenate([both - origin, jnp.zeros((5, 256), f32)], axis=0)


def slab_origin(centres_s):
    _, _, z = lattice(centres_s, 0)
    base_z = (z - (z & 1)).astype(f32) + 0.5
    axis_row = lax.broadcasted_iota(jnp.int32, (3, 1), 0)
    return jnp.where(axis_row == 2, base_z, 1.5), base_z


def store_source_features(pack, origin, geometry, strengths, first):
    row = lax.broadcasted_iota(jnp.int32, (8, per_box), 0)

    def one_box(place, _):
        local = local_facets(pack, place, origin)
        square = jnp.sum(local * local, axis=0, keepdims=True)
        features = jnp.where(row == 3, square, jnp.where(row == 4, 1.0, local))
        high, middle, low = thirds(features)
        rows = stacked_rows((high, high, high, middle, middle, low), per_box)
        geometry[pl.ds(pl.multiple_of((first + place) * depth, depth), depth), :] = rows.astype(bf16)
        start = pl.multiple_of(place * box_rows, 8)
        charges = jnp.concatenate([pack[pl.ds(start, 8), :], pack[pl.ds(start + 8, 8), :]], axis=1)
        products = jnp.concatenate([charges] + [charges * local[a : a + 1] for a in range(3)], axis=0)
        rows = jnp.concatenate([*thirds(products), jnp.zeros((32, per_box), f32)], axis=0)
        strengths[pl.ds(pl.multiple_of((first + place) * per_box, per_box), per_box), :] = jnp.transpose(rows).astype(bf16)
        return 0

    lax.fori_loop(0, plane_boxes, one_box, 0, unroll=2)


def target_place(centres_s, b):
    x, y, z = lattice(centres_s, b)
    plane = z & 1
    place = y * 4 + x
    return x, y, plane, place, plane * plane_boxes + place


def facets_at(low_ref, high_ref, plane, place, origin):
    start = pl.multiple_of(place * box_rows + 16, 8)
    tile = jnp.where(plane == 0, low_ref[pl.ds(start, 8), :], high_ref[pl.ds(start, 8), :])
    return jnp.concatenate([tile[0:3], tile[3:6]], axis=1) - origin


def own_kernel(centres_s, low_ref, high_ref, normals_ref, right, planes, field, left, columns):
    boxes = centres_s.shape[1]
    row = lax.broadcasted_iota(jnp.int32, (8, per_box), 0)
    origin, _ = slab_origin(centres_s)
    store_source_features(low_ref, origin, left, columns, 0)
    store_source_features(high_ref, origin, left, columns, plane_boxes * per_box)

    def target(b, _):
        _, _, plane, place, slot = target_place(centres_s, b)
        local = facets_at(low_ref, high_ref, plane, place, origin)
        normal = normals_ref[:, pl.ds(pl.multiple_of(b * per_box, per_box), per_box)]
        five = jnp.zeros((5, per_box), f32)
        local_8 = jnp.concatenate([local, five], axis=0)
        normal_8 = jnp.concatenate([normal, five], axis=0)
        square = jnp.sum(local_8 * local_8, axis=0, keepdims=True) + soften
        along = jnp.sum(local_8 * normal_8, axis=0, keepdims=True)
        distance = jnp.where(row == 3, 1.0, jnp.where(row == 4, square, -2.0 * local_8))
        high, middle, low = thirds(distance)
        rows = stacked_rows((high, middle, low, high, middle, high), per_box)
        right[pl.ds(pl.multiple_of(slot * depth, depth), depth), :] = rows.astype(bf16)
        planes[pl.ds(pl.multiple_of(slot * 8, 8), 8), :] = jnp.where(row == 3, along, normal_8)
        return 0

    lax.fori_loop(0, boxes, target, 0, unroll=2)
    field[...] = jnp.zeros_like(field)
    for plane in range(2):
        near_plane(low_ref, left, columns, 0, right, planes, plane, field)
        near_plane(high_ref, left, columns, plane_boxes * per_box, right, planes, plane, field)


def near_planes(sources, geometry, strengths, targets, total):
    def source_row(source_y, target_y, rows):
        for first, planes in sources:
            for x in range(4):
                box = first + source_y * 4 + x
                low, high = max(x - 1, 0), min(x + 2, 4)
                size = (high - low) * per_box
                starts = [
                    pl.multiple_of((plane * plane_boxes + (target_y + k) * 4 + low) * per_box, per_box)
                    for plane in planes
                    for k in range(rows)
                ]
                facets = jnp.concatenate([targets[pl.ds(start, size), :] for start in starts], axis=0)
                weights = geometry[pl.ds(pl.multiple_of(box * depth, depth), depth), :]
                inverse = lax.rsqrt(jnp.dot(facets, weights, preferred_element_type=f32))
                cubed = (inverse * inverse * inverse).astype(bf16)
                given = strengths[pl.ds(pl.multiple_of(box * per_box, per_box), per_box), :]
                part = jnp.dot(cubed, given, preferred_element_type=f32)
                for k, start in enumerate(starts):
                    total[pl.ds(start, size), :] += part[k * size : (k + 1) * size]

    def outer(i, _):
        source_row(3 * i, 2 * i, 2)
        return 0

    def inner(i, _):
        source_row(i + 1, i, 3)
        return 0

    lax.fori_loop(0, 2, outer, 0)
    lax.fori_loop(0, 2, inner, 0)


def own_kernel(centres_s, low_ref, high_ref, normals_ref, right, planes, field, left, columns):
    boxes = centres_s.shape[1]
    row = lax.broadcasted_iota(jnp.int32, (8, per_box), 0)
    origin, _ = slab_origin(centres_s)
    store_source_features(low_ref, origin, left, columns, 0)
    store_source_features(high_ref, origin, left, columns, plane_boxes * per_box)

    def target(b, _):
        _, _, plane, place, slot = target_place(centres_s, b)
        local = facets_at(low_ref, high_ref, plane, place, origin)
        normal = normals_ref[:, pl.ds(pl.multiple_of(b * per_box, per_box), per_box)]
        five = jnp.zeros((5, per_box), f32)
        local_8 = jnp.concatenate([local, five], axis=0)
        normal_8 = jnp.concatenate([normal, five], axis=0)
        square = jnp.sum(local_8 * local_8, axis=0, keepdims=True) + soften
        along = jnp.sum(local_8 * normal_8, axis=0, keepdims=True)
        distance = jnp.where(row == 3, 1.0, jnp.where(row == 4, square, -2.0 * local_8))
        high, middle, low = thirds(distance)
        rows = stacked_rows((high, middle, low, high, middle, high), per_box)
        right[pl.ds(pl.multiple_of(slot * depth, depth), depth), :] = rows.astype(bf16)
        planes[pl.ds(pl.multiple_of(slot * 8, 8), 8), :] = jnp.where(row == 3, along, normal_8)
        return 0

    lax.fori_loop(0, boxes, target, 0, unroll=2)
    field[...] = jnp.zeros_like(field)
    for plane in range(2):
        near_plane(low_ref, left, columns, 0, right, planes, plane, field)
        near_plane(high_ref, left, columns, plane_boxes * per_box, right, planes, plane, field)


def near_planes(sources, geometry, strengths, targets, total):
    def near_rows(item, _):
        target_y = (item + 1) // 3
        source_y = target_y + lax.rem(item + 1, 3) - 1
        for first, planes in sources:
            for x in range(4):
                box = first + source_y * 4 + x
                low, high = max(x - 1, 0), min(x + 2, 4)
                size = (high - low) * per_box
                starts = [
                    pl.multiple_of((plane * plane_boxes + target_y * 4 + low) * per_box, per_box) for plane in planes
                ]
                facets = jnp.concatenate([targets[pl.ds(start, size), :] for start in starts], axis=0)
                weights = geometry[pl.ds(pl.multiple_of(box * depth, depth), depth), :]
                inverse = lax.rsqrt(jnp.dot(facets, weights, preferred_element_type=f32))
                cubed = (inverse * inverse * inverse).astype(bf16)
                given = strengths[pl.ds(pl.multiple_of(box * per_box, per_box), per_box), :]
                part = jnp.dot(cubed, given, preferred_element_type=f32)
                for k, start in enumerate(starts):
                    total[pl.ds(start, size), :] += part[k * size : (k + 1) * size]
        return 0

    lax.fori_loop(0, 10, near_rows, 0)


def own_kernel(centres_s, low_ref, high_ref, normals_ref, targets, planes, total, geometry, strengths):
    boxes = centres_s.shape[1]
    row = lax.broadcasted_iota(jnp.int32, (8, per_box), 0)
    origin, _ = slab_origin(centres_s)
    store_source_features(low_ref, origin, geometry, strengths, 0)
    store_source_features(high_ref, origin, geometry, strengths, plane_boxes)

    def target(b, _):
        _, _, plane, place, slot = target_place(centres_s, b)
        local = facets_at(low_ref, high_ref, plane, place, origin)
        normal = normals_ref[:, pl.ds(pl.multiple_of(b * per_box, per_box), per_box)]
        five = jnp.zeros((5, per_box), f32)
        local_8 = jnp.concatenate([local, five], axis=0)
        normal_8 = jnp.concatenate([normal, five], axis=0)
        square = jnp.sum(local_8 * local_8, axis=0, keepdims=True) + soften
        along = jnp.sum(local_8 * normal_8, axis=0, keepdims=True)
        distance = jnp.where(row == 3, 1.0, jnp.where(row == 4, square, -2.0 * local_8))
        high, middle, low = thirds(distance)
        rows = stacked_rows((high, middle, low, high, middle, high), per_box)
        start = pl.multiple_of(slot * per_box, per_box)
        targets[pl.ds(start, per_box), :] = jnp.transpose(rows).astype(bf16)
        planes[pl.ds(pl.multiple_of(slot * 8, 8), 8), :] = jnp.where(row == 3, along, normal_8)
        return 0

    lax.fori_loop(0, boxes, target, 0, unroll=2)
    total[...] = jnp.zeros_like(total)
    near_planes(((0, (0, 1)), (plane_boxes, (0, 1))), geometry, strengths, targets, total)


def halo_kernel(
    centres_s, counts_s, prev_ref, low_ref, high_ref, next_ref, normals_ref, contrast_ref, basis_ref, targets,
    planes, own_total, image_ref, sums_ref, geometry, strengths, total, field, far_centres
):
    boxes = counts_s.shape[0]
    krylov = basis_ref.shape[0]
    origin, base_z = slab_origin(centres_s)
    store_source_features(prev_ref, origin, geometry, strengths, 0)
    store_source_features(next_ref, origin, geometry, strengths, plane_boxes)
    total[...] = jnp.zeros_like(total)
    near_planes(((0, (0,)), (plane_boxes, (1,))), geometry, strengths, targets, total)

    def near_field(slot, _):
        rows = pl.ds(pl.multiple_of(slot * per_box, per_box), per_box)
        turned = jnp.transpose(total[rows, :] + own_total[rows, :])
        sums = turned[:32] + (turned[32:64] + turned[64:96])
        side = planes[pl.ds(pl.multiple_of(slot * 8, 8), 8), :]
        value = side[3:4] * sums[:8] - side[0:1] * sums[8:16]
        value = value - side[1:2] * sums[16:24] - side[2:3] * sums[24:32]
        field[pl.ds(pl.multiple_of(slot * 8, 8), 8), :] = value
        return 0

    lax.fori_loop(0, boxes, near_field, 0, unroll=2)

    for group, pack in enumerate((prev_ref, low_ref, next_ref)):
        columns = jnp.transpose(pack[tail + 8 : tail + 16, :])[:32]
        for a in range(3):
            shift = base_z if a == 2 else 1.5
            far_centres[(group * 3 + a) * 32 : (group * 3 + a + 1) * 32, :] = jnp.broadcast_to(
                columns[:, a : a + 1] - shift, (32, 128)
            )
    far_moments = jnp.concatenate([pack[tail : tail + 8, :] for pack in (prev_ref, low_ref, next_ref)], axis=1)
    far_high = far_moments.astype(bf16).astype(f32)
    far_both = jnp.concatenate([far_high, far_moments - far_high], axis=0)
    far_lane = lax.broadcasted_iota(jnp.int32, (1, 384), 1)
    lane_x = far_lane & 3
    lane_y = (far_lane >> 2) & 3
    lane_z = 2 * (far_lane >> 7) - 2 + ((far_lane >> 4) & 1)

    def far_box(b, _):
        x, y, plane, place, slot = target_place(centres_s, b)
        local = facets_at(low_ref, high_ref, plane, place, origin)
        normal = normals_ref[:, pl.ds(pl.multiple_of(b * per_box, per_box), per_box)]
        coefficients = []
        for group in range(3):
            d = []
            for a in range(3):
                centre = far_centres[(group * 3 + a) * 32 : (group * 3 + a + 1) * 32, :]
                d.append(local[a : a + 1] - jnp.concatenate([centre, centre], axis=1))
            q = d[0] * d[0] + d[1] * d[1] + d[2] * d[2] + soften
            inverse = lax.rsqrt(q)
            inverse_2 = inverse * inverse
            inverse_3 = inverse_2 * inverse
            t = d[0] * normal[0:1] + d[1] * normal[1:2] + d[2] * normal[2:3]
            single = t * inverse_3
            coefficients.append(single)
            steep = 3.0 * single * inverse_2
            for a in range(3):
                coefficients.append(steep * d[a] - normal[a : a + 1] * inverse_3)
        whole = jnp.concatenate(coefficients, axis=0)
        upper = whole.astype(bf16)
        lower = (whole - upper.astype(f32)).astype(bf16)
        near = (jnp.abs(lane_x - x) <= 1) & (jnp.abs(lane_y - y) <= 1) & (jnp.abs(lane_z - plane) <= 1)
        picked = jnp.where(near, 0.0, far_both).astype(bf16)
        first = jnp.dot(picked, upper, preferred_element_type=f32)
        second = jnp.dot(picked, lower, preferred_element_type=f32)
        field[pl.ds(pl.multiple_of(slot * 8, 8), 8), :] += first[:8] + first[8:] + second[:8]
        return 0

    lax.fori_loop(0, boxes, far_box, 0, unroll=2)

    def image_box(b, carry):
        _, _, _, _, slot = target_place(centres_s, b)
        lanes = pl.ds(pl.multiple_of(b * per_box, per_box), per_box)
        live = live_row(counts_s, b)
        current = basis_ref[krylov - 1, :, lanes]
        part = field[pl.ds(pl.multiple_of(slot * 8, 8), 8), :]
        image = live * (current - 2.0 * wide_row(contrast_ref, b) * part)
        image_ref[:, lanes] = image
        sums = []
        for m in range(krylov + 1):
            product = image * (basis_ref[m, :, lanes] if m < krylov else image)
            sums.append(carry[m] + product[:, :128] + product[:, 128:])
        return tuple(sums)

    zeros = jnp.zeros((8, 128), f32)
    sums = lax.fori_loop(0, boxes, image_box, (zeros,) * (krylov + 1), unroll=2)
    pairs = [(m, n) for m in range(krylov) for n in range(m + 1)]

    def gram_box(b, carry):
        lanes = pl.ds(pl.multiple_of(b * per_box, per_box), per_box)
        live = live_row(counts_s, b)
        rows = [basis_ref[m, :, lanes] * live for m in range(krylov)]
        out = []
        for k, (m, n) in enumerate(pairs):
            product = rows[m] * rows[n]
            out.append(carry[k] + product[:, :128] + product[:, 128:])
        return tuple(out)

    gram = lax.fori_loop(0, boxes, gram_box, (zeros,) * len(pairs))
    lane = lax.broadcasted_iota(jnp.int32, (8, 128), 1)
    total = zeros
    for k, value in enumerate([*sums, *gram]):
        total = jnp.where(lane == k, jnp.sum(value, axis=1, keepdims=True), total)
    sums_ref[...] = jnp.broadcast_to(total[None], sums_ref.shape)


def two_sum(a, b):
    s = a + b
    c = s - a
    return s, (a - (s - c)) + (b - c)


def halves(a):
    c = a * 4097.0
    high = c - (c - a)
    return high, a - high


def two_product(a, b):
    p = a * b
    a_high, a_low = halves(a)
    b_high, b_low = halves(b)
    return p, ((a_high * b_high - p) + a_high * b_low + a_low * b_high) + a_low * b_low


def finish_kernel(total_facets, counts_s, tiles_ref, image_ref, basis_ref, next_ref, hessenberg_ref):
    boxes = counts_s.shape[0]
    krylov = basis_ref.shape[0]
    lane = lax.broadcasted_iota(jnp.int32, (8, 128), 1)

    def add_tile(i, carry):
        value, error = two_sum(carry[0], tiles_ref[i])
        return value, carry[1] + error

    sums, rest = lax.fori_loop(0, tiles_ref.shape[0], add_tile, (jnp.zeros((8, 128), f32),) * 2, unroll=8)
    exact = sums + rest
    projections = [exact[:, m : m + 1] / total_facets for m in range(krylov)]
    pairs = [(m, n) for m in range(krylov) for n in range(m + 1)]
    first = jnp.where(lane == krylov, 1.0, 0.0)
    second = jnp.where(lane <= krylov, 1.0, 0.0)
    for m in range(krylov):
        first = jnp.where(lane == m, -2.0 * projections[m], first)
    for k, (m, n) in enumerate(pairs):
        at = lane == krylov + 1 + k
        scale = 1.0 if m == n else 2.0
        first = jnp.where(at, scale * projections[m], first)
        second = jnp.where(at, projections[n], second)
    factor, factor_rest = two_product(first, second)
    value, value_rest = two_product(factor, sums)
    value_rest = value_rest + (factor * rest + factor_rest * sums)
    for shift in (64, 32, 16, 8, 4, 2, 1):
        other = pltpu.roll(value, shift, 1)
        other_rest = pltpu.roll(value_rest, shift, 1)
        value, error = two_sum(value, other)
        value_rest = (value_rest + other_rest) + error
    remaining = jnp.maximum(value + value_rest, 0.0)
    norm = jnp.sqrt(remaining / total_facets + epsilon)
    heads = jnp.where(lane == krylov, norm, 0.0)
    for m in range(krylov):
        heads = jnp.where(lane == m, projections[m], heads)
    hessenberg_ref[...] = heads[:, : krylov + 1]
    wide = [jnp.broadcast_to(p, (8, per_box)) for p in projections]
    scale = jnp.concatenate([1.0 / norm] * (per_box // 128), axis=1)

    def one_box(b, _):
        lanes = pl.ds(pl.multiple_of(b * per_box, per_box), per_box)
        live = live_row(counts_s, b)
        sent = wide[0] * basis_ref[0, :, lanes]
        for m in range(1, krylov):
            sent += wide[m] * basis_ref[m, :, lanes]
        next_ref[:, lanes] = (image_ref[:, lanes] - sent * live) * scale
        return 0

    lax.fori_loop(0, boxes, one_box, 0, unroll=4)


smem = pl.BlockSpec(memory_space=pltpu.SMEM)
vmem = pl.BlockSpec(memory_space=pltpu.VMEM)


def on_device(
    basis, facet_centres, normals, areas, contrast, facet_counts, box_centres, near_boxes, far_boxes
):
    krylov, rhs_local, facet_local = basis.shape
    boxes = facet_counts.shape[0]
    count = lax.axis_size("box")
    total_facets = count * facet_local
    areas = areas.reshape(-1, 128)
    contrast = contrast.reshape(-1, 128)
    pack = jax.ShapeDtypeStruct((pack_rows, 128), f32)
    low, high = pl.pallas_call(
        prep_kernel,
        grid=(1,),
        out_shape=(pack, pack),
        in_specs=[
            smem,
            smem,
            pl.BlockSpec((1, rhs_local, facet_local), lambda i: (krylov - 1, 0, 0)),
            vmem,
            vmem,
        ],
        out_specs=(vmem, vmem),
        scratch_shapes=[pltpu.VMEM((2 * pack_rows, 128), f32)],
        compiler_params=pltpu.CompilerParams(vmem_limit_bytes=8 * 1024 * 1024),
        name="prepare",
    )(box_centres, facet_counts, basis, facet_centres, areas)
    below = lax.ppermute(high, "box", [(i, i + 1) for i in range(count - 1)])
    above = lax.ppermute(low, "box", [(i + 1, i) for i in range(count - 1)])
    slots = boxes * per_box
    targets, planes, own_total = pl.pallas_call(
        own_kernel,
        out_shape=(
            jax.ShapeDtypeStruct((slots, depth), bf16),
            jax.ShapeDtypeStruct((boxes * 8, per_box), f32),
            jax.ShapeDtypeStruct((slots, 128), f32),
        ),
        in_specs=[smem] + [vmem] * 3,
        out_specs=(vmem,) * 3,
        scratch_shapes=[pltpu.VMEM((boxes * depth, per_box), bf16), pltpu.VMEM((slots, 128), bf16)],
        compiler_params=pltpu.CompilerParams(vmem_limit_bytes=24 * 1024 * 1024),
        name="own",
    )(box_centres, low, high, normals)
    image, tiles = pl.pallas_call(
        halo_kernel,
        out_shape=(
            jax.ShapeDtypeStruct((rhs_local, facet_local), f32),
            jax.ShapeDtypeStruct((count, 8, 128), f32),
        ),
        in_specs=[smem, smem] + [vmem] * 10,
        out_specs=(vmem, vmem),
        scratch_shapes=[
            pltpu.VMEM((boxes * depth, per_box), bf16),
            pltpu.VMEM((slots, 128), bf16),
            pltpu.VMEM((slots, 128), f32),
            pltpu.VMEM((boxes * 8, per_box), f32),
            pltpu.VMEM((9 * 32, 128), f32),
        ],
        compiler_params=pltpu.CompilerParams(vmem_limit_bytes=32 * 1024 * 1024),
        name="halo",
    )(box_centres, facet_counts, below, low, high, above, normals, contrast, basis, targets, planes, own_total)
    tiles = lax.all_to_all(tiles, "box", 0, 0, tiled=True)
    next_vector, hessenberg = pl.pallas_call(
        functools.partial(finish_kernel, total_facets),
        out_shape=(
            jax.ShapeDtypeStruct((rhs_local, facet_local), f32),
            jax.ShapeDtypeStruct((rhs_local, krylov + 1), f32),
        ),
        in_specs=[smem] + [vmem] * 3,
        out_specs=(vmem, vmem),
        compiler_params=pltpu.CompilerParams(vmem_limit_bytes=16 * 1024 * 1024),
        name="finish",
    )(facet_counts, tiles, image, basis)
    return next_vector, hessenberg.T


def solution(mesh):
    return jax.shard_map(
        on_device,
        mesh=mesh,
        in_specs=(
            P(None, "rhs", "box"),
            P(None, "box"),
            P(None, "box"),
            P("box"),
            P("box"),
            P("box"),
            P(None, "box"),
            P("box", None),
            P("box", None),
        ),
        out_specs=(P("rhs", "box"), P(None, "rhs")),
        check_vma=False,
    )
```

```python
import functools

import jax
import jax.numpy as jnp
from jax import lax
from jax.experimental import pallas as pl
from jax.experimental.pallas import tpu as pltpu
from jax.sharding import PartitionSpec as P

soften = 0.0025
epsilon = 1e-06
f32 = jnp.float32
bf16 = jnp.bfloat16
box_rows = 24
plane_boxes = 16
per_box = 256
tail = plane_boxes * box_rows
pack_rows = tail + 16
depth = 128


def lattice(centres_s, b):
    x = (centres_s[0, b] + 0.5).astype(jnp.int32)
    y = (centres_s[1, b] + 0.5).astype(jnp.int32)
    z = (centres_s[2, b] + 0.5).astype(jnp.int32)
    return x, y, z


def wide_row(ref, b):
    return jnp.concatenate([ref[pl.ds(2 * b, 1), :], ref[pl.ds(2 * b + 1, 1), :]], axis=1)


def live_row(counts_s, b):
    slots = lax.broadcasted_iota(jnp.int32, (1, per_box), 1)
    return (slots < counts_s[b]).astype(f32)


def prep_kernel(
    centres_h, counts_h, basis_h, facets_h, areas_h, low_ref, high_ref,
    packs, centres_s, counts_s, current_ref, facets_ref, areas_ref, arrived
):
    boxes = counts_s.shape[0]
    moves = [
        (basis_h.at[basis_h.shape[0] - 1], current_ref),
        (facets_h, facets_ref),
        (areas_h, areas_ref),
        (centres_h, centres_s),
        (counts_h, counts_s),
    ]
    copies = [pltpu.make_async_copy(a, b, arrived.at[k]) for k, (a, b) in enumerate(moves)]
    for copy in copies:
        copy.start()
    for copy in copies:
        copy.wait()
    lane = lax.broadcasted_iota(jnp.int32, (8, 128), 1)
    row = lax.broadcasted_iota(jnp.int32, (8, 128), 0)

    def one_box(b, carry):
        moments, centres = carry
        x, y, z = lattice(centres_s, b)
        plane = z & 1
        place = y * 4 + x
        slot = plane * plane_boxes + place
        lanes = pl.ds(pl.multiple_of(b * per_box, per_box), per_box)
        facets = facets_ref[:, lanes]
        live = live_row(counts_s, b)
        weighted = current_ref[:, lanes] * (wide_row(areas_ref, b) * live / per_box)
        charges = weighted.astype(bf16).astype(f32)
        start = pl.multiple_of(plane * pack_rows + place * box_rows, 8)
        packs[pl.ds(start, 8), :] = charges[:, :128]
        packs[pl.ds(start + 8, 8), :] = charges[:, 128:]
        packs[pl.ds(start + 16, 8), :] = jnp.concatenate(
            [facets[:, :128], facets[:, 128:], jnp.zeros((2, 128), f32)], axis=0
        )
        moments += jnp.where(lane == slot, jnp.sum(weighted, axis=1, keepdims=True), 0.0)
        for a in range(3):
            dipole = jnp.sum(weighted * (facets[a : a + 1] - centres_s[a, b]), axis=1, keepdims=True)
            moments += jnp.where(lane == 32 * (a + 1) + slot, dipole, 0.0)
            centres += jnp.where((lane == slot) & (row == a), centres_s[a, b], 0.0)
        return moments, centres

    zeros = jnp.zeros((8, 128), f32)
    moments, centres = lax.fori_loop(0, boxes, one_box, (zeros, zeros), unroll=4)
    for ref, first in ((low_ref, 0), (high_ref, pack_rows)):
        ref[:tail] = packs[first : first + tail]
        ref[tail : tail + 8] = moments
        ref[tail + 8 :] = centres


def thirds(x):
    high = x.astype(bf16).astype(f32)
    rest = x - high
    middle = rest.astype(bf16).astype(f32)
    return high, middle, (rest - middle).astype(bf16).astype(f32)


def stacked_rows(parts, width):
    zeros = jnp.zeros((depth - 8 * len(parts), width), f32)
    return jnp.concatenate([*parts, zeros], axis=0)


def local_facets(pack_ref, place, origin):
    start = pl.multiple_of(place * box_rows + 16, 8)
    tile = pack_ref[pl.ds(start, 8), :]
    both = jnp.concatenate([tile[0:3], tile[3:6]], axis=1)
    return jnp.concatenate([both - origin, jnp.zeros((5, 256), f32)], axis=0)


def slab_origin(centres_s):
    _, _, z = lattice(centres_s, 0)
    base_z = (z - (z & 1)).astype(f32) + 0.5
    axis_row = lax.broadcasted_iota(jnp.int32, (3, 1), 0)
    return jnp.where(axis_row == 2, base_z, 1.5), base_z


def store_source_features(pack, origin, geometry, strengths, first):
    row = lax.broadcasted_iota(jnp.int32, (8, per_box), 0)

    def one_box(place, _):
        local = local_facets(pack, place, origin)
        square = jnp.sum(local * local, axis=0, keepdims=True)
        features = jnp.where(row == 3, square, jnp.where(row == 4, 1.0, local))
        high, middle, low = thirds(features)
        rows = stacked_rows((high, high, high, middle, middle, low), per_box)
        geometry[pl.ds(pl.multiple_of((first + place) * depth, depth), depth), :] = rows.astype(bf16)
        start = pl.multiple_of(place * box_rows, 8)
        charges = jnp.concatenate([pack[pl.ds(start, 8), :], pack[pl.ds(start + 8, 8), :]], axis=1)
        products = jnp.concatenate([charges] + [charges * local[a : a + 1] for a in range(3)], axis=0)
        rows = jnp.concatenate([*thirds(products), jnp.zeros((32, per_box), f32)], axis=0)
        strengths[pl.ds(pl.multiple_of((first + place) * per_box, per_box), per_box), :] = jnp.transpose(rows).astype(bf16)
        return 0

    lax.fori_loop(0, plane_boxes, one_box, 0, unroll=2)


def target_place(centres_s, b):
    x, y, z = lattice(centres_s, b)
    plane = z & 1
    place = y * 4 + x
    return x, y, plane, place, plane * plane_boxes + place


def facets_at(low_ref, high_ref, plane, place, origin):
    start = pl.multiple_of(place * box_rows + 16, 8)
    tile = jnp.where(plane == 0, low_ref[pl.ds(start, 8), :], high_ref[pl.ds(start, 8), :])
    return jnp.concatenate([tile[0:3], tile[3:6]], axis=1) - origin


def own_kernel(centres_s, low_ref, high_ref, normals_ref, right, planes, field, left, columns):
    boxes = centres_s.shape[1]
    row = lax.broadcasted_iota(jnp.int32, (8, per_box), 0)
    origin, _ = slab_origin(centres_s)
    store_source_features(low_ref, origin, left, columns, 0)
    store_source_features(high_ref, origin, left, columns, plane_boxes * per_box)

    def target(b, _):
        _, _, plane, place, slot = target_place(centres_s, b)
        local = facets_at(low_ref, high_ref, plane, place, origin)
        normal = normals_ref[:, pl.ds(pl.multiple_of(b * per_box, per_box), per_box)]
        five = jnp.zeros((5, per_box), f32)
        local_8 = jnp.concatenate([local, five], axis=0)
        normal_8 = jnp.concatenate([normal, five], axis=0)
        square = jnp.sum(local_8 * local_8, axis=0, keepdims=True) + soften
        along = jnp.sum(local_8 * normal_8, axis=0, keepdims=True)
        distance = jnp.where(row == 3, 1.0, jnp.where(row == 4, square, -2.0 * local_8))
        high, middle, low = thirds(distance)
        rows = stacked_rows((high, middle, low, high, middle, high), per_box)
        right[pl.ds(pl.multiple_of(slot * depth, depth), depth), :] = rows.astype(bf16)
        planes[pl.ds(pl.multiple_of(slot * 8, 8), 8), :] = jnp.where(row == 3, along, normal_8)
        return 0

    lax.fori_loop(0, boxes, target, 0, unroll=2)
    field[...] = jnp.zeros_like(field)
    for plane in range(2):
        near_plane(low_ref, left, columns, 0, right, planes, plane, field)
        near_plane(high_ref, left, columns, plane_boxes * per_box, right, planes, plane, field)


def near_planes(sources, geometry, strengths, targets, total):
    def source_row(source_y, target_y, rows):
        runs = []
        for first, planes in sources:
            for x in range(4):
                for plane in planes:
                    for k in range(rows):
                        low, high = max(x - 1, 0), min(x + 2, 4)
                        start = (plane * plane_boxes + (target_y + k) * 4 + low) * per_box
                        rows_of = pl.ds(pl.multiple_of(start, per_box), (high - low) * per_box)
                        runs.append((first + source_y * 4 + x, rows_of))

        def distances(box, rows_of):
            weights = geometry[pl.ds(pl.multiple_of(box * depth, depth), depth), :]
            return jnp.dot(targets[rows_of, :], weights, preferred_element_type=f32)

        ahead = distances(*runs[0])
        for i, (box, rows_of) in enumerate(runs):
            here = ahead
            if i + 1 < len(runs):
                ahead = distances(*runs[i + 1])
            inverse = lax.rsqrt(here)
            cubed = (inverse * inverse * inverse).astype(bf16)
            given = strengths[pl.ds(pl.multiple_of(box * per_box, per_box), per_box), :]
            total[rows_of, :] += jnp.dot(cubed, given, preferred_element_type=f32)

    def outer(i, _):
        source_row(3 * i, 2 * i, 2)
        return 0

    def inner(i, _):
        source_row(i + 1, i, 3)
        return 0

    lax.fori_loop(0, 2, outer, 0)
    lax.fori_loop(0, 2, inner, 0)


def own_kernel(centres_s, low_ref, high_ref, normals_ref, right, planes, field, left, columns):
    boxes = centres_s.shape[1]
    row = lax.broadcasted_iota(jnp.int32, (8, per_box), 0)
    origin, _ = slab_origin(centres_s)
    store_source_features(low_ref, origin, left, columns, 0)
    store_source_features(high_ref, origin, left, columns, plane_boxes * per_box)

    def target(b, _):
        _, _, plane, place, slot = target_place(centres_s, b)
        local = facets_at(low_ref, high_ref, plane, place, origin)
        normal = normals_ref[:, pl.ds(pl.multiple_of(b * per_box, per_box), per_box)]
        five = jnp.zeros((5, per_box), f32)
        local_8 = jnp.concatenate([local, five], axis=0)
        normal_8 = jnp.concatenate([normal, five], axis=0)
        square = jnp.sum(local_8 * local_8, axis=0, keepdims=True) + soften
        along = jnp.sum(local_8 * normal_8, axis=0, keepdims=True)
        distance = jnp.where(row == 3, 1.0, jnp.where(row == 4, square, -2.0 * local_8))
        high, middle, low = thirds(distance)
        rows = stacked_rows((high, middle, low, high, middle, high), per_box)
        right[pl.ds(pl.multiple_of(slot * depth, depth), depth), :] = rows.astype(bf16)
        planes[pl.ds(pl.multiple_of(slot * 8, 8), 8), :] = jnp.where(row == 3, along, normal_8)
        return 0

    lax.fori_loop(0, boxes, target, 0, unroll=2)
    field[...] = jnp.zeros_like(field)
    for plane in range(2):
        near_plane(low_ref, left, columns, 0, right, planes, plane, field)
        near_plane(high_ref, left, columns, plane_boxes * per_box, right, planes, plane, field)


def near_planes(sources, geometry, strengths, targets, total):
    def near_rows(item, _):
        target_y = (item + 1) // 3
        source_y = target_y + lax.rem(item + 1, 3) - 1
        for first, planes in sources:
            for x in range(4):
                box = first + source_y * 4 + x
                low, high = max(x - 1, 0), min(x + 2, 4)
                size = (high - low) * per_box
                starts = [
                    pl.multiple_of((plane * plane_boxes + target_y * 4 + low) * per_box, per_box) for plane in planes
                ]
                facets = jnp.concatenate([targets[pl.ds(start, size), :] for start in starts], axis=0)
                weights = geometry[pl.ds(pl.multiple_of(box * depth, depth), depth), :]
                inverse = lax.rsqrt(jnp.dot(facets, weights, preferred_element_type=f32))
                cubed = (inverse * inverse * inverse).astype(bf16)
                given = strengths[pl.ds(pl.multiple_of(box * per_box, per_box), per_box), :]
                part = jnp.dot(cubed, given, preferred_element_type=f32)
                for k, start in enumerate(starts):
                    total[pl.ds(start, size), :] += part[k * size : (k + 1) * size]
        return 0

    lax.fori_loop(0, 10, near_rows, 0)


def own_kernel(centres_s, low_ref, high_ref, normals_ref, targets, planes, total, geometry, strengths):
    boxes = centres_s.shape[1]
    row = lax.broadcasted_iota(jnp.int32, (8, per_box), 0)
    origin, _ = slab_origin(centres_s)
    store_source_features(low_ref, origin, geometry, strengths, 0)
    store_source_features(high_ref, origin, geometry, strengths, plane_boxes)

    def target(b, _):
        _, _, plane, place, slot = target_place(centres_s, b)
        local = facets_at(low_ref, high_ref, plane, place, origin)
        normal = normals_ref[:, pl.ds(pl.multiple_of(b * per_box, per_box), per_box)]
        five = jnp.zeros((5, per_box), f32)
        local_8 = jnp.concatenate([local, five], axis=0)
        normal_8 = jnp.concatenate([normal, five], axis=0)
        square = jnp.sum(local_8 * local_8, axis=0, keepdims=True) + soften
        along = jnp.sum(local_8 * normal_8, axis=0, keepdims=True)
        distance = jnp.where(row == 3, 1.0, jnp.where(row == 4, square, -2.0 * local_8))
        high, middle, low = thirds(distance)
        rows = stacked_rows((high, middle, low, high, middle, high), per_box)
        start = pl.multiple_of(slot * per_box, per_box)
        targets[pl.ds(start, per_box), :] = jnp.transpose(rows).astype(bf16)
        planes[pl.ds(pl.multiple_of(slot * 8, 8), 8), :] = jnp.where(row == 3, along, normal_8)
        return 0

    lax.fori_loop(0, boxes, target, 0, unroll=2)
    total[...] = jnp.zeros_like(total)
    near_planes(((0, (0, 1)), (plane_boxes, (0, 1))), geometry, strengths, targets, total)


def halo_kernel(
    centres_s, counts_s, prev_ref, low_ref, high_ref, next_ref, normals_ref, contrast_ref, basis_ref, targets,
    planes, own_total, image_ref, sums_ref, geometry, strengths, total, field, far_centres
):
    boxes = counts_s.shape[0]
    krylov = basis_ref.shape[0]
    origin, base_z = slab_origin(centres_s)
    store_source_features(prev_ref, origin, geometry, strengths, 0)
    store_source_features(next_ref, origin, geometry, strengths, plane_boxes)
    total[...] = jnp.zeros_like(total)
    near_planes(((0, (0,)), (plane_boxes, (1,))), geometry, strengths, targets, total)

    def near_field(slot, _):
        rows = pl.ds(pl.multiple_of(slot * per_box, per_box), per_box)
        turned = jnp.transpose(total[rows, :] + own_total[rows, :])
        sums = turned[:32] + (turned[32:64] + turned[64:96])
        side = planes[pl.ds(pl.multiple_of(slot * 8, 8), 8), :]
        value = side[3:4] * sums[:8] - side[0:1] * sums[8:16]
        value = value - side[1:2] * sums[16:24] - side[2:3] * sums[24:32]
        field[pl.ds(pl.multiple_of(slot * 8, 8), 8), :] = value
        return 0

    lax.fori_loop(0, boxes, near_field, 0, unroll=2)

    for group, pack in enumerate((prev_ref, low_ref, next_ref)):
        columns = jnp.transpose(pack[tail + 8 : tail + 16, :])[:32]
        for a in range(3):
            shift = base_z if a == 2 else 1.5
            far_centres[(group * 3 + a) * 32 : (group * 3 + a + 1) * 32, :] = jnp.broadcast_to(
                columns[:, a : a + 1] - shift, (32, 128)
            )
    far_moments = jnp.concatenate([pack[tail : tail + 8, :] for pack in (prev_ref, low_ref, next_ref)], axis=1)
    far_high = far_moments.astype(bf16).astype(f32)
    far_both = jnp.concatenate([far_high, far_moments - far_high], axis=0)
    far_lane = lax.broadcasted_iota(jnp.int32, (1, 384), 1)
    lane_x = far_lane & 3
    lane_y = (far_lane >> 2) & 3
    lane_z = 2 * (far_lane >> 7) - 2 + ((far_lane >> 4) & 1)

    def far_box(b, _):
        x, y, plane, place, slot = target_place(centres_s, b)
        local = facets_at(low_ref, high_ref, plane, place, origin)
        normal = normals_ref[:, pl.ds(pl.multiple_of(b * per_box, per_box), per_box)]
        coefficients = []
        for group in range(3):
            d = []
            for a in range(3):
                centre = far_centres[(group * 3 + a) * 32 : (group * 3 + a + 1) * 32, :]
                d.append(local[a : a + 1] - jnp.concatenate([centre, centre], axis=1))
            q = d[0] * d[0] + d[1] * d[1] + d[2] * d[2] + soften
            inverse = lax.rsqrt(q)
            inverse_2 = inverse * inverse
            inverse_3 = inverse_2 * inverse
            t = d[0] * normal[0:1] + d[1] * normal[1:2] + d[2] * normal[2:3]
            single = t * inverse_3
            coefficients.append(single)
            steep = 3.0 * single * inverse_2
            for a in range(3):
                coefficients.append(steep * d[a] - normal[a : a + 1] * inverse_3)
        whole = jnp.concatenate(coefficients, axis=0)
        upper = whole.astype(bf16)
        lower = (whole - upper.astype(f32)).astype(bf16)
        near = (jnp.abs(lane_x - x) <= 1) & (jnp.abs(lane_y - y) <= 1) & (jnp.abs(lane_z - plane) <= 1)
        picked = jnp.where(near, 0.0, far_both).astype(bf16)
        first = jnp.dot(picked, upper, preferred_element_type=f32)
        second = jnp.dot(picked, lower, preferred_element_type=f32)
        field[pl.ds(pl.multiple_of(slot * 8, 8), 8), :] += first[:8] + first[8:] + second[:8]
        return 0

    lax.fori_loop(0, boxes, far_box, 0, unroll=2)

    def image_box(b, carry):
        _, _, _, _, slot = target_place(centres_s, b)
        lanes = pl.ds(pl.multiple_of(b * per_box, per_box), per_box)
        live = live_row(counts_s, b)
        current = basis_ref[krylov - 1, :, lanes]
        part = field[pl.ds(pl.multiple_of(slot * 8, 8), 8), :]
        image = live * (current - 2.0 * wide_row(contrast_ref, b) * part)
        image_ref[:, lanes] = image
        sums = []
        for m in range(krylov + 1):
            product = image * (basis_ref[m, :, lanes] if m < krylov else image)
            sums.append(carry[m] + product[:, :128] + product[:, 128:])
        return tuple(sums)

    zeros = jnp.zeros((8, 128), f32)
    sums = lax.fori_loop(0, boxes, image_box, (zeros,) * (krylov + 1), unroll=2)
    pairs = [(m, n) for m in range(krylov) for n in range(m + 1)]

    def gram_box(b, carry):
        lanes = pl.ds(pl.multiple_of(b * per_box, per_box), per_box)
        live = live_row(counts_s, b)
        rows = [basis_ref[m, :, lanes] * live for m in range(krylov)]
        out = []
        for k, (m, n) in enumerate(pairs):
            product = rows[m] * rows[n]
            out.append(carry[k] + product[:, :128] + product[:, 128:])
        return tuple(out)

    gram = lax.fori_loop(0, boxes, gram_box, (zeros,) * len(pairs))
    lane = lax.broadcasted_iota(jnp.int32, (8, 128), 1)
    total = zeros
    for k, value in enumerate([*sums, *gram]):
        total = jnp.where(lane == k, jnp.sum(value, axis=1, keepdims=True), total)
    sums_ref[...] = jnp.broadcast_to(total[None], sums_ref.shape)


def two_sum(a, b):
    s = a + b
    c = s - a
    return s, (a - (s - c)) + (b - c)


def halves(a):
    c = a * 4097.0
    high = c - (c - a)
    return high, a - high


def two_product(a, b):
    p = a * b
    a_high, a_low = halves(a)
    b_high, b_low = halves(b)
    return p, ((a_high * b_high - p) + a_high * b_low + a_low * b_high) + a_low * b_low


def finish_kernel(total_facets, counts_s, tiles_ref, image_ref, basis_ref, next_ref, hessenberg_ref):
    boxes = counts_s.shape[0]
    krylov = basis_ref.shape[0]
    lane = lax.broadcasted_iota(jnp.int32, (8, 128), 1)

    def add_tile(i, carry):
        value, error = two_sum(carry[0], tiles_ref[i])
        return value, carry[1] + error

    sums, rest = lax.fori_loop(0, tiles_ref.shape[0], add_tile, (jnp.zeros((8, 128), f32),) * 2, unroll=8)
    exact = sums + rest
    projections = [exact[:, m : m + 1] / total_facets for m in range(krylov)]
    pairs = [(m, n) for m in range(krylov) for n in range(m + 1)]
    first = jnp.where(lane == krylov, 1.0, 0.0)
    second = jnp.where(lane <= krylov, 1.0, 0.0)
    for m in range(krylov):
        first = jnp.where(lane == m, -2.0 * projections[m], first)
    for k, (m, n) in enumerate(pairs):
        at = lane == krylov + 1 + k
        scale = 1.0 if m == n else 2.0
        first = jnp.where(at, scale * projections[m], first)
        second = jnp.where(at, projections[n], second)
    factor, factor_rest = two_product(first, second)
    value, value_rest = two_product(factor, sums)
    value_rest = value_rest + (factor * rest + factor_rest * sums)
    for shift in (64, 32, 16, 8, 4, 2, 1):
        other = pltpu.roll(value, shift, 1)
        other_rest = pltpu.roll(value_rest, shift, 1)
        value, error = two_sum(value, other)
        value_rest = (value_rest + other_rest) + error
    remaining = jnp.maximum(value + value_rest, 0.0)
    norm = jnp.sqrt(remaining / total_facets + epsilon)
    heads = jnp.where(lane == krylov, norm, 0.0)
    for m in range(krylov):
        heads = jnp.where(lane == m, projections[m], heads)
    hessenberg_ref[...] = heads[:, : krylov + 1]
    wide = [jnp.broadcast_to(p, (8, per_box)) for p in projections]
    scale = jnp.concatenate([1.0 / norm] * (per_box // 128), axis=1)

    def one_box(b, _):
        lanes = pl.ds(pl.multiple_of(b * per_box, per_box), per_box)
        live = live_row(counts_s, b)
        sent = wide[0] * basis_ref[0, :, lanes]
        for m in range(1, krylov):
            sent += wide[m] * basis_ref[m, :, lanes]
        next_ref[:, lanes] = (image_ref[:, lanes] - sent * live) * scale
        return 0

    lax.fori_loop(0, boxes, one_box, 0, unroll=4)


smem = pl.BlockSpec(memory_space=pltpu.SMEM)
vmem = pl.BlockSpec(memory_space=pltpu.VMEM)


def on_device(
    basis, facet_centres, normals, areas, contrast, facet_counts, box_centres, near_boxes, far_boxes
):
    krylov, rhs_local, facet_local = basis.shape
    boxes = facet_counts.shape[0]
    count = lax.axis_size("box")
    total_facets = count * facet_local
    areas = areas.reshape(-1, 128)
    contrast = contrast.reshape(-1, 128)
    pack = jax.ShapeDtypeStruct((pack_rows, 128), f32)
    low, high = pl.pallas_call(
        prep_kernel,
        out_shape=(pack, pack),
        in_specs=[pl.BlockSpec(memory_space=pltpu.HBM)] * 5,
        out_specs=(vmem, vmem),
        scratch_shapes=[
            pltpu.VMEM((2 * pack_rows, 128), f32),
            pltpu.SMEM(box_centres.shape, f32),
            pltpu.SMEM(facet_counts.shape, jnp.int32),
            pltpu.VMEM((rhs_local, facet_local), f32),
            pltpu.VMEM(facet_centres.shape, f32),
            pltpu.VMEM(areas.shape, f32),
            pltpu.SemaphoreType.DMA((5,)),
        ],
        compiler_params=pltpu.CompilerParams(vmem_limit_bytes=8 * 1024 * 1024),
        name="prepare",
    )(box_centres, facet_counts, basis, facet_centres, areas)
    below = lax.ppermute(high, "box", [(i, i + 1) for i in range(count - 1)])
    above = lax.ppermute(low, "box", [(i + 1, i) for i in range(count - 1)])
    slots = boxes * per_box
    targets, planes, own_total = pl.pallas_call(
        own_kernel,
        out_shape=(
            jax.ShapeDtypeStruct((slots, depth), bf16),
            jax.ShapeDtypeStruct((boxes * 8, per_box), f32),
            jax.ShapeDtypeStruct((slots, 128), f32),
        ),
        in_specs=[smem] + [vmem] * 3,
        out_specs=(vmem,) * 3,
        scratch_shapes=[pltpu.VMEM((boxes * depth, per_box), bf16), pltpu.VMEM((slots, 128), bf16)],
        compiler_params=pltpu.CompilerParams(vmem_limit_bytes=24 * 1024 * 1024),
        name="own",
    )(box_centres, low, high, normals)
    image, tiles = pl.pallas_call(
        halo_kernel,
        out_shape=(
            jax.ShapeDtypeStruct((rhs_local, facet_local), f32),
            jax.ShapeDtypeStruct((count, 8, 128), f32),
        ),
        in_specs=[smem, smem] + [vmem] * 10,
        out_specs=(vmem, vmem),
        scratch_shapes=[
            pltpu.VMEM((boxes * depth, per_box), bf16),
            pltpu.VMEM((slots, 128), bf16),
            pltpu.VMEM((slots, 128), f32),
            pltpu.VMEM((boxes * 8, per_box), f32),
            pltpu.VMEM((9 * 32, 128), f32),
        ],
        compiler_params=pltpu.CompilerParams(vmem_limit_bytes=32 * 1024 * 1024),
        name="halo",
    )(box_centres, facet_counts, below, low, high, above, normals, contrast, basis, targets, planes, own_total)
    tiles = lax.all_to_all(tiles, "box", 0, 0, tiled=True)
    next_vector, hessenberg = pl.pallas_call(
        functools.partial(finish_kernel, total_facets),
        out_shape=(
            jax.ShapeDtypeStruct((rhs_local, facet_local), f32),
            jax.ShapeDtypeStruct((rhs_local, krylov + 1), f32),
        ),
        in_specs=[smem] + [vmem] * 3,
        out_specs=(vmem, vmem),
        compiler_params=pltpu.CompilerParams(vmem_limit_bytes=16 * 1024 * 1024),
        name="finish",
    )(facet_counts, tiles, image, basis)
    return next_vector, hessenberg.T


def solution(mesh):
    return jax.shard_map(
        on_device,
        mesh=mesh,
        in_specs=(
            P(None, "rhs", "box"),
            P(None, "box"),
            P(None, "box"),
            P("box"),
            P("box"),
            P("box"),
            P(None, "box"),
            P("box", None),
            P("box", None),
        ),
        out_specs=(P("rhs", "box"), P(None, "rhs")),
        check_vma=False,
    )
```

```python
import functools

import jax
import jax.numpy as jnp
from jax import lax
from jax.experimental import pallas as pl
from jax.experimental.pallas import tpu as pltpu
from jax.sharding import PartitionSpec as P

soften = 0.0025
epsilon = 1e-06
f32 = jnp.float32
bf16 = jnp.bfloat16
box_rows = 24
plane_boxes = 16
per_box = 256
tail = plane_boxes * box_rows
pack_rows = tail + 16
depth = 128


def lattice(centres_s, b):
    x = (centres_s[0, b] + 0.5).astype(jnp.int32)
    y = (centres_s[1, b] + 0.5).astype(jnp.int32)
    z = (centres_s[2, b] + 0.5).astype(jnp.int32)
    return x, y, z


def wide_row(ref, b):
    return jnp.concatenate([ref[pl.ds(2 * b, 1), :], ref[pl.ds(2 * b + 1, 1), :]], axis=1)


def live_row(counts_s, b):
    slots = lax.broadcasted_iota(jnp.int32, (1, per_box), 1)
    return (slots < counts_s[b]).astype(f32)


def prep_kernel(
    centres_h, counts_h, basis_h, facets_h, areas_h, low_ref, high_ref, tail_ref,
    packs, centres_s, counts_s, current_ref, facets_ref, areas_ref, arrived
):
    boxes = counts_s.shape[0]
    moves = [
        (basis_h.at[basis_h.shape[0] - 1], current_ref),
        (facets_h, facets_ref),
        (areas_h, areas_ref),
        (centres_h, centres_s),
        (counts_h, counts_s),
    ]
    copies = [pltpu.make_async_copy(a, b, arrived.at[k]) for k, (a, b) in enumerate(moves)]
    for copy in copies:
        copy.start()
    for copy in copies:
        copy.wait()
    lane = lax.broadcasted_iota(jnp.int32, (8, 128), 1)
    row = lax.broadcasted_iota(jnp.int32, (8, 128), 0)

    def one_box(b, carry):
        moments, centres = carry
        x, y, z = lattice(centres_s, b)
        plane = z & 1
        place = y * 4 + x
        slot = plane * plane_boxes + place
        lanes = pl.ds(pl.multiple_of(b * per_box, per_box), per_box)
        facets = facets_ref[:, lanes]
        live = live_row(counts_s, b)
        weighted = current_ref[:, lanes] * (wide_row(areas_ref, b) * live / per_box)
        charges = weighted.astype(bf16).astype(f32)
        start = pl.multiple_of(plane * pack_rows + place * box_rows, 8)
        packs[pl.ds(start, 8), :] = charges[:, :128]
        packs[pl.ds(start + 8, 8), :] = charges[:, 128:]
        packs[pl.ds(start + 16, 8), :] = jnp.concatenate(
            [facets[:, :128], facets[:, 128:], jnp.zeros((2, 128), f32)], axis=0
        )
        moments += jnp.where(lane == slot, jnp.sum(weighted, axis=1, keepdims=True), 0.0)
        for a in range(3):
            dipole = jnp.sum(weighted * (facets[a : a + 1] - centres_s[a, b]), axis=1, keepdims=True)
            moments += jnp.where(lane == 32 * (a + 1) + slot, dipole, 0.0)
            centres += jnp.where((lane == slot) & (row == a), centres_s[a, b], 0.0)
        return moments, centres

    zeros = jnp.zeros((8, 128), f32)
    moments, centres = lax.fori_loop(0, boxes, one_box, (zeros, zeros), unroll=4)
    for ref, first in ((low_ref, 0), (high_ref, pack_rows)):
        ref[:tail] = packs[first : first + tail]
        ref[tail : tail + 8] = moments
        ref[tail + 8 :] = centres
    tail_ref[:8] = moments
    tail_ref[8:] = centres


def thirds(x):
    high = x.astype(bf16).astype(f32)
    rest = x - high
    middle = rest.astype(bf16).astype(f32)
    return high, middle, (rest - middle).astype(bf16).astype(f32)


def stacked_rows(parts, width):
    zeros = jnp.zeros((depth - 8 * len(parts), width), f32)
    return jnp.concatenate([*parts, zeros], axis=0)


def local_facets(pack_ref, place, origin):
    start = pl.multiple_of(place * box_rows + 16, 8)
    tile = pack_ref[pl.ds(start, 8), :]
    both = jnp.concatenate([tile[0:3], tile[3:6]], axis=1)
    return jnp.concatenate([both - origin, jnp.zeros((5, 256), f32)], axis=0)


def slab_origin(centres_s):
    _, _, z = lattice(centres_s, 0)
    base_z = (z - (z & 1)).astype(f32) + 0.5
    axis_row = lax.broadcasted_iota(jnp.int32, (3, 1), 0)
    return jnp.where(axis_row == 2, base_z, 1.5), base_z


def store_source_features(local, charges, box, geometry, strengths):
    row = lax.broadcasted_iota(jnp.int32, (8, per_box), 0)
    square = jnp.sum(local * local, axis=0, keepdims=True)
    features = jnp.where(row == 3, square, jnp.where(row == 4, 1.0, local))
    high, middle, low = thirds(features)
    rows = stacked_rows((high, high, high, middle, middle, low), per_box)
    geometry[pl.ds(pl.multiple_of(box * depth, depth), depth), :] = rows.astype(bf16)
    products = jnp.concatenate([charges] + [charges * local[a : a + 1] for a in range(3)], axis=0)
    rows = jnp.concatenate([*thirds(products), jnp.zeros((32, per_box), f32)], axis=0)
    strengths[pl.ds(pl.multiple_of(box * per_box, per_box), per_box), :] = jnp.transpose(rows).astype(bf16)


def store_pack_features(pack, origin, geometry, strengths, first):
    def one_box(place, _):
        start = pl.multiple_of(place * box_rows, 8)
        charges = jnp.concatenate([pack[pl.ds(start, 8), :], pack[pl.ds(start + 8, 8), :]], axis=1)
        store_source_features(local_facets(pack, place, origin), charges, first + place, geometry, strengths)
        return 0

    lax.fori_loop(0, plane_boxes, one_box, 0, unroll=2)


def target_place(centres_s, b):
    x, y, z = lattice(centres_s, b)
    plane = z & 1
    place = y * 4 + x
    return x, y, plane, place, plane * plane_boxes + place


def near_planes(sources, geometry, strengths, targets, total):
    def near_rows(item, _):
        target_y = (item + 1) // 3
        source_y = target_y + lax.rem(item + 1, 3) - 1
        runs = []
        for first, planes in sources:
            for x in range(4):
                for plane in planes:
                    for near_x in range(max(x - 1, 0), min(x + 2, 4)):
                        start = (plane * plane_boxes + target_y * 4 + near_x) * per_box
                        runs.append((first + source_y * 4 + x, pl.ds(pl.multiple_of(start, per_box), per_box)))

        def distances(box, rows_of):
            weights = geometry[pl.ds(pl.multiple_of(box * depth, depth), depth), :]
            return jnp.dot(targets[rows_of, :], weights, preferred_element_type=f32)

        ahead = distances(*runs[0])
        for i, (box, rows_of) in enumerate(runs):
            here = ahead
            if i + 1 < len(runs):
                ahead = distances(*runs[i + 1])
            inverse = lax.rsqrt(here)
            cubed = (inverse * inverse * inverse).astype(bf16)
            given = strengths[pl.ds(pl.multiple_of(box * per_box, per_box), per_box), :]
            total[rows_of, :] += jnp.dot(cubed, given, preferred_element_type=f32)

        return 0

    lax.fori_loop(0, 10, near_rows, 0)


def own_kernel(
    centres_s, counts_s, basis_ref, facets_ref, areas_ref, normals_ref, targets, planes, total, geometry, strengths
):
    boxes = counts_s.shape[0]
    krylov = basis_ref.shape[0]
    row = lax.broadcasted_iota(jnp.int32, (8, per_box), 0)
    origin, _ = slab_origin(centres_s)

    def target(b, _):
        _, _, _, _, slot = target_place(centres_s, b)
        lanes = pl.ds(pl.multiple_of(b * per_box, per_box), per_box)
        normal = normals_ref[:, lanes]
        five = jnp.zeros((5, per_box), f32)
        local_8 = jnp.concatenate([facets_ref[:, lanes] - origin, five], axis=0)
        normal_8 = jnp.concatenate([normal, five], axis=0)
        live = live_row(counts_s, b)
        weighted = basis_ref[krylov - 1, :, lanes] * (wide_row(areas_ref, b) * live / per_box)
        store_source_features(local_8, weighted.astype(bf16).astype(f32), slot, geometry, strengths)
        square = jnp.sum(local_8 * local_8, axis=0, keepdims=True) + soften
        along = jnp.sum(local_8 * normal_8, axis=0, keepdims=True)
        distance = jnp.where(row == 3, 1.0, jnp.where(row == 4, square, -2.0 * local_8))
        high, middle, low = thirds(distance)
        rows = stacked_rows((high, middle, low, high, middle, high), per_box)
        start = pl.multiple_of(slot * per_box, per_box)
        targets[pl.ds(start, per_box), :] = jnp.transpose(rows).astype(bf16)
        planes[pl.ds(pl.multiple_of(slot * 8, 8), 8), :] = jnp.where(row == 3, along, normal_8)
        return 0

    lax.fori_loop(0, boxes, target, 0, unroll=2)
    total[...] = jnp.zeros_like(total)
    near_planes(((0, (0, 1)), (plane_boxes, (0, 1))), geometry, strengths, targets, total)


def halo_kernel(
    centres_s, counts_s, prev_ref, tail_ref, next_ref, facets_ref, normals_ref, contrast_ref, basis_ref, targets,
    planes, own_total, image_ref, sums_ref, geometry, strengths, total, field, far_centres
):
    boxes = counts_s.shape[0]
    krylov = basis_ref.shape[0]
    origin, base_z = slab_origin(centres_s)
    store_pack_features(prev_ref, origin, geometry, strengths, 0)
    store_pack_features(next_ref, origin, geometry, strengths, plane_boxes)
    total[...] = jnp.zeros_like(total)
    near_planes(((0, (0,)), (plane_boxes, (1,))), geometry, strengths, targets, total)

    def near_field(slot, _):
        rows = pl.ds(pl.multiple_of(slot * per_box, per_box), per_box)
        turned = jnp.transpose(total[rows, :] + own_total[rows, :])
        sums = turned[:32] + (turned[32:64] + turned[64:96])
        side = planes[pl.ds(pl.multiple_of(slot * 8, 8), 8), :]
        value = side[3:4] * sums[:8] - side[0:1] * sums[8:16]
        value = value - side[1:2] * sums[16:24] - side[2:3] * sums[24:32]
        field[pl.ds(pl.multiple_of(slot * 8, 8), 8), :] = value
        return 0

    lax.fori_loop(0, boxes, near_field, 0, unroll=2)

    tails = (prev_ref[tail:, :], tail_ref[...], next_ref[tail:, :])
    for group in range(3):
        columns = jnp.transpose(tails[group][8:])[:32]
        for a in range(3):
            shift = base_z if a == 2 else 1.5
            far_centres[(group * 3 + a) * 32 : (group * 3 + a + 1) * 32, :] = jnp.broadcast_to(
                columns[:, a : a + 1] - shift, (32, 128)
            )
    far_moments = jnp.concatenate([part[:8] for part in tails], axis=1)
    far_high = far_moments.astype(bf16).astype(f32)
    far_both = jnp.concatenate([far_high, far_moments - far_high], axis=0)
    far_lane = lax.broadcasted_iota(jnp.int32, (1, 384), 1)
    lane_x = far_lane & 3
    lane_y = (far_lane >> 2) & 3
    lane_z = 2 * (far_lane >> 7) - 2 + ((far_lane >> 4) & 1)

    def far_box(b, _):
        x, y, plane, _, slot = target_place(centres_s, b)
        lanes = pl.ds(pl.multiple_of(b * per_box, per_box), per_box)
        local = facets_ref[:, lanes] - origin
        normal = normals_ref[:, lanes]
        coefficients = []
        for group in range(3):
            d = []
            for a in range(3):
                centre = far_centres[(group * 3 + a) * 32 : (group * 3 + a + 1) * 32, :]
                d.append(local[a : a + 1] - jnp.concatenate([centre, centre], axis=1))
            q = d[0] * d[0] + d[1] * d[1] + d[2] * d[2] + soften
            inverse = lax.rsqrt(q)
            inverse_2 = inverse * inverse
            inverse_3 = inverse_2 * inverse
            t = d[0] * normal[0:1] + d[1] * normal[1:2] + d[2] * normal[2:3]
            single = t * inverse_3
            coefficients.append(single)
            steep = 3.0 * single * inverse_2
            for a in range(3):
                coefficients.append(steep * d[a] - normal[a : a + 1] * inverse_3)
        whole = jnp.concatenate(coefficients, axis=0)
        upper = whole.astype(bf16)
        lower = (whole - upper.astype(f32)).astype(bf16)
        near = (jnp.abs(lane_x - x) <= 1) & (jnp.abs(lane_y - y) <= 1) & (jnp.abs(lane_z - plane) <= 1)
        picked = jnp.where(near, 0.0, far_both).astype(bf16)
        first = jnp.dot(picked, upper, preferred_element_type=f32)
        second = jnp.dot(picked, lower, preferred_element_type=f32)
        field[pl.ds(pl.multiple_of(slot * 8, 8), 8), :] += first[:8] + first[8:] + second[:8]
        return 0

    lax.fori_loop(0, boxes, far_box, 0, unroll=2)

    def image_box(b, carry):
        _, _, _, _, slot = target_place(centres_s, b)
        lanes = pl.ds(pl.multiple_of(b * per_box, per_box), per_box)
        live = live_row(counts_s, b)
        current = basis_ref[krylov - 1, :, lanes]
        part = field[pl.ds(pl.multiple_of(slot * 8, 8), 8), :]
        image = live * (current - 2.0 * wide_row(contrast_ref, b) * part)
        image_ref[:, lanes] = image
        sums = []
        for m in range(krylov + 1):
            product = image * (basis_ref[m, :, lanes] if m < krylov else image)
            sums.append(carry[m] + product[:, :128] + product[:, 128:])
        return tuple(sums)

    zeros = jnp.zeros((8, 128), f32)
    sums = lax.fori_loop(0, boxes, image_box, (zeros,) * (krylov + 1), unroll=2)
    pairs = [(m, n) for m in range(krylov) for n in range(m + 1)]

    def gram_box(b, carry):
        lanes = pl.ds(pl.multiple_of(b * per_box, per_box), per_box)
        live = live_row(counts_s, b)
        rows = [basis_ref[m, :, lanes] * live for m in range(krylov)]
        out = []
        for k, (m, n) in enumerate(pairs):
            product = rows[m] * rows[n]
            out.append(carry[k] + product[:, :128] + product[:, 128:])
        return tuple(out)

    gram = lax.fori_loop(0, boxes, gram_box, (zeros,) * len(pairs))
    lane = lax.broadcasted_iota(jnp.int32, (8, 128), 1)
    total = zeros
    for k, value in enumerate([*sums, *gram]):
        total = jnp.where(lane == k, jnp.sum(value, axis=1, keepdims=True), total)
    sums_ref[...] = jnp.broadcast_to(total[None], sums_ref.shape)


def two_sum(a, b):
    s = a + b
    c = s - a
    return s, (a - (s - c)) + (b - c)


def halves(a):
    c = a * 4097.0
    high = c - (c - a)
    return high, a - high


def two_product(a, b):
    p = a * b
    a_high, a_low = halves(a)
    b_high, b_low = halves(b)
    return p, ((a_high * b_high - p) + a_high * b_low + a_low * b_high) + a_low * b_low


def finish_kernel(total_facets, counts_s, tiles_ref, image_ref, basis_ref, next_ref, hessenberg_ref):
    boxes = counts_s.shape[0]
    krylov = basis_ref.shape[0]
    lane = lax.broadcasted_iota(jnp.int32, (8, 128), 1)

    def add_tile(i, carry):
        value, error = two_sum(carry[0], tiles_ref[i])
        return value, carry[1] + error

    sums, rest = lax.fori_loop(0, tiles_ref.shape[0], add_tile, (jnp.zeros((8, 128), f32),) * 2, unroll=8)
    exact = sums + rest
    projections = [exact[:, m : m + 1] / total_facets for m in range(krylov)]
    pairs = [(m, n) for m in range(krylov) for n in range(m + 1)]
    first = jnp.where(lane == krylov, 1.0, 0.0)
    second = jnp.where(lane <= krylov, 1.0, 0.0)
    for m in range(krylov):
        first = jnp.where(lane == m, -2.0 * projections[m], first)
    for k, (m, n) in enumerate(pairs):
        at = lane == krylov + 1 + k
        scale = 1.0 if m == n else 2.0
        first = jnp.where(at, scale * projections[m], first)
        second = jnp.where(at, projections[n], second)
    factor, factor_rest = two_product(first, second)
    value, value_rest = two_product(factor, sums)
    value_rest = value_rest + (factor * rest + factor_rest * sums)
    for shift in (64, 32, 16, 8, 4, 2, 1):
        other = pltpu.roll(value, shift, 1)
        other_rest = pltpu.roll(value_rest, shift, 1)
        value, error = two_sum(value, other)
        value_rest = (value_rest + other_rest) + error
    remaining = jnp.maximum(value + value_rest, 0.0)
    norm = jnp.sqrt(remaining / total_facets + epsilon)
    heads = jnp.where(lane == krylov, norm, 0.0)
    for m in range(krylov):
        heads = jnp.where(lane == m, projections[m], heads)
    hessenberg_ref[...] = heads[:, : krylov + 1]
    wide = [jnp.broadcast_to(p, (8, per_box)) for p in projections]
    scale = jnp.concatenate([1.0 / norm] * (per_box // 128), axis=1)

    def one_box(b, _):
        lanes = pl.ds(pl.multiple_of(b * per_box, per_box), per_box)
        live = live_row(counts_s, b)
        sent = wide[0] * basis_ref[0, :, lanes]
        for m in range(1, krylov):
            sent += wide[m] * basis_ref[m, :, lanes]
        next_ref[:, lanes] = (image_ref[:, lanes] - sent * live) * scale
        return 0

    lax.fori_loop(0, boxes, one_box, 0, unroll=4)


smem = pl.BlockSpec(memory_space=pltpu.SMEM)
vmem = pl.BlockSpec(memory_space=pltpu.VMEM)


def on_device(
    basis, facet_centres, normals, areas, contrast, facet_counts, box_centres, near_boxes, far_boxes
):
    krylov, rhs_local, facet_local = basis.shape
    boxes = facet_counts.shape[0]
    count = lax.axis_size("box")
    total_facets = count * facet_local
    areas = areas.reshape(-1, 128)
    contrast = contrast.reshape(-1, 128)
    pack = jax.ShapeDtypeStruct((pack_rows, 128), f32)
    low, high, own_tail = pl.pallas_call(
        prep_kernel,
        out_shape=(pack, pack, jax.ShapeDtypeStruct((16, 128), f32)),
        in_specs=[pl.BlockSpec(memory_space=pl.ANY)] * 5,
        out_specs=(vmem,) * 3,
        scratch_shapes=[
            pltpu.VMEM((2 * pack_rows, 128), f32),
            pltpu.SMEM(box_centres.shape, f32),
            pltpu.SMEM(facet_counts.shape, jnp.int32),
            pltpu.VMEM((rhs_local, facet_local), f32),
            pltpu.VMEM(facet_centres.shape, f32),
            pltpu.VMEM(areas.shape, f32),
            pltpu.SemaphoreType.DMA((5,)),
        ],
        name="prepare",
    )(box_centres, facet_counts, basis, facet_centres, areas)
    below = lax.ppermute(high, "box", [(i, i + 1) for i in range(count - 1)])
    above = lax.ppermute(low, "box", [(i + 1, i) for i in range(count - 1)])
    slots = boxes * per_box
    targets, planes, own_total = pl.pallas_call(
        own_kernel,
        out_shape=(
            jax.ShapeDtypeStruct((slots, depth), bf16),
            jax.ShapeDtypeStruct((boxes * 8, per_box), f32),
            jax.ShapeDtypeStruct((slots, 128), f32),
        ),
        in_specs=[smem, smem] + [vmem] * 4,
        out_specs=(vmem,) * 3,
        scratch_shapes=[pltpu.VMEM((boxes * depth, per_box), bf16), pltpu.VMEM((slots, 128), bf16)],
        compiler_params=pltpu.CompilerParams(vmem_limit_bytes=24 * 1024 * 1024),
        name="own",
    )(box_centres, facet_counts, basis, facet_centres, areas, normals)
    image, tiles = pl.pallas_call(
        halo_kernel,
        out_shape=(
            jax.ShapeDtypeStruct((rhs_local, facet_local), f32),
            jax.ShapeDtypeStruct((count, 8, 128), f32),
        ),
        in_specs=[smem, smem] + [vmem] * 10,
        out_specs=(vmem, vmem),
        scratch_shapes=[
            pltpu.VMEM((boxes * depth, per_box), bf16),
            pltpu.VMEM((slots, 128), bf16),
            pltpu.VMEM((slots, 128), f32),
            pltpu.VMEM((boxes * 8, per_box), f32),
            pltpu.VMEM((9 * 32, 128), f32),
        ],
        compiler_params=pltpu.CompilerParams(vmem_limit_bytes=32 * 1024 * 1024),
        name="halo",
    )(
        box_centres, facet_counts, below, own_tail, above, facet_centres, normals, contrast, basis, targets, planes, own_total
    )
    tiles = lax.all_to_all(tiles, "box", 0, 0, tiled=True)
    next_vector, hessenberg = pl.pallas_call(
        functools.partial(finish_kernel, total_facets),
        out_shape=(
            jax.ShapeDtypeStruct((rhs_local, facet_local), f32),
            jax.ShapeDtypeStruct((rhs_local, krylov + 1), f32),
        ),
        in_specs=[smem] + [vmem] * 3,
        out_specs=(vmem, vmem),
        compiler_params=pltpu.CompilerParams(vmem_limit_bytes=16 * 1024 * 1024),
        name="finish",
    )(facet_counts, tiles, image, basis)
    return next_vector, hessenberg.T


def solution(mesh):
    return jax.shard_map(
        on_device,
        mesh=mesh,
        in_specs=(
            P(None, "rhs", "box"),
            P(None, "box"),
            P(None, "box"),
            P("box"),
            P("box"),
            P("box"),
            P(None, "box"),
            P("box", None),
            P("box", None),
        ),
        out_specs=(P("rhs", "box"), P(None, "rhs")),
        check_vma=False,
    )
```

```python
import functools

import jax
import jax.numpy as jnp
from jax import lax
from jax.experimental import pallas as pl
from jax.experimental.pallas import tpu as pltpu
from jax.sharding import PartitionSpec as P

soften = 0.0025
epsilon = 1e-06
f32 = jnp.float32
bf16 = jnp.bfloat16
box_rows = 24
plane_boxes = 16
per_box = 256
tail = plane_boxes * box_rows
pack_rows = tail + 16
depth = 128


def lattice(centres_s, b):
    x = (centres_s[0, b] + 0.5).astype(jnp.int32)
    y = (centres_s[1, b] + 0.5).astype(jnp.int32)
    z = (centres_s[2, b] + 0.5).astype(jnp.int32)
    return x, y, z


def wide_row(ref, b):
    return jnp.concatenate([ref[pl.ds(2 * b, 1), :], ref[pl.ds(2 * b + 1, 1), :]], axis=1)


def live_row(counts_s, b):
    slots = lax.broadcasted_iota(jnp.int32, (1, per_box), 1)
    return (slots < counts_s[b]).astype(f32)


def prep_kernel(
    centres_h, counts_h, basis_h, facets_h, areas_h, low_ref, high_ref, tail_ref,
    packs, centres_s, counts_s, current_ref, facets_ref, areas_ref, arrived
):
    boxes = counts_s.shape[0]
    moves = [
        (basis_h.at[basis_h.shape[0] - 1], current_ref),
        (facets_h, facets_ref),
        (areas_h, areas_ref),
        (centres_h, centres_s),
        (counts_h, counts_s),
    ]
    copies = [pltpu.make_async_copy(a, b, arrived.at[k]) for k, (a, b) in enumerate(moves)]
    for copy in copies:
        copy.start()
    for copy in copies:
        copy.wait()
    lane = lax.broadcasted_iota(jnp.int32, (8, 128), 1)
    row = lax.broadcasted_iota(jnp.int32, (8, 128), 0)

    def one_box(b, carry):
        moments, centres = carry
        x, y, z = lattice(centres_s, b)
        plane = z & 1
        place = y * 4 + x
        slot = plane * plane_boxes + place
        lanes = pl.ds(pl.multiple_of(b * per_box, per_box), per_box)
        facets = facets_ref[:, lanes]
        live = live_row(counts_s, b)
        weighted = current_ref[:, lanes] * (wide_row(areas_ref, b) * live / per_box)
        charges = weighted.astype(bf16).astype(f32)
        start = pl.multiple_of(plane * pack_rows + place * box_rows, 8)
        packs[pl.ds(start, 8), :] = charges[:, :128]
        packs[pl.ds(start + 8, 8), :] = charges[:, 128:]
        packs[pl.ds(start + 16, 8), :] = jnp.concatenate(
            [facets[:, :128], facets[:, 128:], jnp.zeros((2, 128), f32)], axis=0
        )
        moments += jnp.where(lane == slot, jnp.sum(weighted, axis=1, keepdims=True), 0.0)
        for a in range(3):
            dipole = jnp.sum(weighted * (facets[a : a + 1] - centres_s[a, b]), axis=1, keepdims=True)
            moments += jnp.where(lane == 32 * (a + 1) + slot, dipole, 0.0)
            centres += jnp.where((lane == slot) & (row == a), centres_s[a, b], 0.0)
        return moments, centres

    zeros = jnp.zeros((8, 128), f32)
    moments, centres = lax.fori_loop(0, boxes, one_box, (zeros, zeros), unroll=4)
    for ref, first in ((low_ref, 0), (high_ref, pack_rows)):
        ref[:tail] = packs[first : first + tail]
        ref[tail : tail + 8] = moments
        ref[tail + 8 :] = centres
    tail_ref[:8] = moments
    tail_ref[8:] = centres


def thirds(x):
    high = x.astype(bf16).astype(f32)
    rest = x - high
    middle = rest.astype(bf16).astype(f32)
    return high, middle, (rest - middle).astype(bf16).astype(f32)


def stacked_rows(parts, width):
    zeros = jnp.zeros((depth - 8 * len(parts), width), f32)
    return jnp.concatenate([*parts, zeros], axis=0)


def local_facets(pack_ref, place, origin):
    start = pl.multiple_of(place * box_rows + 16, 8)
    tile = pack_ref[pl.ds(start, 8), :]
    both = jnp.concatenate([tile[0:3], tile[3:6]], axis=1)
    return jnp.concatenate([both - origin, jnp.zeros((5, 256), f32)], axis=0)


def slab_origin(centres_s):
    _, _, z = lattice(centres_s, 0)
    base_z = (z - (z & 1)).astype(f32) + 0.5
    axis_row = lax.broadcasted_iota(jnp.int32, (3, 1), 0)
    return jnp.where(axis_row == 2, base_z, 1.5), base_z


def store_source_features(local, charges, box, geometry, strengths):
    row = lax.broadcasted_iota(jnp.int32, (8, per_box), 0)
    square = jnp.sum(local * local, axis=0, keepdims=True)
    features = jnp.where(row == 3, square, jnp.where(row == 4, 1.0, local))
    high, middle, low = thirds(features)
    rows = stacked_rows((high, high, high, middle, middle, low), per_box)
    geometry[pl.ds(pl.multiple_of(box * depth, depth), depth), :] = rows.astype(bf16)
    products = jnp.concatenate([charges] + [charges * local[a : a + 1] for a in range(3)], axis=0)
    rows = jnp.concatenate([*thirds(products), jnp.zeros((32, per_box), f32)], axis=0)
    strengths[pl.ds(pl.multiple_of(box * per_box, per_box), per_box), :] = jnp.transpose(rows).astype(bf16)


def store_pack_features(pack, origin, geometry, strengths, first):
    def one_box(place, _):
        start = pl.multiple_of(place * box_rows, 8)
        charges = jnp.concatenate([pack[pl.ds(start, 8), :], pack[pl.ds(start + 8, 8), :]], axis=1)
        store_source_features(local_facets(pack, place, origin), charges, first + place, geometry, strengths)
        return 0

    lax.fori_loop(0, plane_boxes, one_box, 0, unroll=2)


def target_place(centres_s, b):
    x, y, z = lattice(centres_s, b)
    plane = z & 1
    place = y * 4 + x
    return x, y, plane, place, plane * plane_boxes + place


def near_planes(sources, geometry, strengths, targets, total, length):
    def near_rows(item, _):
        target_y = (item + 1) // 3
        source_y = target_y + lax.rem(item + 1, 3) - 1
        runs = []
        for first, planes in sources:
            for x in range(4):
                for plane in planes:
                    low, high = max(x - 1, 0), min(x + 2, 4)
                    start = (plane * plane_boxes + target_y * 4 + low) * per_box
                    size = (high - low) * per_box
                    for part in range(0, size, length):
                        rows_of = pl.ds(pl.multiple_of(start + part, 128), min(length, size))
                        runs.append((first + source_y * 4 + x, rows_of))

        def distances(box, rows_of):
            weights = geometry[pl.ds(pl.multiple_of(box * depth, depth), depth), :]
            return jnp.dot(targets[rows_of, :], weights, preferred_element_type=f32)

        ahead = distances(*runs[0])
        for i, (box, rows_of) in enumerate(runs):
            here = ahead
            if i + 1 < len(runs):
                ahead = distances(*runs[i + 1])
            inverse = lax.rsqrt(here)
            cubed = (inverse * inverse * inverse).astype(bf16)
            given = strengths[pl.ds(pl.multiple_of(box * per_box, per_box), per_box), :]
            total[rows_of, :] += jnp.dot(cubed, given, preferred_element_type=f32)

        return 0

    lax.fori_loop(0, 10, near_rows, 0)


def own_kernel(
    centres_s, counts_s, basis_ref, facets_ref, areas_ref, normals_ref, targets, planes, total, geometry, strengths
):
    boxes = counts_s.shape[0]
    krylov = basis_ref.shape[0]
    row = lax.broadcasted_iota(jnp.int32, (8, per_box), 0)
    origin, _ = slab_origin(centres_s)

    def target(b, _):
        _, _, _, _, slot = target_place(centres_s, b)
        lanes = pl.ds(pl.multiple_of(b * per_box, per_box), per_box)
        normal = normals_ref[:, lanes]
        five = jnp.zeros((5, per_box), f32)
        local_8 = jnp.concatenate([facets_ref[:, lanes] - origin, five], axis=0)
        normal_8 = jnp.concatenate([normal, five], axis=0)
        live = live_row(counts_s, b)
        weighted = basis_ref[krylov - 1, :, lanes] * (wide_row(areas_ref, b) * live / per_box)
        store_source_features(local_8, weighted.astype(bf16).astype(f32), slot, geometry, strengths)
        square = jnp.sum(local_8 * local_8, axis=0, keepdims=True) + soften
        along = jnp.sum(local_8 * normal_8, axis=0, keepdims=True)
        distance = jnp.where(row == 3, 1.0, jnp.where(row == 4, square, -2.0 * local_8))
        high, middle, low = thirds(distance)
        rows = stacked_rows((high, middle, low, high, middle, high), per_box)
        start = pl.multiple_of(slot * per_box, per_box)
        targets[pl.ds(start, per_box), :] = jnp.transpose(rows).astype(bf16)
        planes[pl.ds(pl.multiple_of(slot * 8, 8), 8), :] = jnp.where(row == 3, along, normal_8)
        return 0

    lax.fori_loop(0, boxes, target, 0, unroll=2)
    total[...] = jnp.zeros_like(total)
    near_planes(((0, (0, 1)), (plane_boxes, (0, 1))), geometry, strengths, targets, total, 128)


def halo_kernel(
    centres_s, counts_s, prev_ref, tail_ref, next_ref, facets_ref, normals_ref, contrast_ref, basis_ref, targets,
    planes, own_total, image_ref, sums_ref, geometry, strengths, total, field, far_centres
):
    boxes = counts_s.shape[0]
    krylov = basis_ref.shape[0]
    origin, base_z = slab_origin(centres_s)
    store_pack_features(prev_ref, origin, geometry, strengths, 0)
    store_pack_features(next_ref, origin, geometry, strengths, plane_boxes)
    total[...] = jnp.zeros_like(total)
    near_planes(((0, (0,)), (plane_boxes, (1,))), geometry, strengths, targets, total, 768)

    def near_field(slot, _):
        rows = pl.ds(pl.multiple_of(slot * per_box, per_box), per_box)
        turned = jnp.transpose(total[rows, :] + own_total[rows, :])
        sums = turned[:32] + (turned[32:64] + turned[64:96])
        side = planes[pl.ds(pl.multiple_of(slot * 8, 8), 8), :]
        value = side[3:4] * sums[:8] - side[0:1] * sums[8:16]
        value = value - side[1:2] * sums[16:24] - side[2:3] * sums[24:32]
        field[pl.ds(pl.multiple_of(slot * 8, 8), 8), :] = value
        return 0

    lax.fori_loop(0, boxes, near_field, 0, unroll=2)

    tails = (prev_ref[tail:, :], tail_ref[...], next_ref[tail:, :])
    for group in range(3):
        columns = jnp.transpose(tails[group][8:])[:32]
        for a in range(3):
            shift = base_z if a == 2 else 1.5
            far_centres[(group * 3 + a) * 32 : (group * 3 + a + 1) * 32, :] = jnp.broadcast_to(
                columns[:, a : a + 1] - shift, (32, 128)
            )
    far_moments = jnp.concatenate([part[:8] for part in tails], axis=1)
    far_high = far_moments.astype(bf16).astype(f32)
    far_both = jnp.concatenate([far_high, far_moments - far_high], axis=0)
    far_lane = lax.broadcasted_iota(jnp.int32, (1, 384), 1)
    lane_x = far_lane & 3
    lane_y = (far_lane >> 2) & 3
    lane_z = 2 * (far_lane >> 7) - 2 + ((far_lane >> 4) & 1)

    def far_box(b, _):
        x, y, plane, _, slot = target_place(centres_s, b)
        lanes = pl.ds(pl.multiple_of(b * per_box, per_box), per_box)
        local = facets_ref[:, lanes] - origin
        normal = normals_ref[:, lanes]
        coefficients = []
        for group in range(3):
            d = []
            for a in range(3):
                centre = far_centres[(group * 3 + a) * 32 : (group * 3 + a + 1) * 32, :]
                d.append(local[a : a + 1] - jnp.concatenate([centre, centre], axis=1))
            q = d[0] * d[0] + d[1] * d[1] + d[2] * d[2] + soften
            inverse = lax.rsqrt(q)
            inverse_2 = inverse * inverse
            inverse_3 = inverse_2 * inverse
            t = d[0] * normal[0:1] + d[1] * normal[1:2] + d[2] * normal[2:3]
            single = t * inverse_3
            coefficients.append(single)
            steep = 3.0 * single * inverse_2
            for a in range(3):
                coefficients.append(steep * d[a] - normal[a : a + 1] * inverse_3)
        whole = jnp.concatenate(coefficients, axis=0)
        upper = whole.astype(bf16)
        lower = (whole - upper.astype(f32)).astype(bf16)
        near = (jnp.abs(lane_x - x) <= 1) & (jnp.abs(lane_y - y) <= 1) & (jnp.abs(lane_z - plane) <= 1)
        picked = jnp.where(near, 0.0, far_both).astype(bf16)
        first = jnp.dot(picked, upper, preferred_element_type=f32)
        second = jnp.dot(picked, lower, preferred_element_type=f32)
        field[pl.ds(pl.multiple_of(slot * 8, 8), 8), :] += first[:8] + first[8:] + second[:8]
        return 0

    lax.fori_loop(0, boxes, far_box, 0, unroll=2)

    def image_box(b, carry):
        _, _, _, _, slot = target_place(centres_s, b)
        lanes = pl.ds(pl.multiple_of(b * per_box, per_box), per_box)
        live = live_row(counts_s, b)
        current = basis_ref[krylov - 1, :, lanes]
        part = field[pl.ds(pl.multiple_of(slot * 8, 8), 8), :]
        image = live * (current - 2.0 * wide_row(contrast_ref, b) * part)
        image_ref[:, lanes] = image
        sums = []
        for m in range(krylov + 1):
            product = image * (basis_ref[m, :, lanes] if m < krylov else image)
            sums.append(carry[m] + product[:, :128] + product[:, 128:])
        return tuple(sums)

    zeros = jnp.zeros((8, 128), f32)
    sums = lax.fori_loop(0, boxes, image_box, (zeros,) * (krylov + 1), unroll=2)
    pairs = [(m, n) for m in range(krylov) for n in range(m + 1)]

    def gram_box(b, carry):
        lanes = pl.ds(pl.multiple_of(b * per_box, per_box), per_box)
        live = live_row(counts_s, b)
        rows = [basis_ref[m, :, lanes] * live for m in range(krylov)]
        out = []
        for k, (m, n) in enumerate(pairs):
            product = rows[m] * rows[n]
            out.append(carry[k] + product[:, :128] + product[:, 128:])
        return tuple(out)

    gram = lax.fori_loop(0, boxes, gram_box, (zeros,) * len(pairs))
    lane = lax.broadcasted_iota(jnp.int32, (8, 128), 1)
    total = zeros
    for k, value in enumerate([*sums, *gram]):
        total = jnp.where(lane == k, jnp.sum(value, axis=1, keepdims=True), total)
    sums_ref[...] = jnp.broadcast_to(total[None], sums_ref.shape)


def two_sum(a, b):
    s = a + b
    c = s - a
    return s, (a - (s - c)) + (b - c)


def halves(a):
    c = a * 4097.0
    high = c - (c - a)
    return high, a - high


def two_product(a, b):
    p = a * b
    a_high, a_low = halves(a)
    b_high, b_low = halves(b)
    return p, ((a_high * b_high - p) + a_high * b_low + a_low * b_high) + a_low * b_low


def finish_kernel(total_facets, counts_s, tiles_ref, image_ref, basis_ref, next_ref, hessenberg_ref):
    boxes = counts_s.shape[0]
    krylov = basis_ref.shape[0]
    lane = lax.broadcasted_iota(jnp.int32, (8, 128), 1)

    def add_tile(i, carry):
        value, error = two_sum(carry[0], tiles_ref[i])
        return value, carry[1] + error

    sums, rest = lax.fori_loop(0, tiles_ref.shape[0], add_tile, (jnp.zeros((8, 128), f32),) * 2, unroll=8)
    exact = sums + rest
    projections = [exact[:, m : m + 1] / total_facets for m in range(krylov)]
    pairs = [(m, n) for m in range(krylov) for n in range(m + 1)]
    first = jnp.where(lane == krylov, 1.0, 0.0)
    second = jnp.where(lane <= krylov, 1.0, 0.0)
    for m in range(krylov):
        first = jnp.where(lane == m, -2.0 * projections[m], first)
    for k, (m, n) in enumerate(pairs):
        at = lane == krylov + 1 + k
        scale = 1.0 if m == n else 2.0
        first = jnp.where(at, scale * projections[m], first)
        second = jnp.where(at, projections[n], second)
    factor, factor_rest = two_product(first, second)
    value, value_rest = two_product(factor, sums)
    value_rest = value_rest + (factor * rest + factor_rest * sums)
    for shift in (64, 32, 16, 8, 4, 2, 1):
        other = pltpu.roll(value, shift, 1)
        other_rest = pltpu.roll(value_rest, shift, 1)
        value, error = two_sum(value, other)
        value_rest = (value_rest + other_rest) + error
    remaining = jnp.maximum(value + value_rest, 0.0)
    norm = jnp.sqrt(remaining / total_facets + epsilon)
    heads = jnp.where(lane == krylov, norm, 0.0)
    for m in range(krylov):
        heads = jnp.where(lane == m, projections[m], heads)
    hessenberg_ref[...] = heads[:, : krylov + 1]
    wide = [jnp.broadcast_to(p, (8, per_box)) for p in projections]
    scale = jnp.concatenate([1.0 / norm] * (per_box // 128), axis=1)

    def one_box(b, _):
        lanes = pl.ds(pl.multiple_of(b * per_box, per_box), per_box)
        live = live_row(counts_s, b)
        sent = wide[0] * basis_ref[0, :, lanes]
        for m in range(1, krylov):
            sent += wide[m] * basis_ref[m, :, lanes]
        next_ref[:, lanes] = (image_ref[:, lanes] - sent * live) * scale
        return 0

    lax.fori_loop(0, boxes, one_box, 0, unroll=4)


smem = pl.BlockSpec(memory_space=pltpu.SMEM)
vmem = pl.BlockSpec(memory_space=pltpu.VMEM)


def on_device(
    basis, facet_centres, normals, areas, contrast, facet_counts, box_centres, near_boxes, far_boxes
):
    krylov, rhs_local, facet_local = basis.shape
    boxes = facet_counts.shape[0]
    count = lax.axis_size("box")
    total_facets = count * facet_local
    areas = areas.reshape(-1, 128)
    contrast = contrast.reshape(-1, 128)
    pack = jax.ShapeDtypeStruct((pack_rows, 128), f32)
    low, high, own_tail = pl.pallas_call(
        prep_kernel,
        out_shape=(pack, pack, jax.ShapeDtypeStruct((16, 128), f32)),
        in_specs=[pl.BlockSpec(memory_space=pl.ANY)] * 5,
        out_specs=(vmem,) * 3,
        scratch_shapes=[
            pltpu.VMEM((2 * pack_rows, 128), f32),
            pltpu.SMEM(box_centres.shape, f32),
            pltpu.SMEM(facet_counts.shape, jnp.int32),
            pltpu.VMEM((rhs_local, facet_local), f32),
            pltpu.VMEM(facet_centres.shape, f32),
            pltpu.VMEM(areas.shape, f32),
            pltpu.SemaphoreType.DMA((5,)),
        ],
        name="prepare",
    )(box_centres, facet_counts, basis, facet_centres, areas)
    below = lax.ppermute(high, "box", [(i, i + 1) for i in range(count - 1)])
    above = lax.ppermute(low, "box", [(i + 1, i) for i in range(count - 1)])
    slots = boxes * per_box
    targets, planes, own_total = pl.pallas_call(
        own_kernel,
        out_shape=(
            jax.ShapeDtypeStruct((slots, depth), bf16),
            jax.ShapeDtypeStruct((boxes * 8, per_box), f32),
            jax.ShapeDtypeStruct((slots, 128), f32),
        ),
        in_specs=[smem, smem] + [vmem] * 4,
        out_specs=(vmem,) * 3,
        scratch_shapes=[pltpu.VMEM((boxes * depth, per_box), bf16), pltpu.VMEM((slots, 128), bf16)],
        compiler_params=pltpu.CompilerParams(vmem_limit_bytes=24 * 1024 * 1024),
        name="own",
    )(box_centres, facet_counts, basis, facet_centres, areas, normals)
    image, tiles = pl.pallas_call(
        halo_kernel,
        out_shape=(
            jax.ShapeDtypeStruct((rhs_local, facet_local), f32),
            jax.ShapeDtypeStruct((count, 8, 128), f32),
        ),
        in_specs=[smem, smem] + [vmem] * 10,
        out_specs=(vmem, vmem),
        scratch_shapes=[
            pltpu.VMEM((boxes * depth, per_box), bf16),
            pltpu.VMEM((slots, 128), bf16),
            pltpu.VMEM((slots, 128), f32),
            pltpu.VMEM((boxes * 8, per_box), f32),
            pltpu.VMEM((9 * 32, 128), f32),
        ],
        compiler_params=pltpu.CompilerParams(vmem_limit_bytes=32 * 1024 * 1024),
        name="halo",
    )(
        box_centres, facet_counts, below, own_tail, above, facet_centres, normals, contrast, basis, targets, planes, own_total
    )
    tiles = lax.all_to_all(tiles, "box", 0, 0, tiled=True)
    next_vector, hessenberg = pl.pallas_call(
        functools.partial(finish_kernel, total_facets),
        out_shape=(
            jax.ShapeDtypeStruct((rhs_local, facet_local), f32),
            jax.ShapeDtypeStruct((rhs_local, krylov + 1), f32),
        ),
        in_specs=[smem] + [vmem] * 3,
        out_specs=(vmem, vmem),
        compiler_params=pltpu.CompilerParams(vmem_limit_bytes=16 * 1024 * 1024),
        name="finish",
    )(facet_counts, tiles, image, basis)
    return next_vector, hessenberg.T


def solution(mesh):
    return jax.shard_map(
        on_device,
        mesh=mesh,
        in_specs=(
            P(None, "rhs", "box"),
            P(None, "box"),
            P(None, "box"),
            P("box"),
            P("box"),
            P("box"),
            P(None, "box"),
            P("box", None),
            P("box", None),
        ),
        out_specs=(P("rhs", "box"), P(None, "rhs")),
        check_vma=False,
    )
```

```python
import functools

import jax
import jax.numpy as jnp
from jax import lax
from jax.experimental import pallas as pl
from jax.experimental.pallas import tpu as pltpu
from jax.sharding import PartitionSpec as P

soften = 0.0025
epsilon = 1e-06
f32 = jnp.float32
bf16 = jnp.bfloat16
box_rows = 24
plane_boxes = 16
per_box = 256
tail = plane_boxes * box_rows
pack_rows = tail + 16
depth = 128


def lattice(centres_s, b):
    x = (centres_s[0, b] + 0.5).astype(jnp.int32)
    y = (centres_s[1, b] + 0.5).astype(jnp.int32)
    z = (centres_s[2, b] + 0.5).astype(jnp.int32)
    return x, y, z


def wide_row(ref, b):
    return jnp.concatenate([ref[pl.ds(2 * b, 1), :], ref[pl.ds(2 * b + 1, 1), :]], axis=1)


def live_row(counts_s, b):
    slots = lax.broadcasted_iota(jnp.int32, (1, per_box), 1)
    return (slots < counts_s[b]).astype(f32)


def prep_kernel(
    centres_h, counts_h, basis_h, facets_h, areas_h, low_ref, high_ref, tail_ref,
    packs, centres_s, counts_s, current_ref, facets_ref, areas_ref, arrived
):
    boxes = counts_s.shape[0]
    moves = [
        (basis_h.at[basis_h.shape[0] - 1], current_ref),
        (facets_h, facets_ref),
        (areas_h, areas_ref),
        (centres_h, centres_s),
        (counts_h, counts_s),
    ]
    copies = [pltpu.make_async_copy(a, b, arrived.at[k]) for k, (a, b) in enumerate(moves)]
    for copy in copies:
        copy.start()
    for copy in copies:
        copy.wait()
    lane = lax.broadcasted_iota(jnp.int32, (8, 128), 1)
    row = lax.broadcasted_iota(jnp.int32, (8, 128), 0)

    def one_box(b, carry):
        moments, centres = carry
        x, y, z = lattice(centres_s, b)
        plane = z & 1
        place = y * 4 + x
        slot = plane * plane_boxes + place
        lanes = pl.ds(pl.multiple_of(b * per_box, per_box), per_box)
        facets = facets_ref[:, lanes]
        live = live_row(counts_s, b)
        weighted = current_ref[:, lanes] * (wide_row(areas_ref, b) * live / per_box)
        charges = weighted.astype(bf16).astype(f32)
        start = pl.multiple_of(plane * pack_rows + place * box_rows, 8)
        packs[pl.ds(start, 8), :] = charges[:, :128]
        packs[pl.ds(start + 8, 8), :] = charges[:, 128:]
        packs[pl.ds(start + 16, 8), :] = jnp.concatenate(
            [facets[:, :128], facets[:, 128:], jnp.zeros((2, 128), f32)], axis=0
        )
        moments += jnp.where(lane == slot, jnp.sum(weighted, axis=1, keepdims=True), 0.0)
        for a in range(3):
            dipole = jnp.sum(weighted * (facets[a : a + 1] - centres_s[a, b]), axis=1, keepdims=True)
            moments += jnp.where(lane == 32 * (a + 1) + slot, dipole, 0.0)
            centres += jnp.where((lane == slot) & (row == a), centres_s[a, b], 0.0)
        return moments, centres

    zeros = jnp.zeros((8, 128), f32)
    moments, centres = lax.fori_loop(0, boxes, one_box, (zeros, zeros), unroll=4)
    for ref, first in ((low_ref, 0), (high_ref, pack_rows)):
        ref[:tail] = packs[first : first + tail]
        ref[tail : tail + 8] = moments
        ref[tail + 8 :] = centres
    tail_ref[:8] = moments
    tail_ref[8:] = centres


def thirds(x):
    high = x.astype(bf16).astype(f32)
    rest = x - high
    middle = rest.astype(bf16).astype(f32)
    return high, middle, (rest - middle).astype(bf16).astype(f32)


def stacked_rows(parts, width):
    zeros = jnp.zeros((depth - 8 * len(parts), width), f32)
    return jnp.concatenate([*parts, zeros], axis=0)


def local_facets(pack_ref, place, origin):
    start = pl.multiple_of(place * box_rows + 16, 8)
    tile = pack_ref[pl.ds(start, 8), :]
    both = jnp.concatenate([tile[0:3], tile[3:6]], axis=1)
    return jnp.concatenate([both - origin, jnp.zeros((5, 256), f32)], axis=0)


def slab_origin(centres_s):
    _, _, z = lattice(centres_s, 0)
    base_z = (z - (z & 1)).astype(f32) + 0.5
    axis_row = lax.broadcasted_iota(jnp.int32, (3, 1), 0)
    return jnp.where(axis_row == 2, base_z, 1.5), base_z


def store_source_features(local, charges, box, geometry, strengths):
    row = lax.broadcasted_iota(jnp.int32, (8, per_box), 0)
    square = jnp.sum(local * local, axis=0, keepdims=True)
    features = jnp.where(row == 3, square, jnp.where(row == 4, 1.0, local))
    high, middle, low = thirds(features)
    rows = stacked_rows((high, high, high, middle, middle, low), per_box)
    geometry[pl.ds(pl.multiple_of(box * depth, depth), depth), :] = rows.astype(bf16)
    products = jnp.concatenate([charges] + [charges * local[a : a + 1] for a in range(3)], axis=0)
    rows = jnp.concatenate([*thirds(products), jnp.zeros((32, per_box), f32)], axis=0)
    strengths[pl.ds(pl.multiple_of(box * per_box, per_box), per_box), :] = jnp.transpose(rows).astype(bf16)


def store_pack_features(pack, origin, geometry, strengths, first):
    def one_box(place, _):
        start = pl.multiple_of(place * box_rows, 8)
        charges = jnp.concatenate([pack[pl.ds(start, 8), :], pack[pl.ds(start + 8, 8), :]], axis=1)
        store_source_features(local_facets(pack, place, origin), charges, first + place, geometry, strengths)
        return 0

    lax.fori_loop(0, plane_boxes, one_box, 0, unroll=2)


def target_place(centres_s, b):
    x, y, z = lattice(centres_s, b)
    plane = z & 1
    place = y * 4 + x
    return x, y, plane, place, plane * plane_boxes + place


def near_planes(sources, geometry, strengths, targets, total, beside=None):
    def near_rows(item, _):
        target_y = (item + 1) // 3
        source_y = target_y + lax.rem(item + 1, 3) - 1
        runs = []
        for first, planes in sources:
            for x in range(4):
                for plane in planes:
                    low, high = max(x - 1, 0), min(x + 2, 4)
                    start = (plane * plane_boxes + target_y * 4 + low) * per_box
                    size = (high - low) * per_box
                    for part in range(0, size, per_box):
                        rows_of = pl.ds(pl.multiple_of(start + part, per_box), per_box)
                        runs.append((first + source_y * 4 + x, rows_of))

        def distances(box, rows_of):
            weights = geometry[pl.ds(pl.multiple_of(box * depth, depth), depth), :]
            return jnp.dot(targets[rows_of, :], weights, preferred_element_type=f32)

        ahead = distances(*runs[0])
        for i, (box, rows_of) in enumerate(runs):
            if beside is not None and i % 5 == 0:
                beside(item * 4 + i // 5)
            here = ahead
            if i + 1 < len(runs):
                ahead = distances(*runs[i + 1])
            inverse = lax.rsqrt(here)
            cubed = (inverse * inverse * inverse).astype(bf16)
            given = strengths[pl.ds(pl.multiple_of(box * per_box, per_box), per_box), :]
            total[rows_of, :] += jnp.dot(cubed, given, preferred_element_type=f32)

        return 0

    lax.fori_loop(0, 10, near_rows, 0)


def own_kernel(
    centres_s, counts_s, basis_ref, facets_ref, areas_ref, normals_ref, targets, planes, total, geometry, strengths
):
    boxes = counts_s.shape[0]
    krylov = basis_ref.shape[0]
    row = lax.broadcasted_iota(jnp.int32, (8, per_box), 0)
    origin, _ = slab_origin(centres_s)

    def target(b, _):
        _, _, _, _, slot = target_place(centres_s, b)
        lanes = pl.ds(pl.multiple_of(b * per_box, per_box), per_box)
        normal = normals_ref[:, lanes]
        five = jnp.zeros((5, per_box), f32)
        local_8 = jnp.concatenate([facets_ref[:, lanes] - origin, five], axis=0)
        normal_8 = jnp.concatenate([normal, five], axis=0)
        live = live_row(counts_s, b)
        weighted = basis_ref[krylov - 1, :, lanes] * (wide_row(areas_ref, b) * live / per_box)
        store_source_features(local_8, weighted.astype(bf16).astype(f32), slot, geometry, strengths)
        square = jnp.sum(local_8 * local_8, axis=0, keepdims=True) + soften
        along = jnp.sum(local_8 * normal_8, axis=0, keepdims=True)
        distance = jnp.where(row == 3, 1.0, jnp.where(row == 4, square, -2.0 * local_8))
        high, middle, low = thirds(distance)
        rows = stacked_rows((high, middle, low, high, middle, high), per_box)
        start = pl.multiple_of(slot * per_box, per_box)
        targets[pl.ds(start, per_box), :] = jnp.transpose(rows).astype(bf16)
        planes[pl.ds(pl.multiple_of(slot * 8, 8), 8), :] = jnp.where(row == 3, along, normal_8)
        return 0

    lax.fori_loop(0, boxes, target, 0, unroll=2)
    total[...] = jnp.zeros_like(total)
    near_planes(((0, (0, 1)), (plane_boxes, (0, 1))), geometry, strengths, targets, total)


def halo_kernel(
    centres_s, counts_s, prev_ref, tail_ref, next_ref, facets_ref, normals_ref, contrast_ref, basis_ref, targets,
    planes, own_total, image_ref, sums_ref, geometry, strengths, total, field, far_centres
):
    boxes = counts_s.shape[0]
    krylov = basis_ref.shape[0]
    origin, base_z = slab_origin(centres_s)
    store_pack_features(prev_ref, origin, geometry, strengths, 0)
    store_pack_features(next_ref, origin, geometry, strengths, plane_boxes)
    total[...] = jnp.zeros_like(total)

    tails = (prev_ref[tail:, :], tail_ref[...], next_ref[tail:, :])
    for group in range(3):
        columns = jnp.transpose(tails[group][8:])[:32]
        for a in range(3):
            shift = base_z if a == 2 else 1.5
            far_centres[(group * 3 + a) * 32 : (group * 3 + a + 1) * 32, :] = jnp.broadcast_to(
                columns[:, a : a + 1] - shift, (32, 128)
            )
    far_moments = jnp.concatenate([part[:8] for part in tails], axis=1)
    far_high = far_moments.astype(bf16).astype(f32)
    far_both = jnp.concatenate([far_high, far_moments - far_high], axis=0)
    far_lane = lax.broadcasted_iota(jnp.int32, (1, 384), 1)
    lane_x = far_lane & 3
    lane_y = (far_lane >> 2) & 3
    lane_z = 2 * (far_lane >> 7) - 2 + ((far_lane >> 4) & 1)

    def far_box(k):
        b = jnp.minimum(k, boxes - 1)
        x, y, plane, _, slot = target_place(centres_s, b)
        lanes = pl.ds(pl.multiple_of(b * per_box, per_box), per_box)
        local = facets_ref[:, lanes] - origin
        normal = normals_ref[:, lanes]
        coefficients = []
        for group in range(3):
            d = []
            for a in range(3):
                centre = far_centres[(group * 3 + a) * 32 : (group * 3 + a + 1) * 32, :]
                d.append(local[a : a + 1] - jnp.concatenate([centre, centre], axis=1))
            q = d[0] * d[0] + d[1] * d[1] + d[2] * d[2] + soften
            inverse = lax.rsqrt(q)
            inverse_2 = inverse * inverse
            inverse_3 = inverse_2 * inverse
            t = d[0] * normal[0:1] + d[1] * normal[1:2] + d[2] * normal[2:3]
            single = t * inverse_3
            coefficients.append(single)
            steep = 3.0 * single * inverse_2
            for a in range(3):
                coefficients.append(steep * d[a] - normal[a : a + 1] * inverse_3)
        whole = jnp.concatenate(coefficients, axis=0)
        upper = whole.astype(bf16)
        lower = (whole - upper.astype(f32)).astype(bf16)
        near = (jnp.abs(lane_x - x) <= 1) & (jnp.abs(lane_y - y) <= 1) & (jnp.abs(lane_z - plane) <= 1)
        picked = jnp.where(near, 0.0, far_both).astype(bf16)
        first = jnp.dot(picked, upper, preferred_element_type=f32)
        second = jnp.dot(picked, lower, preferred_element_type=f32)
        field[pl.ds(pl.multiple_of(slot * 8, 8), 8), :] = first[:8] + first[8:] + second[:8]

    near_planes(((0, (0,)), (plane_boxes, (1,))), geometry, strengths, targets, total, far_box)

    def near_field(slot, _):
        rows = pl.ds(pl.multiple_of(slot * per_box, per_box), per_box)
        turned = jnp.transpose(total[rows, :] + own_total[rows, :])
        sums = turned[:32] + (turned[32:64] + turned[64:96])
        side = planes[pl.ds(pl.multiple_of(slot * 8, 8), 8), :]
        value = side[3:4] * sums[:8] - side[0:1] * sums[8:16]
        value = value - side[1:2] * sums[16:24] - side[2:3] * sums[24:32]
        field[pl.ds(pl.multiple_of(slot * 8, 8), 8), :] += value
        return 0

    lax.fori_loop(0, boxes, near_field, 0, unroll=2)

    def image_box(b, carry):
        _, _, _, _, slot = target_place(centres_s, b)
        lanes = pl.ds(pl.multiple_of(b * per_box, per_box), per_box)
        live = live_row(counts_s, b)
        current = basis_ref[krylov - 1, :, lanes]
        part = field[pl.ds(pl.multiple_of(slot * 8, 8), 8), :]
        image = live * (current - 2.0 * wide_row(contrast_ref, b) * part)
        image_ref[:, lanes] = image
        sums = []
        for m in range(krylov + 1):
            product = image * (basis_ref[m, :, lanes] if m < krylov else image)
            sums.append(carry[m] + product[:, :128] + product[:, 128:])
        return tuple(sums)

    zeros = jnp.zeros((8, 128), f32)
    sums = lax.fori_loop(0, boxes, image_box, (zeros,) * (krylov + 1), unroll=2)
    pairs = [(m, n) for m in range(krylov) for n in range(m + 1)]

    def gram_box(b, carry):
        lanes = pl.ds(pl.multiple_of(b * per_box, per_box), per_box)
        live = live_row(counts_s, b)
        rows = [basis_ref[m, :, lanes] * live for m in range(krylov)]
        out = []
        for k, (m, n) in enumerate(pairs):
            product = rows[m] * rows[n]
            out.append(carry[k] + product[:, :128] + product[:, 128:])
        return tuple(out)

    gram = lax.fori_loop(0, boxes, gram_box, (zeros,) * len(pairs))
    lane = lax.broadcasted_iota(jnp.int32, (8, 128), 1)
    total_sums = zeros
    for k, value in enumerate([*sums, *gram]):
        total_sums = jnp.where(lane == k, jnp.sum(value, axis=1, keepdims=True), total_sums)
    sums_ref[...] = total_sums


def two_sum(a, b):
    s = a + b
    c = s - a
    return s, (a - (s - c)) + (b - c)


def halves(a):
    c = a * 4097.0
    high = c - (c - a)
    return high, a - high


def two_product(a, b):
    p = a * b
    a_high, a_low = halves(a)
    b_high, b_low = halves(b)
    return p, ((a_high * b_high - p) + a_high * b_low + a_low * b_high) + a_low * b_low


def finish_kernel(total_facets, counts_s, tiles_ref, image_ref, basis_ref, next_ref, hessenberg_ref):
    boxes = counts_s.shape[0]
    krylov = basis_ref.shape[0]
    lane = lax.broadcasted_iota(jnp.int32, (8, 128), 1)

    def add_tile(i, carry):
        value, error = two_sum(carry[0], tiles_ref[i])
        return value, carry[1] + error

    sums, rest = lax.fori_loop(0, tiles_ref.shape[0], add_tile, (jnp.zeros((8, 128), f32),) * 2, unroll=8)
    exact = sums + rest
    projections = [exact[:, m : m + 1] / total_facets for m in range(krylov)]
    pairs = [(m, n) for m in range(krylov) for n in range(m + 1)]
    first = jnp.where(lane == krylov, 1.0, 0.0)
    second = jnp.where(lane <= krylov, 1.0, 0.0)
    for m in range(krylov):
        first = jnp.where(lane == m, -2.0 * projections[m], first)
    for k, (m, n) in enumerate(pairs):
        at = lane == krylov + 1 + k
        scale = 1.0 if m == n else 2.0
        first = jnp.where(at, scale * projections[m], first)
        second = jnp.where(at, projections[n], second)
    factor, factor_rest = two_product(first, second)
    value, value_rest = two_product(factor, sums)
    value_rest = value_rest + (factor * rest + factor_rest * sums)
    for shift in (64, 32, 16, 8, 4, 2, 1):
        other = pltpu.roll(value, shift, 1)
        other_rest = pltpu.roll(value_rest, shift, 1)
        value, error = two_sum(value, other)
        value_rest = (value_rest + other_rest) + error
    remaining = jnp.maximum(value + value_rest, 0.0)
    norm = jnp.sqrt(remaining / total_facets + epsilon)
    heads = jnp.where(lane == krylov, norm, 0.0)
    for m in range(krylov):
        heads = jnp.where(lane == m, projections[m], heads)
    hessenberg_ref[...] = heads[:, : krylov + 1]
    wide = [jnp.broadcast_to(p, (8, per_box)) for p in projections]
    scale = jnp.concatenate([1.0 / norm] * (per_box // 128), axis=1)

    def one_box(b, _):
        lanes = pl.ds(pl.multiple_of(b * per_box, per_box), per_box)
        live = live_row(counts_s, b)
        sent = wide[0] * basis_ref[0, :, lanes]
        for m in range(1, krylov):
            sent += wide[m] * basis_ref[m, :, lanes]
        next_ref[:, lanes] = (image_ref[:, lanes] - sent * live) * scale
        return 0

    lax.fori_loop(0, boxes, one_box, 0, unroll=4)


smem = pl.BlockSpec(memory_space=pltpu.SMEM)
vmem = pl.BlockSpec(memory_space=pltpu.VMEM)


def on_device(
    basis, facet_centres, normals, areas, contrast, facet_counts, box_centres, near_boxes, far_boxes
):
    krylov, rhs_local, facet_local = basis.shape
    boxes = facet_counts.shape[0]
    count = lax.axis_size("box")
    total_facets = count * facet_local
    areas = areas.reshape(-1, 128)
    contrast = contrast.reshape(-1, 128)
    pack = jax.ShapeDtypeStruct((pack_rows, 128), f32)
    low, high, own_tail = pl.pallas_call(
        prep_kernel,
        out_shape=(pack, pack, jax.ShapeDtypeStruct((16, 128), f32)),
        in_specs=[pl.BlockSpec(memory_space=pl.ANY)] * 5,
        out_specs=(vmem,) * 3,
        scratch_shapes=[
            pltpu.VMEM((2 * pack_rows, 128), f32),
            pltpu.SMEM(box_centres.shape, f32),
            pltpu.SMEM(facet_counts.shape, jnp.int32),
            pltpu.VMEM((rhs_local, facet_local), f32),
            pltpu.VMEM(facet_centres.shape, f32),
            pltpu.VMEM(areas.shape, f32),
            pltpu.SemaphoreType.DMA((5,)),
        ],
        name="prepare",
    )(box_centres, facet_counts, basis, facet_centres, areas)
    below = lax.ppermute(high, "box", [(i, i + 1) for i in range(count - 1)])
    above = lax.ppermute(low, "box", [(i + 1, i) for i in range(count - 1)])
    slots = boxes * per_box
    targets, planes, own_total = pl.pallas_call(
        own_kernel,
        out_shape=(
            jax.ShapeDtypeStruct((slots, depth), bf16),
            jax.ShapeDtypeStruct((boxes * 8, per_box), f32),
            jax.ShapeDtypeStruct((slots, 128), f32),
        ),
        in_specs=[smem, smem] + [vmem] * 4,
        out_specs=(vmem,) * 3,
        scratch_shapes=[pltpu.VMEM((boxes * depth, per_box), bf16), pltpu.VMEM((slots, 128), bf16)],
        compiler_params=pltpu.CompilerParams(vmem_limit_bytes=24 * 1024 * 1024),
        name="own",
    )(box_centres, facet_counts, basis, facet_centres, areas, normals)
    image, tiles = pl.pallas_call(
        halo_kernel,
        out_shape=(
            jax.ShapeDtypeStruct((rhs_local, facet_local), f32),
            jax.ShapeDtypeStruct((8, 128), f32),
        ),
        in_specs=[smem, smem] + [vmem] * 10,
        out_specs=(vmem, vmem),
        scratch_shapes=[
            pltpu.VMEM((boxes * depth, per_box), bf16),
            pltpu.VMEM((slots, 128), bf16),
            pltpu.VMEM((slots, 128), f32),
            pltpu.VMEM((boxes * 8, per_box), f32),
            pltpu.VMEM((9 * 32, 128), f32),
        ],
        compiler_params=pltpu.CompilerParams(vmem_limit_bytes=32 * 1024 * 1024),
        name="halo",
    )(
        box_centres, facet_counts, below, own_tail, above, facet_centres, normals, contrast, basis, targets, planes, own_total
    )
    tiles = lax.all_gather(tiles, "box")
    next_vector, hessenberg = pl.pallas_call(
        functools.partial(finish_kernel, total_facets),
        out_shape=(
            jax.ShapeDtypeStruct((rhs_local, facet_local), f32),
            jax.ShapeDtypeStruct((rhs_local, krylov + 1), f32),
        ),
        in_specs=[smem] + [vmem] * 3,
        out_specs=(vmem, vmem),
        compiler_params=pltpu.CompilerParams(vmem_limit_bytes=16 * 1024 * 1024),
        name="finish",
    )(facet_counts, tiles, image, basis)
    return next_vector, hessenberg.T


def solution(mesh):
    return jax.shard_map(
        on_device,
        mesh=mesh,
        in_specs=(
            P(None, "rhs", "box"),
            P(None, "box"),
            P(None, "box"),
            P("box"),
            P("box"),
            P("box"),
            P(None, "box"),
            P("box", None),
            P("box", None),
        ),
        out_specs=(P("rhs", "box"), P(None, "rhs")),
        check_vma=False,
    )
```

```python
import functools

import jax
import jax.numpy as jnp
from jax import lax
from jax.experimental import pallas as pl
from jax.experimental.pallas import tpu as pltpu
from jax.sharding import PartitionSpec as P

soften = 0.0025
epsilon = 1e-06
f32 = jnp.float32
bf16 = jnp.bfloat16
plane_boxes = 16
per_box = 256
depth = 128


def lattice(centres_s, b):
    x = (centres_s[0, b] + 0.5).astype(jnp.int32)
    y = (centres_s[1, b] + 0.5).astype(jnp.int32)
    z = (centres_s[2, b] + 0.5).astype(jnp.int32)
    return x, y, z


def slot_of(centres_s, b):
    x, y, z = lattice(centres_s, b)
    return (z & 1) * plane_boxes + y * 4 + x


def boxes_by_slot(centres_s, boxes_s):
    def one_box(b, _):
        boxes_s[slot_of(centres_s, b)] = b
        return 0

    lax.fori_loop(0, centres_s.shape[1], one_box, 0)


def wide_row(ref, b):
    return jnp.concatenate([ref[pl.ds(2 * b, 1), :], ref[pl.ds(2 * b + 1, 1), :]], axis=1)


def live_row(counts_s, b):
    slots = lax.broadcasted_iota(jnp.int32, (1, per_box), 1)
    return (slots < counts_s[b]).astype(f32)


def prep_kernel(
    centres_h, counts_h, basis_h, facets_h, areas_h, cross_ref, first_ref, second_ref, tail_ref,
    charges_v, places_v, centres_s, counts_s, current_ref, facets_ref, areas_ref, arrived
):
    boxes = counts_s.shape[0]
    moves = [
        (basis_h.at[basis_h.shape[0] - 1], current_ref),
        (facets_h, facets_ref),
        (areas_h, areas_ref),
        (centres_h, centres_s),
        (counts_h, counts_s),
    ]
    copies = [pltpu.make_async_copy(a, b, arrived.at[k]) for k, (a, b) in enumerate(moves)]
    for copy in copies:
        copy.start()
    for copy in copies:
        copy.wait()
    lane = lax.broadcasted_iota(jnp.int32, (8, 128), 1)
    row = lax.broadcasted_iota(jnp.int32, (8, 128), 0)

    def one_box(b, carry):
        moments, centres = carry
        slot = slot_of(centres_s, b)
        lanes = pl.ds(pl.multiple_of(b * per_box, per_box), per_box)
        facets = facets_ref[:, lanes]
        live = live_row(counts_s, b)
        weighted = current_ref[:, lanes] * (wide_row(areas_ref, b) * live / per_box)
        charges = weighted.astype(bf16).astype(f32)
        start = pl.multiple_of(slot * 16, 16)
        charges_v[pl.ds(start, 8), :] = charges[:, :128]
        charges_v[pl.ds(start + 8, 8), :] = charges[:, 128:]
        places_v[pl.ds(pl.multiple_of(slot * 8, 8), 8), :] = jnp.concatenate(
            [facets[:, :128], facets[:, 128:], jnp.zeros((2, 128), f32)], axis=0
        )
        moments += jnp.where(lane == slot, jnp.sum(weighted, axis=1, keepdims=True), 0.0)
        for a in range(3):
            dipole = jnp.sum(weighted * (facets[a : a + 1] - centres_s[a, b]), axis=1, keepdims=True)
            moments += jnp.where(lane == 32 * (a + 1) + slot, dipole, 0.0)
            centres += jnp.where((lane == slot) & (row == a), centres_s[a, b], 0.0)
        return moments, centres

    zeros = jnp.zeros((8, 128), f32)
    moments, centres = lax.fori_loop(0, boxes, one_box, (zeros, zeros), unroll=4)
    half = lax.axis_index("rhs")
    cross_ref[:512] = charges_v[...]
    cross_ref[512:] = moments
    first_ref[:256] = charges_v[pl.ds(pl.multiple_of((1 - half) * 256, 256), 256), :]
    first_ref[256:384] = places_v[pl.ds(pl.multiple_of((1 - half) * 128, 128), 128), :]
    first_ref[384:392] = moments
    first_ref[392:] = centres
    second_ref[:256] = charges_v[pl.ds(pl.multiple_of(half * 256, 256), 256), :]
    second_ref[256:] = moments
    tail_ref[:8] = moments
    tail_ref[8:] = centres


def thirds(x):
    high = x.astype(bf16).astype(f32)
    rest = x - high
    middle = rest.astype(bf16).astype(f32)
    return high, middle, (rest - middle).astype(bf16).astype(f32)


def stacked_rows(parts, width):
    zeros = jnp.zeros((depth - 8 * len(parts), width), f32)
    return jnp.concatenate([*parts, zeros], axis=0)


def slab_origin(centres_s):
    _, _, z = lattice(centres_s, 0)
    base_z = (z - (z & 1)).astype(f32) + 0.5
    axis_row = lax.broadcasted_iota(jnp.int32, (3, 1), 0)
    return jnp.where(axis_row == 2, base_z, 1.5), base_z


def padded(rows):
    return jnp.concatenate([rows, jnp.zeros((8 - rows.shape[0], rows.shape[1]), f32)], axis=0)


def wide_charges(ref, start):
    start = pl.multiple_of(start, 16)
    return jnp.concatenate([ref[pl.ds(start, 8), :], ref[pl.ds(start + 8, 8), :]], axis=1)


def store_source_features(local, charges, box, geometry, strengths):
    row = lax.broadcasted_iota(jnp.int32, (8, per_box), 0)
    square = jnp.sum(local * local, axis=0, keepdims=True)
    features = jnp.where(row == 3, square, jnp.where(row == 4, 1.0, local))
    high, middle, low = thirds(features)
    rows = stacked_rows((high, high, high, middle, middle, low), per_box)
    geometry[pl.ds(pl.multiple_of(box * depth, depth), depth), :] = rows.astype(bf16)
    products = jnp.concatenate([charges] + [charges * local[a : a + 1] for a in range(3)], axis=0)
    rows = jnp.concatenate([*thirds(products), jnp.zeros((64, per_box), f32)], axis=0)
    strengths[pl.ds(pl.multiple_of(box * per_box, per_box), per_box), :] = jnp.transpose(rows).astype(bf16)


def near_planes(sources, geometry, strengths, targets, total, beside=None):
    def near_rows(item, _):
        target_y = (item + 1) // 3
        source_y = target_y + lax.rem(item + 1, 3) - 1
        runs = []
        for first in sources:
            for x in range(4):
                for near_x in range(max(x - 1, 0), min(x + 2, 4)):
                    start = pl.multiple_of((target_y * 4 + near_x) * per_box, per_box)
                    runs.append((first + source_y * 4 + x, pl.ds(start, per_box)))

        def distances(box, rows_of):
            weights = geometry[pl.ds(pl.multiple_of(box * depth, depth), depth), :]
            return jnp.dot(targets[rows_of, :], weights, preferred_element_type=f32)

        ahead = distances(*runs[0])
        for i, (box, rows_of) in enumerate(runs):
            here = ahead
            if i + 1 < len(runs):
                ahead = distances(*runs[i + 1])
            inverse = lax.rsqrt(here)
            cubed = (inverse * inverse * inverse).astype(bf16)
            given = strengths[pl.ds(pl.multiple_of(box * per_box, per_box), per_box), :]
            total[rows_of, :] += jnp.dot(cubed, given, preferred_element_type=f32)
        if beside is not None:
            beside(item)
        return 0

    lax.fori_loop(0, 10, near_rows, 0)


def own_kernel(
    centres_s, counts_s, basis_ref, facets_ref, areas_ref, normals_ref, cross_ref, targets, planes, total,
    geometry, strengths, boxes_s
):
    boxes = counts_s.shape[0]
    krylov = basis_ref.shape[0]
    row = lax.broadcasted_iota(jnp.int32, (8, per_box), 0)
    origin, _ = slab_origin(centres_s)
    boxes_by_slot(centres_s, boxes_s)
    half = lax.axis_index("rhs")

    def source(slot, _):
        b = boxes_s[slot]
        lanes = pl.ds(pl.multiple_of(b * per_box, per_box), per_box)
        live = live_row(counts_s, b)
        weighted = basis_ref[krylov - 1, :, lanes] * (wide_row(areas_ref, b) * live / per_box)
        charges = jnp.concatenate([weighted.astype(bf16).astype(f32), wide_charges(cross_ref, slot * 16)], axis=0)
        store_source_features(padded(facets_ref[:, lanes] - origin), charges, slot, geometry, strengths)
        return 0

    lax.fori_loop(0, boxes, source, 0, unroll=2)

    def target(place, _):
        b = boxes_s[half * plane_boxes + place]
        lanes = pl.ds(pl.multiple_of(b * per_box, per_box), per_box)
        local = padded(facets_ref[:, lanes] - origin)
        normal = padded(normals_ref[:, lanes])
        square = jnp.sum(local * local, axis=0, keepdims=True) + soften
        along = jnp.sum(local * normal, axis=0, keepdims=True)
        distance = jnp.where(row == 3, 1.0, jnp.where(row == 4, square, -2.0 * local))
        high, middle, low = thirds(distance)
        rows = stacked_rows((high, middle, low, high, middle, high), per_box)
        start = pl.multiple_of(place * per_box, per_box)
        targets[pl.ds(start, per_box), :] = jnp.transpose(rows).astype(bf16)
        planes[pl.ds(pl.multiple_of(place * 8, 8), 8), :] = jnp.where(row == 3, along, normal)
        return 0

    lax.fori_loop(0, plane_boxes, target, 0, unroll=2)
    total[...] = jnp.zeros_like(total)
    near_planes((0, plane_boxes), geometry, strengths, targets, total)


def halo_kernel(
    centres_s, first_ref, second_ref, tail_ref, cross_ref, facets_ref, normals_ref, targets, planes, own_total,
    mine_ref, theirs_ref, geometry, strengths, total, far_halo, far_own, far_centres, boxes_s
):
    boxes = centres_s.shape[1]
    origin, base_z = slab_origin(centres_s)
    boxes_by_slot(centres_s, boxes_s)
    half = lax.axis_index("rhs")

    def source(place, _):
        tile = first_ref[pl.ds(pl.multiple_of(256 + place * 8, 8), 8), :]
        local = padded(jnp.concatenate([tile[0:3], tile[3:6]], axis=1) - origin)
        charges = jnp.concatenate([wide_charges(first_ref, place * 16), wide_charges(second_ref, place * 16)], axis=0)
        store_source_features(local, charges, place, geometry, strengths)
        return 0

    lax.fori_loop(0, plane_boxes, source, 0, unroll=2)
    total[...] = own_total[...]

    moments = []
    for group, (centres, mine, theirs) in enumerate(
        (
            (first_ref[392:400], first_ref[384:392], second_ref[256:264]),
            (tail_ref[8:16], tail_ref[:8], cross_ref[512:520]),
        )
    ):
        columns = jnp.transpose(centres)[:32]
        for a in range(3):
            shift = base_z if a == 2 else 1.5
            far_centres[(group * 3 + a) * 32 : (group * 3 + a + 1) * 32, :] = jnp.broadcast_to(
                columns[:, a : a + 1] - shift, (32, 128)
            )
        both = jnp.concatenate([mine, theirs], axis=0)
        high = both.astype(bf16).astype(f32)
        moments.append(jnp.concatenate([high, both - high], axis=0))
    lane = lax.broadcasted_iota(jnp.int32, (1, 128), 1)
    lane_x = lane & 3
    lane_y = (lane >> 2) & 3
    lane_plane = (lane >> 4) & 1

    def far_field(slot, group):
        b = boxes_s[slot]
        x, y, plane = slot & 3, (slot >> 2) & 3, slot >> 4
        lanes = pl.ds(pl.multiple_of(b * per_box, per_box), per_box)
        local = facets_ref[:, lanes] - origin
        normal = normals_ref[:, lanes]
        d = []
        for a in range(3):
            centre = far_centres[(group * 3 + a) * 32 : (group * 3 + a + 1) * 32, :]
            d.append(local[a : a + 1] - jnp.concatenate([centre, centre], axis=1))
        q = d[0] * d[0] + d[1] * d[1] + d[2] * d[2] + soften
        inverse = lax.rsqrt(q)
        inverse_2 = inverse * inverse
        inverse_3 = inverse_2 * inverse
        t = d[0] * normal[0:1] + d[1] * normal[1:2] + d[2] * normal[2:3]
        single = t * inverse_3
        steep = 3.0 * single * inverse_2
        coefficients = [single] + [steep * d[a] - normal[a : a + 1] * inverse_3 for a in range(3)]
        whole = jnp.concatenate(coefficients, axis=0)
        upper = whole.astype(bf16)
        lower = (whole - upper.astype(f32)).astype(bf16)
        lane_z = lane_plane + (4 * half - 2 if group == 0 else 0)
        near = (jnp.abs(lane_x - x) <= 1) & (jnp.abs(lane_y - y) <= 1) & (jnp.abs(lane_z - plane) <= 1)
        picked = jnp.where(near, 0.0, moments[group]).astype(bf16)
        first = jnp.dot(picked, upper, preferred_element_type=f32)
        second = jnp.dot(picked, lower, preferred_element_type=f32)
        return first[:16] + first[16:] + second[:16]

    def far_boxes(item):
        for k in range(4):
            slot = jnp.minimum(item * 4 + k, boxes - 1)
            far_halo[pl.ds(pl.multiple_of(slot * 16, 16), 16), :] = far_field(slot, 0)
        for k in range(2):
            place = jnp.minimum(item * 2 + k, plane_boxes - 1)
            far_own[pl.ds(pl.multiple_of(place * 16, 16), 16), :] = far_field(half * plane_boxes + place, 1)

    near_planes((0,), geometry, strengths, targets, total, far_boxes)

    def near_field(place, _):
        turned = jnp.transpose(total[pl.ds(pl.multiple_of(place * per_box, per_box), per_box), :])
        sums = turned[:64] + (turned[64:128] + turned[128:192])
        side = planes[pl.ds(pl.multiple_of(place * 8, 8), 8), :]
        value = side[3:4] * sums[:16] - side[0:1] * sums[16:32]
        value = value - side[1:2] * sums[32:48] - side[2:3] * sums[48:64]
        slot = half * plane_boxes + place
        rows = pl.ds(pl.multiple_of(slot * 16, 16), 16)
        far_halo[rows, :] += value + far_own[pl.ds(pl.multiple_of(place * 16, 16), 16), :]
        return 0

    lax.fori_loop(0, plane_boxes, near_field, 0, unroll=2)
    for slot in range(boxes):
        mine_ref[slot * 8 : slot * 8 + 8] = far_halo[slot * 16 : slot * 16 + 8]
        theirs_ref[slot * 8 : slot * 8 + 8] = far_halo[slot * 16 + 8 : slot * 16 + 16]


def gram_kernel(counts_s, basis_ref, sums_ref):
    krylov = basis_ref.shape[0]
    pairs = [(m, n) for m in range(krylov) for n in range(m + 1)]

    def one_box(b, carry):
        lanes = pl.ds(pl.multiple_of(b * per_box, per_box), per_box)
        live = live_row(counts_s, b)
        rows = [basis_ref[m, :, lanes] * live for m in range(krylov)]
        out = []
        for k, (m, n) in enumerate(pairs):
            product = rows[m] * rows[n]
            out.append(carry[k] + product[:, :128] + product[:, 128:])
        return tuple(out)

    zeros = jnp.zeros((8, 128), f32)
    gram = lax.fori_loop(0, counts_s.shape[0], one_box, (zeros,) * len(pairs))
    lane = lax.broadcasted_iota(jnp.int32, (8, 128), 1)
    total = zeros
    for k, value in enumerate(gram):
        total = jnp.where(lane == krylov + 1 + k, jnp.sum(value, axis=1, keepdims=True), total)
    sums_ref[...] = total


def image_kernel(centres_s, counts_s, mine_ref, theirs_ref, gram_ref, contrast_ref, basis_ref, image_ref, sums_ref):
    krylov = basis_ref.shape[0]

    def one_box(b, carry):
        lanes = pl.ds(pl.multiple_of(b * per_box, per_box), per_box)
        rows = pl.ds(pl.multiple_of(slot_of(centres_s, b) * 8, 8), 8)
        live = live_row(counts_s, b)
        part = mine_ref[rows, :] + theirs_ref[rows, :]
        image = live * (basis_ref[krylov - 1, :, lanes] - 2.0 * wide_row(contrast_ref, b) * part)
        image_ref[:, lanes] = image
        sums = []
        for m in range(krylov + 1):
            product = image * (basis_ref[m, :, lanes] if m < krylov else image)
            sums.append(carry[m] + product[:, :128] + product[:, 128:])
        return tuple(sums)

    zeros = jnp.zeros((8, 128), f32)
    sums = lax.fori_loop(0, counts_s.shape[0], one_box, (zeros,) * (krylov + 1), unroll=4)
    lane = lax.broadcasted_iota(jnp.int32, (8, 128), 1)
    total = gram_ref[...]
    for k, value in enumerate(sums):
        total = jnp.where(lane == k, jnp.sum(value, axis=1, keepdims=True), total)
    sums_ref[...] = jnp.broadcast_to(total[None], sums_ref.shape)


def two_sum(a, b):
    s = a + b
    c = s - a
    return s, (a - (s - c)) + (b - c)


def halves(a):
    c = a * 4097.0
    high = c - (c - a)
    return high, a - high


def two_product(a, b):
    p = a * b
    a_high, a_low = halves(a)
    b_high, b_low = halves(b)
    return p, ((a_high * b_high - p) + a_high * b_low + a_low * b_high) + a_low * b_low


def finish_kernel(total_facets, counts_s, tiles_ref, image_ref, basis_ref, next_ref, hessenberg_ref):
    boxes = counts_s.shape[0]
    krylov = basis_ref.shape[0]
    lane = lax.broadcasted_iota(jnp.int32, (8, 128), 1)

    def add_tile(i, carry):
        value, error = two_sum(carry[0], tiles_ref[i])
        return value, carry[1] + error

    sums, rest = lax.fori_loop(0, tiles_ref.shape[0], add_tile, (jnp.zeros((8, 128), f32),) * 2, unroll=8)
    exact = sums + rest
    projections = [exact[:, m : m + 1] / total_facets for m in range(krylov)]
    pairs = [(m, n) for m in range(krylov) for n in range(m + 1)]
    first = jnp.where(lane == krylov, 1.0, 0.0)
    second = jnp.where(lane <= krylov, 1.0, 0.0)
    for m in range(krylov):
        first = jnp.where(lane == m, -2.0 * projections[m], first)
    for k, (m, n) in enumerate(pairs):
        at = lane == krylov + 1 + k
        scale = 1.0 if m == n else 2.0
        first = jnp.where(at, scale * projections[m], first)
        second = jnp.where(at, projections[n], second)
    factor, factor_rest = two_product(first, second)
    value, value_rest = two_product(factor, sums)
    value_rest = value_rest + (factor * rest + factor_rest * sums)
    for shift in (64, 32, 16, 8, 4, 2, 1):
        other = pltpu.roll(value, shift, 1)
        other_rest = pltpu.roll(value_rest, shift, 1)
        value, error = two_sum(value, other)
        value_rest = (value_rest + other_rest) + error
    remaining = jnp.maximum(value + value_rest, 0.0)
    norm = jnp.sqrt(remaining / total_facets + epsilon)
    heads = jnp.where(lane == krylov, norm, 0.0)
    for m in range(krylov):
        heads = jnp.where(lane == m, projections[m], heads)
    hessenberg_ref[...] = heads[:, : krylov + 1]
    wide = [jnp.broadcast_to(p, (8, per_box)) for p in projections]
    scale = jnp.concatenate([1.0 / norm] * (per_box // 128), axis=1)

    def one_box(b, _):
        lanes = pl.ds(pl.multiple_of(b * per_box, per_box), per_box)
        live = live_row(counts_s, b)
        sent = wide[0] * basis_ref[0, :, lanes]
        for m in range(1, krylov):
            sent += wide[m] * basis_ref[m, :, lanes]
        next_ref[:, lanes] = (image_ref[:, lanes] - sent * live) * scale
        return 0

    lax.fori_loop(0, boxes, one_box, 0, unroll=4)


smem = pl.BlockSpec(memory_space=pltpu.SMEM)
vmem = pl.BlockSpec(memory_space=pltpu.VMEM)


def on_device(
    basis, facet_centres, normals, areas, contrast, facet_counts, box_centres, near_boxes, far_boxes
):
    krylov, rhs_local, facet_local = basis.shape
    boxes = facet_counts.shape[0]
    count = lax.axis_size("box")
    total_facets = count * facet_local
    areas = areas.reshape(-1, 128)
    contrast = contrast.reshape(-1, 128)

    def rows(number, width=128, dtype=f32):
        return jax.ShapeDtypeStruct((number, width), dtype)

    def limit(mebibytes):
        return pltpu.CompilerParams(vmem_limit_bytes=mebibytes * 1024 * 1024)

    cross, first, second, tail = pl.pallas_call(
        prep_kernel,
        out_shape=(rows(520), rows(400), rows(264), rows(16)),
        in_specs=[pl.BlockSpec(memory_space=pl.ANY)] * 5,
        out_specs=(vmem,) * 4,
        scratch_shapes=[
            pltpu.VMEM((512, 128), f32),
            pltpu.VMEM((256, 128), f32),
            pltpu.SMEM(box_centres.shape, f32),
            pltpu.SMEM(facet_counts.shape, jnp.int32),
            pltpu.VMEM((rhs_local, facet_local), f32),
            pltpu.VMEM(facet_centres.shape, f32),
            pltpu.VMEM(areas.shape, f32),
            pltpu.SemaphoreType.DMA((5,)),
        ],
        name="prepare",
    )(box_centres, facet_counts, basis, facet_centres, areas)
    swap = [(0, 1), (1, 0)]
    ups = range(count - 1)
    cross = lax.ppermute(cross, "rhs", swap)
    first = lax.ppermute(
        first, ("box", "rhs"), [(2 * i, 2 * i + 2) for i in ups] + [(2 * i + 3, 2 * i + 1) for i in ups]
    )
    second = lax.ppermute(
        second, ("box", "rhs"), [(2 * i + 1, 2 * i + 2) for i in ups] + [(2 * i + 2, 2 * i + 1) for i in ups]
    )
    plane_slots = plane_boxes * per_box
    targets, planes, own_total = pl.pallas_call(
        own_kernel,
        out_shape=(rows(plane_slots, depth, bf16), rows(plane_boxes * 8, per_box), rows(plane_slots, 256)),
        in_specs=[smem, smem] + [vmem] * 5,
        out_specs=(vmem,) * 3,
        scratch_shapes=[
            pltpu.VMEM((boxes * depth, per_box), bf16),
            pltpu.VMEM((boxes * per_box, 256), bf16),
            pltpu.SMEM((boxes,), jnp.int32),
        ],
        compiler_params=limit(24),
        name="own",
    )(box_centres, facet_counts, basis, facet_centres, areas, normals, cross)
    mine, theirs = pl.pallas_call(
        halo_kernel,
        out_shape=(rows(boxes * 8, per_box),) * 2,
        in_specs=[smem] + [vmem] * 9,
        out_specs=(vmem, vmem),
        scratch_shapes=[
            pltpu.VMEM((plane_boxes * depth, per_box), bf16),
            pltpu.VMEM((plane_slots, 256), bf16),
            pltpu.VMEM((plane_slots, 256), f32),
            pltpu.VMEM((boxes * 16, per_box), f32),
            pltpu.VMEM((plane_boxes * 16, per_box), f32),
            pltpu.VMEM((6 * 32, 128), f32),
            pltpu.SMEM((boxes,), jnp.int32),
        ],
        compiler_params=limit(24),
        name="halo",
    )(box_centres, first, second, tail, cross, facet_centres, normals, targets, planes, own_total)
    theirs = lax.ppermute(theirs, "rhs", swap)
    gram = pl.pallas_call(
        gram_kernel,
        out_shape=rows(8),
        in_specs=[smem, vmem],
        out_specs=vmem,
        compiler_params=limit(8),
        name="gram",
    )(facet_counts, basis)
    image, tiles = pl.pallas_call(
        image_kernel,
        out_shape=(rows(rhs_local, facet_local), jax.ShapeDtypeStruct((count, 8, 128), f32)),
        in_specs=[smem, smem] + [vmem] * 5,
        out_specs=(vmem, vmem),
        compiler_params=limit(8),
        name="image",
    )(box_centres, facet_counts, mine, theirs, gram, contrast, basis)
    tiles = lax.all_to_all(tiles, "box", 0, 0, tiled=True)
    next_vector, hessenberg = pl.pallas_call(
        functools.partial(finish_kernel, total_facets),
        out_shape=(
            jax.ShapeDtypeStruct((rhs_local, facet_local), f32),
            jax.ShapeDtypeStruct((rhs_local, krylov + 1), f32),
        ),
        in_specs=[smem] + [vmem] * 3,
        out_specs=(vmem, vmem),
        compiler_params=pltpu.CompilerParams(vmem_limit_bytes=16 * 1024 * 1024),
        name="finish",
    )(facet_counts, tiles, image, basis)
    return next_vector, hessenberg.T


def solution(mesh):
    return jax.shard_map(
        on_device,
        mesh=mesh,
        in_specs=(
            P(None, "rhs", "box"),
            P(None, "box"),
            P(None, "box"),
            P("box"),
            P("box"),
            P("box"),
            P(None, "box"),
            P("box", None),
            P("box", None),
        ),
        out_specs=(P("rhs", "box"), P(None, "rhs")),
        check_vma=False,
    )
```

```python
import functools

import jax
import jax.numpy as jnp
from jax import lax
from jax.experimental import pallas as pl
from jax.experimental.pallas import tpu as pltpu
from jax.sharding import PartitionSpec as P

soften = 0.0025
epsilon = 1e-06
f32 = jnp.float32
bf16 = jnp.bfloat16
plane_boxes = 16
per_box = 256
depth = 128


def lattice(centres_s, b):
    x = (centres_s[0, b] + 0.5).astype(jnp.int32)
    y = (centres_s[1, b] + 0.5).astype(jnp.int32)
    z = (centres_s[2, b] + 0.5).astype(jnp.int32)
    return x, y, z


def slot_of(centres_s, b):
    x, y, z = lattice(centres_s, b)
    return (z & 1) * plane_boxes + y * 4 + x


def wide_row(ref, b):
    return jnp.concatenate([ref[pl.ds(2 * b, 1), :], ref[pl.ds(2 * b + 1, 1), :]], axis=1)


def live_row(counts_s, b):
    slots = lax.broadcasted_iota(jnp.int32, (1, per_box), 1)
    return (slots < counts_s[b]).astype(f32)


def prep_kernel(
    centres_h, counts_h, basis_h, facets_h, areas_h, normals_h, cross_ref, first_ref, second_ref, local_ref,
    charges_v, centres_s, counts_s, current_ref, facets_ref, areas_ref, normals_ref, arrived
):
    boxes = counts_s.shape[0]
    moves = [
        (basis_h.at[basis_h.shape[0] - 1], current_ref),
        (facets_h, facets_ref),
        (areas_h, areas_ref),
        (normals_h, normals_ref),
        (centres_h, centres_s),
        (counts_h, counts_s),
    ]
    copies = [pltpu.make_async_copy(a, b, arrived.at[k]) for k, (a, b) in enumerate(moves)]
    for copy in copies:
        copy.start()
    for copy in copies:
        copy.wait()
    lane = lax.broadcasted_iota(jnp.int32, (8, 128), 1)
    row = lax.broadcasted_iota(jnp.int32, (8, 128), 0)
    empty = jnp.zeros((2, 128), f32)

    def one_box(b, carry):
        moments, centres = carry
        slot = slot_of(centres_s, b)
        lanes = pl.ds(pl.multiple_of(b * per_box, per_box), per_box)
        facets = facets_ref[:, lanes]
        normals = normals_ref[:, lanes]
        live = live_row(counts_s, b)
        weighted = current_ref[:, lanes] * (wide_row(areas_ref, b) * live / per_box)
        start = pl.multiple_of(slot * 16, 16)
        charges_v[pl.ds(start, 16), :] = jnp.concatenate([weighted[:, :128], weighted[:, 128:]], axis=0)
        local_ref[pl.ds(start, 16), :] = jnp.concatenate(
            [facets[:, :128], facets[:, 128:], empty, normals[:, :128], normals[:, 128:], empty], axis=0
        )
        moments += jnp.where(lane == slot, jnp.sum(weighted, axis=1, keepdims=True), 0.0)
        for a in range(3):
            dipole = jnp.sum(weighted * (facets[a : a + 1] - centres_s[a, b]), axis=1, keepdims=True)
            moments += jnp.where(lane == 32 * (a + 1) + slot, dipole, 0.0)
            centres += jnp.where((lane == slot) & (row == a), centres_s[a, b], 0.0)
        return moments, centres

    zeros = jnp.zeros((8, 128), f32)
    moments, centres = lax.fori_loop(0, boxes, one_box, (zeros, zeros), unroll=4)
    _, _, z = lattice(centres_s, 0)
    base_z = (z - (z & 1)).astype(f32) + 0.5
    centres = jnp.where((row == 3) | (row == 4), 1.5, jnp.where(row == 5, base_z, centres))
    half = lax.axis_index("rhs")
    away = pl.multiple_of((1 - half) * 256, 256)
    here = pl.multiple_of(half * 256, 256)
    pieces = jnp.concatenate([*thirds(moments), zeros], axis=0).astype(bf16)
    cross_ref[:512] = charges_v[...].astype(bf16)
    cross_ref[512:] = pieces
    second_ref[:256] = charges_v[pl.ds(here, 256), :].astype(bf16)
    second_ref[256:] = pieces
    first_ref[:256] = charges_v[pl.ds(away, 256), :].astype(bf16).astype(f32)
    for place in range(plane_boxes):
        first_ref[256 + 8 * place : 264 + 8 * place] = local_ref[pl.ds(away + 16 * place, 8), :]
    first_ref[384:392] = moments
    first_ref[392:] = centres
    local_ref[512:520] = moments
    local_ref[520:] = centres


def thirds(x):
    high = x.astype(bf16).astype(f32)
    rest = x - high
    middle = rest.astype(bf16).astype(f32)
    return high, middle, (rest - middle).astype(bf16).astype(f32)


def stacked_rows(parts, width):
    zeros = jnp.zeros((depth - 8 * len(parts), width), f32)
    return jnp.concatenate([*parts, zeros], axis=0)


def padded(rows):
    return jnp.concatenate([rows, jnp.zeros((8 - rows.shape[0], rows.shape[1]), f32)], axis=0)


def wide_charges(ref, place):
    both = ref[pl.ds(pl.multiple_of(place * 16, 16), 16), :].astype(f32)
    return jnp.concatenate([both[:8], both[8:]], axis=1)


def wide_tile(ref, start):
    tile = ref[pl.ds(pl.multiple_of(start, 8), 8), :]
    return jnp.concatenate([tile[0:3], tile[3:6]], axis=1)


def whole_moments(pieces):
    return pieces[:8] + (pieces[8:16] + pieces[16:24])


def store_source_features(local, charges, box, geometry, strengths):
    row = lax.broadcasted_iota(jnp.int32, (8, per_box), 0)
    square = jnp.sum(local * local, axis=0, keepdims=True)
    features = jnp.where(row == 3, square, jnp.where(row == 4, 1.0, local))
    high, middle, low = thirds(features)
    rows = stacked_rows((high, high, high, middle, middle, low), per_box)
    geometry[pl.ds(pl.multiple_of(box * depth, depth), depth), :] = rows.astype(bf16)
    products = jnp.concatenate([charges] + [charges * local[a : a + 1] for a in range(3)], axis=0)
    rows = jnp.concatenate([*thirds(products), jnp.zeros((64, per_box), f32)], axis=0)
    strengths[pl.ds(pl.multiple_of(box * 256, 256), 256), :] = rows.astype(bf16)


def near_planes(sources, geometry, strengths, targets, total, beside=None):
    def near_rows(item, _):
        target_y = (item + 1) // 3
        source_y = target_y + lax.rem(item + 1, 3) - 1
        runs = []
        for first in sources:
            for x in range(4):
                for near_x in range(max(x - 1, 0), min(x + 2, 4)):
                    start = pl.multiple_of((target_y * 4 + near_x) * per_box, per_box)
                    runs.append((first + source_y * 4 + x, pl.ds(start, per_box)))

        def distances(box, rows_of):
            weights = geometry[pl.ds(pl.multiple_of(box * depth, depth), depth), :]
            return jnp.dot(targets[rows_of, :], weights, preferred_element_type=f32)

        ahead = distances(*runs[0])
        for i, (box, rows_of) in enumerate(runs):
            here = ahead
            if i + 1 < len(runs):
                ahead = distances(*runs[i + 1])
            inverse = lax.rsqrt(here)
            cubed = (inverse * inverse * inverse).astype(bf16)
            given = strengths[pl.ds(pl.multiple_of(box * 256, 256), 256), :]
            total[rows_of, :] += lax.dot_general(
                cubed, given, (((1,), (1,)), ((), ())), preferred_element_type=f32
            )
        if beside is not None:
            beside(item)
        return 0

    lax.fori_loop(0, 10, near_rows, 0)


def field_kernel(
    local_ref, sent_ref, cross_ref, first_ref, second_ref, mine_ref, theirs_ref,
    geometry, strengths, targets, planes, total, far_halo, far_own, far_centres
):
    boxes = 2 * plane_boxes
    half = lax.axis_index("rhs")
    origin = local_ref[523:526, 0:1]
    row = lax.broadcasted_iota(jnp.int32, (8, per_box), 0)

    def source(slot, _):
        local = padded(wide_tile(local_ref, slot * 16) - origin)
        charges = jnp.concatenate([wide_charges(sent_ref, slot), wide_charges(cross_ref, slot)], axis=0)
        store_source_features(local, charges, slot, geometry, strengths)
        return 0

    lax.fori_loop(0, boxes, source, 0, unroll=2)

    def halo_source(place, _):
        local = padded(wide_tile(first_ref, 256 + place * 8) - origin)
        charges = jnp.concatenate([wide_charges(first_ref, place), wide_charges(second_ref, place)], axis=0)
        store_source_features(local, charges, boxes + place, geometry, strengths)
        return 0

    lax.fori_loop(0, plane_boxes, halo_source, 0, unroll=2)

    def target(place, _):
        start = (half * plane_boxes + place) * 16
        local = padded(wide_tile(local_ref, start) - origin)
        normal = padded(wide_tile(local_ref, start + 8))
        square = jnp.sum(local * local, axis=0, keepdims=True) + soften
        along = jnp.sum(local * normal, axis=0, keepdims=True)
        distance = jnp.where(row == 3, 1.0, jnp.where(row == 4, square, -2.0 * local))
        high, middle, low = thirds(distance)
        rows = stacked_rows((high, middle, low, high, middle, high), per_box)
        start = pl.multiple_of(place * per_box, per_box)
        targets[pl.ds(start, per_box), :] = jnp.transpose(rows).astype(bf16)
        planes[pl.ds(pl.multiple_of(place * 8, 8), 8), :] = jnp.where(row == 3, along, normal)
        return 0

    lax.fori_loop(0, plane_boxes, target, 0, unroll=2)
    total[...] = jnp.zeros_like(total)

    moments = []
    for group, (centres, mine, theirs) in enumerate(
        (
            (first_ref[392:400], first_ref[384:392], second_ref[256:288]),
            (local_ref[520:528], local_ref[512:520], cross_ref[512:544]),
        )
    ):
        columns = jnp.transpose(jnp.concatenate([centres[:3] - origin, centres[3:]], axis=0))[:32]
        for a in range(3):
            far_centres[(group * 3 + a) * 32 : (group * 3 + a + 1) * 32, :] = jnp.broadcast_to(
                columns[:, a : a + 1], (32, 128)
            )
        both = jnp.concatenate([mine, whole_moments(theirs.astype(f32))], axis=0)
        high = both.astype(bf16).astype(f32)
        moments.append(jnp.concatenate([high, both - high], axis=0))
    lane = lax.broadcasted_iota(jnp.int32, (1, 128), 1)
    lane_x = lane & 3
    lane_y = (lane >> 2) & 3
    lane_plane = (lane >> 4) & 1

    def far_field(slot, group):
        x, y, plane = slot & 3, (slot >> 2) & 3, slot >> 4
        local = wide_tile(local_ref, slot * 16) - origin
        normal = wide_tile(local_ref, slot * 16 + 8)
        d = []
        for a in range(3):
            centre = far_centres[(group * 3 + a) * 32 : (group * 3 + a + 1) * 32, :]
            d.append(local[a : a + 1] - jnp.concatenate([centre, centre], axis=1))
        q = d[0] * d[0] + d[1] * d[1] + d[2] * d[2] + soften
        inverse = lax.rsqrt(q)
        inverse_2 = inverse * inverse
        inverse_3 = inverse_2 * inverse
        t = d[0] * normal[0:1] + d[1] * normal[1:2] + d[2] * normal[2:3]
        single = t * inverse_3
        steep = 3.0 * single * inverse_2
        coefficients = [single] + [steep * d[a] - normal[a : a + 1] * inverse_3 for a in range(3)]
        whole = jnp.concatenate(coefficients, axis=0)
        upper = whole.astype(bf16)
        lower = (whole - upper.astype(f32)).astype(bf16)
        lane_z = lane_plane + (4 * half - 2 if group == 0 else 0)
        near = (jnp.abs(lane_x - x) <= 1) & (jnp.abs(lane_y - y) <= 1) & (jnp.abs(lane_z - plane) <= 1)
        picked = jnp.where(near, 0.0, moments[group]).astype(bf16)
        first = jnp.dot(picked, upper, preferred_element_type=f32)
        second = jnp.dot(picked, lower, preferred_element_type=f32)
        return first[:16] + first[16:] + second[:16]

    def far_boxes(item):
        for k in range(4):
            slot = jnp.minimum(item * 4 + k, boxes - 1)
            far_halo[pl.ds(pl.multiple_of(slot * 16, 16), 16), :] = far_field(slot, 0)
        for k in range(2):
            place = jnp.minimum(item * 2 + k, plane_boxes - 1)
            far_own[pl.ds(pl.multiple_of(place * 16, 16), 16), :] = far_field(half * plane_boxes + place, 1)

    near_planes((0, plane_boxes, 2 * plane_boxes), geometry, strengths, targets, total, far_boxes)

    def near_field(place, _):
        turned = jnp.transpose(total[pl.ds(pl.multiple_of(place * per_box, per_box), per_box), :])
        sums = turned[:64] + (turned[64:128] + turned[128:192])
        side = planes[pl.ds(pl.multiple_of(place * 8, 8), 8), :]
        value = side[3:4] * sums[:16] - side[0:1] * sums[16:32]
        value = value - side[1:2] * sums[32:48] - side[2:3] * sums[48:64]
        slot = half * plane_boxes + place
        rows = pl.ds(pl.multiple_of(slot * 16, 16), 16)
        far_halo[rows, :] += value + far_own[pl.ds(pl.multiple_of(place * 16, 16), 16), :]
        return 0

    lax.fori_loop(0, plane_boxes, near_field, 0, unroll=2)
    for slot in range(boxes):
        mine_ref[slot * 8 : slot * 8 + 8] = far_halo[slot * 16 : slot * 16 + 8]
        theirs_ref[slot * 8 : slot * 8 + 8] = far_halo[slot * 16 + 8 : slot * 16 + 16]


def gram_kernel(counts_s, basis_ref, sums_ref):
    krylov = basis_ref.shape[0]
    pairs = [(m, n) for m in range(krylov) for n in range(m + 1)]

    def one_box(b, carry):
        lanes = pl.ds(pl.multiple_of(b * per_box, per_box), per_box)
        live = live_row(counts_s, b)
        rows = [basis_ref[m, :, lanes] * live for m in range(krylov)]
        out = []
        for k, (m, n) in enumerate(pairs):
            product = rows[m] * rows[n]
            out.append(carry[k] + product[:, :128] + product[:, 128:])
        return tuple(out)

    zeros = jnp.zeros((8, 128), f32)
    gram = lax.fori_loop(0, counts_s.shape[0], one_box, (zeros,) * len(pairs))
    lane = lax.broadcasted_iota(jnp.int32, (8, 128), 1)
    total = zeros
    for k, value in enumerate(gram):
        total = jnp.where(lane == krylov + 1 + k, jnp.sum(value, axis=1, keepdims=True), total)
    sums_ref[...] = total


def image_kernel(centres_s, counts_s, mine_ref, theirs_ref, gram_ref, contrast_ref, basis_ref, image_ref, sums_ref):
    krylov = basis_ref.shape[0]

    def one_box(b, carry):
        lanes = pl.ds(pl.multiple_of(b * per_box, per_box), per_box)
        rows = pl.ds(pl.multiple_of(slot_of(centres_s, b) * 8, 8), 8)
        live = live_row(counts_s, b)
        part = mine_ref[rows, :] + theirs_ref[rows, :]
        image = live * (basis_ref[krylov - 1, :, lanes] - 2.0 * wide_row(contrast_ref, b) * part)
        image_ref[:, lanes] = image
        sums = []
        for m in range(krylov + 1):
            product = image * (basis_ref[m, :, lanes] if m < krylov else image)
            sums.append(carry[m] + product[:, :128] + product[:, 128:])
        return tuple(sums)

    zeros = jnp.zeros((8, 128), f32)
    sums = lax.fori_loop(0, counts_s.shape[0], one_box, (zeros,) * (krylov + 1), unroll=4)
    lane = lax.broadcasted_iota(jnp.int32, (8, 128), 1)
    total = gram_ref[...]
    for k, value in enumerate(sums):
        total = jnp.where(lane == k, jnp.sum(value, axis=1, keepdims=True), total)
    sums_ref[...] = jnp.broadcast_to(total[None], sums_ref.shape)


def two_sum(a, b):
    s = a + b
    c = s - a
    return s, (a - (s - c)) + (b - c)


def halves(a):
    c = a * 4097.0
    high = c - (c - a)
    return high, a - high


def two_product(a, b):
    p = a * b
    a_high, a_low = halves(a)
    b_high, b_low = halves(b)
    return p, ((a_high * b_high - p) + a_high * b_low + a_low * b_high) + a_low * b_low


def finish_kernel(total_facets, counts_s, tiles_ref, image_ref, basis_ref, next_ref, hessenberg_ref):
    boxes = counts_s.shape[0]
    krylov = basis_ref.shape[0]
    lane = lax.broadcasted_iota(jnp.int32, (8, 128), 1)

    def add_tile(i, carry):
        value, error = two_sum(carry[0], tiles_ref[i])
        return value, carry[1] + error

    sums, rest = lax.fori_loop(0, tiles_ref.shape[0], add_tile, (jnp.zeros((8, 128), f32),) * 2, unroll=8)
    exact = sums + rest
    projections = [exact[:, m : m + 1] / total_facets for m in range(krylov)]
    pairs = [(m, n) for m in range(krylov) for n in range(m + 1)]
    first = jnp.where(lane == krylov, 1.0, 0.0)
    second = jnp.where(lane <= krylov, 1.0, 0.0)
    for m in range(krylov):
        first = jnp.where(lane == m, -2.0 * projections[m], first)
    for k, (m, n) in enumerate(pairs):
        at = lane == krylov + 1 + k
        scale = 1.0 if m == n else 2.0
        first = jnp.where(at, scale * projections[m], first)
        second = jnp.where(at, projections[n], second)
    factor, factor_rest = two_product(first, second)
    value, value_rest = two_product(factor, sums)
    value_rest = value_rest + (factor * rest + factor_rest * sums)
    for shift in (64, 32, 16, 8, 4, 2, 1):
        other = pltpu.roll(value, shift, 1)
        other_rest = pltpu.roll(value_rest, shift, 1)
        value, error = two_sum(value, other)
        value_rest = (value_rest + other_rest) + error
    remaining = jnp.maximum(value + value_rest, 0.0)
    norm = jnp.sqrt(remaining / total_facets + epsilon)
    heads = jnp.where(lane == krylov, norm, 0.0)
    for m in range(krylov):
        heads = jnp.where(lane == m, projections[m], heads)
    hessenberg_ref[...] = heads[:, : krylov + 1]
    wide = [jnp.broadcast_to(p, (8, per_box)) for p in projections]
    scale = jnp.concatenate([1.0 / norm] * (per_box // 128), axis=1)

    def one_box(b, _):
        lanes = pl.ds(pl.multiple_of(b * per_box, per_box), per_box)
        live = live_row(counts_s, b)
        sent = wide[0] * basis_ref[0, :, lanes]
        for m in range(1, krylov):
            sent += wide[m] * basis_ref[m, :, lanes]
        next_ref[:, lanes] = (image_ref[:, lanes] - sent * live) * scale
        return 0

    lax.fori_loop(0, boxes, one_box, 0, unroll=4)


smem = pl.BlockSpec(memory_space=pltpu.SMEM)
vmem = pl.BlockSpec(memory_space=pltpu.VMEM)


def on_device(
    basis, facet_centres, normals, areas, contrast, facet_counts, box_centres, near_boxes, far_boxes
):
    krylov, rhs_local, facet_local = basis.shape
    boxes = facet_counts.shape[0]
    count = lax.axis_size("box")
    total_facets = count * facet_local
    areas = areas.reshape(-1, 128)
    contrast = contrast.reshape(-1, 128)

    def rows(number, width=128, dtype=f32):
        return jax.ShapeDtypeStruct((number, width), dtype)

    def limit(mebibytes):
        return pltpu.CompilerParams(vmem_limit_bytes=mebibytes * 1024 * 1024)

    sent, first, second, local = pl.pallas_call(
        prep_kernel,
        out_shape=(rows(544, dtype=bf16), rows(400), rows(288, dtype=bf16), rows(528)),
        in_specs=[pl.BlockSpec(memory_space=pl.ANY)] * 6,
        out_specs=(vmem,) * 4,
        scratch_shapes=[
            pltpu.VMEM((512, 128), f32),
            pltpu.SMEM(box_centres.shape, f32),
            pltpu.SMEM(facet_counts.shape, jnp.int32),
            pltpu.VMEM((rhs_local, facet_local), f32),
            pltpu.VMEM(facet_centres.shape, f32),
            pltpu.VMEM(areas.shape, f32),
            pltpu.VMEM(normals.shape, f32),
            pltpu.SemaphoreType.DMA((6,)),
        ],
        name="prepare",
    )(box_centres, facet_counts, basis, facet_centres, areas, normals)
    swap = [(0, 1), (1, 0)]
    ups = range(count - 1)
    cross = lax.ppermute(sent, "rhs", swap)
    first = lax.ppermute(
        first, ("box", "rhs"), [(2 * i, 2 * i + 2) for i in ups] + [(2 * i + 3, 2 * i + 1) for i in ups]
    )
    second = lax.ppermute(
        second, ("box", "rhs"), [(2 * i + 1, 2 * i + 2) for i in ups] + [(2 * i + 2, 2 * i + 1) for i in ups]
    )
    plane_slots = plane_boxes * per_box
    mine, theirs = pl.pallas_call(
        field_kernel,
        out_shape=(rows(boxes * 8, per_box),) * 2,
        in_specs=[vmem] * 5,
        out_specs=(vmem, vmem),
        scratch_shapes=[
            pltpu.VMEM((3 * plane_boxes * depth, per_box), bf16),
            pltpu.VMEM((3 * plane_boxes * 256, per_box), bf16),
            pltpu.VMEM((plane_slots, depth), bf16),
            pltpu.VMEM((plane_boxes * 8, per_box), f32),
            pltpu.VMEM((plane_slots, 256), f32),
            pltpu.VMEM((boxes * 16, per_box), f32),
            pltpu.VMEM((plane_boxes * 16, per_box), f32),
            pltpu.VMEM((6 * 32, 128), f32),
        ],
        compiler_params=limit(60),
        name="fields",
    )(local, sent, cross, first, second)
    theirs = lax.ppermute(theirs, "rhs", swap)
    gram = pl.pallas_call(
        gram_kernel,
        out_shape=rows(8),
        in_specs=[smem, vmem],
        out_specs=vmem,
        compiler_params=limit(8),
        name="gram",
    )(facet_counts, basis)
    image, tiles = pl.pallas_call(
        image_kernel,
        out_shape=(rows(rhs_local, facet_local), jax.ShapeDtypeStruct((count, 8, 128), f32)),
        in_specs=[smem, smem] + [vmem] * 5,
        out_specs=(vmem, vmem),
        compiler_params=limit(8),
        name="image",
    )(box_centres, facet_counts, mine, theirs, gram, contrast, basis)
    tiles = lax.all_to_all(tiles, "box", 0, 0, tiled=True)
    next_vector, hessenberg = pl.pallas_call(
        functools.partial(finish_kernel, total_facets),
        out_shape=(
            jax.ShapeDtypeStruct((rhs_local, facet_local), f32),
            jax.ShapeDtypeStruct((rhs_local, krylov + 1), f32),
        ),
        in_specs=[smem] + [vmem] * 3,
        out_specs=(vmem, vmem),
        compiler_params=pltpu.CompilerParams(vmem_limit_bytes=16 * 1024 * 1024),
        name="finish",
    )(facet_counts, tiles, image, basis)
    return next_vector, hessenberg.T


def solution(mesh):
    return jax.shard_map(
        on_device,
        mesh=mesh,
        in_specs=(
            P(None, "rhs", "box"),
            P(None, "box"),
            P(None, "box"),
            P("box"),
            P("box"),
            P("box"),
            P(None, "box"),
            P("box", None),
            P("box", None),
        ),
        out_specs=(P("rhs", "box"), P(None, "rhs")),
        check_vma=False,
    )
```

```python
import functools

import jax
import jax.numpy as jnp
from jax import lax
from jax.experimental import pallas as pl
from jax.experimental.pallas import tpu as pltpu
from jax.sharding import PartitionSpec as P

soften = 0.0025
epsilon = 1e-06
f32 = jnp.float32
bf16 = jnp.bfloat16
plane_boxes = 16
per_box = 256
depth = 128


def lattice(centres_s, b):
    x = (centres_s[0, b] + 0.5).astype(jnp.int32)
    y = (centres_s[1, b] + 0.5).astype(jnp.int32)
    z = (centres_s[2, b] + 0.5).astype(jnp.int32)
    return x, y, z


def slot_of(centres_s, b):
    x, y, z = lattice(centres_s, b)
    return (z & 1) * plane_boxes + y * 4 + x


def wide_row(ref, b):
    return jnp.concatenate([ref[pl.ds(2 * b, 1), :], ref[pl.ds(2 * b + 1, 1), :]], axis=1)


def live_row(counts_s, b):
    slots = lax.broadcasted_iota(jnp.int32, (1, per_box), 1)
    return (slots < counts_s[b]).astype(f32)


def prep_kernel(
    centres_h, counts_h, basis_h, facets_h, areas_h, normals_h, cross_ref, first_ref, second_ref, local_ref,
    charges_v, centres_s, counts_s, current_ref, facets_ref, areas_ref, normals_ref, arrived
):
    boxes = counts_s.shape[0]
    moves = [
        (basis_h.at[basis_h.shape[0] - 1], current_ref),
        (facets_h, facets_ref),
        (areas_h, areas_ref),
        (normals_h, normals_ref),
        (centres_h, centres_s),
        (counts_h, counts_s),
    ]
    copies = [pltpu.make_async_copy(a, b, arrived.at[k]) for k, (a, b) in enumerate(moves)]
    for copy in copies:
        copy.start()
    for copy in copies:
        copy.wait()
    lane = lax.broadcasted_iota(jnp.int32, (8, 128), 1)
    row = lax.broadcasted_iota(jnp.int32, (8, 128), 0)
    empty = jnp.zeros((2, 128), f32)

    def one_box(b, carry):
        moments, centres = carry
        slot = slot_of(centres_s, b)
        lanes = pl.ds(pl.multiple_of(b * per_box, per_box), per_box)
        facets = facets_ref[:, lanes]
        normals = normals_ref[:, lanes]
        live = live_row(counts_s, b)
        weighted = current_ref[:, lanes] * (wide_row(areas_ref, b) * live / per_box)
        start = pl.multiple_of(slot * 16, 16)
        charges_v[pl.ds(start, 16), :] = jnp.concatenate([weighted[:, :128], weighted[:, 128:]], axis=0)
        local_ref[pl.ds(start, 16), :] = jnp.concatenate(
            [facets[:, :128], facets[:, 128:], empty, normals[:, :128], normals[:, 128:], empty], axis=0
        )
        moments += jnp.where(lane == slot, jnp.sum(weighted, axis=1, keepdims=True), 0.0)
        for a in range(3):
            dipole = jnp.sum(weighted * (facets[a : a + 1] - centres_s[a, b]), axis=1, keepdims=True)
            moments += jnp.where(lane == 32 * (a + 1) + slot, dipole, 0.0)
            centres += jnp.where((lane == slot) & (row == a), centres_s[a, b], 0.0)
        return moments, centres

    zeros = jnp.zeros((8, 128), f32)
    moments, centres = lax.fori_loop(0, boxes, one_box, (zeros, zeros), unroll=4)
    _, _, z = lattice(centres_s, 0)
    base_z = (z - (z & 1)).astype(f32) + 0.5
    centres = jnp.where((row == 3) | (row == 4), 1.5, jnp.where(row == 5, base_z, centres))
    half = lax.axis_index("rhs")
    away = pl.multiple_of((1 - half) * 256, 256)
    here = pl.multiple_of(half * 256, 256)
    pieces = jnp.concatenate([*thirds(moments), zeros], axis=0).astype(bf16)
    cross_ref[:512] = charges_v[...].astype(bf16)
    cross_ref[512:] = pieces
    second_ref[:256] = charges_v[pl.ds(here, 256), :].astype(bf16)
    second_ref[256:] = pieces
    first_ref[:256] = charges_v[pl.ds(away, 256), :].astype(bf16).astype(f32)
    for place in range(plane_boxes):
        first_ref[256 + 8 * place : 264 + 8 * place] = local_ref[pl.ds(away + 16 * place, 8), :]
    first_ref[384:392] = moments
    first_ref[392:] = centres
    local_ref[512:520] = moments
    local_ref[520:] = centres


def thirds(x):
    high = x.astype(bf16).astype(f32)
    rest = x - high
    middle = rest.astype(bf16).astype(f32)
    return high, middle, (rest - middle).astype(bf16).astype(f32)


def stacked_rows(parts, width):
    zeros = jnp.zeros((depth - 8 * len(parts), width), f32)
    return jnp.concatenate([*parts, zeros], axis=0)


def padded(rows):
    return jnp.concatenate([rows, jnp.zeros((8 - rows.shape[0], rows.shape[1]), f32)], axis=0)


def wide_charges(ref, place):
    both = ref[pl.ds(pl.multiple_of(place * 16, 16), 16), :].astype(f32)
    return jnp.concatenate([both[:8], both[8:]], axis=1)


def wide_tile(ref, start):
    tile = ref[pl.ds(pl.multiple_of(start, 8), 8), :]
    return jnp.concatenate([tile[0:3], tile[3:6]], axis=1)


def whole_moments(pieces):
    return pieces[:8] + (pieces[8:16] + pieces[16:24])


def store_source_features(local, charges, box, geometry, strengths):
    row = lax.broadcasted_iota(jnp.int32, (8, per_box), 0)
    square = jnp.sum(local * local, axis=0, keepdims=True)
    features = jnp.where(row == 3, square, jnp.where(row == 4, 1.0, local))
    high, middle, low = thirds(features)
    rows = stacked_rows((high, high, high, middle, middle, low), per_box)
    geometry[pl.ds(pl.multiple_of(box * depth, depth), depth), :] = rows.astype(bf16)
    products = jnp.concatenate([charges] + [charges * local[a : a + 1] for a in range(3)], axis=0)
    rows = jnp.concatenate([*thirds(products), jnp.zeros((64, per_box), f32)], axis=0)
    strengths[pl.ds(pl.multiple_of(box * 256, 256), 256), :] = rows.astype(bf16)


def near_planes(sources, geometry, strengths, targets, total, beside=None):
    def near_rows(item, _):
        target_y = (item + 1) // 3
        source_y = target_y + lax.rem(item + 1, 3) - 1
        runs = []
        for near_x in range(4):
            for first in sources:
                for x in range(max(near_x - 1, 0), min(near_x + 2, 4)):
                    runs.append((near_x, first + source_y * 4 + x))

        def distances(near_x, box):
            start = pl.multiple_of((target_y * 4 + near_x) * per_box, per_box)
            weights = geometry[pl.ds(pl.multiple_of(box * depth, depth), depth), :]
            return jnp.dot(targets[pl.ds(start, per_box), :], weights, preferred_element_type=f32)

        ahead = distances(*runs[0])
        cubed = []
        given = []
        for i, (near_x, box) in enumerate(runs):
            here = ahead
            if i + 1 < len(runs):
                ahead = distances(*runs[i + 1])
            inverse = lax.rsqrt(here)
            cubed.append((inverse * inverse * inverse).astype(bf16))
            given.append(strengths[pl.ds(pl.multiple_of(box * 256, 256), 256), :])
            if i + 1 == len(runs) or runs[i + 1][0] != near_x:
                rows_of = pl.ds(pl.multiple_of((target_y * 4 + near_x) * per_box, per_box), per_box)
                total[rows_of, :] += lax.dot_general(
                    jnp.concatenate(cubed, axis=1),
                    jnp.concatenate(given, axis=1),
                    (((1,), (1,)), ((), ())),
                    preferred_element_type=f32,
                )
                cubed = []
                given = []
        if beside is not None:
            beside(item)
        return 0

    lax.fori_loop(0, 10, near_rows, 0)


def field_kernel(
    local_ref, sent_ref, cross_ref, first_ref, second_ref, mine_ref, theirs_ref,
    geometry, strengths, targets, planes, total, far_halo, far_own, far_centres
):
    boxes = 2 * plane_boxes
    half = lax.axis_index("rhs")
    origin = local_ref[523:526, 0:1]
    row = lax.broadcasted_iota(jnp.int32, (8, per_box), 0)

    def source(slot, _):
        local = padded(wide_tile(local_ref, slot * 16) - origin)
        charges = jnp.concatenate([wide_charges(sent_ref, slot), wide_charges(cross_ref, slot)], axis=0)
        store_source_features(local, charges, slot, geometry, strengths)
        return 0

    lax.fori_loop(0, boxes, source, 0, unroll=2)

    def halo_source(place, _):
        local = padded(wide_tile(first_ref, 256 + place * 8) - origin)
        charges = jnp.concatenate([wide_charges(first_ref, place), wide_charges(second_ref, place)], axis=0)
        store_source_features(local, charges, boxes + place, geometry, strengths)
        return 0

    lax.fori_loop(0, plane_boxes, halo_source, 0, unroll=2)

    def target(place, _):
        start = (half * plane_boxes + place) * 16
        local = padded(wide_tile(local_ref, start) - origin)
        normal = padded(wide_tile(local_ref, start + 8))
        square = jnp.sum(local * local, axis=0, keepdims=True) + soften
        along = jnp.sum(local * normal, axis=0, keepdims=True)
        distance = jnp.where(row == 3, 1.0, jnp.where(row == 4, square, -2.0 * local))
        high, middle, low = thirds(distance)
        rows = stacked_rows((high, middle, low, high, middle, high), per_box)
        start = pl.multiple_of(place * per_box, per_box)
        targets[pl.ds(start, per_box), :] = jnp.transpose(rows).astype(bf16)
        planes[pl.ds(pl.multiple_of(place * 8, 8), 8), :] = jnp.where(row == 3, along, normal)
        return 0

    lax.fori_loop(0, plane_boxes, target, 0, unroll=2)
    total[...] = jnp.zeros_like(total)

    moments = []
    for group, (centres, mine, theirs) in enumerate(
        (
            (first_ref[392:400], first_ref[384:392], second_ref[256:288]),
            (local_ref[520:528], local_ref[512:520], cross_ref[512:544]),
        )
    ):
        columns = jnp.transpose(jnp.concatenate([centres[:3] - origin, centres[3:]], axis=0))[:32]
        for a in range(3):
            far_centres[(group * 3 + a) * 32 : (group * 3 + a + 1) * 32, :] = jnp.broadcast_to(
                columns[:, a : a + 1], (32, 128)
            )
        both = jnp.concatenate([mine, whole_moments(theirs.astype(f32))], axis=0)
        high = both.astype(bf16).astype(f32)
        moments.append(jnp.concatenate([high, both - high], axis=0))
    lane = lax.broadcasted_iota(jnp.int32, (1, 128), 1)
    lane_x = lane & 3
    lane_y = (lane >> 2) & 3
    lane_plane = (lane >> 4) & 1

    def far_field(slot, group):
        x, y, plane = slot & 3, (slot >> 2) & 3, slot >> 4
        local = wide_tile(local_ref, slot * 16) - origin
        normal = wide_tile(local_ref, slot * 16 + 8)
        d = []
        for a in range(3):
            centre = far_centres[(group * 3 + a) * 32 : (group * 3 + a + 1) * 32, :]
            d.append(local[a : a + 1] - jnp.concatenate([centre, centre], axis=1))
        q = d[0] * d[0] + d[1] * d[1] + d[2] * d[2] + soften
        inverse = lax.rsqrt(q)
        inverse_2 = inverse * inverse
        inverse_3 = inverse_2 * inverse
        t = d[0] * normal[0:1] + d[1] * normal[1:2] + d[2] * normal[2:3]
        single = t * inverse_3
        steep = 3.0 * single * inverse_2
        coefficients = [single] + [steep * d[a] - normal[a : a + 1] * inverse_3 for a in range(3)]
        whole = jnp.concatenate(coefficients, axis=0)
        upper = whole.astype(bf16)
        lower = (whole - upper.astype(f32)).astype(bf16)
        lane_z = lane_plane + (4 * half - 2 if group == 0 else 0)
        near = (jnp.abs(lane_x - x) <= 1) & (jnp.abs(lane_y - y) <= 1) & (jnp.abs(lane_z - plane) <= 1)
        picked = jnp.where(near, 0.0, moments[group]).astype(bf16)
        first = jnp.dot(picked, upper, preferred_element_type=f32)
        second = jnp.dot(picked, lower, preferred_element_type=f32)
        return first[:16] + first[16:] + second[:16]

    def far_boxes(item):
        for k in range(4):
            slot = jnp.minimum(item * 4 + k, boxes - 1)
            far_halo[pl.ds(pl.multiple_of(slot * 16, 16), 16), :] = far_field(slot, 0)
        for k in range(2):
            place = jnp.minimum(item * 2 + k, plane_boxes - 1)
            far_own[pl.ds(pl.multiple_of(place * 16, 16), 16), :] = far_field(half * plane_boxes + place, 1)

    near_planes((0, plane_boxes, 2 * plane_boxes), geometry, strengths, targets, total, far_boxes)

    def near_field(place, _):
        turned = jnp.transpose(total[pl.ds(pl.multiple_of(place * per_box, per_box), per_box), :])
        sums = turned[:64] + (turned[64:128] + turned[128:192])
        side = planes[pl.ds(pl.multiple_of(place * 8, 8), 8), :]
        value = side[3:4] * sums[:16] - side[0:1] * sums[16:32]
        value = value - side[1:2] * sums[32:48] - side[2:3] * sums[48:64]
        slot = half * plane_boxes + place
        rows = pl.ds(pl.multiple_of(slot * 16, 16), 16)
        far_halo[rows, :] += value + far_own[pl.ds(pl.multiple_of(place * 16, 16), 16), :]
        return 0

    lax.fori_loop(0, plane_boxes, near_field, 0, unroll=2)
    for slot in range(boxes):
        mine_ref[slot * 8 : slot * 8 + 8] = far_halo[slot * 16 : slot * 16 + 8]
        theirs_ref[slot * 8 : slot * 8 + 8] = far_halo[slot * 16 + 8 : slot * 16 + 16]


def gram_kernel(counts_s, basis_ref, sums_ref):
    krylov = basis_ref.shape[0]
    pairs = [(m, n) for m in range(krylov) for n in range(m + 1)]

    def one_box(b, carry):
        lanes = pl.ds(pl.multiple_of(b * per_box, per_box), per_box)
        live = live_row(counts_s, b)
        rows = [basis_ref[m, :, lanes] * live for m in range(krylov)]
        out = []
        for k, (m, n) in enumerate(pairs):
            product = rows[m] * rows[n]
            out.append(carry[k] + product[:, :128] + product[:, 128:])
        return tuple(out)

    zeros = jnp.zeros((8, 128), f32)
    gram = lax.fori_loop(0, counts_s.shape[0], one_box, (zeros,) * len(pairs))
    lane = lax.broadcasted_iota(jnp.int32, (8, 128), 1)
    total = zeros
    for k, value in enumerate(gram):
        total = jnp.where(lane == krylov + 1 + k, jnp.sum(value, axis=1, keepdims=True), total)
    sums_ref[...] = total


def image_kernel(centres_s, counts_s, mine_ref, theirs_ref, gram_ref, contrast_ref, basis_ref, image_ref, sums_ref):
    krylov = basis_ref.shape[0]

    def one_box(b, carry):
        lanes = pl.ds(pl.multiple_of(b * per_box, per_box), per_box)
        rows = pl.ds(pl.multiple_of(slot_of(centres_s, b) * 8, 8), 8)
        live = live_row(counts_s, b)
        part = mine_ref[rows, :] + theirs_ref[rows, :]
        image = live * (basis_ref[krylov - 1, :, lanes] - 2.0 * wide_row(contrast_ref, b) * part)
        image_ref[:, lanes] = image
        sums = []
        for m in range(krylov + 1):
            product = image * (basis_ref[m, :, lanes] if m < krylov else image)
            sums.append(carry[m] + product[:, :128] + product[:, 128:])
        return tuple(sums)

    zeros = jnp.zeros((8, 128), f32)
    sums = lax.fori_loop(0, counts_s.shape[0], one_box, (zeros,) * (krylov + 1), unroll=4)
    lane = lax.broadcasted_iota(jnp.int32, (8, 128), 1)
    total = gram_ref[...]
    for k, value in enumerate(sums):
        total = jnp.where(lane == k, jnp.sum(value, axis=1, keepdims=True), total)
    sums_ref[...] = jnp.broadcast_to(total[None], sums_ref.shape)


def two_sum(a, b):
    s = a + b
    c = s - a
    return s, (a - (s - c)) + (b - c)


def halves(a):
    c = a * 4097.0
    high = c - (c - a)
    return high, a - high


def two_product(a, b):
    p = a * b
    a_high, a_low = halves(a)
    b_high, b_low = halves(b)
    return p, ((a_high * b_high - p) + a_high * b_low + a_low * b_high) + a_low * b_low


def finish_kernel(total_facets, counts_s, tiles_ref, image_ref, basis_ref, next_ref, hessenberg_ref):
    boxes = counts_s.shape[0]
    krylov = basis_ref.shape[0]
    lane = lax.broadcasted_iota(jnp.int32, (8, 128), 1)

    def add_tile(i, carry):
        value, error = two_sum(carry[0], tiles_ref[i])
        return value, carry[1] + error

    sums, rest = lax.fori_loop(0, tiles_ref.shape[0], add_tile, (jnp.zeros((8, 128), f32),) * 2, unroll=8)
    exact = sums + rest
    projections = [exact[:, m : m + 1] / total_facets for m in range(krylov)]
    pairs = [(m, n) for m in range(krylov) for n in range(m + 1)]
    first = jnp.where(lane == krylov, 1.0, 0.0)
    second = jnp.where(lane <= krylov, 1.0, 0.0)
    for m in range(krylov):
        first = jnp.where(lane == m, -2.0 * projections[m], first)
    for k, (m, n) in enumerate(pairs):
        at = lane == krylov + 1 + k
        scale = 1.0 if m == n else 2.0
        first = jnp.where(at, scale * projections[m], first)
        second = jnp.where(at, projections[n], second)
    factor, factor_rest = two_product(first, second)
    value, value_rest = two_product(factor, sums)
    value_rest = value_rest + (factor * rest + factor_rest * sums)
    for shift in (64, 32, 16, 8, 4, 2, 1):
        other = pltpu.roll(value, shift, 1)
        other_rest = pltpu.roll(value_rest, shift, 1)
        value, error = two_sum(value, other)
        value_rest = (value_rest + other_rest) + error
    remaining = jnp.maximum(value + value_rest, 0.0)
    norm = jnp.sqrt(remaining / total_facets + epsilon)
    heads = jnp.where(lane == krylov, norm, 0.0)
    for m in range(krylov):
        heads = jnp.where(lane == m, projections[m], heads)
    hessenberg_ref[...] = heads[:, : krylov + 1]
    wide = [jnp.broadcast_to(p, (8, per_box)) for p in projections]
    scale = jnp.concatenate([1.0 / norm] * (per_box // 128), axis=1)

    def one_box(b, _):
        lanes = pl.ds(pl.multiple_of(b * per_box, per_box), per_box)
        live = live_row(counts_s, b)
        sent = wide[0] * basis_ref[0, :, lanes]
        for m in range(1, krylov):
            sent += wide[m] * basis_ref[m, :, lanes]
        next_ref[:, lanes] = (image_ref[:, lanes] - sent * live) * scale
        return 0

    lax.fori_loop(0, boxes, one_box, 0, unroll=4)


smem = pl.BlockSpec(memory_space=pltpu.SMEM)
vmem = pl.BlockSpec(memory_space=pltpu.VMEM)


def on_device(
    basis, facet_centres, normals, areas, contrast, facet_counts, box_centres, near_boxes, far_boxes
):
    krylov, rhs_local, facet_local = basis.shape
    boxes = facet_counts.shape[0]
    count = lax.axis_size("box")
    total_facets = count * facet_local
    areas = areas.reshape(-1, 128)
    contrast = contrast.reshape(-1, 128)

    def rows(number, width=128, dtype=f32):
        return jax.ShapeDtypeStruct((number, width), dtype)

    def limit(mebibytes):
        return pltpu.CompilerParams(vmem_limit_bytes=mebibytes * 1024 * 1024)

    sent, first, second, local = pl.pallas_call(
        prep_kernel,
        out_shape=(rows(544, dtype=bf16), rows(400), rows(288, dtype=bf16), rows(528)),
        in_specs=[pl.BlockSpec(memory_space=pl.ANY)] * 6,
        out_specs=(vmem,) * 4,
        scratch_shapes=[
            pltpu.VMEM((512, 128), f32),
            pltpu.SMEM(box_centres.shape, f32),
            pltpu.SMEM(facet_counts.shape, jnp.int32),
            pltpu.VMEM((rhs_local, facet_local), f32),
            pltpu.VMEM(facet_centres.shape, f32),
            pltpu.VMEM(areas.shape, f32),
            pltpu.VMEM(normals.shape, f32),
            pltpu.SemaphoreType.DMA((6,)),
        ],
        name="prepare",
    )(box_centres, facet_counts, basis, facet_centres, areas, normals)
    swap = [(0, 1), (1, 0)]
    ups = range(count - 1)
    cross = lax.ppermute(sent, "rhs", swap)
    first = lax.ppermute(
        first, ("box", "rhs"), [(2 * i, 2 * i + 2) for i in ups] + [(2 * i + 3, 2 * i + 1) for i in ups]
    )
    second = lax.ppermute(
        second, ("box", "rhs"), [(2 * i + 1, 2 * i + 2) for i in ups] + [(2 * i + 2, 2 * i + 1) for i in ups]
    )
    plane_slots = plane_boxes * per_box
    mine, theirs = pl.pallas_call(
        field_kernel,
        out_shape=(rows(boxes * 8, per_box),) * 2,
        in_specs=[vmem] * 5,
        out_specs=(vmem, vmem),
        scratch_shapes=[
            pltpu.VMEM((3 * plane_boxes * depth, per_box), bf16),
            pltpu.VMEM((3 * plane_boxes * 256, per_box), bf16),
            pltpu.VMEM((plane_slots, depth), bf16),
            pltpu.VMEM((plane_boxes * 8, per_box), f32),
            pltpu.VMEM((plane_slots, 256), f32),
            pltpu.VMEM((boxes * 16, per_box), f32),
            pltpu.VMEM((plane_boxes * 16, per_box), f32),
            pltpu.VMEM((6 * 32, 128), f32),
        ],
        compiler_params=limit(60),
        name="fields",
    )(local, sent, cross, first, second)
    theirs = lax.ppermute(theirs, "rhs", swap)
    gram = pl.pallas_call(
        gram_kernel,
        out_shape=rows(8),
        in_specs=[smem, vmem],
        out_specs=vmem,
        compiler_params=limit(8),
        name="gram",
    )(facet_counts, basis)
    image, tiles = pl.pallas_call(
        image_kernel,
        out_shape=(rows(rhs_local, facet_local), jax.ShapeDtypeStruct((count, 8, 128), f32)),
        in_specs=[smem, smem] + [vmem] * 5,
        out_specs=(vmem, vmem),
        compiler_params=limit(8),
        name="image",
    )(box_centres, facet_counts, mine, theirs, gram, contrast, basis)
    tiles = lax.all_to_all(tiles, "box", 0, 0, tiled=True)
    next_vector, hessenberg = pl.pallas_call(
        functools.partial(finish_kernel, total_facets),
        out_shape=(
            jax.ShapeDtypeStruct((rhs_local, facet_local), f32),
            jax.ShapeDtypeStruct((rhs_local, krylov + 1), f32),
        ),
        in_specs=[smem] + [vmem] * 3,
        out_specs=(vmem, vmem),
        compiler_params=pltpu.CompilerParams(vmem_limit_bytes=16 * 1024 * 1024),
        name="finish",
    )(facet_counts, tiles, image, basis)
    return next_vector, hessenberg.T


def solution(mesh):
    return jax.shard_map(
        on_device,
        mesh=mesh,
        in_specs=(
            P(None, "rhs", "box"),
            P(None, "box"),
            P(None, "box"),
            P("box"),
            P("box"),
            P("box"),
            P(None, "box"),
            P("box", None),
            P("box", None),
        ),
        out_specs=(P("rhs", "box"), P(None, "rhs")),
        check_vma=False,
    )
```

```python
import functools

import jax
import jax.numpy as jnp
from jax import lax
from jax.experimental import pallas as pl
from jax.experimental.pallas import tpu as pltpu
from jax.sharding import PartitionSpec as P

soften = 0.0025
epsilon = 1e-06
f32 = jnp.float32
bf16 = jnp.bfloat16
plane_boxes = 16
per_box = 256
depth = 128


def lattice(centres_s, b):
    x = (centres_s[0, b] + 0.5).astype(jnp.int32)
    y = (centres_s[1, b] + 0.5).astype(jnp.int32)
    z = (centres_s[2, b] + 0.5).astype(jnp.int32)
    return x, y, z


def slot_of(centres_s, b):
    x, y, z = lattice(centres_s, b)
    return (z & 1) * plane_boxes + y * 4 + x


def wide_row(ref, b):
    return jnp.concatenate([ref[pl.ds(2 * b, 1), :], ref[pl.ds(2 * b + 1, 1), :]], axis=1)


def live_row(counts_s, b):
    slots = lax.broadcasted_iota(jnp.int32, (1, per_box), 1)
    return (slots < counts_s[b]).astype(f32)


def prep_kernel(
    centres_h, counts_h, basis_h, facets_h, areas_h, normals_h, cross_ref, first_ref, second_ref, local_ref,
    charges_v, centres_s, counts_s, current_ref, facets_ref, areas_ref, normals_ref, arrived
):
    boxes = counts_s.shape[0]
    moves = [
        (basis_h.at[basis_h.shape[0] - 1], current_ref),
        (facets_h, facets_ref),
        (areas_h, areas_ref),
        (normals_h, normals_ref),
        (centres_h, centres_s),
        (counts_h, counts_s),
    ]
    copies = [pltpu.make_async_copy(a, b, arrived.at[k]) for k, (a, b) in enumerate(moves)]
    for copy in copies:
        copy.start()
    for copy in copies:
        copy.wait()
    lane = lax.broadcasted_iota(jnp.int32, (8, 128), 1)
    row = lax.broadcasted_iota(jnp.int32, (8, 128), 0)
    empty = jnp.zeros((2, 128), f32)

    def one_box(b, carry):
        moments, centres = carry
        slot = slot_of(centres_s, b)
        lanes = pl.ds(pl.multiple_of(b * per_box, per_box), per_box)
        facets = facets_ref[:, lanes]
        normals = normals_ref[:, lanes]
        live = live_row(counts_s, b)
        weighted = current_ref[:, lanes] * (wide_row(areas_ref, b) * live / per_box)
        start = pl.multiple_of(slot * 16, 16)
        charges_v[pl.ds(start, 16), :] = jnp.concatenate([weighted[:, :128], weighted[:, 128:]], axis=0)
        local_ref[pl.ds(start, 16), :] = jnp.concatenate(
            [facets[:, :128], facets[:, 128:], empty, normals[:, :128], normals[:, 128:], empty], axis=0
        )
        moments += jnp.where(lane == slot, jnp.sum(weighted, axis=1, keepdims=True), 0.0)
        for a in range(3):
            dipole = jnp.sum(weighted * (facets[a : a + 1] - centres_s[a, b]), axis=1, keepdims=True)
            moments += jnp.where(lane == 32 * (a + 1) + slot, dipole, 0.0)
            centres += jnp.where((lane == slot) & (row == a), centres_s[a, b], 0.0)
        return moments, centres

    zeros = jnp.zeros((8, 128), f32)
    moments, centres = lax.fori_loop(0, boxes, one_box, (zeros, zeros), unroll=4)
    _, _, z = lattice(centres_s, 0)
    base_z = (z - (z & 1)).astype(f32) + 0.5
    centres = jnp.where((row == 3) | (row == 4), 1.5, jnp.where(row == 5, base_z, centres))
    half = lax.axis_index("rhs")
    away = pl.multiple_of((1 - half) * 256, 256)
    here = pl.multiple_of(half * 256, 256)
    pieces = jnp.concatenate([*thirds(moments), zeros], axis=0).astype(bf16)
    cross_ref[:512] = charges_v[...].astype(bf16)
    cross_ref[512:] = pieces
    second_ref[:256] = charges_v[pl.ds(here, 256), :].astype(bf16)
    second_ref[256:] = pieces
    first_ref[:256] = charges_v[pl.ds(away, 256), :].astype(bf16).astype(f32)
    for place in range(plane_boxes):
        first_ref[256 + 8 * place : 264 + 8 * place] = local_ref[pl.ds(away + 16 * place, 8), :]
    first_ref[384:392] = moments
    first_ref[392:] = centres
    local_ref[512:520] = moments
    local_ref[520:] = centres


def thirds(x):
    high = x.astype(bf16).astype(f32)
    rest = x - high
    middle = rest.astype(bf16).astype(f32)
    return high, middle, (rest - middle).astype(bf16).astype(f32)


def stacked_rows(parts, width):
    zeros = jnp.zeros((depth - 8 * len(parts), width), f32)
    return jnp.concatenate([*parts, zeros], axis=0)


def padded(rows):
    return jnp.concatenate([rows, jnp.zeros((8 - rows.shape[0], rows.shape[1]), f32)], axis=0)


def wide_charges(ref, place):
    both = ref[pl.ds(pl.multiple_of(place * 16, 16), 16), :].astype(f32)
    return jnp.concatenate([both[:8], both[8:]], axis=1)


def wide_tile(ref, start):
    tile = ref[pl.ds(pl.multiple_of(start, 8), 8), :]
    return jnp.concatenate([tile[0:3], tile[3:6]], axis=1)


def whole_moments(pieces):
    return pieces[:8] + (pieces[8:16] + pieces[16:24])


def store_source_features(local, charges, box, geometry, strengths):
    row = lax.broadcasted_iota(jnp.int32, (8, per_box), 0)
    square = jnp.sum(local * local, axis=0, keepdims=True)
    features = jnp.where(row == 3, square, jnp.where(row == 4, 1.0, local))
    high, middle, low = thirds(features)
    rows = stacked_rows((high, high, high, middle, middle, low), per_box)
    geometry[pl.ds(pl.multiple_of(box * depth, depth), depth), :] = rows.astype(bf16)
    products = jnp.concatenate([charges] + [charges * local[a : a + 1] for a in range(3)], axis=0)
    rows = jnp.concatenate([*thirds(products), jnp.zeros((64, per_box), f32)], axis=0)
    strengths[pl.ds(pl.multiple_of(box * 256, 256), 256), :] = rows.astype(bf16)


def near_planes(sources, geometry, strengths, targets, total, beside=None):
    def near_rows(item, _):
        target_y = (item + 1) // 3
        source_y = target_y + lax.rem(item + 1, 3) - 1
        runs = []
        for near_x in range(4):
            for first in sources:
                for x in range(max(near_x - 1, 0), min(near_x + 2, 4)):
                    runs.append((near_x, first + source_y * 4 + x))

        def distances(near_x, box):
            start = pl.multiple_of((target_y * 4 + near_x) * per_box, per_box)
            weights = geometry[pl.ds(pl.multiple_of(box * depth, depth), depth), :]
            return jnp.dot(targets[pl.ds(start, per_box), :], weights, preferred_element_type=f32)

        ahead = distances(*runs[0])
        cubed = []
        given = []
        for i, (near_x, box) in enumerate(runs):
            here = ahead
            if i + 1 < len(runs):
                ahead = distances(*runs[i + 1])
            inverse = lax.rsqrt(here)
            cubed.append((inverse * inverse * inverse).astype(bf16))
            given.append(strengths[pl.ds(pl.multiple_of(box * 256, 256), 256), :])
            if i + 1 == len(runs) or runs[i + 1][0] != near_x:
                rows_of = pl.ds(pl.multiple_of((target_y * 4 + near_x) * per_box, per_box), per_box)
                total[rows_of, :] += lax.dot_general(
                    jnp.concatenate(cubed, axis=1),
                    jnp.concatenate(given, axis=1),
                    (((1,), (1,)), ((), ())),
                    preferred_element_type=f32,
                )
                cubed = []
                given = []
        if beside is not None:
            beside(item)
        return 0

    lax.fori_loop(0, 10, near_rows, 0)


def field_kernel(
    centres_s, local_ref, sent_ref, cross_ref, first_ref, second_ref, mine_ref, theirs_ref,
    geometry, strengths, targets, planes, total, far, far_centres, far_moments
):
    boxes = 2 * plane_boxes
    half = lax.axis_index("rhs")
    origin = local_ref[523:526, 0:1]
    row = lax.broadcasted_iota(jnp.int32, (8, per_box), 0)

    def source(slot, _):
        local = padded(wide_tile(local_ref, slot * 16) - origin)
        charges = jnp.concatenate([wide_charges(sent_ref, slot), wide_charges(cross_ref, slot)], axis=0)
        store_source_features(local, charges, slot, geometry, strengths)
        return 0

    lax.fori_loop(0, boxes, source, 0, unroll=4)

    def halo_source(place, _):
        local = padded(wide_tile(first_ref, 256 + place * 8) - origin)
        charges = jnp.concatenate([wide_charges(first_ref, place), wide_charges(second_ref, place)], axis=0)
        store_source_features(local, charges, boxes + place, geometry, strengths)
        return 0

    lax.fori_loop(0, plane_boxes, halo_source, 0, unroll=4)

    def target(place, _):
        start = (half * plane_boxes + place) * 16
        local = padded(wide_tile(local_ref, start) - origin)
        normal = padded(wide_tile(local_ref, start + 8))
        square = jnp.sum(local * local, axis=0, keepdims=True) + soften
        along = jnp.sum(local * normal, axis=0, keepdims=True)
        distance = jnp.where(row == 3, 1.0, jnp.where(row == 4, square, -2.0 * local))
        high, middle, low = thirds(distance)
        rows = stacked_rows((high, middle, low, high, middle, high), per_box)
        start = pl.multiple_of(place * per_box, per_box)
        targets[pl.ds(start, per_box), :] = jnp.transpose(rows).astype(bf16)
        planes[pl.ds(pl.multiple_of(place * 8, 8), 8), :] = jnp.where(row == 3, along, normal)
        return 0

    lax.fori_loop(0, plane_boxes, target, 0, unroll=4)
    total[...] = jnp.zeros_like(total)

    for group, (centres, mine, theirs) in enumerate(
        (
            (first_ref[392:400], first_ref[384:392], second_ref[256:288]),
            (local_ref[520:528], local_ref[512:520], cross_ref[512:544]),
        )
    ):
        columns = jnp.transpose(jnp.concatenate([centres[:3] - origin, centres[3:]], axis=0))[:32]
        for a in range(3):
            far_centres[(group * 3 + a) * 32 : (group * 3 + a + 1) * 32, :] = jnp.broadcast_to(
                columns[:, a : a + 1], (32, 128)
            )
        both = jnp.concatenate([mine, whole_moments(theirs.astype(f32))], axis=0)
        high = both.astype(bf16).astype(f32)
        far_moments[group * 32 : group * 32 + 32, :] = jnp.concatenate([high, both - high], axis=0)
    lane = lax.broadcasted_iota(jnp.int32, (1, 128), 1)
    lane_x = lane & 3
    lane_y = (lane >> 2) & 3
    lane_plane = (lane >> 4) & 1

    def far_field(k):
        group = (k >= boxes).astype(jnp.int32)
        slot = jnp.where(k < boxes, k, half * plane_boxes + k - boxes)
        x, y, plane = slot & 3, (slot >> 2) & 3, slot >> 4
        local = wide_tile(local_ref, slot * 16) - origin
        normal = wide_tile(local_ref, slot * 16 + 8)
        d = []
        for a in range(3):
            centre = far_centres[pl.ds(pl.multiple_of((group * 3 + a) * 32, 32), 32), :]
            d.append(local[a : a + 1] - jnp.concatenate([centre, centre], axis=1))
        q = d[0] * d[0] + d[1] * d[1] + d[2] * d[2] + soften
        inverse = lax.rsqrt(q)
        inverse_2 = inverse * inverse
        inverse_3 = inverse_2 * inverse
        t = d[0] * normal[0:1] + d[1] * normal[1:2] + d[2] * normal[2:3]
        single = t * inverse_3
        steep = 3.0 * single * inverse_2
        coefficients = [single] + [steep * d[a] - normal[a : a + 1] * inverse_3 for a in range(3)]
        whole = jnp.concatenate(coefficients, axis=0)
        upper = whole.astype(bf16)
        lower = (whole - upper.astype(f32)).astype(bf16)
        lane_z = lane_plane + jnp.where(group == 0, 4 * half - 2, 0)
        near = (jnp.abs(lane_x - x) <= 1) & (jnp.abs(lane_y - y) <= 1) & (jnp.abs(lane_z - plane) <= 1)
        picked = jnp.where(near, 0.0, far_moments[pl.ds(pl.multiple_of(group * 32, 32), 32), :]).astype(bf16)
        first = jnp.dot(picked, upper, preferred_element_type=f32)
        second = jnp.dot(picked, lower, preferred_element_type=f32)
        return first[:16] + first[16:] + second[:16]

    def far_boxes(item):
        for i in range(5):
            k = jnp.minimum(item * 5 + i, 3 * plane_boxes - 1)
            far[pl.ds(pl.multiple_of(k * 16, 16), 16), :] = far_field(k)

    near_planes((0, plane_boxes, 2 * plane_boxes), geometry, strengths, targets, total, far_boxes)

    def near_field(place, _):
        turned = jnp.transpose(total[pl.ds(pl.multiple_of(place * per_box, per_box), per_box), :])
        sums = turned[:64] + (turned[64:128] + turned[128:192])
        side = planes[pl.ds(pl.multiple_of(place * 8, 8), 8), :]
        value = side[3:4] * sums[:16] - side[0:1] * sums[16:32]
        value = value - side[1:2] * sums[32:48] - side[2:3] * sums[48:64]
        slot = half * plane_boxes + place
        rows = pl.ds(pl.multiple_of(slot * 16, 16), 16)
        far[rows, :] += value + far[pl.ds(pl.multiple_of((boxes + place) * 16, 16), 16), :]
        return 0

    lax.fori_loop(0, plane_boxes, near_field, 0, unroll=4)

    def given_back(b, _):
        start = pl.multiple_of(slot_of(centres_s, b) * 16, 16)
        rows = pl.ds(pl.multiple_of(b * 8, 8), 8)
        mine_ref[rows, :] = far[pl.ds(start, 8), :]
        theirs_ref[rows, :] = far[pl.ds(start + 8, 8), :]
        return 0

    lax.fori_loop(0, boxes, given_back, 0, unroll=4)


def gram_kernel(counts_s, basis_ref, sums_ref, live_ref):
    krylov = basis_ref.shape[0]
    pairs = [(m, n) for m in range(krylov) for n in range(m + 1)]

    def one_box(b, carry):
        lanes = pl.ds(pl.multiple_of(b * per_box, per_box), per_box)
        live = live_row(counts_s, b)
        live_ref[pl.ds(2 * b, 1), :] = live[:, :128]
        live_ref[pl.ds(2 * b + 1, 1), :] = live[:, 128:]
        rows = [basis_ref[m, :, lanes] * live for m in range(krylov)]
        out = []
        for k, (m, n) in enumerate(pairs):
            product = rows[m] * rows[n]
            out.append(carry[k] + product[:, :128] + product[:, 128:])
        return tuple(out)

    zeros = jnp.zeros((8, 128), f32)
    gram = lax.fori_loop(0, counts_s.shape[0], one_box, (zeros,) * len(pairs))
    lane = lax.broadcasted_iota(jnp.int32, (8, 128), 1)
    total = zeros
    for k, value in enumerate(gram):
        total = jnp.where(lane == krylov + 1 + k, jnp.sum(value, axis=1, keepdims=True), total)
    sums_ref[...] = total


def image_kernel(mine_ref, theirs_ref, gram_ref, live_ref, contrast_ref, basis_ref, image_ref, sums_ref):
    krylov = basis_ref.shape[0]

    def one_box(b, carry):
        lanes = pl.ds(pl.multiple_of(b * per_box, per_box), per_box)
        rows = pl.ds(pl.multiple_of(b * 8, 8), 8)
        live = wide_row(live_ref, b)
        part = mine_ref[rows, :] + theirs_ref[rows, :]
        image = live * (basis_ref[krylov - 1, :, lanes] - 2.0 * wide_row(contrast_ref, b) * part)
        image_ref[:, lanes] = image
        sums = []
        for m in range(krylov + 1):
            product = image * (basis_ref[m, :, lanes] if m < krylov else image)
            sums.append(carry[m] + product[:, :128] + product[:, 128:])
        return tuple(sums)

    zeros = jnp.zeros((8, 128), f32)
    sums = lax.fori_loop(0, live_ref.shape[0] // 2, one_box, (zeros,) * (krylov + 1), unroll=4)
    lane = lax.broadcasted_iota(jnp.int32, (8, 128), 1)
    total = gram_ref[...]
    for k, value in enumerate(sums):
        total = jnp.where(lane == k, jnp.sum(value, axis=1, keepdims=True), total)
    sums_ref[...] = jnp.broadcast_to(total[None], sums_ref.shape)


def two_sum(a, b):
    s = a + b
    c = s - a
    return s, (a - (s - c)) + (b - c)


def halves(a):
    c = a * 4097.0
    high = c - (c - a)
    return high, a - high


def two_product(a, b):
    p = a * b
    a_high, a_low = halves(a)
    b_high, b_low = halves(b)
    return p, ((a_high * b_high - p) + a_high * b_low + a_low * b_high) + a_low * b_low


def finish_kernel(total_facets, tiles_ref, live_ref, image_ref, basis_ref, next_ref, hessenberg_ref):
    boxes = live_ref.shape[0] // 2
    krylov = basis_ref.shape[0]
    lane = lax.broadcasted_iota(jnp.int32, (8, 128), 1)

    sums, rest = tiles_ref[0, 0], tiles_ref[0, 1]
    for i in range(1, tiles_ref.shape[0]):
        sums, error = two_sum(sums, tiles_ref[i, 0])
        rest = (rest + tiles_ref[i, 1]) + error
    exact = sums + rest
    projections = [exact[:, m : m + 1] / total_facets for m in range(krylov)]
    pairs = [(m, n) for m in range(krylov) for n in range(m + 1)]
    first = jnp.where(lane == krylov, 1.0, 0.0)
    second = jnp.where(lane <= krylov, 1.0, 0.0)
    for m in range(krylov):
        first = jnp.where(lane == m, -2.0 * projections[m], first)
    for k, (m, n) in enumerate(pairs):
        at = lane == krylov + 1 + k
        scale = 1.0 if m == n else 2.0
        first = jnp.where(at, scale * projections[m], first)
        second = jnp.where(at, projections[n], second)
    factor, factor_rest = two_product(first, second)
    value, value_rest = two_product(factor, sums)
    value_rest = value_rest + (factor * rest + factor_rest * sums)
    for shift in (64, 32, 16, 8, 4, 2, 1):
        other = pltpu.roll(value, shift, 1)
        other_rest = pltpu.roll(value_rest, shift, 1)
        value, error = two_sum(value, other)
        value_rest = (value_rest + other_rest) + error
    remaining = jnp.maximum(value + value_rest, 0.0)
    norm = jnp.sqrt(remaining / total_facets + epsilon)
    heads = jnp.where(lane == krylov, norm, 0.0)
    for m in range(krylov):
        heads = jnp.where(lane == m, projections[m], heads)
    hessenberg_ref[...] = heads[:, : krylov + 1]
    wide = [jnp.broadcast_to(p, (8, per_box)) for p in projections]
    scale = jnp.concatenate([1.0 / norm] * (per_box // 128), axis=1)

    def one_box(b, _):
        lanes = pl.ds(pl.multiple_of(b * per_box, per_box), per_box)
        live = wide_row(live_ref, b)
        sent = wide[0] * basis_ref[0, :, lanes]
        for m in range(1, krylov):
            sent += wide[m] * basis_ref[m, :, lanes]
        next_ref[:, lanes] = (image_ref[:, lanes] - sent * live) * scale
        return 0

    lax.fori_loop(0, boxes, one_box, 0, unroll=4)


smem = pl.BlockSpec(memory_space=pltpu.SMEM)
vmem = pl.BlockSpec(memory_space=pltpu.VMEM)


def on_device(
    basis, facet_centres, normals, areas, contrast, facet_counts, box_centres, near_boxes, far_boxes
):
    krylov, rhs_local, facet_local = basis.shape
    boxes = facet_counts.shape[0]
    count = lax.axis_size("box")
    total_facets = count * facet_local
    areas = areas.reshape(-1, 128)
    contrast = contrast.reshape(-1, 128)

    def rows(number, width=128, dtype=f32):
        return jax.ShapeDtypeStruct((number, width), dtype)

    def limit(mebibytes):
        return pltpu.CompilerParams(vmem_limit_bytes=mebibytes * 1024 * 1024)

    sent, first, second, local = pl.pallas_call(
        prep_kernel,
        out_shape=(rows(544, dtype=bf16), rows(400), rows(288, dtype=bf16), rows(528)),
        in_specs=[pl.BlockSpec(memory_space=pl.ANY)] * 6,
        out_specs=(vmem,) * 4,
        scratch_shapes=[
            pltpu.VMEM((512, 128), f32),
            pltpu.SMEM(box_centres.shape, f32),
            pltpu.SMEM(facet_counts.shape, jnp.int32),
            pltpu.VMEM((rhs_local, facet_local), f32),
            pltpu.VMEM(facet_centres.shape, f32),
            pltpu.VMEM(areas.shape, f32),
            pltpu.VMEM(normals.shape, f32),
            pltpu.SemaphoreType.DMA((6,)),
        ],
        name="prepare",
    )(box_centres, facet_counts, basis, facet_centres, areas, normals)
    swap = [(0, 1), (1, 0)]
    ups = range(count - 1)
    cross = lax.ppermute(sent, "rhs", swap)
    first = lax.ppermute(
        first, ("box", "rhs"), [(2 * i, 2 * i + 2) for i in ups] + [(2 * i + 3, 2 * i + 1) for i in ups]
    )
    second = lax.ppermute(
        second, ("box", "rhs"), [(2 * i + 1, 2 * i + 2) for i in ups] + [(2 * i + 2, 2 * i + 1) for i in ups]
    )
    plane_slots = plane_boxes * per_box
    mine, theirs = pl.pallas_call(
        field_kernel,
        out_shape=(rows(boxes * 8, per_box),) * 2,
        in_specs=[smem] + [vmem] * 5,
        out_specs=(vmem, vmem),
        scratch_shapes=[
            pltpu.VMEM((3 * plane_boxes * depth, per_box), bf16),
            pltpu.VMEM((3 * plane_boxes * 256, per_box), bf16),
            pltpu.VMEM((plane_slots, depth), bf16),
            pltpu.VMEM((plane_boxes * 8, per_box), f32),
            pltpu.VMEM((plane_slots, 256), f32),
            pltpu.VMEM((3 * plane_boxes * 16, per_box), f32),
            pltpu.VMEM((6 * 32, 128), f32),
            pltpu.VMEM((2 * 32, 128), f32),
        ],
        compiler_params=limit(32),
        name="fields",
    )(box_centres, local, sent, cross, first, second)
    theirs = lax.ppermute(theirs, "rhs", swap)
    gram, live = pl.pallas_call(
        gram_kernel,
        out_shape=(rows(8), rows(2 * boxes)),
        in_specs=[smem, vmem],
        out_specs=(vmem, vmem),
        compiler_params=limit(8),
        name="gram",
    )(facet_counts, basis)
    few = 4 if count % 4 == 0 else 1
    image, tiles = pl.pallas_call(
        image_kernel,
        out_shape=(rows(rhs_local, facet_local), jax.ShapeDtypeStruct((few, 8, 128), f32)),
        in_specs=[vmem] * 6,
        out_specs=(vmem, vmem),
        compiler_params=limit(8),
        name="image",
    )(mine, theirs, gram, live, contrast, basis)
    tiles = lax.all_to_all(
        tiles, "box", 0, 0, axis_index_groups=[[i + k for k in range(few)] for i in range(0, count, few)], tiled=True
    )
    value, rest = tiles[0], jnp.zeros_like(tiles[0])
    for i in range(1, few):
        value, error = two_sum(value, tiles[i])
        rest = rest + error
    tiles = jnp.broadcast_to(jnp.stack([value, rest])[None], (count // few, 2, 8, 128))
    tiles = lax.all_to_all(
        tiles, "box", 0, 0, axis_index_groups=[list(range(i, count, few)) for i in range(few)], tiled=True
    )
    next_vector, hessenberg = pl.pallas_call(
        functools.partial(finish_kernel, total_facets),
        out_shape=(rows(rhs_local, facet_local), rows(rhs_local, krylov + 1)),
        in_specs=[vmem] * 4,
        out_specs=(vmem, vmem),
        compiler_params=limit(16),
        name="finish",
    )(tiles, live, image, basis)
    return next_vector, hessenberg.T


def solution(mesh):
    return jax.shard_map(
        on_device,
        mesh=mesh,
        in_specs=(
            P(None, "rhs", "box"),
            P(None, "box"),
            P(None, "box"),
            P("box"),
            P("box"),
            P("box"),
            P(None, "box"),
            P("box", None),
            P("box", None),
        ),
        out_specs=(P("rhs", "box"), P(None, "rhs")),
        check_vma=False,
    )
```

```python
import functools

import jax
import jax.numpy as jnp
from jax import lax
from jax.experimental import pallas as pl
from jax.experimental.pallas import tpu as pltpu
from jax.sharding import PartitionSpec as P

soften = 0.0025
epsilon = 1e-06
f32 = jnp.float32
bf16 = jnp.bfloat16
plane_boxes = 16
per_box = 256
depth = 128


def lattice(centres_s, b):
    x = (centres_s[0, b] + 0.5).astype(jnp.int32)
    y = (centres_s[1, b] + 0.5).astype(jnp.int32)
    z = (centres_s[2, b] + 0.5).astype(jnp.int32)
    return x, y, z


def slot_of(centres_s, b):
    x, y, z = lattice(centres_s, b)
    return (z & 1) * plane_boxes + y * 4 + x


def wide_row(ref, b):
    return jnp.concatenate([ref[pl.ds(2 * b, 1), :], ref[pl.ds(2 * b + 1, 1), :]], axis=1)


def live_row(counts_s, b):
    slots = lax.broadcasted_iota(jnp.int32, (1, per_box), 1)
    return (slots < counts_s[b]).astype(f32)


def prep_kernel(
    centres_h, counts_h, basis_h, facets_h, areas_h, normals_h, cross_ref, first_ref, second_ref, local_ref,
    charges_v, centres_s, counts_s, current_ref, facets_ref, areas_ref, normals_ref, arrived
):
    boxes = counts_s.shape[0]
    moves = [
        (basis_h.at[basis_h.shape[0] - 1], current_ref),
        (facets_h, facets_ref),
        (areas_h, areas_ref),
        (normals_h, normals_ref),
        (centres_h, centres_s),
        (counts_h, counts_s),
    ]
    copies = [pltpu.make_async_copy(a, b, arrived.at[k]) for k, (a, b) in enumerate(moves)]
    for copy in copies:
        copy.start()
    for copy in copies:
        copy.wait()
    lane = lax.broadcasted_iota(jnp.int32, (8, 128), 1)
    row = lax.broadcasted_iota(jnp.int32, (8, 128), 0)
    empty = jnp.zeros((2, 128), f32)

    def one_box(b, carry):
        moments, centres = carry
        slot = slot_of(centres_s, b)
        lanes = pl.ds(pl.multiple_of(b * per_box, per_box), per_box)
        facets = facets_ref[:, lanes]
        normals = normals_ref[:, lanes]
        live = live_row(counts_s, b)
        weighted = current_ref[:, lanes] * (wide_row(areas_ref, b) * live / per_box)
        start = pl.multiple_of(slot * 16, 16)
        charges_v[pl.ds(start, 16), :] = jnp.concatenate([weighted[:, :128], weighted[:, 128:]], axis=0)
        local_ref[pl.ds(start, 16), :] = jnp.concatenate(
            [facets[:, :128], facets[:, 128:], empty, normals[:, :128], normals[:, 128:], empty], axis=0
        )
        moments += jnp.where(lane == slot, jnp.sum(weighted, axis=1, keepdims=True), 0.0)
        for a in range(3):
            dipole = jnp.sum(weighted * (facets[a : a + 1] - centres_s[a, b]), axis=1, keepdims=True)
            moments += jnp.where(lane == 32 * (a + 1) + slot, dipole, 0.0)
            centres += jnp.where((lane == slot) & (row == a), centres_s[a, b], 0.0)
        return moments, centres

    zeros = jnp.zeros((8, 128), f32)
    moments, centres = lax.fori_loop(0, boxes, one_box, (zeros, zeros), unroll=4)
    _, _, z = lattice(centres_s, 0)
    base_z = (z - (z & 1)).astype(f32) + 0.5
    centres = jnp.where((row == 3) | (row == 4), 1.5, jnp.where(row == 5, base_z, centres))
    half = lax.axis_index("rhs")
    away = pl.multiple_of((1 - half) * 256, 256)
    here = pl.multiple_of(half * 256, 256)
    pieces = jnp.concatenate([*thirds(moments), zeros], axis=0).astype(bf16)
    cross_ref[:512] = charges_v[...].astype(bf16)
    cross_ref[512:] = pieces
    second_ref[:256] = charges_v[pl.ds(here, 256), :].astype(bf16)
    second_ref[256:] = pieces
    first_ref[:256] = charges_v[pl.ds(away, 256), :].astype(bf16).astype(f32)
    for place in range(plane_boxes):
        first_ref[256 + 8 * place : 264 + 8 * place] = local_ref[pl.ds(away + 16 * place, 8), :]
    first_ref[384:392] = moments
    first_ref[392:] = centres
    local_ref[512:520] = moments
    local_ref[520:] = centres


def thirds(x):
    high = x.astype(bf16).astype(f32)
    rest = x - high
    middle = rest.astype(bf16).astype(f32)
    return high, middle, (rest - middle).astype(bf16).astype(f32)


def stacked_rows(parts, width):
    zeros = jnp.zeros((depth - 8 * len(parts), width), f32)
    return jnp.concatenate([*parts, zeros], axis=0)


def padded(rows):
    return jnp.concatenate([rows, jnp.zeros((8 - rows.shape[0], rows.shape[1]), f32)], axis=0)


def wide_charges(ref, place):
    both = ref[pl.ds(pl.multiple_of(place * 16, 16), 16), :].astype(f32)
    return jnp.concatenate([both[:8], both[8:]], axis=1)


def wide_tile(ref, start):
    tile = ref[pl.ds(pl.multiple_of(start, 8), 8), :]
    return jnp.concatenate([tile[0:3], tile[3:6]], axis=1)


def whole_moments(pieces):
    return pieces[:8] + (pieces[8:16] + pieces[16:24])


def store_geometry(local, box, geometry):
    row = lax.broadcasted_iota(jnp.int32, (8, per_box), 0)
    square = jnp.sum(local * local, axis=0, keepdims=True)
    features = jnp.where(row == 3, square, jnp.where(row == 4, 1.0, local))
    high, middle, low = thirds(features)
    rows = stacked_rows((high, high, high, middle, middle, low), per_box)
    geometry[pl.ds(pl.multiple_of(box * depth, depth), depth), :] = rows.astype(bf16)


def store_strengths(local, charges, box, strengths):
    products = jnp.concatenate([charges] + [charges * local[a : a + 1] for a in range(3)], axis=0)
    rows = jnp.concatenate(thirds(products), axis=0)
    strengths[pl.ds(pl.multiple_of(box * 96, 96), 96), :] = rows.astype(bf16)


def feature_kernel(local_ref, sent_ref, geometry, mine, targets, planes):
    boxes = 2 * plane_boxes
    half = lax.axis_index("rhs")
    origin = local_ref[523:526, 0:1]
    row = lax.broadcasted_iota(jnp.int32, (8, per_box), 0)

    def source(slot, _):
        local = padded(wide_tile(local_ref, slot * 16) - origin)
        store_geometry(local, slot, geometry)
        store_strengths(local, wide_charges(sent_ref, slot), slot, mine)
        return 0

    lax.fori_loop(0, boxes, source, 0, unroll=4)

    def target(place, _):
        start = (half * plane_boxes + place) * 16
        local = padded(wide_tile(local_ref, start) - origin)
        normal = padded(wide_tile(local_ref, start + 8))
        square = jnp.sum(local * local, axis=0, keepdims=True) + soften
        along = jnp.sum(local * normal, axis=0, keepdims=True)
        distance = jnp.where(row == 3, 1.0, jnp.where(row == 4, square, -2.0 * local))
        high, middle, low = thirds(distance)
        rows = stacked_rows((high, middle, low, high, middle, high), per_box)
        start = pl.multiple_of(place * per_box, per_box)
        targets[pl.ds(start, per_box), :] = jnp.transpose(rows).astype(bf16)
        planes[pl.ds(pl.multiple_of(place * 8, 8), 8), :] = jnp.where(row == 3, along, normal)
        return 0

    lax.fori_loop(0, plane_boxes, target, 0, unroll=4)


def near_planes(sources, targets, total, beside):
    def near_rows(item, _):
        target_y = (item + 1) // 3
        source_y = target_y + lax.rem(item + 1, 3) - 1
        runs = []
        for near_x in range(4):
            for source in sources:
                for x in range(max(near_x - 1, 0), min(near_x + 2, 4)):
                    runs.append((near_x, source, source_y * 4 + x))

        def rows_at(pair, place, number):
            ref, first = pair
            return ref[pl.ds(pl.multiple_of((first + place) * number, number), number), :]

        def distances(near_x, source, place):
            start = pl.multiple_of((target_y * 4 + near_x) * per_box, per_box)
            weights = rows_at(source[0], place, depth)
            return jnp.dot(targets[pl.ds(start, per_box), :], weights, preferred_element_type=f32)

        ahead = distances(*runs[0])
        cubed = []
        given = []
        empty = jnp.zeros((64, per_box), bf16)
        for i, (near_x, source, place) in enumerate(runs):
            here = ahead
            if i + 1 < len(runs):
                ahead = distances(*runs[i + 1])
            inverse = lax.rsqrt(here)
            cubed.append((inverse * inverse * inverse).astype(bf16))
            given.append(jnp.concatenate([rows_at(source[1], place, 96), rows_at(source[2], place, 96), empty], axis=0))
            if i + 1 == len(runs) or runs[i + 1][0] != near_x:
                rows_of = pl.ds(pl.multiple_of((target_y * 4 + near_x) * per_box, per_box), per_box)
                total[rows_of, :] += lax.dot_general(
                    jnp.concatenate(cubed, axis=1),
                    jnp.concatenate(given, axis=1),
                    (((1,), (1,)), ((), ())),
                    preferred_element_type=f32,
                )
                cubed = []
                given = []
        beside(item)
        return 0

    lax.fori_loop(0, 10, near_rows, 0)


def field_kernel(
    centres_s, local_ref, cross_ref, first_ref, second_ref, geometry, mine, targets, planes, mine_ref, theirs_ref,
    halo_geometry, halo_mine, theirs, total, far, far_centres, far_moments
):
    boxes = 2 * plane_boxes
    half = lax.axis_index("rhs")
    origin = local_ref[523:526, 0:1]

    def source(slot, _):
        local = wide_tile(local_ref, slot * 16) - origin
        store_strengths(local, wide_charges(cross_ref, slot), slot, theirs)
        return 0

    lax.fori_loop(0, boxes, source, 0, unroll=4)

    def halo_source(place, _):
        local = padded(wide_tile(first_ref, 256 + place * 8) - origin)
        store_geometry(local, place, halo_geometry)
        store_strengths(local, wide_charges(first_ref, place), place, halo_mine)
        store_strengths(local, wide_charges(second_ref, place), boxes + place, theirs)
        return 0

    lax.fori_loop(0, plane_boxes, halo_source, 0, unroll=4)
    total[...] = jnp.zeros_like(total)

    for group, (centres, ours, others) in enumerate(
        (
            (first_ref[392:400], first_ref[384:392], second_ref[256:288]),
            (local_ref[520:528], local_ref[512:520], cross_ref[512:544]),
        )
    ):
        columns = jnp.transpose(jnp.concatenate([centres[:3] - origin, centres[3:]], axis=0))[:32]
        for a in range(3):
            far_centres[(group * 3 + a) * 32 : (group * 3 + a + 1) * 32, :] = jnp.broadcast_to(
                columns[:, a : a + 1], (32, 128)
            )
        both = jnp.concatenate([ours, whole_moments(others.astype(f32))], axis=0)
        high = both.astype(bf16).astype(f32)
        far_moments[group * 32 : group * 32 + 32, :] = jnp.concatenate([high, both - high], axis=0)
    lane = lax.broadcasted_iota(jnp.int32, (1, 128), 1)
    lane_x = lane & 3
    lane_y = (lane >> 2) & 3
    lane_plane = (lane >> 4) & 1

    def far_field(k):
        group = (k >= boxes).astype(jnp.int32)
        slot = jnp.where(k < boxes, k, half * plane_boxes + k - boxes)
        x, y, plane = slot & 3, (slot >> 2) & 3, slot >> 4
        local = wide_tile(local_ref, slot * 16) - origin
        normal = wide_tile(local_ref, slot * 16 + 8)
        d = []
        for a in range(3):
            centre = far_centres[pl.ds(pl.multiple_of((group * 3 + a) * 32, 32), 32), :]
            d.append(local[a : a + 1] - jnp.concatenate([centre, centre], axis=1))
        q = d[0] * d[0] + d[1] * d[1] + d[2] * d[2] + soften
        inverse = lax.rsqrt(q)
        inverse_2 = inverse * inverse
        inverse_3 = inverse_2 * inverse
        t = d[0] * normal[0:1] + d[1] * normal[1:2] + d[2] * normal[2:3]
        single = t * inverse_3
        steep = 3.0 * single * inverse_2
        coefficients = [single] + [steep * d[a] - normal[a : a + 1] * inverse_3 for a in range(3)]
        whole = jnp.concatenate(coefficients, axis=0)
        upper = whole.astype(bf16)
        lower = (whole - upper.astype(f32)).astype(bf16)
        lane_z = lane_plane + jnp.where(group == 0, 4 * half - 2, 0)
        near = (jnp.abs(lane_x - x) <= 1) & (jnp.abs(lane_y - y) <= 1) & (jnp.abs(lane_z - plane) <= 1)
        picked = jnp.where(near, 0.0, far_moments[pl.ds(pl.multiple_of(group * 32, 32), 32), :]).astype(bf16)
        first = jnp.dot(picked, upper, preferred_element_type=f32)
        second = jnp.dot(picked, lower, preferred_element_type=f32)
        return first[:16] + first[16:] + second[:16]

    def far_boxes(item):
        for i in range(5):
            k = jnp.minimum(item * 5 + i, 3 * plane_boxes - 1)
            far[pl.ds(pl.multiple_of(k * 16, 16), 16), :] = far_field(k)

    sources = [((geometry, p), (mine, p), (theirs, p)) for p in (0, plane_boxes)]
    sources.append(((halo_geometry, 0), (halo_mine, 0), (theirs, boxes)))
    near_planes(sources, targets, total, far_boxes)

    def near_field(place, _):
        turned = jnp.transpose(total[pl.ds(pl.multiple_of(place * per_box, per_box), per_box), :])
        side = planes[pl.ds(pl.multiple_of(place * 8, 8), 8), :]
        values = []
        for start in (0, 96):
            sums = turned[start : start + 32] + (turned[start + 32 : start + 64] + turned[start + 64 : start + 96])
            value = side[3:4] * sums[:8] - side[0:1] * sums[8:16]
            values.append(value - side[1:2] * sums[16:24] - side[2:3] * sums[24:32])
        value = jnp.concatenate(values, axis=0)
        slot = half * plane_boxes + place
        rows = pl.ds(pl.multiple_of(slot * 16, 16), 16)
        far[rows, :] += value + far[pl.ds(pl.multiple_of((boxes + place) * 16, 16), 16), :]
        return 0

    lax.fori_loop(0, plane_boxes, near_field, 0, unroll=4)

    def given_back(b, _):
        start = pl.multiple_of(slot_of(centres_s, b) * 16, 16)
        rows = pl.ds(pl.multiple_of(b * 8, 8), 8)
        mine_ref[rows, :] = far[pl.ds(start, 8), :]
        theirs_ref[rows, :] = far[pl.ds(start + 8, 8), :]
        return 0

    lax.fori_loop(0, boxes, given_back, 0, unroll=4)


def gram_kernel(counts_s, basis_ref, sums_ref, live_ref):
    krylov = basis_ref.shape[0]
    pairs = [(m, n) for m in range(krylov) for n in range(m + 1)]

    def one_box(b, carry):
        lanes = pl.ds(pl.multiple_of(b * per_box, per_box), per_box)
        live = live_row(counts_s, b)
        live_ref[pl.ds(2 * b, 1), :] = live[:, :128]
        live_ref[pl.ds(2 * b + 1, 1), :] = live[:, 128:]
        rows = [basis_ref[m, :, lanes] * live for m in range(krylov)]
        out = []
        for k, (m, n) in enumerate(pairs):
            product = rows[m] * rows[n]
            out.append(carry[k] + product[:, :128] + product[:, 128:])
        return tuple(out)

    zeros = jnp.zeros((8, 128), f32)
    gram = lax.fori_loop(0, counts_s.shape[0], one_box, (zeros,) * len(pairs))
    lane = lax.broadcasted_iota(jnp.int32, (8, 128), 1)
    total = zeros
    for k, value in enumerate(gram):
        total = jnp.where(lane == krylov + 1 + k, jnp.sum(value, axis=1, keepdims=True), total)
    sums_ref[...] = total


def image_kernel(mine_ref, theirs_ref, gram_ref, live_ref, contrast_ref, basis_ref, image_ref, sums_ref):
    krylov = basis_ref.shape[0]

    def one_box(b, carry):
        lanes = pl.ds(pl.multiple_of(b * per_box, per_box), per_box)
        rows = pl.ds(pl.multiple_of(b * 8, 8), 8)
        live = wide_row(live_ref, b)
        part = mine_ref[rows, :] + theirs_ref[rows, :]
        image = live * (basis_ref[krylov - 1, :, lanes] - 2.0 * wide_row(contrast_ref, b) * part)
        image_ref[:, lanes] = image
        sums = []
        for m in range(krylov + 1):
            product = image * (basis_ref[m, :, lanes] if m < krylov else image)
            sums.append(carry[m] + product[:, :128] + product[:, 128:])
        return tuple(sums)

    zeros = jnp.zeros((8, 128), f32)
    sums = lax.fori_loop(0, live_ref.shape[0] // 2, one_box, (zeros,) * (krylov + 1), unroll=4)
    lane = lax.broadcasted_iota(jnp.int32, (8, 128), 1)
    total = gram_ref[...]
    for k, value in enumerate(sums):
        total = jnp.where(lane == k, jnp.sum(value, axis=1, keepdims=True), total)
    sums_ref[...] = jnp.broadcast_to(total[None], sums_ref.shape)


def two_sum(a, b):
    s = a + b
    c = s - a
    return s, (a - (s - c)) + (b - c)


def halves(a):
    c = a * 4097.0
    high = c - (c - a)
    return high, a - high


def two_product(a, b):
    p = a * b
    a_high, a_low = halves(a)
    b_high, b_low = halves(b)
    return p, ((a_high * b_high - p) + a_high * b_low + a_low * b_high) + a_low * b_low


def finish_kernel(total_facets, tiles_ref, live_ref, image_ref, basis_ref, next_ref, hessenberg_ref):
    boxes = live_ref.shape[0] // 2
    krylov = basis_ref.shape[0]
    lane = lax.broadcasted_iota(jnp.int32, (8, 128), 1)

    sums, rest = tiles_ref[0], jnp.zeros((8, 128), f32)
    for i in range(1, tiles_ref.shape[0]):
        sums, error = two_sum(sums, tiles_ref[i])
        rest = rest + error
    exact = sums + rest
    projections = [exact[:, m : m + 1] / total_facets for m in range(krylov)]
    pairs = [(m, n) for m in range(krylov) for n in range(m + 1)]
    first = jnp.where(lane == krylov, 1.0, 0.0)
    second = jnp.where(lane <= krylov, 1.0, 0.0)
    for m in range(krylov):
        first = jnp.where(lane == m, -2.0 * projections[m], first)
    for k, (m, n) in enumerate(pairs):
        at = lane == krylov + 1 + k
        scale = 1.0 if m == n else 2.0
        first = jnp.where(at, scale * projections[m], first)
        second = jnp.where(at, projections[n], second)
    factor, factor_rest = two_product(first, second)
    value, value_rest = two_product(factor, sums)
    value_rest = value_rest + (factor * rest + factor_rest * sums)
    for shift in (64, 32, 16, 8, 4, 2, 1):
        other = pltpu.roll(value, shift, 1)
        other_rest = pltpu.roll(value_rest, shift, 1)
        value, error = two_sum(value, other)
        value_rest = (value_rest + other_rest) + error
    remaining = jnp.maximum(value + value_rest, 0.0)
    norm = jnp.sqrt(remaining / total_facets + epsilon)
    heads = jnp.where(lane == krylov, norm, 0.0)
    for m in range(krylov):
        heads = jnp.where(lane == m, projections[m], heads)
    hessenberg_ref[...] = heads[:, : krylov + 1]
    wide = [jnp.broadcast_to(p, (8, per_box)) for p in projections]
    scale = jnp.concatenate([1.0 / norm] * (per_box // 128), axis=1)

    def one_box(b, _):
        lanes = pl.ds(pl.multiple_of(b * per_box, per_box), per_box)
        live = wide_row(live_ref, b)
        sent = wide[0] * basis_ref[0, :, lanes]
        for m in range(1, krylov):
            sent += wide[m] * basis_ref[m, :, lanes]
        next_ref[:, lanes] = (image_ref[:, lanes] - sent * live) * scale
        return 0

    lax.fori_loop(0, boxes, one_box, 0, unroll=4)


smem = pl.BlockSpec(memory_space=pltpu.SMEM)
vmem = pl.BlockSpec(memory_space=pltpu.VMEM)


def on_device(
    basis, facet_centres, normals, areas, contrast, facet_counts, box_centres, near_boxes, far_boxes
):
    krylov, rhs_local, facet_local = basis.shape
    boxes = facet_counts.shape[0]
    count = lax.axis_size("box")
    total_facets = count * facet_local
    areas = areas.reshape(-1, 128)
    contrast = contrast.reshape(-1, 128)

    def rows(number, width=128, dtype=f32):
        return jax.ShapeDtypeStruct((number, width), dtype)

    def limit(mebibytes):
        return pltpu.CompilerParams(vmem_limit_bytes=mebibytes * 1024 * 1024)

    sent, first, second, local = pl.pallas_call(
        prep_kernel,
        out_shape=(rows(544, dtype=bf16), rows(400), rows(288, dtype=bf16), rows(528)),
        in_specs=[pl.BlockSpec(memory_space=pl.ANY)] * 6,
        out_specs=(vmem,) * 4,
        scratch_shapes=[
            pltpu.VMEM((512, 128), f32),
            pltpu.SMEM(box_centres.shape, f32),
            pltpu.SMEM(facet_counts.shape, jnp.int32),
            pltpu.VMEM((rhs_local, facet_local), f32),
            pltpu.VMEM(facet_centres.shape, f32),
            pltpu.VMEM(areas.shape, f32),
            pltpu.VMEM(normals.shape, f32),
            pltpu.SemaphoreType.DMA((6,)),
        ],
        name="prepare",
    )(box_centres, facet_counts, basis, facet_centres, areas, normals)
    swap = [(0, 1), (1, 0)]
    ups = range(count - 1)
    cross = lax.ppermute(sent, "rhs", swap)
    first = lax.ppermute(
        first, ("box", "rhs"), [(2 * i, 2 * i + 2) for i in ups] + [(2 * i + 3, 2 * i + 1) for i in ups]
    )
    second = lax.ppermute(
        second, ("box", "rhs"), [(2 * i + 1, 2 * i + 2) for i in ups] + [(2 * i + 2, 2 * i + 1) for i in ups]
    )
    plane_slots = plane_boxes * per_box
    geometry, strengths, targets, planes = pl.pallas_call(
        feature_kernel,
        out_shape=(
            rows(boxes * depth, per_box, bf16),
            rows(boxes * 96, per_box, bf16),
            rows(plane_slots, depth, bf16),
            rows(plane_boxes * 8, per_box),
        ),
        in_specs=[vmem] * 2,
        out_specs=(vmem,) * 4,
        compiler_params=limit(12),
        name="features",
    )(local, sent)
    mine, theirs = pl.pallas_call(
        field_kernel,
        out_shape=(rows(boxes * 8, per_box),) * 2,
        in_specs=[smem] + [vmem] * 8,
        out_specs=(vmem, vmem),
        scratch_shapes=[
            pltpu.VMEM((plane_boxes * depth, per_box), bf16),
            pltpu.VMEM((plane_boxes * 96, per_box), bf16),
            pltpu.VMEM((3 * plane_boxes * 96, per_box), bf16),
            pltpu.VMEM((plane_slots, 256), f32),
            pltpu.VMEM((3 * plane_boxes * 16, per_box), f32),
            pltpu.VMEM((6 * 32, 128), f32),
            pltpu.VMEM((2 * 32, 128), f32),
        ],
        compiler_params=limit(32),
        name="fields",
    )(box_centres, local, cross, first, second, geometry, strengths, targets, planes)
    theirs = lax.ppermute(theirs, "rhs", swap)
    gram, live = pl.pallas_call(
        gram_kernel,
        out_shape=(rows(8), rows(2 * boxes)),
        in_specs=[smem, vmem],
        out_specs=(vmem, vmem),
        compiler_params=limit(8),
        name="gram",
    )(facet_counts, basis)
    image, tiles = pl.pallas_call(
        image_kernel,
        out_shape=(rows(rhs_local, facet_local), jax.ShapeDtypeStruct((count, 8, 128), f32)),
        in_specs=[vmem] * 6,
        out_specs=(vmem, vmem),
        compiler_params=limit(8),
        name="image",
    )(mine, theirs, gram, live, contrast, basis)
    tiles = lax.all_to_all(tiles, "box", 0, 0, tiled=True)
    next_vector, hessenberg = pl.pallas_call(
        functools.partial(finish_kernel, total_facets),
        out_shape=(rows(rhs_local, facet_local), rows(rhs_local, krylov + 1)),
        in_specs=[vmem] * 4,
        out_specs=(vmem, vmem),
        compiler_params=limit(16),
        name="finish",
    )(tiles, live, image, basis)
    return next_vector, hessenberg.T


def solution(mesh):
    return jax.shard_map(
        on_device,
        mesh=mesh,
        in_specs=(
            P(None, "rhs", "box"),
            P(None, "box"),
            P(None, "box"),
            P("box"),
            P("box"),
            P("box"),
            P(None, "box"),
            P("box", None),
            P("box", None),
        ),
        out_specs=(P("rhs", "box"), P(None, "rhs")),
        check_vma=False,
    )
```

```python
import functools

import jax
import jax.numpy as jnp
from jax import lax
from jax.experimental import pallas as pl
from jax.experimental.pallas import tpu as pltpu
from jax.sharding import PartitionSpec as P

soften = 0.0025
epsilon = 1e-06
f32 = jnp.float32
bf16 = jnp.bfloat16
plane_boxes = 16
per_box = 256
depth = 128


def lattice(centres_s, b):
    x = (centres_s[0, b] + 0.5).astype(jnp.int32)
    y = (centres_s[1, b] + 0.5).astype(jnp.int32)
    z = (centres_s[2, b] + 0.5).astype(jnp.int32)
    return x, y, z


def slot_of(centres_s, b):
    x, y, z = lattice(centres_s, b)
    return (z & 1) * plane_boxes + y * 4 + x


def wide_row(ref, b):
    return jnp.concatenate([ref[pl.ds(2 * b, 1), :], ref[pl.ds(2 * b + 1, 1), :]], axis=1)


def live_row(counts_s, b):
    slots = lax.broadcasted_iota(jnp.int32, (1, per_box), 1)
    return (slots < counts_s[b]).astype(f32)


def prep_kernel(
    centres_h, counts_h, basis_h, facets_h, areas_h, normals_h, cross_ref, first_ref, second_ref, local_ref,
    charges_v, centres_s, counts_s, current_ref, facets_ref, areas_ref, normals_ref, arrived
):
    boxes = counts_s.shape[0]
    moves = [
        (basis_h.at[basis_h.shape[0] - 1], current_ref),
        (facets_h, facets_ref),
        (areas_h, areas_ref),
        (normals_h, normals_ref),
        (centres_h, centres_s),
        (counts_h, counts_s),
    ]
    copies = [pltpu.make_async_copy(a, b, arrived.at[k]) for k, (a, b) in enumerate(moves)]
    for copy in copies:
        copy.start()
    for copy in copies:
        copy.wait()
    lane = lax.broadcasted_iota(jnp.int32, (8, 128), 1)
    row = lax.broadcasted_iota(jnp.int32, (8, 128), 0)
    empty = jnp.zeros((2, 128), f32)

    def one_box(b, carry):
        moments, centres = carry
        slot = slot_of(centres_s, b)
        lanes = pl.ds(pl.multiple_of(b * per_box, per_box), per_box)
        facets = facets_ref[:, lanes]
        normals = normals_ref[:, lanes]
        live = live_row(counts_s, b)
        weighted = current_ref[:, lanes] * (wide_row(areas_ref, b) * live / per_box)
        start = pl.multiple_of(slot * 16, 16)
        charges_v[pl.ds(start, 16), :] = jnp.concatenate([weighted[:, :128], weighted[:, 128:]], axis=0)
        local_ref[pl.ds(start, 16), :] = jnp.concatenate(
            [facets[:, :128], facets[:, 128:], empty, normals[:, :128], normals[:, 128:], empty], axis=0
        )
        moments += jnp.where(lane == slot, jnp.sum(weighted, axis=1, keepdims=True), 0.0)
        for a in range(3):
            dipole = jnp.sum(weighted * (facets[a : a + 1] - centres_s[a, b]), axis=1, keepdims=True)
            moments += jnp.where(lane == 32 * (a + 1) + slot, dipole, 0.0)
            centres += jnp.where((lane == slot) & (row == a), centres_s[a, b], 0.0)
        return moments, centres

    zeros = jnp.zeros((8, 128), f32)
    moments, centres = lax.fori_loop(0, boxes, one_box, (zeros, zeros), unroll=4)
    _, _, z = lattice(centres_s, 0)
    base_z = (z - (z & 1)).astype(f32) + 0.5
    centres = jnp.where((row == 3) | (row == 4), 1.5, jnp.where(row == 5, base_z, centres))
    half = lax.axis_index("rhs")
    away = pl.multiple_of((1 - half) * 256, 256)
    here = pl.multiple_of(half * 256, 256)
    pieces = jnp.concatenate([*thirds(moments), zeros], axis=0).astype(bf16)
    cross_ref[:512] = charges_v[...].astype(bf16)
    cross_ref[512:] = pieces
    second_ref[:256] = charges_v[pl.ds(here, 256), :].astype(bf16)
    second_ref[256:] = pieces
    first_ref[:256] = charges_v[pl.ds(away, 256), :].astype(bf16).astype(f32)
    for place in range(plane_boxes):
        first_ref[256 + 8 * place : 264 + 8 * place] = local_ref[pl.ds(away + 16 * place, 8), :]
    first_ref[384:392] = moments
    first_ref[392:] = centres
    local_ref[512:520] = moments
    local_ref[520:] = centres


def thirds(x):
    high = x.astype(bf16).astype(f32)
    rest = x - high
    middle = rest.astype(bf16).astype(f32)
    return high, middle, (rest - middle).astype(bf16).astype(f32)


def stacked_rows(parts, width):
    zeros = jnp.zeros((depth - 8 * len(parts), width), f32)
    return jnp.concatenate([*parts, zeros], axis=0)


def padded(rows):
    return jnp.concatenate([rows, jnp.zeros((8 - rows.shape[0], rows.shape[1]), f32)], axis=0)


def wide_charges(ref, place):
    both = ref[pl.ds(pl.multiple_of(place * 16, 16), 16), :].astype(f32)
    return jnp.concatenate([both[:8], both[8:]], axis=1)


def wide_tile(ref, start):
    tile = ref[pl.ds(pl.multiple_of(start, 8), 8), :]
    return jnp.concatenate([tile[0:3], tile[3:6]], axis=1)


def whole_moments(pieces):
    return pieces[:8] + (pieces[8:16] + pieces[16:24])


def store_geometry(local, box, geometry):
    row = lax.broadcasted_iota(jnp.int32, (8, per_box), 0)
    square = jnp.sum(local * local, axis=0, keepdims=True)
    features = jnp.where(row == 3, square, jnp.where(row == 4, 1.0, local))
    high, middle, low = thirds(features)
    rows = stacked_rows((high, high, high, middle, middle, low), per_box)
    geometry[pl.ds(pl.multiple_of(box * depth, depth), depth), :] = rows.astype(bf16)


def store_strengths(local, charges, box, strengths):
    products = jnp.concatenate([charges * local[a : a + 1] for a in range(3)], axis=0)
    rows = jnp.concatenate([charges, *thirds(products)], axis=0)
    strengths[pl.ds(pl.multiple_of(box * 80, 80), 80), :] = rows.astype(bf16)


def feature_kernel(local_ref, sent_ref, geometry, mine, targets, planes, local_out):
    boxes = 2 * plane_boxes
    half = lax.axis_index("rhs")
    origin = local_ref[523:526, 0:1]
    row = lax.broadcasted_iota(jnp.int32, (8, per_box), 0)

    def source(slot, _):
        local = padded(wide_tile(local_ref, slot * 16) - origin)
        store_geometry(local, slot, geometry)
        store_strengths(local, wide_charges(sent_ref, slot), slot, mine)
        return 0

    lax.fori_loop(0, boxes, source, 0, unroll=4)

    def target(place, _):
        start = (half * plane_boxes + place) * 16
        local = padded(wide_tile(local_ref, start) - origin)
        normal = padded(wide_tile(local_ref, start + 8))
        square = jnp.sum(local * local, axis=0, keepdims=True) + soften
        along = jnp.sum(local * normal, axis=0, keepdims=True)
        distance = jnp.where(row == 3, 1.0, jnp.where(row == 4, square, -2.0 * local))
        high, middle, low = thirds(distance)
        rows = stacked_rows((high, middle, low, high, middle, high), per_box)
        start = pl.multiple_of(place * per_box, per_box)
        targets[pl.ds(start, per_box), :] = jnp.transpose(rows).astype(bf16)
        planes[pl.ds(pl.multiple_of(place * 8, 8), 8), :] = jnp.where(row == 3, along, normal)
        return 0

    lax.fori_loop(0, plane_boxes, target, 0, unroll=4)
    local_out[...] = local_ref[...]


def near_planes(sources, targets, total, beside):
    def near_rows(item, _):
        target_y = (item + 1) // 3
        source_y = target_y + lax.rem(item + 1, 3) - 1
        runs = []
        for near_x in range(4):
            for source in sources:
                for x in range(max(near_x - 1, 0), min(near_x + 2, 4)):
                    runs.append((near_x, source, source_y * 4 + x))

        def rows_at(pair, place, number):
            ref, first = pair
            return ref[pl.ds(pl.multiple_of((first + place) * number, number), number), :]

        def distances(near_x, source, place):
            start = pl.multiple_of((target_y * 4 + near_x) * per_box, per_box)
            weights = rows_at(source[0], place, depth)
            return jnp.dot(targets[pl.ds(start, per_box), :], weights, preferred_element_type=f32)

        ahead = distances(*runs[0])
        cubed = []
        given = []
        for i, (near_x, source, place) in enumerate(runs):
            here = ahead
            if i + 1 < len(runs):
                ahead = distances(*runs[i + 1])
            inverse = lax.rsqrt(here)
            cubed.append((inverse * inverse * inverse).astype(bf16))
            given.append(jnp.concatenate([rows_at(source[1], place, 80), rows_at(source[2], place, 80)], axis=0))
            if i + 1 == len(runs) or runs[i + 1][0] != near_x:
                rows_of = pl.ds(pl.multiple_of((target_y * 4 + near_x) * 160, 160), 160)
                total[rows_of, :] += lax.dot_general(
                    jnp.concatenate(given, axis=1),
                    jnp.concatenate(cubed, axis=1),
                    (((1,), (1,)), ((), ())),
                    preferred_element_type=f32,
                )
                cubed = []
                given = []
        beside(item)
        return 0

    lax.fori_loop(0, 10, near_rows, 0)


def field_kernel(
    centres_s, local_ref, cross_ref, first_ref, second_ref, geometry, mine, targets, planes, mine_ref, theirs_ref,
    halo_geometry, halo_mine, theirs, total, far, far_centres, far_moments
):
    boxes = 2 * plane_boxes
    half = lax.axis_index("rhs")
    origin = local_ref[523:526, 0:1]

    def source(slot, _):
        local = wide_tile(local_ref, slot * 16) - origin
        store_strengths(local, wide_charges(cross_ref, slot), slot, theirs)
        return 0

    lax.fori_loop(0, boxes, source, 0, unroll=4)

    def halo_source(place, _):
        local = padded(wide_tile(first_ref, 256 + place * 8) - origin)
        store_geometry(local, place, halo_geometry)
        store_strengths(local, wide_charges(first_ref, place), place, halo_mine)
        store_strengths(local, wide_charges(second_ref, place), boxes + place, theirs)
        return 0

    lax.fori_loop(0, plane_boxes, halo_source, 0, unroll=4)
    total[...] = jnp.zeros_like(total)

    for group, (centres, ours, others) in enumerate(
        (
            (first_ref[392:400], first_ref[384:392], second_ref[256:288]),
            (local_ref[520:528], local_ref[512:520], cross_ref[512:544]),
        )
    ):
        columns = jnp.transpose(jnp.concatenate([centres[:3] - origin, centres[3:]], axis=0))[:32]
        for a in range(3):
            far_centres[(group * 3 + a) * 32 : (group * 3 + a + 1) * 32, :] = jnp.broadcast_to(
                columns[:, a : a + 1], (32, 128)
            )
        both = jnp.concatenate([ours, whole_moments(others.astype(f32))], axis=0)
        high = both.astype(bf16).astype(f32)
        far_moments[group * 32 : group * 32 + 32, :] = jnp.concatenate([high, both - high], axis=0)
    lane = lax.broadcasted_iota(jnp.int32, (1, 128), 1)
    lane_x = lane & 3
    lane_y = (lane >> 2) & 3
    lane_plane = (lane >> 4) & 1

    def far_field(k):
        group = (k >= boxes).astype(jnp.int32)
        slot = jnp.where(k < boxes, k, half * plane_boxes + k - boxes)
        x, y, plane = slot & 3, (slot >> 2) & 3, slot >> 4
        local = wide_tile(local_ref, slot * 16) - origin
        normal = wide_tile(local_ref, slot * 16 + 8)
        d = []
        for a in range(3):
            centre = far_centres[pl.ds(pl.multiple_of((group * 3 + a) * 32, 32), 32), :]
            d.append(local[a : a + 1] - jnp.concatenate([centre, centre], axis=1))
        q = d[0] * d[0] + d[1] * d[1] + d[2] * d[2] + soften
        inverse = lax.rsqrt(q)
        inverse_2 = inverse * inverse
        inverse_3 = inverse_2 * inverse
        t = d[0] * normal[0:1] + d[1] * normal[1:2] + d[2] * normal[2:3]
        single = t * inverse_3
        steep = 3.0 * single * inverse_2
        coefficients = [single] + [steep * d[a] - normal[a : a + 1] * inverse_3 for a in range(3)]
        whole = jnp.concatenate(coefficients, axis=0)
        upper = whole.astype(bf16)
        lower = (whole - upper.astype(f32)).astype(bf16)
        lane_z = lane_plane + jnp.where(group == 0, 4 * half - 2, 0)
        near = (jnp.abs(lane_x - x) <= 1) & (jnp.abs(lane_y - y) <= 1) & (jnp.abs(lane_z - plane) <= 1)
        picked = jnp.where(near, 0.0, far_moments[pl.ds(pl.multiple_of(group * 32, 32), 32), :]).astype(bf16)
        first = jnp.dot(picked, upper, preferred_element_type=f32)
        second = jnp.dot(picked, lower, preferred_element_type=f32)
        return first[:16] + first[16:] + second[:16]

    def far_boxes(item):
        for i in range(5):
            k = jnp.minimum(item * 5 + i, 3 * plane_boxes - 1)
            far[pl.ds(pl.multiple_of(k * 16, 16), 16), :] = far_field(k)

    sources = [((geometry, p), (mine, p), (theirs, p)) for p in (0, plane_boxes)]
    sources.append(((halo_geometry, 0), (halo_mine, 0), (theirs, boxes)))
    near_planes(sources, targets, total, far_boxes)

    def near_field(place, _):
        sums = total[pl.ds(pl.multiple_of(place * 160, 160), 160), :]
        side = planes[pl.ds(pl.multiple_of(place * 8, 8), 8), :]
        values = []
        for start in (0, 80):
            value = side[3:4] * sums[start : start + 8]
            for a in range(3):
                high, middle, low = (sums[i : i + 8] for i in range(start + 8 + 8 * a, start + 80, 24))
                value = value - side[a : a + 1] * (high + (middle + low))
            values.append(value)
        value = jnp.concatenate(values, axis=0)
        slot = half * plane_boxes + place
        rows = pl.ds(pl.multiple_of(slot * 16, 16), 16)
        far[rows, :] += value + far[pl.ds(pl.multiple_of((boxes + place) * 16, 16), 16), :]
        return 0

    lax.fori_loop(0, plane_boxes, near_field, 0, unroll=4)

    def given_back(b, _):
        start = pl.multiple_of(slot_of(centres_s, b) * 16, 16)
        rows = pl.ds(pl.multiple_of(b * 8, 8), 8)
        mine_ref[rows, :] = far[pl.ds(start, 8), :]
        theirs_ref[rows, :] = far[pl.ds(start + 8, 8), :]
        return 0

    lax.fori_loop(0, boxes, given_back, 0, unroll=4)


def gram_kernel(counts_s, basis_ref, sums_ref, live_ref):
    krylov = basis_ref.shape[0]
    pairs = [(m, n) for m in range(krylov) for n in range(m + 1)]

    def one_box(b, carry):
        lanes = pl.ds(pl.multiple_of(b * per_box, per_box), per_box)
        live = live_row(counts_s, b)
        live_ref[pl.ds(2 * b, 1), :] = live[:, :128]
        live_ref[pl.ds(2 * b + 1, 1), :] = live[:, 128:]
        rows = [basis_ref[m, :, lanes] * live for m in range(krylov)]
        out = []
        for k, (m, n) in enumerate(pairs):
            product = rows[m] * rows[n]
            out.append(carry[k] + product[:, :128] + product[:, 128:])
        return tuple(out)

    zeros = jnp.zeros((8, 128), f32)
    gram = lax.fori_loop(0, counts_s.shape[0], one_box, (zeros,) * len(pairs))
    lane = lax.broadcasted_iota(jnp.int32, (8, 128), 1)
    total = zeros
    for k, value in enumerate(gram):
        total = jnp.where(lane == krylov + 1 + k, jnp.sum(value, axis=1, keepdims=True), total)
    sums_ref[...] = total


def image_kernel(mine_ref, theirs_ref, gram_ref, live_ref, contrast_ref, basis_ref, image_ref, sums_ref):
    krylov = basis_ref.shape[0]

    def one_box(b, carry):
        lanes = pl.ds(pl.multiple_of(b * per_box, per_box), per_box)
        rows = pl.ds(pl.multiple_of(b * 8, 8), 8)
        live = wide_row(live_ref, b)
        part = mine_ref[rows, :] + theirs_ref[rows, :]
        image = live * (basis_ref[krylov - 1, :, lanes] - 2.0 * wide_row(contrast_ref, b) * part)
        image_ref[:, lanes] = image
        sums = []
        for m in range(krylov + 1):
            product = image * (basis_ref[m, :, lanes] if m < krylov else image)
            sums.append(carry[m] + product[:, :128] + product[:, 128:])
        return tuple(sums)

    zeros = jnp.zeros((8, 128), f32)
    sums = lax.fori_loop(0, live_ref.shape[0] // 2, one_box, (zeros,) * (krylov + 1), unroll=4)
    lane = lax.broadcasted_iota(jnp.int32, (8, 128), 1)
    total = gram_ref[...]
    for k, value in enumerate(sums):
        total = jnp.where(lane == k, jnp.sum(value, axis=1, keepdims=True), total)
    sums_ref[...] = jnp.broadcast_to(total[None], sums_ref.shape)


def two_sum(a, b):
    s = a + b
    c = s - a
    return s, (a - (s - c)) + (b - c)


def halves(a):
    c = a * 4097.0
    high = c - (c - a)
    return high, a - high


def two_product(a, b):
    p = a * b
    a_high, a_low = halves(a)
    b_high, b_low = halves(b)
    return p, ((a_high * b_high - p) + a_high * b_low + a_low * b_high) + a_low * b_low


def finish_kernel(total_facets, tiles_ref, live_ref, image_ref, basis_ref, next_ref, hessenberg_ref):
    boxes = live_ref.shape[0] // 2
    krylov = basis_ref.shape[0]
    lane = lax.broadcasted_iota(jnp.int32, (8, 128), 1)

    sums, rest = tiles_ref[0], jnp.zeros((8, 128), f32)
    for i in range(1, tiles_ref.shape[0]):
        sums, error = two_sum(sums, tiles_ref[i])
        rest = rest + error
    exact = sums + rest
    projections = [exact[:, m : m + 1] / total_facets for m in range(krylov)]
    pairs = [(m, n) for m in range(krylov) for n in range(m + 1)]
    first = jnp.where(lane == krylov, 1.0, 0.0)
    second = jnp.where(lane <= krylov, 1.0, 0.0)
    for m in range(krylov):
        first = jnp.where(lane == m, -2.0 * projections[m], first)
    for k, (m, n) in enumerate(pairs):
        at = lane == krylov + 1 + k
        scale = 1.0 if m == n else 2.0
        first = jnp.where(at, scale * projections[m], first)
        second = jnp.where(at, projections[n], second)
    factor, factor_rest = two_product(first, second)
    value, value_rest = two_product(factor, sums)
    value_rest = value_rest + (factor * rest + factor_rest * sums)
    for shift in (64, 32, 16, 8, 4, 2, 1):
        other = pltpu.roll(value, shift, 1)
        other_rest = pltpu.roll(value_rest, shift, 1)
        value, error = two_sum(value, other)
        value_rest = (value_rest + other_rest) + error
    remaining = jnp.maximum(value + value_rest, 0.0)
    norm = jnp.sqrt(remaining / total_facets + epsilon)
    heads = jnp.where(lane == krylov, norm, 0.0)
    for m in range(krylov):
        heads = jnp.where(lane == m, projections[m], heads)
    hessenberg_ref[...] = heads[:, : krylov + 1]
    wide = [jnp.broadcast_to(p, (8, per_box)) for p in projections]
    scale = jnp.concatenate([1.0 / norm] * (per_box // 128), axis=1)

    def one_box(b, _):
        lanes = pl.ds(pl.multiple_of(b * per_box, per_box), per_box)
        live = wide_row(live_ref, b)
        sent = wide[0] * basis_ref[0, :, lanes]
        for m in range(1, krylov):
            sent += wide[m] * basis_ref[m, :, lanes]
        next_ref[:, lanes] = (image_ref[:, lanes] - sent * live) * scale
        return 0

    lax.fori_loop(0, boxes, one_box, 0, unroll=4)


smem = pl.BlockSpec(memory_space=pltpu.SMEM)
vmem = pl.BlockSpec(memory_space=pltpu.VMEM)


def on_device(
    basis, facet_centres, normals, areas, contrast, facet_counts, box_centres, near_boxes, far_boxes
):
    krylov, rhs_local, facet_local = basis.shape
    boxes = facet_counts.shape[0]
    count = lax.axis_size("box")
    total_facets = count * facet_local
    areas = areas.reshape(-1, 128)
    contrast = contrast.reshape(-1, 128)

    def rows(number, width=128, dtype=f32):
        return jax.ShapeDtypeStruct((number, width), dtype)

    def limit(mebibytes):
        return pltpu.CompilerParams(vmem_limit_bytes=mebibytes * 1024 * 1024)

    sent, first, second, local = pl.pallas_call(
        prep_kernel,
        out_shape=(rows(544, dtype=bf16), rows(400), rows(288, dtype=bf16), rows(528)),
        in_specs=[pl.BlockSpec(memory_space=pl.ANY)] * 6,
        out_specs=(vmem,) * 4,
        scratch_shapes=[
            pltpu.VMEM((512, 128), f32),
            pltpu.SMEM(box_centres.shape, f32),
            pltpu.SMEM(facet_counts.shape, jnp.int32),
            pltpu.VMEM((rhs_local, facet_local), f32),
            pltpu.VMEM(facet_centres.shape, f32),
            pltpu.VMEM(areas.shape, f32),
            pltpu.VMEM(normals.shape, f32),
            pltpu.SemaphoreType.DMA((6,)),
        ],
        name="prepare",
    )(box_centres, facet_counts, basis, facet_centres, areas, normals)
    swap = [(0, 1), (1, 0)]
    ups = range(count - 1)
    cross = lax.ppermute(sent, "rhs", swap)
    first = lax.ppermute(
        first, ("box", "rhs"), [(2 * i, 2 * i + 2) for i in ups] + [(2 * i + 3, 2 * i + 1) for i in ups]
    )
    second = lax.ppermute(
        second, ("box", "rhs"), [(2 * i + 1, 2 * i + 2) for i in ups] + [(2 * i + 2, 2 * i + 1) for i in ups]
    )
    plane_slots = plane_boxes * per_box
    geometry, strengths, targets, planes, local = pl.pallas_call(
        feature_kernel,
        out_shape=(
            rows(boxes * depth, per_box, bf16),
            rows(boxes * 80, per_box, bf16),
            rows(plane_slots, depth, bf16),
            rows(plane_boxes * 8, per_box),
            rows(528),
        ),
        in_specs=[vmem] * 2,
        out_specs=(vmem,) * 5,
        compiler_params=limit(12),
        name="features",
    )(local, sent)
    mine, theirs = pl.pallas_call(
        field_kernel,
        out_shape=(rows(boxes * 8, per_box),) * 2,
        in_specs=[smem] + [vmem] * 8,
        out_specs=(vmem, vmem),
        scratch_shapes=[
            pltpu.VMEM((plane_boxes * depth, per_box), bf16),
            pltpu.VMEM((plane_boxes * 80, per_box), bf16),
            pltpu.VMEM((3 * plane_boxes * 80, per_box), bf16),
            pltpu.VMEM((plane_boxes * 160, per_box), f32),
            pltpu.VMEM((3 * plane_boxes * 16, per_box), f32),
            pltpu.VMEM((6 * 32, 128), f32),
            pltpu.VMEM((2 * 32, 128), f32),
        ],
        compiler_params=limit(32),
        name="fields",
    )(box_centres, local, cross, first, second, geometry, strengths, targets, planes)
    theirs = lax.ppermute(theirs, "rhs", swap)
    gram, live = pl.pallas_call(
        gram_kernel,
        out_shape=(rows(8), rows(2 * boxes)),
        in_specs=[smem, vmem],
        out_specs=(vmem, vmem),
        compiler_params=limit(8),
        name="gram",
    )(facet_counts, basis)
    image, tiles = pl.pallas_call(
        image_kernel,
        out_shape=(rows(rhs_local, facet_local), jax.ShapeDtypeStruct((count, 8, 128), f32)),
        in_specs=[vmem] * 6,
        out_specs=(vmem, vmem),
        compiler_params=limit(8),
        name="image",
    )(mine, theirs, gram, live, contrast, basis)
    tiles = lax.all_to_all(tiles, "box", 0, 0, tiled=True)
    next_vector, hessenberg = pl.pallas_call(
        functools.partial(finish_kernel, total_facets),
        out_shape=(rows(rhs_local, facet_local), rows(rhs_local, krylov + 1)),
        in_specs=[vmem] * 4,
        out_specs=(vmem, vmem),
        compiler_params=limit(16),
        name="finish",
    )(tiles, live, image, basis)
    return next_vector, hessenberg.T


def solution(mesh):
    return jax.shard_map(
        on_device,
        mesh=mesh,
        in_specs=(
            P(None, "rhs", "box"),
            P(None, "box"),
            P(None, "box"),
            P("box"),
            P("box"),
            P("box"),
            P(None, "box"),
            P("box", None),
            P("box", None),
        ),
        out_specs=(P("rhs", "box"), P(None, "rhs")),
        check_vma=False,
    )
```

```python
import functools

import jax
import jax.numpy as jnp
from jax import lax
from jax.experimental import pallas as pl
from jax.experimental.pallas import tpu as pltpu
from jax.sharding import PartitionSpec as P

soften = 0.0025
epsilon = 1e-06
f32 = jnp.float32
bf16 = jnp.bfloat16
plane_boxes = 16
per_box = 256
depth = 64


def lattice(centres_s, b):
    x = (centres_s[0, b] + 0.5).astype(jnp.int32)
    y = (centres_s[1, b] + 0.5).astype(jnp.int32)
    z = (centres_s[2, b] + 0.5).astype(jnp.int32)
    return x, y, z


def slot_of(centres_s, b):
    x, y, z = lattice(centres_s, b)
    return (z & 1) * plane_boxes + y * 4 + x


def wide_row(ref, b):
    return jnp.concatenate([ref[pl.ds(2 * b, 1), :], ref[pl.ds(2 * b + 1, 1), :]], axis=1)


def live_row(counts_s, b):
    slots = lax.broadcasted_iota(jnp.int32, (1, per_box), 1)
    return (slots < counts_s[b]).astype(f32)


def prep_kernel(
    centres_h, counts_h, basis_h, facets_h, areas_h, normals_h, cross_ref, first_ref, second_ref, local_ref,
    charges_v, centres_s, counts_s, current_ref, facets_ref, areas_ref, normals_ref, arrived
):
    boxes = counts_s.shape[0]
    moves = [
        (basis_h.at[basis_h.shape[0] - 1], current_ref),
        (facets_h, facets_ref),
        (areas_h, areas_ref),
        (normals_h, normals_ref),
        (centres_h, centres_s),
        (counts_h, counts_s),
    ]
    copies = [pltpu.make_async_copy(a, b, arrived.at[k]) for k, (a, b) in enumerate(moves)]
    for copy in copies:
        copy.start()
    for copy in copies:
        copy.wait()
    lane = lax.broadcasted_iota(jnp.int32, (8, 128), 1)
    row = lax.broadcasted_iota(jnp.int32, (8, 128), 0)
    empty = jnp.zeros((2, 128), f32)

    def one_box(b, carry):
        moments, centres = carry
        slot = slot_of(centres_s, b)
        lanes = pl.ds(pl.multiple_of(b * per_box, per_box), per_box)
        facets = facets_ref[:, lanes]
        normals = normals_ref[:, lanes]
        live = live_row(counts_s, b)
        weighted = current_ref[:, lanes] * (wide_row(areas_ref, b) * live / per_box)
        start = pl.multiple_of(slot * 16, 16)
        charges_v[pl.ds(start, 16), :] = jnp.concatenate([weighted[:, :128], weighted[:, 128:]], axis=0)
        local_ref[pl.ds(start, 16), :] = jnp.concatenate(
            [facets[:, :128], facets[:, 128:], empty, normals[:, :128], normals[:, 128:], empty], axis=0
        )
        moments += jnp.where(lane == slot, jnp.sum(weighted, axis=1, keepdims=True), 0.0)
        for a in range(3):
            dipole = jnp.sum(weighted * (facets[a : a + 1] - centres_s[a, b]), axis=1, keepdims=True)
            moments += jnp.where(lane == 32 * (a + 1) + slot, dipole, 0.0)
            centres += jnp.where((lane == slot) & (row == a), centres_s[a, b], 0.0)
        return moments, centres

    zeros = jnp.zeros((8, 128), f32)
    moments, centres = lax.fori_loop(0, boxes, one_box, (zeros, zeros), unroll=4)
    _, _, z = lattice(centres_s, 0)
    base_z = (z - (z & 1)).astype(f32) + 0.5
    centres = jnp.where((row == 3) | (row == 4), 1.5, jnp.where(row == 5, base_z, centres))
    half = lax.axis_index("rhs")
    away = pl.multiple_of((1 - half) * 256, 256)
    here = pl.multiple_of(half * 256, 256)
    pieces = jnp.concatenate([*thirds(moments), zeros], axis=0).astype(bf16)
    cross_ref[:512] = charges_v[...].astype(bf16)
    cross_ref[512:] = pieces
    second_ref[:256] = charges_v[pl.ds(here, 256), :].astype(bf16)
    second_ref[256:] = pieces
    first_ref[:256] = charges_v[pl.ds(away, 256), :].astype(bf16).astype(f32)
    for place in range(plane_boxes):
        first_ref[256 + 8 * place : 264 + 8 * place] = local_ref[pl.ds(away + 16 * place, 8), :]
    first_ref[384:392] = moments
    first_ref[392:] = centres
    local_ref[512:520] = moments
    local_ref[520:] = centres


def thirds(x):
    high = x.astype(bf16).astype(f32)
    rest = x - high
    middle = rest.astype(bf16).astype(f32)
    return high, middle, (rest - middle).astype(bf16).astype(f32)


def stacked_rows(parts, width):
    zeros = jnp.zeros((depth - 8 * len(parts), width), f32)
    return jnp.concatenate([*parts, zeros], axis=0)


def padded(rows):
    return jnp.concatenate([rows, jnp.zeros((8 - rows.shape[0], rows.shape[1]), f32)], axis=0)


def wide_charges(ref, place):
    both = ref[pl.ds(pl.multiple_of(place * 16, 16), 16), :].astype(f32)
    return jnp.concatenate([both[:8], both[8:]], axis=1)


def wide_tile(ref, start):
    tile = ref[pl.ds(pl.multiple_of(start, 8), 8), :]
    return jnp.concatenate([tile[0:3], tile[3:6]], axis=1)


def whole_moments(pieces):
    return pieces[:8] + (pieces[8:16] + pieces[16:24])


def store_geometry(local, box, geometry):
    row = lax.broadcasted_iota(jnp.int32, (8, per_box), 0)
    square = jnp.sum(local * local, axis=0, keepdims=True)
    features = jnp.where(row == 3, square, jnp.where(row == 4, 1.0, local))
    high, middle, low = thirds(features)
    rows = stacked_rows((high, high, high, middle, middle, low), per_box)
    geometry[pl.ds(pl.multiple_of(box * depth, depth), depth), :] = rows.astype(bf16)


def store_strengths(local, charges, box, strengths):
    products = jnp.concatenate([charges * local[a : a + 1] for a in range(3)], axis=0)
    rows = jnp.concatenate([charges, *thirds(products)], axis=0)
    strengths[pl.ds(pl.multiple_of(box * 80, 80), 80), :] = rows.astype(bf16)


def feature_kernel(local_ref, sent_ref, geometry, mine, targets, planes, local_out):
    boxes = 2 * plane_boxes
    half = lax.axis_index("rhs")
    origin = local_ref[523:526, 0:1]
    row = lax.broadcasted_iota(jnp.int32, (8, per_box), 0)

    def source(slot, _):
        local = padded(wide_tile(local_ref, slot * 16) - origin)
        store_geometry(local, slot, geometry)
        store_strengths(local, wide_charges(sent_ref, slot), slot, mine)
        return 0

    lax.fori_loop(0, boxes, source, 0, unroll=4)

    def target(place, _):
        start = (half * plane_boxes + place) * 16
        local = padded(wide_tile(local_ref, start) - origin)
        normal = padded(wide_tile(local_ref, start + 8))
        square = jnp.sum(local * local, axis=0, keepdims=True) + soften
        along = jnp.sum(local * normal, axis=0, keepdims=True)
        distance = jnp.where(row == 3, 1.0, jnp.where(row == 4, square, -2.0 * local))
        high, middle, low = thirds(distance)
        rows = stacked_rows((high, middle, low, high, middle, high), per_box)
        start = pl.multiple_of(place * per_box, per_box)
        targets[pl.ds(start, per_box), :] = jnp.transpose(rows).astype(bf16)
        planes[pl.ds(pl.multiple_of(place * 8, 8), 8), :] = jnp.where(row == 3, along, normal)
        return 0

    lax.fori_loop(0, plane_boxes, target, 0, unroll=4)
    local_out[...] = local_ref[...]


def near_planes(sources, targets, total, beside):
    def near_rows(item, _):
        target_y = (item + 1) // 3
        source_y = target_y + lax.rem(item + 1, 3) - 1
        runs = []
        for near_x in range(4):
            for source in sources:
                for x in range(max(near_x - 1, 0), min(near_x + 2, 4)):
                    runs.append((near_x, source, source_y * 4 + x))

        def rows_at(pair, place, number):
            ref, first = pair
            return ref[pl.ds(pl.multiple_of((first + place) * number, number), number), :]

        def distances(near_x, source, place):
            start = pl.multiple_of((target_y * 4 + near_x) * per_box, per_box)
            weights = rows_at(source[0], place, depth)
            return jnp.dot(targets[pl.ds(start, per_box), :], weights, preferred_element_type=f32)

        ahead = distances(*runs[0])
        cubed = []
        given = []
        for i, (near_x, source, place) in enumerate(runs):
            here = ahead
            if i + 1 < len(runs):
                ahead = distances(*runs[i + 1])
            inverse = lax.rsqrt(here)
            cubed.append((inverse * inverse * inverse).astype(bf16))
            given.append(jnp.concatenate([rows_at(source[1], place, 80), rows_at(source[2], place, 80)], axis=0))
            if i + 1 == len(runs) or runs[i + 1][0] != near_x:
                rows_of = pl.ds(pl.multiple_of((target_y * 4 + near_x) * 160, 160), 160)
                total[rows_of, :] += lax.dot_general(
                    jnp.concatenate(given, axis=1),
                    jnp.concatenate(cubed, axis=1),
                    (((1,), (1,)), ((), ())),
                    preferred_element_type=f32,
                )
                cubed = []
                given = []
        beside(item)
        return 0

    lax.fori_loop(0, 10, near_rows, 0)


def field_kernel(
    centres_s, local_ref, cross_ref, first_ref, second_ref, geometry, mine, targets, planes, mine_ref, theirs_ref,
    halo_geometry, halo_mine, theirs, total, far, far_centres, far_moments
):
    boxes = 2 * plane_boxes
    half = lax.axis_index("rhs")
    origin = local_ref[523:526, 0:1]

    def source(slot, _):
        local = wide_tile(local_ref, slot * 16) - origin
        store_strengths(local, wide_charges(cross_ref, slot), slot, theirs)
        return 0

    lax.fori_loop(0, boxes, source, 0, unroll=4)

    def halo_source(place, _):
        local = padded(wide_tile(first_ref, 256 + place * 8) - origin)
        store_geometry(local, place, halo_geometry)
        store_strengths(local, wide_charges(first_ref, place), place, halo_mine)
        store_strengths(local, wide_charges(second_ref, place), boxes + place, theirs)
        return 0

    lax.fori_loop(0, plane_boxes, halo_source, 0, unroll=4)
    total[...] = jnp.zeros_like(total)

    for group, (centres, ours, others) in enumerate(
        (
            (first_ref[392:400], first_ref[384:392], second_ref[256:288]),
            (local_ref[520:528], local_ref[512:520], cross_ref[512:544]),
        )
    ):
        columns = jnp.transpose(jnp.concatenate([centres[:3] - origin, centres[3:]], axis=0))[:32]
        for a in range(3):
            far_centres[(group * 3 + a) * 32 : (group * 3 + a + 1) * 32, :] = jnp.broadcast_to(
                columns[:, a : a + 1], (32, 128)
            )
        both = jnp.concatenate([ours, whole_moments(others.astype(f32))], axis=0)
        high = both.astype(bf16).astype(f32)
        far_moments[group * 32 : group * 32 + 32, :] = jnp.concatenate([high, both - high], axis=0)
    lane = lax.broadcasted_iota(jnp.int32, (1, 128), 1)
    lane_x = lane & 3
    lane_y = (lane >> 2) & 3
    lane_plane = (lane >> 4) & 1

    def far_field(k):
        group = (k >= boxes).astype(jnp.int32)
        slot = jnp.where(k < boxes, k, half * plane_boxes + k - boxes)
        x, y, plane = slot & 3, (slot >> 2) & 3, slot >> 4
        local = wide_tile(local_ref, slot * 16) - origin
        normal = wide_tile(local_ref, slot * 16 + 8)
        d = []
        for a in range(3):
            centre = far_centres[pl.ds(pl.multiple_of((group * 3 + a) * 32, 32), 32), :]
            d.append(local[a : a + 1] - jnp.concatenate([centre, centre], axis=1))
        q = d[0] * d[0] + d[1] * d[1] + d[2] * d[2] + soften
        inverse = lax.rsqrt(q)
        inverse_2 = inverse * inverse
        inverse_3 = inverse_2 * inverse
        t = d[0] * normal[0:1] + d[1] * normal[1:2] + d[2] * normal[2:3]
        single = t * inverse_3
        steep = 3.0 * single * inverse_2
        coefficients = [single] + [steep * d[a] - normal[a : a + 1] * inverse_3 for a in range(3)]
        whole = jnp.concatenate(coefficients, axis=0)
        upper = whole.astype(bf16)
        lower = (whole - upper.astype(f32)).astype(bf16)
        lane_z = lane_plane + jnp.where(group == 0, 4 * half - 2, 0)
        near = (jnp.abs(lane_x - x) <= 1) & (jnp.abs(lane_y - y) <= 1) & (jnp.abs(lane_z - plane) <= 1)
        picked = jnp.where(near, 0.0, far_moments[pl.ds(pl.multiple_of(group * 32, 32), 32), :]).astype(bf16)
        first = jnp.dot(picked, upper, preferred_element_type=f32)
        second = jnp.dot(picked, lower, preferred_element_type=f32)
        return first[:16] + first[16:] + second[:16]

    def far_boxes(item):
        for i in range(5):
            k = jnp.minimum(item * 5 + i, 3 * plane_boxes - 1)
            far[pl.ds(pl.multiple_of(k * 16, 16), 16), :] = far_field(k)

    sources = [((geometry, p), (mine, p), (theirs, p)) for p in (0, plane_boxes)]
    sources.append(((halo_geometry, 0), (halo_mine, 0), (theirs, boxes)))
    near_planes(sources, targets, total, far_boxes)

    def near_field(place, _):
        sums = total[pl.ds(pl.multiple_of(place * 160, 160), 160), :]
        side = planes[pl.ds(pl.multiple_of(place * 8, 8), 8), :]
        values = []
        for start in (0, 80):
            value = side[3:4] * sums[start : start + 8]
            for a in range(3):
                high, middle, low = (sums[i : i + 8] for i in range(start + 8 + 8 * a, start + 80, 24))
                value = value - side[a : a + 1] * (high + (middle + low))
            values.append(value)
        value = jnp.concatenate(values, axis=0)
        slot = half * plane_boxes + place
        rows = pl.ds(pl.multiple_of(slot * 16, 16), 16)
        far[rows, :] += value + far[pl.ds(pl.multiple_of((boxes + place) * 16, 16), 16), :]
        return 0

    lax.fori_loop(0, plane_boxes, near_field, 0, unroll=4)

    def given_back(b, _):
        start = pl.multiple_of(slot_of(centres_s, b) * 16, 16)
        rows = pl.ds(pl.multiple_of(b * 8, 8), 8)
        mine_ref[rows, :] = far[pl.ds(start, 8), :]
        theirs_ref[rows, :] = far[pl.ds(start + 8, 8), :]
        return 0

    lax.fori_loop(0, boxes, given_back, 0, unroll=4)


def gram_kernel(counts_s, basis_ref, sums_ref, live_ref):
    krylov = basis_ref.shape[0]
    pairs = [(m, n) for m in range(krylov) for n in range(m + 1)]

    def one_box(b, carry):
        lanes = pl.ds(pl.multiple_of(b * per_box, per_box), per_box)
        live = live_row(counts_s, b)
        live_ref[pl.ds(2 * b, 1), :] = live[:, :128]
        live_ref[pl.ds(2 * b + 1, 1), :] = live[:, 128:]
        rows = [basis_ref[m, :, lanes] * live for m in range(krylov)]
        out = []
        for k, (m, n) in enumerate(pairs):
            product = rows[m] * rows[n]
            out.append(carry[k] + product[:, :128] + product[:, 128:])
        return tuple(out)

    zeros = jnp.zeros((8, 128), f32)
    gram = lax.fori_loop(0, counts_s.shape[0], one_box, (zeros,) * len(pairs))
    lane = lax.broadcasted_iota(jnp.int32, (8, 128), 1)
    total = zeros
    for k, value in enumerate(gram):
        total = jnp.where(lane == krylov + 1 + k, jnp.sum(value, axis=1, keepdims=True), total)
    sums_ref[...] = total


def image_kernel(mine_ref, theirs_ref, gram_ref, live_ref, contrast_ref, basis_ref, image_ref, sums_ref):
    krylov = basis_ref.shape[0]

    def one_box(b, carry):
        lanes = pl.ds(pl.multiple_of(b * per_box, per_box), per_box)
        rows = pl.ds(pl.multiple_of(b * 8, 8), 8)
        live = wide_row(live_ref, b)
        part = mine_ref[rows, :] + theirs_ref[rows, :]
        image = live * (basis_ref[krylov - 1, :, lanes] - 2.0 * wide_row(contrast_ref, b) * part)
        image_ref[:, lanes] = image
        sums = []
        for m in range(krylov + 1):
            product = image * (basis_ref[m, :, lanes] if m < krylov else image)
            sums.append(carry[m] + product[:, :128] + product[:, 128:])
        return tuple(sums)

    zeros = jnp.zeros((8, 128), f32)
    sums = lax.fori_loop(0, live_ref.shape[0] // 2, one_box, (zeros,) * (krylov + 1), unroll=4)
    lane = lax.broadcasted_iota(jnp.int32, (8, 128), 1)
    total = gram_ref[...]
    for k, value in enumerate(sums):
        total = jnp.where(lane == k, jnp.sum(value, axis=1, keepdims=True), total)
    sums_ref[...] = jnp.broadcast_to(total[None], sums_ref.shape)


def two_sum(a, b):
    s = a + b
    c = s - a
    return s, (a - (s - c)) + (b - c)


def halves(a):
    c = a * 4097.0
    high = c - (c - a)
    return high, a - high


def two_product(a, b):
    p = a * b
    a_high, a_low = halves(a)
    b_high, b_low = halves(b)
    return p, ((a_high * b_high - p) + a_high * b_low + a_low * b_high) + a_low * b_low


def finish_kernel(total_facets, tiles_ref, live_ref, image_ref, basis_ref, next_ref, hessenberg_ref):
    boxes = live_ref.shape[0] // 2
    krylov = basis_ref.shape[0]
    lane = lax.broadcasted_iota(jnp.int32, (8, 128), 1)

    sums, rest = tiles_ref[0], jnp.zeros((8, 128), f32)
    for i in range(1, tiles_ref.shape[0]):
        sums, error = two_sum(sums, tiles_ref[i])
        rest = rest + error
    exact = sums + rest
    projections = [exact[:, m : m + 1] / total_facets for m in range(krylov)]
    pairs = [(m, n) for m in range(krylov) for n in range(m + 1)]
    first = jnp.where(lane == krylov, 1.0, 0.0)
    second = jnp.where(lane <= krylov, 1.0, 0.0)
    for m in range(krylov):
        first = jnp.where(lane == m, -2.0 * projections[m], first)
    for k, (m, n) in enumerate(pairs):
        at = lane == krylov + 1 + k
        scale = 1.0 if m == n else 2.0
        first = jnp.where(at, scale * projections[m], first)
        second = jnp.where(at, projections[n], second)
    factor, factor_rest = two_product(first, second)
    value, value_rest = two_product(factor, sums)
    value_rest = value_rest + (factor * rest + factor_rest * sums)
    for shift in (64, 32, 16, 8, 4, 2, 1):
        other = pltpu.roll(value, shift, 1)
        other_rest = pltpu.roll(value_rest, shift, 1)
        value, error = two_sum(value, other)
        value_rest = (value_rest + other_rest) + error
    remaining = jnp.maximum(value + value_rest, 0.0)
    norm = jnp.sqrt(remaining / total_facets + epsilon)
    heads = jnp.where(lane == krylov, norm, 0.0)
    for m in range(krylov):
        heads = jnp.where(lane == m, projections[m], heads)
    hessenberg_ref[...] = heads[:, : krylov + 1]
    wide = [jnp.broadcast_to(p, (8, per_box)) for p in projections]
    scale = jnp.concatenate([1.0 / norm] * (per_box // 128), axis=1)

    def one_box(b, _):
        lanes = pl.ds(pl.multiple_of(b * per_box, per_box), per_box)
        live = wide_row(live_ref, b)
        sent = wide[0] * basis_ref[0, :, lanes]
        for m in range(1, krylov):
            sent += wide[m] * basis_ref[m, :, lanes]
        next_ref[:, lanes] = (image_ref[:, lanes] - sent * live) * scale
        return 0

    lax.fori_loop(0, boxes, one_box, 0, unroll=4)


smem = pl.BlockSpec(memory_space=pltpu.SMEM)
vmem = pl.BlockSpec(memory_space=pltpu.VMEM)


def on_device(
    basis, facet_centres, normals, areas, contrast, facet_counts, box_centres, near_boxes, far_boxes
):
    krylov, rhs_local, facet_local = basis.shape
    boxes = facet_counts.shape[0]
    count = lax.axis_size("box")
    total_facets = count * facet_local
    areas = areas.reshape(-1, 128)
    contrast = contrast.reshape(-1, 128)

    def rows(number, width=128, dtype=f32):
        return jax.ShapeDtypeStruct((number, width), dtype)

    def limit(mebibytes):
        return pltpu.CompilerParams(vmem_limit_bytes=mebibytes * 1024 * 1024)

    sent, first, second, local = pl.pallas_call(
        prep_kernel,
        out_shape=(rows(544, dtype=bf16), rows(400), rows(288, dtype=bf16), rows(528)),
        in_specs=[pl.BlockSpec(memory_space=pl.ANY)] * 6,
        out_specs=(vmem,) * 4,
        scratch_shapes=[
            pltpu.VMEM((512, 128), f32),
            pltpu.SMEM(box_centres.shape, f32),
            pltpu.SMEM(facet_counts.shape, jnp.int32),
            pltpu.VMEM((rhs_local, facet_local), f32),
            pltpu.VMEM(facet_centres.shape, f32),
            pltpu.VMEM(areas.shape, f32),
            pltpu.VMEM(normals.shape, f32),
            pltpu.SemaphoreType.DMA((6,)),
        ],
        name="prepare",
    )(box_centres, facet_counts, basis, facet_centres, areas, normals)
    swap = [(0, 1), (1, 0)]
    ups = range(count - 1)
    cross = lax.ppermute(sent, "rhs", swap)
    first = lax.ppermute(
        first, ("box", "rhs"), [(2 * i, 2 * i + 2) for i in ups] + [(2 * i + 3, 2 * i + 1) for i in ups]
    )
    second = lax.ppermute(
        second, ("box", "rhs"), [(2 * i + 1, 2 * i + 2) for i in ups] + [(2 * i + 2, 2 * i + 1) for i in ups]
    )
    plane_slots = plane_boxes * per_box
    geometry, strengths, targets, planes, local = pl.pallas_call(
        feature_kernel,
        out_shape=(
            rows(boxes * depth, per_box, bf16),
            rows(boxes * 80, per_box, bf16),
            rows(plane_slots, depth, bf16),
            rows(plane_boxes * 8, per_box),
            rows(528),
        ),
        in_specs=[vmem] * 2,
        out_specs=(vmem,) * 5,
        compiler_params=limit(12),
        name="features",
    )(local, sent)
    mine, theirs = pl.pallas_call(
        field_kernel,
        out_shape=(rows(boxes * 8, per_box),) * 2,
        in_specs=[smem] + [vmem] * 8,
        out_specs=(vmem, vmem),
        scratch_shapes=[
            pltpu.VMEM((plane_boxes * depth, per_box), bf16),
            pltpu.VMEM((plane_boxes * 80, per_box), bf16),
            pltpu.VMEM((3 * plane_boxes * 80, per_box), bf16),
            pltpu.VMEM((plane_boxes * 160, per_box), f32),
            pltpu.VMEM((3 * plane_boxes * 16, per_box), f32),
            pltpu.VMEM((6 * 32, 128), f32),
            pltpu.VMEM((2 * 32, 128), f32),
        ],
        compiler_params=limit(32),
        name="fields",
    )(box_centres, local, cross, first, second, geometry, strengths, targets, planes)
    theirs = lax.ppermute(theirs, "rhs", swap)
    gram, live = pl.pallas_call(
        gram_kernel,
        out_shape=(rows(8), rows(2 * boxes)),
        in_specs=[smem, vmem],
        out_specs=(vmem, vmem),
        compiler_params=limit(8),
        name="gram",
    )(facet_counts, basis)
    image, tiles = pl.pallas_call(
        image_kernel,
        out_shape=(rows(rhs_local, facet_local), jax.ShapeDtypeStruct((count, 8, 128), f32)),
        in_specs=[vmem] * 6,
        out_specs=(vmem, vmem),
        compiler_params=limit(8),
        name="image",
    )(mine, theirs, gram, live, contrast, basis)
    tiles = lax.all_to_all(tiles, "box", 0, 0, tiled=True)
    next_vector, hessenberg = pl.pallas_call(
        functools.partial(finish_kernel, total_facets),
        out_shape=(rows(rhs_local, facet_local), rows(rhs_local, krylov + 1)),
        in_specs=[vmem] * 4,
        out_specs=(vmem, vmem),
        compiler_params=limit(16),
        name="finish",
    )(tiles, live, image, basis)
    return next_vector, hessenberg.T


def solution(mesh):
    return jax.shard_map(
        on_device,
        mesh=mesh,
        in_specs=(
            P(None, "rhs", "box"),
            P(None, "box"),
            P(None, "box"),
            P("box"),
            P("box"),
            P("box"),
            P(None, "box"),
            P("box", None),
            P("box", None),
        ),
        out_specs=(P("rhs", "box"), P(None, "rhs")),
        check_vma=False,
    )
```

```python
import functools

import jax
import jax.numpy as jnp
from jax import lax
from jax.experimental import pallas as pl
from jax.experimental.pallas import tpu as pltpu
from jax.sharding import PartitionSpec as P

soften = 0.0025
epsilon = 1e-06
f32 = jnp.float32
bf16 = jnp.bfloat16
plane_boxes = 16
per_box = 256
depth = 64


def lattice(centres_s, b):
    x = (centres_s[0, b] + 0.5).astype(jnp.int32)
    y = (centres_s[1, b] + 0.5).astype(jnp.int32)
    z = (centres_s[2, b] + 0.5).astype(jnp.int32)
    return x, y, z


def slot_of(centres_s, b):
    x, y, z = lattice(centres_s, b)
    return (z & 1) * plane_boxes + y * 4 + x


def wide_row(ref, b):
    return jnp.concatenate([ref[pl.ds(2 * b, 1), :], ref[pl.ds(2 * b + 1, 1), :]], axis=1)


def live_row(counts_s, b):
    slots = lax.broadcasted_iota(jnp.int32, (1, per_box), 1)
    return (slots < counts_s[b]).astype(f32)


def prep_kernel(
    centres_h, counts_h, basis_h, facets_h, areas_h, normals_h, cross_ref, first_ref, second_ref, local_ref,
    charges_v, centres_s, counts_s, current_ref, facets_ref, areas_ref, normals_ref, arrived
):
    boxes = counts_s.shape[0]
    moves = [
        (basis_h.at[basis_h.shape[0] - 1], current_ref),
        (facets_h, facets_ref),
        (areas_h, areas_ref),
        (normals_h, normals_ref),
        (centres_h, centres_s),
        (counts_h, counts_s),
    ]
    copies = [pltpu.make_async_copy(a, b, arrived.at[k]) for k, (a, b) in enumerate(moves)]
    for copy in copies:
        copy.start()
    for copy in copies:
        copy.wait()
    lane = lax.broadcasted_iota(jnp.int32, (8, 128), 1)
    row = lax.broadcasted_iota(jnp.int32, (8, 128), 0)
    empty = jnp.zeros((2, 128), f32)

    def one_box(b, carry):
        moments, centres = carry
        slot = slot_of(centres_s, b)
        lanes = pl.ds(pl.multiple_of(b * per_box, per_box), per_box)
        facets = facets_ref[:, lanes]
        normals = normals_ref[:, lanes]
        live = live_row(counts_s, b)
        weighted = current_ref[:, lanes] * (wide_row(areas_ref, b) * live / per_box)
        start = pl.multiple_of(slot * 16, 16)
        charges_v[pl.ds(start, 16), :] = jnp.concatenate([weighted[:, :128], weighted[:, 128:]], axis=0)
        local_ref[pl.ds(start, 16), :] = jnp.concatenate(
            [facets[:, :128], facets[:, 128:], empty, normals[:, :128], normals[:, 128:], empty], axis=0
        )
        moments += jnp.where(lane == slot, jnp.sum(weighted, axis=1, keepdims=True), 0.0)
        for a in range(3):
            dipole = jnp.sum(weighted * (facets[a : a + 1] - centres_s[a, b]), axis=1, keepdims=True)
            moments += jnp.where(lane == 32 * (a + 1) + slot, dipole, 0.0)
            centres += jnp.where((lane == slot) & (row == a), centres_s[a, b], 0.0)
        return moments, centres

    zeros = jnp.zeros((8, 128), f32)
    moments, centres = lax.fori_loop(0, boxes, one_box, (zeros, zeros), unroll=4)
    _, _, z = lattice(centres_s, 0)
    base_z = (z - (z & 1)).astype(f32) + 0.5
    centres = jnp.where((row == 3) | (row == 4), 1.5, jnp.where(row == 5, base_z, centres))
    half = lax.axis_index("rhs")
    away = pl.multiple_of((1 - half) * 256, 256)
    here = pl.multiple_of(half * 256, 256)
    pieces = jnp.concatenate([*thirds(moments), zeros], axis=0).astype(bf16)
    cross_ref[:512] = charges_v[...].astype(bf16)
    cross_ref[512:] = pieces
    second_ref[:256] = charges_v[pl.ds(here, 256), :].astype(bf16)
    second_ref[256:] = pieces
    first_ref[:256] = charges_v[pl.ds(away, 256), :].astype(bf16).astype(f32)
    for place in range(plane_boxes):
        first_ref[256 + 8 * place : 264 + 8 * place] = local_ref[pl.ds(away + 16 * place, 8), :]
    first_ref[384:392] = moments
    first_ref[392:] = centres
    local_ref[512:520] = moments
    local_ref[520:] = centres


def thirds(x):
    high = x.astype(bf16).astype(f32)
    rest = x - high
    middle = rest.astype(bf16).astype(f32)
    return high, middle, (rest - middle).astype(bf16).astype(f32)


def stacked_rows(parts, width):
    zeros = jnp.zeros((depth - 8 * len(parts), width), f32)
    return jnp.concatenate([*parts, zeros], axis=0)


def padded(rows):
    return jnp.concatenate([rows, jnp.zeros((8 - rows.shape[0], rows.shape[1]), f32)], axis=0)


def wide_charges(ref, place):
    both = ref[pl.ds(pl.multiple_of(place * 16, 16), 16), :].astype(f32)
    return jnp.concatenate([both[:8], both[8:]], axis=1)


def wide_tile(ref, start):
    tile = ref[pl.ds(pl.multiple_of(start, 8), 8), :]
    return jnp.concatenate([tile[0:3], tile[3:6]], axis=1)


def whole_moments(pieces):
    return pieces[:8] + (pieces[8:16] + pieces[16:24])


def store_geometry(local, box, geometry):
    row = lax.broadcasted_iota(jnp.int32, (8, per_box), 0)
    square = jnp.sum(local * local, axis=0, keepdims=True)
    features = jnp.where(row == 3, square, jnp.where(row == 4, 1.0, local))
    high, middle, low = thirds(features)
    rows = stacked_rows((high, high, high, middle, middle, low), per_box)
    geometry[pl.ds(pl.multiple_of(box * depth, depth), depth), :] = rows.astype(bf16)


def store_strengths(local, charges, box, strengths):
    products = jnp.concatenate([charges * local[a : a + 1] for a in range(3)], axis=0)
    rows = jnp.concatenate([charges, *thirds(products)], axis=0)
    strengths[pl.ds(pl.multiple_of(box * 80, 80), 80), :] = rows.astype(bf16)


def feature_kernel(local_ref, sent_ref, geometry, mine, targets, planes, local_out):
    boxes = 2 * plane_boxes
    half = lax.axis_index("rhs")
    origin = local_ref[523:526, 0:1]
    row = lax.broadcasted_iota(jnp.int32, (8, per_box), 0)

    def source(slot, _):
        local = padded(wide_tile(local_ref, slot * 16) - origin)
        store_geometry(local, slot, geometry)
        store_strengths(local, wide_charges(sent_ref, slot), slot, mine)
        return 0

    lax.fori_loop(0, boxes, source, 0, unroll=4)

    def target(place, _):
        start = (half * plane_boxes + place) * 16
        local = padded(wide_tile(local_ref, start) - origin)
        normal = padded(wide_tile(local_ref, start + 8))
        square = jnp.sum(local * local, axis=0, keepdims=True) + soften
        along = jnp.sum(local * normal, axis=0, keepdims=True)
        distance = jnp.where(row == 3, 1.0, jnp.where(row == 4, square, -2.0 * local))
        high, middle, low = thirds(distance)
        rows = stacked_rows((high, middle, low, high, middle, high), per_box)
        start = pl.multiple_of(place * per_box, per_box)
        targets[pl.ds(start, per_box), :] = jnp.transpose(rows).astype(bf16)
        planes[pl.ds(pl.multiple_of(place * 8, 8), 8), :] = jnp.where(row == 3, along, normal)
        return 0

    lax.fori_loop(0, plane_boxes, target, 0, unroll=4)
    local_out[...] = local_ref[...]


def near_planes(sources, targets, total):
    def rows_at(pair, place, number):
        ref, first = pair
        return ref[pl.ds(pl.multiple_of((first + place) * number, number), number), :]

    def near_box(item, near_x, source_x, width):
        target_y = (item + 1) // 3
        source_y = target_y + lax.rem(item + 1, 3) - 1
        place = target_y * 4 + near_x
        facets = targets[pl.ds(pl.multiple_of(place * per_box, per_box), per_box), :]
        runs = [(source, source_y * 4 + source_x + k) for source in sources for k in range(width)]

        def distances(source, place):
            return jnp.dot(facets, rows_at(source[0], place, depth), preferred_element_type=f32)

        ahead = distances(*runs[0])
        cubed = []
        given = []
        for i, (source, source_place) in enumerate(runs):
            here = ahead
            if i + 1 < len(runs):
                ahead = distances(*runs[i + 1])
            inverse = lax.rsqrt(here)
            cubed.append((inverse * inverse * inverse).astype(bf16))
            given.append(
                jnp.concatenate([rows_at(source[1], source_place, 80), rows_at(source[2], source_place, 80)], axis=0)
            )
        total[pl.ds(pl.multiple_of(place * 160, 160), 160), :] += lax.dot_general(
            jnp.concatenate(given, axis=1),
            jnp.concatenate(cubed, axis=1),
            (((1,), (1,)), ((), ())),
            preferred_element_type=f32,
        )

    def inner(step, _):
        near_x = 1 + lax.rem(step, 2)
        near_box(step // 2, near_x, near_x - 1, 3)
        return 0

    def outer(step, _):
        side = lax.rem(step, 2)
        near_box(step // 2, 3 * side, 2 * side, 2)
        return 0

    lax.fori_loop(0, 20, inner, 0)
    lax.fori_loop(0, 20, outer, 0)


def far_kernel(local_ref, cross_ref, first_ref, second_ref, far, far_centres, far_moments):
    boxes = 2 * plane_boxes
    half = lax.axis_index("rhs")
    origin = local_ref[523:526, 0:1]

    for group, (centres, ours, others) in enumerate(
        (
            (first_ref[392:400], first_ref[384:392], second_ref[256:288]),
            (local_ref[520:528], local_ref[512:520], cross_ref[512:544]),
        )
    ):
        columns = jnp.transpose(jnp.concatenate([centres[:3] - origin, centres[3:]], axis=0))[:32]
        for a in range(3):
            far_centres[(group * 3 + a) * 32 : (group * 3 + a + 1) * 32, :] = jnp.broadcast_to(
                columns[:, a : a + 1], (32, 128)
            )
        both = jnp.concatenate([ours, whole_moments(others.astype(f32))], axis=0)
        high = both.astype(bf16).astype(f32)
        far_moments[group * 32 : group * 32 + 32, :] = jnp.concatenate([high, both - high], axis=0)
    lane = lax.broadcasted_iota(jnp.int32, (1, 128), 1)
    lane_x = lane & 3
    lane_y = (lane >> 2) & 3
    lane_plane = (lane >> 4) & 1

    def far_field(k):
        group = (k >= boxes).astype(jnp.int32)
        slot = jnp.where(k < boxes, k, half * plane_boxes + k - boxes)
        x, y, plane = slot & 3, (slot >> 2) & 3, slot >> 4
        local = wide_tile(local_ref, slot * 16) - origin
        normal = wide_tile(local_ref, slot * 16 + 8)
        d = []
        for a in range(3):
            centre = far_centres[pl.ds(pl.multiple_of((group * 3 + a) * 32, 32), 32), :]
            d.append(local[a : a + 1] - jnp.concatenate([centre, centre], axis=1))
        q = d[0] * d[0] + d[1] * d[1] + d[2] * d[2] + soften
        inverse = lax.rsqrt(q)
        inverse_2 = inverse * inverse
        inverse_3 = inverse_2 * inverse
        t = d[0] * normal[0:1] + d[1] * normal[1:2] + d[2] * normal[2:3]
        single = t * inverse_3
        steep = 3.0 * single * inverse_2
        coefficients = [single] + [steep * d[a] - normal[a : a + 1] * inverse_3 for a in range(3)]
        whole = jnp.concatenate(coefficients, axis=0)
        upper = whole.astype(bf16)
        lower = (whole - upper.astype(f32)).astype(bf16)
        lane_z = lane_plane + jnp.where(group == 0, 4 * half - 2, 0)
        near = (jnp.abs(lane_x - x) <= 1) & (jnp.abs(lane_y - y) <= 1) & (jnp.abs(lane_z - plane) <= 1)
        picked = jnp.where(near, 0.0, far_moments[pl.ds(pl.multiple_of(group * 32, 32), 32), :]).astype(bf16)
        first = jnp.dot(picked, upper, preferred_element_type=f32)
        second = jnp.dot(picked, lower, preferred_element_type=f32)
        return first[:16] + first[16:] + second[:16]

    def far_boxes(k, _):
        far[pl.ds(pl.multiple_of(k * 16, 16), 16), :] = far_field(k)
        return 0

    lax.fori_loop(0, 3 * plane_boxes, far_boxes, 0, unroll=4)


def field_kernel(
    centres_s, local_ref, cross_ref, first_ref, second_ref, geometry, mine, targets, planes, far_ref,
    mine_ref, theirs_ref, halo_geometry, halo_mine, theirs, total, far
):
    boxes = 2 * plane_boxes
    half = lax.axis_index("rhs")
    origin = local_ref[523:526, 0:1]

    def source(slot, _):
        local = wide_tile(local_ref, slot * 16) - origin
        store_strengths(local, wide_charges(cross_ref, slot), slot, theirs)
        return 0

    lax.fori_loop(0, boxes, source, 0, unroll=4)

    def halo_source(place, _):
        local = padded(wide_tile(first_ref, 256 + place * 8) - origin)
        store_geometry(local, place, halo_geometry)
        store_strengths(local, wide_charges(first_ref, place), place, halo_mine)
        store_strengths(local, wide_charges(second_ref, place), boxes + place, theirs)
        return 0

    lax.fori_loop(0, plane_boxes, halo_source, 0, unroll=4)
    total[...] = jnp.zeros_like(total)
    far[...] = far_ref[: 16 * boxes]

    sources = [((geometry, p), (mine, p), (theirs, p)) for p in (0, plane_boxes)]
    sources.append(((halo_geometry, 0), (halo_mine, 0), (theirs, boxes)))
    near_planes(sources, targets, total)

    def near_field(place, _):
        sums = total[pl.ds(pl.multiple_of(place * 160, 160), 160), :]
        side = planes[pl.ds(pl.multiple_of(place * 8, 8), 8), :]
        values = []
        for start in (0, 80):
            value = side[3:4] * sums[start : start + 8]
            for a in range(3):
                high, middle, low = (sums[i : i + 8] for i in range(start + 8 + 8 * a, start + 80, 24))
                value = value - side[a : a + 1] * (high + (middle + low))
            values.append(value)
        value = jnp.concatenate(values, axis=0)
        slot = half * plane_boxes + place
        rows = pl.ds(pl.multiple_of(slot * 16, 16), 16)
        far[rows, :] = value + far_ref[rows, :] + far_ref[pl.ds(pl.multiple_of((boxes + place) * 16, 16), 16), :]
        return 0

    lax.fori_loop(0, plane_boxes, near_field, 0, unroll=4)

    def given_back(b, _):
        start = pl.multiple_of(slot_of(centres_s, b) * 16, 16)
        rows = pl.ds(pl.multiple_of(b * 8, 8), 8)
        mine_ref[rows, :] = far[pl.ds(start, 8), :]
        theirs_ref[rows, :] = far[pl.ds(start + 8, 8), :]
        return 0

    lax.fori_loop(0, boxes, given_back, 0, unroll=4)


def gram_kernel(counts_s, basis_ref, sums_ref, live_ref):
    krylov = basis_ref.shape[0]
    pairs = [(m, n) for m in range(krylov) for n in range(m + 1)]

    def one_box(b, carry):
        lanes = pl.ds(pl.multiple_of(b * per_box, per_box), per_box)
        live = live_row(counts_s, b)
        live_ref[pl.ds(2 * b, 1), :] = live[:, :128]
        live_ref[pl.ds(2 * b + 1, 1), :] = live[:, 128:]
        rows = [basis_ref[m, :, lanes] * live for m in range(krylov)]
        out = []
        for k, (m, n) in enumerate(pairs):
            product = rows[m] * rows[n]
            out.append(carry[k] + product[:, :128] + product[:, 128:])
        return tuple(out)

    zeros = jnp.zeros((8, 128), f32)
    gram = lax.fori_loop(0, counts_s.shape[0], one_box, (zeros,) * len(pairs))
    lane = lax.broadcasted_iota(jnp.int32, (8, 128), 1)
    total = zeros
    for k, value in enumerate(gram):
        total = jnp.where(lane == krylov + 1 + k, jnp.sum(value, axis=1, keepdims=True), total)
    sums_ref[...] = total


def image_kernel(mine_ref, theirs_ref, gram_ref, live_ref, contrast_ref, basis_ref, image_ref, sums_ref):
    krylov = basis_ref.shape[0]

    def one_box(b, carry):
        lanes = pl.ds(pl.multiple_of(b * per_box, per_box), per_box)
        rows = pl.ds(pl.multiple_of(b * 8, 8), 8)
        live = wide_row(live_ref, b)
        part = mine_ref[rows, :] + theirs_ref[rows, :]
        image = live * (basis_ref[krylov - 1, :, lanes] - 2.0 * wide_row(contrast_ref, b) * part)
        image_ref[:, lanes] = image
        sums = []
        for m in range(krylov + 1):
            product = image * (basis_ref[m, :, lanes] if m < krylov else image)
            sums.append(carry[m] + product[:, :128] + product[:, 128:])
        return tuple(sums)

    zeros = jnp.zeros((8, 128), f32)
    sums = lax.fori_loop(0, live_ref.shape[0] // 2, one_box, (zeros,) * (krylov + 1), unroll=4)
    lane = lax.broadcasted_iota(jnp.int32, (8, 128), 1)
    total = gram_ref[...]
    for k, value in enumerate(sums):
        total = jnp.where(lane == k, jnp.sum(value, axis=1, keepdims=True), total)
    sums_ref[...] = jnp.broadcast_to(total[None], sums_ref.shape)


def two_sum(a, b):
    s = a + b
    c = s - a
    return s, (a - (s - c)) + (b - c)


def halves(a):
    c = a * 4097.0
    high = c - (c - a)
    return high, a - high


def two_product(a, b):
    p = a * b
    a_high, a_low = halves(a)
    b_high, b_low = halves(b)
    return p, ((a_high * b_high - p) + a_high * b_low + a_low * b_high) + a_low * b_low


def finish_kernel(total_facets, tiles_ref, live_ref, image_ref, basis_ref, next_ref, hessenberg_ref):
    boxes = live_ref.shape[0] // 2
    krylov = basis_ref.shape[0]
    lane = lax.broadcasted_iota(jnp.int32, (8, 128), 1)

    sums, rest = tiles_ref[0], jnp.zeros((8, 128), f32)
    for i in range(1, tiles_ref.shape[0]):
        sums, error = two_sum(sums, tiles_ref[i])
        rest = rest + error
    exact = sums + rest
    projections = [exact[:, m : m + 1] / total_facets for m in range(krylov)]
    pairs = [(m, n) for m in range(krylov) for n in range(m + 1)]
    first = jnp.where(lane == krylov, 1.0, 0.0)
    second = jnp.where(lane <= krylov, 1.0, 0.0)
    for m in range(krylov):
        first = jnp.where(lane == m, -2.0 * projections[m], first)
    for k, (m, n) in enumerate(pairs):
        at = lane == krylov + 1 + k
        scale = 1.0 if m == n else 2.0
        first = jnp.where(at, scale * projections[m], first)
        second = jnp.where(at, projections[n], second)
    factor, factor_rest = two_product(first, second)
    value, value_rest = two_product(factor, sums)
    value_rest = value_rest + (factor * rest + factor_rest * sums)
    for shift in (64, 32, 16, 8, 4, 2, 1):
        other = pltpu.roll(value, shift, 1)
        other_rest = pltpu.roll(value_rest, shift, 1)
        value, error = two_sum(value, other)
        value_rest = (value_rest + other_rest) + error
    remaining = jnp.maximum(value + value_rest, 0.0)
    norm = jnp.sqrt(remaining / total_facets + epsilon)
    heads = jnp.where(lane == krylov, norm, 0.0)
    for m in range(krylov):
        heads = jnp.where(lane == m, projections[m], heads)
    hessenberg_ref[...] = heads[:, : krylov + 1]
    wide = [jnp.broadcast_to(p, (8, per_box)) for p in projections]
    scale = jnp.concatenate([1.0 / norm] * (per_box // 128), axis=1)

    def one_box(b, _):
        lanes = pl.ds(pl.multiple_of(b * per_box, per_box), per_box)
        live = wide_row(live_ref, b)
        sent = wide[0] * basis_ref[0, :, lanes]
        for m in range(1, krylov):
            sent += wide[m] * basis_ref[m, :, lanes]
        next_ref[:, lanes] = (image_ref[:, lanes] - sent * live) * scale
        return 0

    lax.fori_loop(0, boxes, one_box, 0, unroll=4)


smem = pl.BlockSpec(memory_space=pltpu.SMEM)
vmem = pl.BlockSpec(memory_space=pltpu.VMEM)


def on_device(
    basis, facet_centres, normals, areas, contrast, facet_counts, box_centres, near_boxes, far_boxes
):
    krylov, rhs_local, facet_local = basis.shape
    boxes = facet_counts.shape[0]
    count = lax.axis_size("box")
    total_facets = count * facet_local
    areas = areas.reshape(-1, 128)
    contrast = contrast.reshape(-1, 128)

    def rows(number, width=128, dtype=f32):
        return jax.ShapeDtypeStruct((number, width), dtype)

    def limit(mebibytes):
        return pltpu.CompilerParams(vmem_limit_bytes=mebibytes * 1024 * 1024)

    sent, first, second, local = pl.pallas_call(
        prep_kernel,
        out_shape=(rows(544, dtype=bf16), rows(400), rows(288, dtype=bf16), rows(528)),
        in_specs=[pl.BlockSpec(memory_space=pl.ANY)] * 6,
        out_specs=(vmem,) * 4,
        scratch_shapes=[
            pltpu.VMEM((512, 128), f32),
            pltpu.SMEM(box_centres.shape, f32),
            pltpu.SMEM(facet_counts.shape, jnp.int32),
            pltpu.VMEM((rhs_local, facet_local), f32),
            pltpu.VMEM(facet_centres.shape, f32),
            pltpu.VMEM(areas.shape, f32),
            pltpu.VMEM(normals.shape, f32),
            pltpu.SemaphoreType.DMA((6,)),
        ],
        name="prepare",
    )(box_centres, facet_counts, basis, facet_centres, areas, normals)
    swap = [(0, 1), (1, 0)]
    ups = range(count - 1)
    cross = lax.ppermute(sent, "rhs", swap)
    first = lax.ppermute(
        first, ("box", "rhs"), [(2 * i, 2 * i + 2) for i in ups] + [(2 * i + 3, 2 * i + 1) for i in ups]
    )
    second = lax.ppermute(
        second, ("box", "rhs"), [(2 * i + 1, 2 * i + 2) for i in ups] + [(2 * i + 2, 2 * i + 1) for i in ups]
    )
    plane_slots = plane_boxes * per_box
    geometry, strengths, targets, planes, local = pl.pallas_call(
        feature_kernel,
        out_shape=(
            rows(boxes * depth, per_box, bf16),
            rows(boxes * 80, per_box, bf16),
            rows(plane_slots, depth, bf16),
            rows(plane_boxes * 8, per_box),
            rows(528),
        ),
        in_specs=[vmem] * 2,
        out_specs=(vmem,) * 5,
        compiler_params=limit(12),
        name="features",
    )(local, sent)
    far = pl.pallas_call(
        far_kernel,
        out_shape=rows(3 * plane_boxes * 16, per_box),
        in_specs=[vmem] * 4,
        out_specs=vmem,
        scratch_shapes=[pltpu.VMEM((6 * 32, 128), f32), pltpu.VMEM((2 * 32, 128), f32)],
        compiler_params=limit(8),
        name="far",
    )(local, cross, first, second)
    mine, theirs = pl.pallas_call(
        field_kernel,
        out_shape=(rows(boxes * 8, per_box),) * 2,
        in_specs=[smem] + [vmem] * 9,
        out_specs=(vmem, vmem),
        scratch_shapes=[
            pltpu.VMEM((plane_boxes * depth, per_box), bf16),
            pltpu.VMEM((plane_boxes * 80, per_box), bf16),
            pltpu.VMEM((3 * plane_boxes * 80, per_box), bf16),
            pltpu.VMEM((plane_boxes * 160, per_box), f32),
            pltpu.VMEM((boxes * 16, per_box), f32),
        ],
        compiler_params=limit(32),
        name="fields",
    )(box_centres, local, cross, first, second, geometry, strengths, targets, planes, far)
    theirs = lax.ppermute(theirs, "rhs", swap)
    gram, live = pl.pallas_call(
        gram_kernel,
        out_shape=(rows(8), rows(2 * boxes)),
        in_specs=[smem, vmem],
        out_specs=(vmem, vmem),
        compiler_params=limit(8),
        name="gram",
    )(facet_counts, basis)
    image, tiles = pl.pallas_call(
        image_kernel,
        out_shape=(rows(rhs_local, facet_local), jax.ShapeDtypeStruct((count, 8, 128), f32)),
        in_specs=[vmem] * 6,
        out_specs=(vmem, vmem),
        compiler_params=limit(8),
        name="image",
    )(mine, theirs, gram, live, contrast, basis)
    tiles = lax.all_to_all(tiles, "box", 0, 0, tiled=True)
    next_vector, hessenberg = pl.pallas_call(
        functools.partial(finish_kernel, total_facets),
        out_shape=(rows(rhs_local, facet_local), rows(rhs_local, krylov + 1)),
        in_specs=[vmem] * 4,
        out_specs=(vmem, vmem),
        compiler_params=limit(16),
        name="finish",
    )(tiles, live, image, basis)
    return next_vector, hessenberg.T


def solution(mesh):
    return jax.shard_map(
        on_device,
        mesh=mesh,
        in_specs=(
            P(None, "rhs", "box"),
            P(None, "box"),
            P(None, "box"),
            P("box"),
            P("box"),
            P("box"),
            P(None, "box"),
            P("box", None),
            P("box", None),
        ),
        out_specs=(P("rhs", "box"), P(None, "rhs")),
        check_vma=False,
    )
```

```python
import functools

import jax
import jax.numpy as jnp
from jax import lax
from jax.experimental import pallas as pl
from jax.experimental.pallas import tpu as pltpu
from jax.sharding import PartitionSpec as P

soften = 0.0025
epsilon = 1e-06
f32 = jnp.float32
bf16 = jnp.bfloat16
plane_boxes = 16
per_box = 256
step_items = 2
depth = 64


def lattice(centres_s, b):
    x = (centres_s[0, b] + 0.5).astype(jnp.int32)
    y = (centres_s[1, b] + 0.5).astype(jnp.int32)
    z = (centres_s[2, b] + 0.5).astype(jnp.int32)
    return x, y, z


def slot_of(centres_s, b):
    x, y, z = lattice(centres_s, b)
    return (z & 1) * plane_boxes + y * 4 + x


def wide_row(ref, b):
    return jnp.concatenate([ref[pl.ds(2 * b, 1), :], ref[pl.ds(2 * b + 1, 1), :]], axis=1)


def live_row(counts_s, b):
    slots = lax.broadcasted_iota(jnp.int32, (1, per_box), 1)
    return (slots < counts_s[b]).astype(f32)


def prep_kernel(
    centres_h, counts_h, basis_h, facets_h, areas_h, normals_h, cross_ref, first_ref, second_ref, local_ref,
    charges_v, centres_s, counts_s, current_ref, facets_ref, areas_ref, normals_ref, arrived
):
    boxes = counts_s.shape[0]
    moves = [
        (basis_h.at[basis_h.shape[0] - 1], current_ref),
        (facets_h, facets_ref),
        (areas_h, areas_ref),
        (normals_h, normals_ref),
        (centres_h, centres_s),
        (counts_h, counts_s),
    ]
    copies = [pltpu.make_async_copy(a, b, arrived.at[k]) for k, (a, b) in enumerate(moves)]
    for copy in copies:
        copy.start()
    for copy in copies:
        copy.wait()
    lane = lax.broadcasted_iota(jnp.int32, (8, 128), 1)
    row = lax.broadcasted_iota(jnp.int32, (8, 128), 0)
    empty = jnp.zeros((2, 128), f32)

    def one_box(b, carry):
        moments, centres = carry
        slot = slot_of(centres_s, b)
        lanes = pl.ds(pl.multiple_of(b * per_box, per_box), per_box)
        facets = facets_ref[:, lanes]
        normals = normals_ref[:, lanes]
        live = live_row(counts_s, b)
        weighted = current_ref[:, lanes] * (wide_row(areas_ref, b) * live / per_box)
        start = pl.multiple_of(slot * 16, 16)
        charges_v[pl.ds(start, 16), :] = jnp.concatenate([weighted[:, :128], weighted[:, 128:]], axis=0)
        local_ref[pl.ds(start, 16), :] = jnp.concatenate(
            [facets[:, :128], facets[:, 128:], empty, normals[:, :128], normals[:, 128:], empty], axis=0
        )
        moments += jnp.where(lane == slot, jnp.sum(weighted, axis=1, keepdims=True), 0.0)
        for a in range(3):
            dipole = jnp.sum(weighted * (facets[a : a + 1] - centres_s[a, b]), axis=1, keepdims=True)
            moments += jnp.where(lane == 32 * (a + 1) + slot, dipole, 0.0)
            centres += jnp.where((lane == slot) & (row == a), centres_s[a, b], 0.0)
        return moments, centres

    zeros = jnp.zeros((8, 128), f32)
    moments, centres = lax.fori_loop(0, boxes, one_box, (zeros, zeros), unroll=4)
    _, _, z = lattice(centres_s, 0)
    base_z = (z - (z & 1)).astype(f32) + 0.5
    centres = jnp.where((row == 3) | (row == 4), 1.5, jnp.where(row == 5, base_z, centres))
    half = lax.axis_index("rhs")
    away = pl.multiple_of((1 - half) * 256, 256)
    here = pl.multiple_of(half * 256, 256)
    pieces = jnp.concatenate([*thirds(moments), zeros], axis=0).astype(bf16)
    cross_ref[:512] = charges_v[...].astype(bf16)
    cross_ref[512:] = pieces
    second_ref[:256] = charges_v[pl.ds(here, 256), :].astype(bf16)
    second_ref[256:] = pieces
    first_ref[:256] = charges_v[pl.ds(away, 256), :].astype(bf16).astype(f32)
    for place in range(plane_boxes):
        first_ref[256 + 8 * place : 264 + 8 * place] = local_ref[pl.ds(away + 16 * place, 8), :]
    first_ref[384:392] = moments
    first_ref[392:] = centres
    local_ref[512:520] = moments
    local_ref[520:] = centres


def thirds(x):
    high = x.astype(bf16).astype(f32)
    rest = x - high
    middle = rest.astype(bf16).astype(f32)
    return high, middle, (rest - middle).astype(bf16).astype(f32)


def stacked_rows(parts, width):
    zeros = jnp.zeros((depth - 8 * len(parts), width), f32)
    return jnp.concatenate([*parts, zeros], axis=0)


def padded(rows):
    return jnp.concatenate([rows, jnp.zeros((8 - rows.shape[0], rows.shape[1]), f32)], axis=0)


def wide_charges(ref, place):
    both = ref[pl.ds(pl.multiple_of(place * 16, 16), 16), :].astype(f32)
    return jnp.concatenate([both[:8], both[8:]], axis=1)


def wide_tile(ref, start):
    tile = ref[pl.ds(pl.multiple_of(start, 8), 8), :]
    return jnp.concatenate([tile[0:3], tile[3:6]], axis=1)


def whole_moments(pieces):
    return pieces[:8] + (pieces[8:16] + pieces[16:24])


def store_geometry(local, box, geometry):
    row = lax.broadcasted_iota(jnp.int32, (8, per_box), 0)
    square = jnp.sum(local * local, axis=0, keepdims=True)
    features = jnp.where(row == 3, square, jnp.where(row == 4, 1.0, local))
    high, middle, low = thirds(features)
    rows = stacked_rows((high, high, high, middle, middle, low), per_box)
    geometry[pl.ds(pl.multiple_of(box * depth, depth), depth), :] = rows.astype(bf16)


def store_strengths(local, charges, box, strengths):
    products = jnp.concatenate([charges * local[a : a + 1] for a in range(3)], axis=0)
    rows = jnp.concatenate([charges, *thirds(products)], axis=0)
    strengths[pl.ds(pl.multiple_of(box * 80, 80), 80), :] = rows.astype(bf16)


def feature_kernel(local_ref, sent_ref, geometry, mine, targets, planes, local_out):
    boxes = 2 * plane_boxes
    half = lax.axis_index("rhs")
    origin = local_ref[523:526, 0:1]
    row = lax.broadcasted_iota(jnp.int32, (8, per_box), 0)

    def source(slot, _):
        local = padded(wide_tile(local_ref, slot * 16) - origin)
        store_geometry(local, slot, geometry)
        store_strengths(local, wide_charges(sent_ref, slot), slot, mine)
        return 0

    lax.fori_loop(0, boxes, source, 0, unroll=4)

    def target(place, _):
        start = (half * plane_boxes + place) * 16
        local = padded(wide_tile(local_ref, start) - origin)
        normal = padded(wide_tile(local_ref, start + 8))
        square = jnp.sum(local * local, axis=0, keepdims=True) + soften
        along = jnp.sum(local * normal, axis=0, keepdims=True)
        distance = jnp.where(row == 3, 1.0, jnp.where(row == 4, square, -2.0 * local))
        high, middle, low = thirds(distance)
        rows = stacked_rows((high, middle, low, high, middle, high), per_box)
        start = pl.multiple_of(place * per_box, per_box)
        targets[pl.ds(start, per_box), :] = jnp.transpose(rows).astype(bf16)
        planes[pl.ds(pl.multiple_of(place * 8, 8), 8), :] = jnp.where(row == 3, along, normal)
        return 0

    lax.fori_loop(0, plane_boxes, target, 0, unroll=4)
    local_out[...] = local_ref[...]


def near_planes(sources, targets, total, beside):
    def near_rows(step, _):
        runs = []
        for item in range(step_items):
            item = step * step_items + item
            target_y = (item + 1) // 3
            source_y = target_y + lax.rem(item + 1, 3) - 1
            for near_x in range(4):
                target = target_y * 4 + near_x
                for source in sources:
                    for x in range(max(near_x - 1, 0), min(near_x + 2, 4)):
                        runs.append((target, source, source_y * 4 + x))

        def rows_at(pair, place, number):
            ref, first = pair
            return ref[pl.ds(pl.multiple_of((first + place) * number, number), number), :]

        def distances(target, source, place):
            facets = targets[pl.ds(pl.multiple_of(target * per_box, per_box), per_box), :]
            return jnp.dot(facets, rows_at(source[0], place, depth), preferred_element_type=f32)

        ahead = distances(*runs[0])
        cubed = []
        given = []
        for i, (target, source, place) in enumerate(runs):
            here = ahead
            if i + 1 < len(runs):
                ahead = distances(*runs[i + 1])
            inverse = lax.rsqrt(here)
            cubed.append((inverse * inverse * inverse).astype(bf16))
            given.append(jnp.concatenate([rows_at(source[1], place, 80), rows_at(source[2], place, 80)], axis=0))
            if i + 1 == len(runs) or runs[i + 1][0] is not target:
                rows_of = pl.ds(pl.multiple_of(target * 160, 160), 160)
                total[rows_of, :] += lax.dot_general(
                    jnp.concatenate(given, axis=1),
                    jnp.concatenate(cubed, axis=1),
                    (((1,), (1,)), ((), ())),
                    preferred_element_type=f32,
                )
                cubed = []
                given = []
        beside(step)
        return 0

    lax.fori_loop(0, 10 // step_items, near_rows, 0)


def field_kernel(
    centres_s, local_ref, cross_ref, first_ref, second_ref, geometry, mine, targets, planes, mine_ref, theirs_ref,
    halo_geometry, halo_mine, theirs, total, far, far_centres, far_moments
):
    boxes = 2 * plane_boxes
    half = lax.axis_index("rhs")
    origin = local_ref[523:526, 0:1]

    def source(slot, _):
        local = wide_tile(local_ref, slot * 16) - origin
        store_strengths(local, wide_charges(cross_ref, slot), slot, theirs)
        return 0

    lax.fori_loop(0, boxes, source, 0, unroll=4)

    def halo_source(place, _):
        local = padded(wide_tile(first_ref, 256 + place * 8) - origin)
        store_geometry(local, place, halo_geometry)
        store_strengths(local, wide_charges(first_ref, place), place, halo_mine)
        store_strengths(local, wide_charges(second_ref, place), boxes + place, theirs)
        return 0

    lax.fori_loop(0, plane_boxes, halo_source, 0, unroll=4)
    total[...] = jnp.zeros_like(total)

    for group, (centres, ours, others) in enumerate(
        (
            (first_ref[392:400], first_ref[384:392], second_ref[256:288]),
            (local_ref[520:528], local_ref[512:520], cross_ref[512:544]),
        )
    ):
        columns = jnp.transpose(jnp.concatenate([centres[:3] - origin, centres[3:]], axis=0))[:32]
        for a in range(3):
            far_centres[(group * 3 + a) * 32 : (group * 3 + a + 1) * 32, :] = jnp.broadcast_to(
                columns[:, a : a + 1], (32, 128)
            )
        both = jnp.concatenate([ours, whole_moments(others.astype(f32))], axis=0)
        high = both.astype(bf16).astype(f32)
        far_moments[group * 32 : group * 32 + 32, :] = jnp.concatenate([high, both - high], axis=0)
    lane = lax.broadcasted_iota(jnp.int32, (1, 128), 1)
    lane_x = lane & 3
    lane_y = (lane >> 2) & 3
    lane_plane = (lane >> 4) & 1

    def far_field(k):
        group = (k >= boxes).astype(jnp.int32)
        slot = jnp.where(k < boxes, k, half * plane_boxes + k - boxes)
        x, y, plane = slot & 3, (slot >> 2) & 3, slot >> 4
        local = wide_tile(local_ref, slot * 16) - origin
        normal = wide_tile(local_ref, slot * 16 + 8)
        d = []
        for a in range(3):
            centre = far_centres[pl.ds(pl.multiple_of((group * 3 + a) * 32, 32), 32), :]
            d.append(local[a : a + 1] - jnp.concatenate([centre, centre], axis=1))
        q = d[0] * d[0] + d[1] * d[1] + d[2] * d[2] + soften
        inverse = lax.rsqrt(q)
        inverse_2 = inverse * inverse
        inverse_3 = inverse_2 * inverse
        t = d[0] * normal[0:1] + d[1] * normal[1:2] + d[2] * normal[2:3]
        single = t * inverse_3
        steep = 3.0 * single * inverse_2
        coefficients = [single] + [steep * d[a] - normal[a : a + 1] * inverse_3 for a in range(3)]
        whole = jnp.concatenate(coefficients, axis=0)
        upper = whole.astype(bf16)
        lower = (whole - upper.astype(f32)).astype(bf16)
        lane_z = lane_plane + jnp.where(group == 0, 4 * half - 2, 0)
        near = (jnp.abs(lane_x - x) <= 1) & (jnp.abs(lane_y - y) <= 1) & (jnp.abs(lane_z - plane) <= 1)
        picked = jnp.where(near, 0.0, far_moments[pl.ds(pl.multiple_of(group * 32, 32), 32), :]).astype(bf16)
        first = jnp.dot(picked, upper, preferred_element_type=f32)
        second = jnp.dot(picked, lower, preferred_element_type=f32)
        return first[:16] + first[16:] + second[:16]

    def far_boxes(step):
        for i in range(5 * step_items):
            k = jnp.minimum(step * 5 * step_items + i, 3 * plane_boxes - 1)
            far[pl.ds(pl.multiple_of(k * 16, 16), 16), :] = far_field(k)

    sources = [((geometry, p), (mine, p), (theirs, p)) for p in (0, plane_boxes)]
    sources.append(((halo_geometry, 0), (halo_mine, 0), (theirs, boxes)))
    near_planes(sources, targets, total, far_boxes)

    def near_field(place, _):
        sums = total[pl.ds(pl.multiple_of(place * 160, 160), 160), :]
        side = planes[pl.ds(pl.multiple_of(place * 8, 8), 8), :]
        values = []
        for start in (0, 80):
            value = side[3:4] * sums[start : start + 8]
            for a in range(3):
                high, middle, low = (sums[i : i + 8] for i in range(start + 8 + 8 * a, start + 80, 24))
                value = value - side[a : a + 1] * (high + (middle + low))
            values.append(value)
        value = jnp.concatenate(values, axis=0)
        slot = half * plane_boxes + place
        rows = pl.ds(pl.multiple_of(slot * 16, 16), 16)
        far[rows, :] += value + far[pl.ds(pl.multiple_of((boxes + place) * 16, 16), 16), :]
        return 0

    lax.fori_loop(0, plane_boxes, near_field, 0, unroll=4)

    def given_back(b, _):
        start = pl.multiple_of(slot_of(centres_s, b) * 16, 16)
        rows = pl.ds(pl.multiple_of(b * 8, 8), 8)
        mine_ref[rows, :] = far[pl.ds(start, 8), :]
        theirs_ref[rows, :] = far[pl.ds(start + 8, 8), :]
        return 0

    lax.fori_loop(0, boxes, given_back, 0, unroll=4)


def gram_kernel(counts_s, basis_ref, sums_ref, live_ref):
    krylov = basis_ref.shape[0]
    pairs = [(m, n) for m in range(krylov) for n in range(m + 1)]

    def one_box(b, carry):
        lanes = pl.ds(pl.multiple_of(b * per_box, per_box), per_box)
        live = live_row(counts_s, b)
        live_ref[pl.ds(2 * b, 1), :] = live[:, :128]
        live_ref[pl.ds(2 * b + 1, 1), :] = live[:, 128:]
        rows = [basis_ref[m, :, lanes] * live for m in range(krylov)]
        out = []
        for k, (m, n) in enumerate(pairs):
            product = rows[m] * rows[n]
            out.append(carry[k] + product[:, :128] + product[:, 128:])
        return tuple(out)

    zeros = jnp.zeros((8, 128), f32)
    gram = lax.fori_loop(0, counts_s.shape[0], one_box, (zeros,) * len(pairs))
    lane = lax.broadcasted_iota(jnp.int32, (8, 128), 1)
    total = zeros
    for k, value in enumerate(gram):
        total = jnp.where(lane == krylov + 1 + k, jnp.sum(value, axis=1, keepdims=True), total)
    sums_ref[...] = total


def image_kernel(mine_ref, theirs_ref, gram_ref, live_ref, contrast_ref, basis_ref, image_ref, sums_ref):
    krylov = basis_ref.shape[0]

    def one_box(b, carry):
        lanes = pl.ds(pl.multiple_of(b * per_box, per_box), per_box)
        rows = pl.ds(pl.multiple_of(b * 8, 8), 8)
        live = wide_row(live_ref, b)
        part = mine_ref[rows, :] + theirs_ref[rows, :]
        image = live * (basis_ref[krylov - 1, :, lanes] - 2.0 * wide_row(contrast_ref, b) * part)
        image_ref[:, lanes] = image
        sums = []
        for m in range(krylov + 1):
            product = image * (basis_ref[m, :, lanes] if m < krylov else image)
            sums.append(carry[m] + product[:, :128] + product[:, 128:])
        return tuple(sums)

    zeros = jnp.zeros((8, 128), f32)
    sums = lax.fori_loop(0, live_ref.shape[0] // 2, one_box, (zeros,) * (krylov + 1), unroll=4)
    lane = lax.broadcasted_iota(jnp.int32, (8, 128), 1)
    total = gram_ref[...]
    for k, value in enumerate(sums):
        total = jnp.where(lane == k, jnp.sum(value, axis=1, keepdims=True), total)
    sums_ref[...] = jnp.broadcast_to(total[None], sums_ref.shape)


def two_sum(a, b):
    s = a + b
    c = s - a
    return s, (a - (s - c)) + (b - c)


def halves(a):
    c = a * 4097.0
    high = c - (c - a)
    return high, a - high


def two_product(a, b):
    p = a * b
    a_high, a_low = halves(a)
    b_high, b_low = halves(b)
    return p, ((a_high * b_high - p) + a_high * b_low + a_low * b_high) + a_low * b_low


def finish_kernel(total_facets, tiles_ref, live_ref, image_ref, basis_ref, next_ref, hessenberg_ref):
    boxes = live_ref.shape[0] // 2
    krylov = basis_ref.shape[0]
    lane = lax.broadcasted_iota(jnp.int32, (8, 128), 1)

    sums, rest = tiles_ref[0], jnp.zeros((8, 128), f32)
    for i in range(1, tiles_ref.shape[0]):
        sums, error = two_sum(sums, tiles_ref[i])
        rest = rest + error
    exact = sums + rest
    projections = [exact[:, m : m + 1] / total_facets for m in range(krylov)]
    pairs = [(m, n) for m in range(krylov) for n in range(m + 1)]
    first = jnp.where(lane == krylov, 1.0, 0.0)
    second = jnp.where(lane <= krylov, 1.0, 0.0)
    for m in range(krylov):
        first = jnp.where(lane == m, -2.0 * projections[m], first)
    for k, (m, n) in enumerate(pairs):
        at = lane == krylov + 1 + k
        scale = 1.0 if m == n else 2.0
        first = jnp.where(at, scale * projections[m], first)
        second = jnp.where(at, projections[n], second)
    factor, factor_rest = two_product(first, second)
    value, value_rest = two_product(factor, sums)
    value_rest = value_rest + (factor * rest + factor_rest * sums)
    for shift in (64, 32, 16, 8, 4, 2, 1):
        other = pltpu.roll(value, shift, 1)
        other_rest = pltpu.roll(value_rest, shift, 1)
        value, error = two_sum(value, other)
        value_rest = (value_rest + other_rest) + error
    remaining = jnp.maximum(value + value_rest, 0.0)
    norm = jnp.sqrt(remaining / total_facets + epsilon)
    heads = jnp.where(lane == krylov, norm, 0.0)
    for m in range(krylov):
        heads = jnp.where(lane == m, projections[m], heads)
    hessenberg_ref[...] = heads[:, : krylov + 1]
    wide = [jnp.broadcast_to(p, (8, per_box)) for p in projections]
    scale = jnp.concatenate([1.0 / norm] * (per_box // 128), axis=1)

    def one_box(b, _):
        lanes = pl.ds(pl.multiple_of(b * per_box, per_box), per_box)
        live = wide_row(live_ref, b)
        sent = wide[0] * basis_ref[0, :, lanes]
        for m in range(1, krylov):
            sent += wide[m] * basis_ref[m, :, lanes]
        next_ref[:, lanes] = (image_ref[:, lanes] - sent * live) * scale
        return 0

    lax.fori_loop(0, boxes, one_box, 0, unroll=4)


smem = pl.BlockSpec(memory_space=pltpu.SMEM)
vmem = pl.BlockSpec(memory_space=pltpu.VMEM)


def on_device(
    basis, facet_centres, normals, areas, contrast, facet_counts, box_centres, near_boxes, far_boxes
):
    krylov, rhs_local, facet_local = basis.shape
    boxes = facet_counts.shape[0]
    count = lax.axis_size("box")
    total_facets = count * facet_local
    areas = areas.reshape(-1, 128)
    contrast = contrast.reshape(-1, 128)

    def rows(number, width=128, dtype=f32):
        return jax.ShapeDtypeStruct((number, width), dtype)

    def limit(mebibytes):
        return pltpu.CompilerParams(vmem_limit_bytes=mebibytes * 1024 * 1024)

    sent, first, second, local = pl.pallas_call(
        prep_kernel,
        out_shape=(rows(544, dtype=bf16), rows(400), rows(288, dtype=bf16), rows(528)),
        in_specs=[pl.BlockSpec(memory_space=pl.ANY)] * 6,
        out_specs=(vmem,) * 4,
        scratch_shapes=[
            pltpu.VMEM((512, 128), f32),
            pltpu.SMEM(box_centres.shape, f32),
            pltpu.SMEM(facet_counts.shape, jnp.int32),
            pltpu.VMEM((rhs_local, facet_local), f32),
            pltpu.VMEM(facet_centres.shape, f32),
            pltpu.VMEM(areas.shape, f32),
            pltpu.VMEM(normals.shape, f32),
            pltpu.SemaphoreType.DMA((6,)),
        ],
        name="prepare",
    )(box_centres, facet_counts, basis, facet_centres, areas, normals)
    swap = [(0, 1), (1, 0)]
    ups = range(count - 1)
    cross = lax.ppermute(sent, "rhs", swap)
    first = lax.ppermute(
        first, ("box", "rhs"), [(2 * i, 2 * i + 2) for i in ups] + [(2 * i + 3, 2 * i + 1) for i in ups]
    )
    second = lax.ppermute(
        second, ("box", "rhs"), [(2 * i + 1, 2 * i + 2) for i in ups] + [(2 * i + 2, 2 * i + 1) for i in ups]
    )
    plane_slots = plane_boxes * per_box
    geometry, strengths, targets, planes, local = pl.pallas_call(
        feature_kernel,
        out_shape=(
            rows(boxes * depth, per_box, bf16),
            rows(boxes * 80, per_box, bf16),
            rows(plane_slots, depth, bf16),
            rows(plane_boxes * 8, per_box),
            rows(528),
        ),
        in_specs=[vmem] * 2,
        out_specs=(vmem,) * 5,
        compiler_params=limit(12),
        name="features",
    )(local, sent)
    mine, theirs = pl.pallas_call(
        field_kernel,
        out_shape=(rows(boxes * 8, per_box),) * 2,
        in_specs=[smem] + [vmem] * 8,
        out_specs=(vmem, vmem),
        scratch_shapes=[
            pltpu.VMEM((plane_boxes * depth, per_box), bf16),
            pltpu.VMEM((plane_boxes * 80, per_box), bf16),
            pltpu.VMEM((3 * plane_boxes * 80, per_box), bf16),
            pltpu.VMEM((plane_boxes * 160, per_box), f32),
            pltpu.VMEM((3 * plane_boxes * 16, per_box), f32),
            pltpu.VMEM((6 * 32, 128), f32),
            pltpu.VMEM((2 * 32, 128), f32),
        ],
        compiler_params=limit(32),
        name="fields",
    )(box_centres, local, cross, first, second, geometry, strengths, targets, planes)
    theirs = lax.ppermute(theirs, "rhs", swap)
    gram, live = pl.pallas_call(
        gram_kernel,
        out_shape=(rows(8), rows(2 * boxes)),
        in_specs=[smem, vmem],
        out_specs=(vmem, vmem),
        compiler_params=limit(8),
        name="gram",
    )(facet_counts, basis)
    image, tiles = pl.pallas_call(
        image_kernel,
        out_shape=(rows(rhs_local, facet_local), jax.ShapeDtypeStruct((count, 8, 128), f32)),
        in_specs=[vmem] * 6,
        out_specs=(vmem, vmem),
        compiler_params=limit(8),
        name="image",
    )(mine, theirs, gram, live, contrast, basis)
    tiles = lax.all_to_all(tiles, "box", 0, 0, tiled=True)
    next_vector, hessenberg = pl.pallas_call(
        functools.partial(finish_kernel, total_facets),
        out_shape=(rows(rhs_local, facet_local), rows(rhs_local, krylov + 1)),
        in_specs=[vmem] * 4,
        out_specs=(vmem, vmem),
        compiler_params=limit(16),
        name="finish",
    )(tiles, live, image, basis)
    return next_vector, hessenberg.T


def solution(mesh):
    return jax.shard_map(
        on_device,
        mesh=mesh,
        in_specs=(
            P(None, "rhs", "box"),
            P(None, "box"),
            P(None, "box"),
            P("box"),
            P("box"),
            P("box"),
            P(None, "box"),
            P("box", None),
            P("box", None),
        ),
        out_specs=(P("rhs", "box"), P(None, "rhs")),
        check_vma=False,
    )
```

```python
import functools

import jax
import jax.numpy as jnp
from jax import lax
from jax.experimental import pallas as pl
from jax.experimental.pallas import tpu as pltpu
from jax.sharding import PartitionSpec as P

soften = 0.0025
epsilon = 1e-06
f32 = jnp.float32
bf16 = jnp.bfloat16
plane_boxes = 16
per_box = 256
depth = 64


def lattice(centres_s, b):
    x = (centres_s[0, b] + 0.5).astype(jnp.int32)
    y = (centres_s[1, b] + 0.5).astype(jnp.int32)
    z = (centres_s[2, b] + 0.5).astype(jnp.int32)
    return x, y, z


def slot_of(centres_s, b):
    x, y, z = lattice(centres_s, b)
    return (z & 1) * plane_boxes + y * 4 + x


def wide_row(ref, b):
    return jnp.concatenate([ref[pl.ds(2 * b, 1), :], ref[pl.ds(2 * b + 1, 1), :]], axis=1)


def live_row(counts_s, b):
    slots = lax.broadcasted_iota(jnp.int32, (1, per_box), 1)
    return (slots < counts_s[b]).astype(f32)


def prep_kernel(
    centres_h, counts_h, basis_h, facets_h, areas_h, normals_h, cross_ref, first_ref, second_ref, local_ref,
    charges_v, centres_s, counts_s, current_ref, facets_ref, areas_ref, normals_ref, arrived
):
    boxes = counts_s.shape[0]
    moves = [
        (basis_h.at[basis_h.shape[0] - 1], current_ref),
        (facets_h, facets_ref),
        (areas_h, areas_ref),
        (normals_h, normals_ref),
        (centres_h, centres_s),
        (counts_h, counts_s),
    ]
    copies = [pltpu.make_async_copy(a, b, arrived.at[k]) for k, (a, b) in enumerate(moves)]
    for copy in copies:
        copy.start()
    for copy in copies:
        copy.wait()
    lane = lax.broadcasted_iota(jnp.int32, (8, 128), 1)
    row = lax.broadcasted_iota(jnp.int32, (8, 128), 0)
    empty = jnp.zeros((2, 128), f32)

    def one_box(b, carry):
        moments, centres = carry
        slot = slot_of(centres_s, b)
        lanes = pl.ds(pl.multiple_of(b * per_box, per_box), per_box)
        facets = facets_ref[:, lanes]
        normals = normals_ref[:, lanes]
        live = live_row(counts_s, b)
        weighted = current_ref[:, lanes] * (wide_row(areas_ref, b) * live / per_box)
        start = pl.multiple_of(slot * 16, 16)
        charges_v[pl.ds(start, 16), :] = jnp.concatenate([weighted[:, :128], weighted[:, 128:]], axis=0)
        local_ref[pl.ds(start, 16), :] = jnp.concatenate(
            [facets[:, :128], facets[:, 128:], empty, normals[:, :128], normals[:, 128:], empty], axis=0
        )
        moments += jnp.where(lane == slot, jnp.sum(weighted, axis=1, keepdims=True), 0.0)
        for a in range(3):
            dipole = jnp.sum(weighted * (facets[a : a + 1] - centres_s[a, b]), axis=1, keepdims=True)
            moments += jnp.where(lane == 32 * (a + 1) + slot, dipole, 0.0)
            centres += jnp.where((lane == slot) & (row == a), centres_s[a, b], 0.0)
        return moments, centres

    zeros = jnp.zeros((8, 128), f32)
    moments, centres = lax.fori_loop(0, boxes, one_box, (zeros, zeros), unroll=4)
    _, _, z = lattice(centres_s, 0)
    base_z = (z - (z & 1)).astype(f32) + 0.5
    centres = jnp.where((row == 3) | (row == 4), 1.5, jnp.where(row == 5, base_z, centres))
    half = lax.axis_index("rhs")
    away = pl.multiple_of((1 - half) * 256, 256)
    here = pl.multiple_of(half * 256, 256)
    pieces = jnp.concatenate([*thirds(moments), zeros], axis=0).astype(bf16)
    cross_ref[:512] = charges_v[...].astype(bf16)
    cross_ref[512:] = pieces
    second_ref[:256] = charges_v[pl.ds(here, 256), :].astype(bf16)
    second_ref[256:] = pieces
    first_ref[:256] = charges_v[pl.ds(away, 256), :].astype(bf16).astype(f32)
    for place in range(plane_boxes):
        first_ref[256 + 8 * place : 264 + 8 * place] = local_ref[pl.ds(away + 16 * place, 8), :]
    first_ref[384:392] = moments
    first_ref[392:] = centres
    local_ref[512:520] = moments
    local_ref[520:] = centres


def thirds(x):
    high = x.astype(bf16).astype(f32)
    rest = x - high
    middle = rest.astype(bf16).astype(f32)
    return high, middle, (rest - middle).astype(bf16).astype(f32)


def stacked_rows(parts, width):
    zeros = jnp.zeros((depth - 8 * len(parts), width), f32)
    return jnp.concatenate([*parts, zeros], axis=0)


def padded(rows):
    return jnp.concatenate([rows, jnp.zeros((8 - rows.shape[0], rows.shape[1]), f32)], axis=0)


def wide_charges(ref, place):
    both = ref[pl.ds(pl.multiple_of(place * 16, 16), 16), :].astype(f32)
    return jnp.concatenate([both[:8], both[8:]], axis=1)


def wide_tile(ref, start):
    tile = ref[pl.ds(pl.multiple_of(start, 8), 8), :]
    return jnp.concatenate([tile[0:3], tile[3:6]], axis=1)


def whole_moments(pieces):
    return pieces[:8] + (pieces[8:16] + pieces[16:24])


def store_geometry(local, box, geometry):
    row = lax.broadcasted_iota(jnp.int32, (8, per_box), 0)
    square = jnp.sum(local * local, axis=0, keepdims=True)
    features = jnp.where(row == 3, square, jnp.where(row == 4, 1.0, local))
    high, middle, low = thirds(features)
    rows = stacked_rows((high, high, high, middle, middle, low), per_box)
    geometry[pl.ds(pl.multiple_of(box * depth, depth), depth), :] = rows.astype(bf16)


def store_strengths(local, charges, box, strengths):
    products = jnp.concatenate([charges * local[a : a + 1] for a in range(3)], axis=0)
    rows = jnp.concatenate([charges, *thirds(products)], axis=0)
    strengths[pl.ds(pl.multiple_of(box * 80, 80), 80), :] = rows.astype(bf16)


def feature_kernel(local_ref, sent_ref, geometry, mine, targets, planes, local_out):
    boxes = 2 * plane_boxes
    half = lax.axis_index("rhs")
    origin = local_ref[523:526, 0:1]
    row = lax.broadcasted_iota(jnp.int32, (8, per_box), 0)

    def source(slot, _):
        local = padded(wide_tile(local_ref, slot * 16) - origin)
        store_geometry(local, slot, geometry)
        store_strengths(local, wide_charges(sent_ref, slot), slot, mine)
        return 0

    lax.fori_loop(0, boxes, source, 0, unroll=4)

    def target(place, _):
        start = (half * plane_boxes + place) * 16
        local = padded(wide_tile(local_ref, start) - origin)
        normal = padded(wide_tile(local_ref, start + 8))
        square = jnp.sum(local * local, axis=0, keepdims=True) + soften
        along = jnp.sum(local * normal, axis=0, keepdims=True)
        distance = jnp.where(row == 3, 1.0, jnp.where(row == 4, square, -2.0 * local))
        high, middle, low = thirds(distance)
        rows = stacked_rows((high, middle, low, high, middle, high), per_box)
        start = pl.multiple_of(place * per_box, per_box)
        targets[pl.ds(start, per_box), :] = jnp.transpose(rows).astype(bf16)
        planes[pl.ds(pl.multiple_of(place * 8, 8), 8), :] = jnp.where(row == 3, along, normal)
        return 0

    lax.fori_loop(0, plane_boxes, target, 0, unroll=4)
    local_out[...] = local_ref[...]


def near_planes(sources, targets, total, beside):
    def near_rows(item, _):
        target_y = (item + 1) // 3
        source_y = target_y + lax.rem(item + 1, 3) - 1
        runs = []
        for near_x in range(4):
            for source in sources:
                for x in range(max(near_x - 1, 0), min(near_x + 2, 4)):
                    runs.append((near_x, source, source_y * 4 + x))

        def rows_at(pair, place, number):
            ref, first = pair
            return ref[pl.ds(pl.multiple_of((first + place) * number, number), number), :]

        def distances(near_x, source, place):
            start = pl.multiple_of((target_y * 4 + near_x) * per_box, per_box)
            weights = rows_at(source[0], place, depth)
            return jnp.dot(targets[pl.ds(start, per_box), :], weights, preferred_element_type=f32)

        ahead = distances(*runs[0])
        cubed = []
        given = []
        part = None
        for i, (near_x, source, place) in enumerate(runs):
            here = ahead
            if i + 1 < len(runs):
                ahead = distances(*runs[i + 1])
            inverse = lax.rsqrt(here)
            cubed.append((inverse * inverse * inverse).astype(bf16))
            given.append(jnp.concatenate([rows_at(source[1], place, 80), rows_at(source[2], place, 80)], axis=0))
            last = i + 1 == len(runs) or runs[i + 1][0] != near_x
            if last or runs[i + 1][1] is not source:
                sums = lax.dot_general(
                    jnp.concatenate(given, axis=1),
                    jnp.concatenate(cubed, axis=1),
                    (((1,), (1,)), ((), ())),
                    preferred_element_type=f32,
                )
                part = sums if part is None else part + sums
                cubed = []
                given = []
            if last:
                total[pl.ds(pl.multiple_of((target_y * 4 + near_x) * 160, 160), 160), :] += part
                part = None
        beside(item)
        return 0

    lax.fori_loop(0, 10, near_rows, 0)


def field_kernel(
    centres_s, local_ref, cross_ref, first_ref, second_ref, geometry, mine, targets, planes, mine_ref, theirs_ref,
    halo_geometry, halo_mine, theirs, total, far, far_centres, far_moments
):
    boxes = 2 * plane_boxes
    half = lax.axis_index("rhs")
    origin = local_ref[523:526, 0:1]

    def source(slot, _):
        local = wide_tile(local_ref, slot * 16) - origin
        store_strengths(local, wide_charges(cross_ref, slot), slot, theirs)
        return 0

    lax.fori_loop(0, boxes, source, 0, unroll=4)

    def halo_source(place, _):
        local = padded(wide_tile(first_ref, 256 + place * 8) - origin)
        store_geometry(local, place, halo_geometry)
        store_strengths(local, wide_charges(first_ref, place), place, halo_mine)
        store_strengths(local, wide_charges(second_ref, place), boxes + place, theirs)
        return 0

    lax.fori_loop(0, plane_boxes, halo_source, 0, unroll=4)
    total[...] = jnp.zeros_like(total)

    for group, (centres, ours, others) in enumerate(
        (
            (first_ref[392:400], first_ref[384:392], second_ref[256:288]),
            (local_ref[520:528], local_ref[512:520], cross_ref[512:544]),
        )
    ):
        columns = jnp.transpose(jnp.concatenate([centres[:3] - origin, centres[3:]], axis=0))[:32]
        for a in range(3):
            far_centres[(group * 3 + a) * 32 : (group * 3 + a + 1) * 32, :] = jnp.broadcast_to(
                columns[:, a : a + 1], (32, 128)
            )
        both = jnp.concatenate([ours, whole_moments(others.astype(f32))], axis=0)
        high = both.astype(bf16).astype(f32)
        far_moments[group * 32 : group * 32 + 32, :] = jnp.concatenate([high, both - high], axis=0)
    lane = lax.broadcasted_iota(jnp.int32, (1, 128), 1)
    lane_x = lane & 3
    lane_y = (lane >> 2) & 3
    lane_plane = (lane >> 4) & 1

    def far_field(k):
        group = (k >= boxes).astype(jnp.int32)
        slot = jnp.where(k < boxes, k, half * plane_boxes + k - boxes)
        x, y, plane = slot & 3, (slot >> 2) & 3, slot >> 4
        local = wide_tile(local_ref, slot * 16) - origin
        normal = wide_tile(local_ref, slot * 16 + 8)
        d = []
        for a in range(3):
            centre = far_centres[pl.ds(pl.multiple_of((group * 3 + a) * 32, 32), 32), :]
            d.append(local[a : a + 1] - jnp.concatenate([centre, centre], axis=1))
        q = d[0] * d[0] + d[1] * d[1] + d[2] * d[2] + soften
        inverse = lax.rsqrt(q)
        inverse_2 = inverse * inverse
        inverse_3 = inverse_2 * inverse
        t = d[0] * normal[0:1] + d[1] * normal[1:2] + d[2] * normal[2:3]
        single = t * inverse_3
        steep = 3.0 * single * inverse_2
        coefficients = [single] + [steep * d[a] - normal[a : a + 1] * inverse_3 for a in range(3)]
        whole = jnp.concatenate(coefficients, axis=0)
        upper = whole.astype(bf16)
        lower = (whole - upper.astype(f32)).astype(bf16)
        lane_z = lane_plane + jnp.where(group == 0, 4 * half - 2, 0)
        near = (jnp.abs(lane_x - x) <= 1) & (jnp.abs(lane_y - y) <= 1) & (jnp.abs(lane_z - plane) <= 1)
        picked = jnp.where(near, 0.0, far_moments[pl.ds(pl.multiple_of(group * 32, 32), 32), :]).astype(bf16)
        first = jnp.dot(picked, upper, preferred_element_type=f32)
        second = jnp.dot(picked, lower, preferred_element_type=f32)
        return first[:16] + first[16:] + second[:16]

    def far_boxes(item):
        for i in range(5):
            k = jnp.minimum(item * 5 + i, 3 * plane_boxes - 1)
            far[pl.ds(pl.multiple_of(k * 16, 16), 16), :] = far_field(k)

    sources = [((geometry, p), (mine, p), (theirs, p)) for p in (0, plane_boxes)]
    sources.append(((halo_geometry, 0), (halo_mine, 0), (theirs, boxes)))
    near_planes(sources, targets, total, far_boxes)

    def near_field(place, _):
        sums = total[pl.ds(pl.multiple_of(place * 160, 160), 160), :]
        side = planes[pl.ds(pl.multiple_of(place * 8, 8), 8), :]
        values = []
        for start in (0, 80):
            value = side[3:4] * sums[start : start + 8]
            for a in range(3):
                high, middle, low = (sums[i : i + 8] for i in range(start + 8 + 8 * a, start + 80, 24))
                value = value - side[a : a + 1] * (high + (middle + low))
            values.append(value)
        value = jnp.concatenate(values, axis=0)
        slot = half * plane_boxes + place
        rows = pl.ds(pl.multiple_of(slot * 16, 16), 16)
        far[rows, :] += value + far[pl.ds(pl.multiple_of((boxes + place) * 16, 16), 16), :]
        return 0

    lax.fori_loop(0, plane_boxes, near_field, 0, unroll=4)

    def given_back(b, _):
        start = pl.multiple_of(slot_of(centres_s, b) * 16, 16)
        rows = pl.ds(pl.multiple_of(b * 8, 8), 8)
        mine_ref[rows, :] = far[pl.ds(start, 8), :]
        theirs_ref[rows, :] = far[pl.ds(start + 8, 8), :]
        return 0

    lax.fori_loop(0, boxes, given_back, 0, unroll=4)


def gram_kernel(counts_s, basis_ref, sums_ref, live_ref):
    krylov = basis_ref.shape[0]
    pairs = [(m, n) for m in range(krylov) for n in range(m + 1)]

    def one_box(b, carry):
        lanes = pl.ds(pl.multiple_of(b * per_box, per_box), per_box)
        live = live_row(counts_s, b)
        live_ref[pl.ds(2 * b, 1), :] = live[:, :128]
        live_ref[pl.ds(2 * b + 1, 1), :] = live[:, 128:]
        rows = [basis_ref[m, :, lanes] * live for m in range(krylov)]
        out = []
        for k, (m, n) in enumerate(pairs):
            product = rows[m] * rows[n]
            out.append(carry[k] + product[:, :128] + product[:, 128:])
        return tuple(out)

    zeros = jnp.zeros((8, 128), f32)
    gram = lax.fori_loop(0, counts_s.shape[0], one_box, (zeros,) * len(pairs))
    lane = lax.broadcasted_iota(jnp.int32, (8, 128), 1)
    total = zeros
    for k, value in enumerate(gram):
        total = jnp.where(lane == krylov + 1 + k, jnp.sum(value, axis=1, keepdims=True), total)
    sums_ref[...] = total


def image_kernel(mine_ref, theirs_ref, gram_ref, live_ref, contrast_ref, basis_ref, image_ref, sums_ref):
    krylov = basis_ref.shape[0]

    def one_box(b, carry):
        lanes = pl.ds(pl.multiple_of(b * per_box, per_box), per_box)
        rows = pl.ds(pl.multiple_of(b * 8, 8), 8)
        live = wide_row(live_ref, b)
        part = mine_ref[rows, :] + theirs_ref[rows, :]
        image = live * (basis_ref[krylov - 1, :, lanes] - 2.0 * wide_row(contrast_ref, b) * part)
        image_ref[:, lanes] = image
        sums = []
        for m in range(krylov + 1):
            product = image * (basis_ref[m, :, lanes] if m < krylov else image)
            sums.append(carry[m] + product[:, :128] + product[:, 128:])
        return tuple(sums)

    zeros = jnp.zeros((8, 128), f32)
    sums = lax.fori_loop(0, live_ref.shape[0] // 2, one_box, (zeros,) * (krylov + 1), unroll=4)
    lane = lax.broadcasted_iota(jnp.int32, (8, 128), 1)
    total = gram_ref[...]
    for k, value in enumerate(sums):
        total = jnp.where(lane == k, jnp.sum(value, axis=1, keepdims=True), total)
    sums_ref[...] = jnp.broadcast_to(total[None], sums_ref.shape)


def two_sum(a, b):
    s = a + b
    c = s - a
    return s, (a - (s - c)) + (b - c)


def halves(a):
    c = a * 4097.0
    high = c - (c - a)
    return high, a - high


def two_product(a, b):
    p = a * b
    a_high, a_low = halves(a)
    b_high, b_low = halves(b)
    return p, ((a_high * b_high - p) + a_high * b_low + a_low * b_high) + a_low * b_low


def finish_kernel(total_facets, tiles_ref, live_ref, image_ref, basis_ref, next_ref, hessenberg_ref):
    boxes = live_ref.shape[0] // 2
    krylov = basis_ref.shape[0]
    lane = lax.broadcasted_iota(jnp.int32, (8, 128), 1)

    sums, rest = tiles_ref[0], jnp.zeros((8, 128), f32)
    for i in range(1, tiles_ref.shape[0]):
        sums, error = two_sum(sums, tiles_ref[i])
        rest = rest + error
    exact = sums + rest
    projections = [exact[:, m : m + 1] / total_facets for m in range(krylov)]
    pairs = [(m, n) for m in range(krylov) for n in range(m + 1)]
    first = jnp.where(lane == krylov, 1.0, 0.0)
    second = jnp.where(lane <= krylov, 1.0, 0.0)
    for m in range(krylov):
        first = jnp.where(lane == m, -2.0 * projections[m], first)
    for k, (m, n) in enumerate(pairs):
        at = lane == krylov + 1 + k
        scale = 1.0 if m == n else 2.0
        first = jnp.where(at, scale * projections[m], first)
        second = jnp.where(at, projections[n], second)
    factor, factor_rest = two_product(first, second)
    value, value_rest = two_product(factor, sums)
    value_rest = value_rest + (factor * rest + factor_rest * sums)
    for shift in (64, 32, 16, 8, 4, 2, 1):
        other = pltpu.roll(value, shift, 1)
        other_rest = pltpu.roll(value_rest, shift, 1)
        value, error = two_sum(value, other)
        value_rest = (value_rest + other_rest) + error
    remaining = jnp.maximum(value + value_rest, 0.0)
    norm = jnp.sqrt(remaining / total_facets + epsilon)
    heads = jnp.where(lane == krylov, norm, 0.0)
    for m in range(krylov):
        heads = jnp.where(lane == m, projections[m], heads)
    hessenberg_ref[...] = heads[:, : krylov + 1]
    wide = [jnp.broadcast_to(p, (8, per_box)) for p in projections]
    scale = jnp.concatenate([1.0 / norm] * (per_box // 128), axis=1)

    def one_box(b, _):
        lanes = pl.ds(pl.multiple_of(b * per_box, per_box), per_box)
        live = wide_row(live_ref, b)
        sent = wide[0] * basis_ref[0, :, lanes]
        for m in range(1, krylov):
            sent += wide[m] * basis_ref[m, :, lanes]
        next_ref[:, lanes] = (image_ref[:, lanes] - sent * live) * scale
        return 0

    lax.fori_loop(0, boxes, one_box, 0, unroll=4)


smem = pl.BlockSpec(memory_space=pltpu.SMEM)
vmem = pl.BlockSpec(memory_space=pltpu.VMEM)


def on_device(
    basis, facet_centres, normals, areas, contrast, facet_counts, box_centres, near_boxes, far_boxes
):
    krylov, rhs_local, facet_local = basis.shape
    boxes = facet_counts.shape[0]
    count = lax.axis_size("box")
    total_facets = count * facet_local
    areas = areas.reshape(-1, 128)
    contrast = contrast.reshape(-1, 128)

    def rows(number, width=128, dtype=f32):
        return jax.ShapeDtypeStruct((number, width), dtype)

    def limit(mebibytes):
        return pltpu.CompilerParams(vmem_limit_bytes=mebibytes * 1024 * 1024)

    sent, first, second, local = pl.pallas_call(
        prep_kernel,
        out_shape=(rows(544, dtype=bf16), rows(400), rows(288, dtype=bf16), rows(528)),
        in_specs=[pl.BlockSpec(memory_space=pl.ANY)] * 6,
        out_specs=(vmem,) * 4,
        scratch_shapes=[
            pltpu.VMEM((512, 128), f32),
            pltpu.SMEM(box_centres.shape, f32),
            pltpu.SMEM(facet_counts.shape, jnp.int32),
            pltpu.VMEM((rhs_local, facet_local), f32),
            pltpu.VMEM(facet_centres.shape, f32),
            pltpu.VMEM(areas.shape, f32),
            pltpu.VMEM(normals.shape, f32),
            pltpu.SemaphoreType.DMA((6,)),
        ],
        name="prepare",
    )(box_centres, facet_counts, basis, facet_centres, areas, normals)
    swap = [(0, 1), (1, 0)]
    ups = range(count - 1)
    cross = lax.ppermute(sent, "rhs", swap)
    first = lax.ppermute(
        first, ("box", "rhs"), [(2 * i, 2 * i + 2) for i in ups] + [(2 * i + 3, 2 * i + 1) for i in ups]
    )
    second = lax.ppermute(
        second, ("box", "rhs"), [(2 * i + 1, 2 * i + 2) for i in ups] + [(2 * i + 2, 2 * i + 1) for i in ups]
    )
    plane_slots = plane_boxes * per_box
    geometry, strengths, targets, planes, local = pl.pallas_call(
        feature_kernel,
        out_shape=(
            rows(boxes * depth, per_box, bf16),
            rows(boxes * 80, per_box, bf16),
            rows(plane_slots, depth, bf16),
            rows(plane_boxes * 8, per_box),
            rows(528),
        ),
        in_specs=[vmem] * 2,
        out_specs=(vmem,) * 5,
        compiler_params=limit(12),
        name="features",
    )(local, sent)
    mine, theirs = pl.pallas_call(
        field_kernel,
        out_shape=(rows(boxes * 8, per_box),) * 2,
        in_specs=[smem] + [vmem] * 8,
        out_specs=(vmem, vmem),
        scratch_shapes=[
            pltpu.VMEM((plane_boxes * depth, per_box), bf16),
            pltpu.VMEM((plane_boxes * 80, per_box), bf16),
            pltpu.VMEM((3 * plane_boxes * 80, per_box), bf16),
            pltpu.VMEM((plane_boxes * 160, per_box), f32),
            pltpu.VMEM((3 * plane_boxes * 16, per_box), f32),
            pltpu.VMEM((6 * 32, 128), f32),
            pltpu.VMEM((2 * 32, 128), f32),
        ],
        compiler_params=limit(32),
        name="fields",
    )(box_centres, local, cross, first, second, geometry, strengths, targets, planes)
    theirs = lax.ppermute(theirs, "rhs", swap)
    gram, live = pl.pallas_call(
        gram_kernel,
        out_shape=(rows(8), rows(2 * boxes)),
        in_specs=[smem, vmem],
        out_specs=(vmem, vmem),
        compiler_params=limit(8),
        name="gram",
    )(facet_counts, basis)
    image, tiles = pl.pallas_call(
        image_kernel,
        out_shape=(rows(rhs_local, facet_local), jax.ShapeDtypeStruct((count, 8, 128), f32)),
        in_specs=[vmem] * 6,
        out_specs=(vmem, vmem),
        compiler_params=limit(8),
        name="image",
    )(mine, theirs, gram, live, contrast, basis)
    tiles = lax.all_to_all(tiles, "box", 0, 0, tiled=True)
    next_vector, hessenberg = pl.pallas_call(
        functools.partial(finish_kernel, total_facets),
        out_shape=(rows(rhs_local, facet_local), rows(rhs_local, krylov + 1)),
        in_specs=[vmem] * 4,
        out_specs=(vmem, vmem),
        compiler_params=limit(16),
        name="finish",
    )(tiles, live, image, basis)
    return next_vector, hessenberg.T


def solution(mesh):
    return jax.shard_map(
        on_device,
        mesh=mesh,
        in_specs=(
            P(None, "rhs", "box"),
            P(None, "box"),
            P(None, "box"),
            P("box"),
            P("box"),
            P("box"),
            P(None, "box"),
            P("box", None),
            P("box", None),
        ),
        out_specs=(P("rhs", "box"), P(None, "rhs")),
        check_vma=False,
    )
```

```python
import functools

import jax
import jax.numpy as jnp
from jax import lax
from jax.experimental import pallas as pl
from jax.experimental.pallas import tpu as pltpu
from jax.sharding import PartitionSpec as P

soften = 0.0025
epsilon = 1e-06
f32 = jnp.float32
bf16 = jnp.bfloat16
plane_boxes = 16
per_box = 256
depth = 64


def lattice(centres_s, b):
    x = (centres_s[0, b] + 0.5).astype(jnp.int32)
    y = (centres_s[1, b] + 0.5).astype(jnp.int32)
    z = (centres_s[2, b] + 0.5).astype(jnp.int32)
    return x, y, z


def slot_of(centres_s, b):
    x, y, z = lattice(centres_s, b)
    return (z & 1) * plane_boxes + y * 4 + x


def wide_row(ref, b):
    return jnp.concatenate([ref[pl.ds(2 * b, 1), :], ref[pl.ds(2 * b + 1, 1), :]], axis=1)


def live_row(counts_s, b):
    slots = lax.broadcasted_iota(jnp.int32, (1, per_box), 1)
    return (slots < counts_s[b]).astype(f32)


def prep_kernel(
    centres_h, counts_h, basis_h, facets_h, areas_h, normals_h, cross_ref, first_ref, second_ref, local_ref,
    charges_v, centres_s, counts_s, current_ref, facets_ref, areas_ref, normals_ref, arrived
):
    boxes = counts_s.shape[0]
    moves = [
        (basis_h.at[basis_h.shape[0] - 1], current_ref),
        (facets_h, facets_ref),
        (areas_h, areas_ref),
        (normals_h, normals_ref),
        (centres_h, centres_s),
        (counts_h, counts_s),
    ]
    copies = [pltpu.make_async_copy(a, b, arrived.at[k]) for k, (a, b) in enumerate(moves)]
    for copy in copies:
        copy.start()
    for copy in copies:
        copy.wait()
    lane = lax.broadcasted_iota(jnp.int32, (8, 128), 1)
    row = lax.broadcasted_iota(jnp.int32, (8, 128), 0)
    empty = jnp.zeros((2, 128), f32)

    def one_box(b, carry):
        moments, centres = carry
        slot = slot_of(centres_s, b)
        lanes = pl.ds(pl.multiple_of(b * per_box, per_box), per_box)
        facets = facets_ref[:, lanes]
        normals = normals_ref[:, lanes]
        live = live_row(counts_s, b)
        weighted = current_ref[:, lanes] * (wide_row(areas_ref, b) * live / per_box)
        start = pl.multiple_of(slot * 16, 16)
        charges_v[pl.ds(start, 16), :] = jnp.concatenate([weighted[:, :128], weighted[:, 128:]], axis=0)
        local_ref[pl.ds(start, 16), :] = jnp.concatenate(
            [facets[:, :128], facets[:, 128:], empty, normals[:, :128], normals[:, 128:], empty], axis=0
        )
        moments += jnp.where(lane == slot, jnp.sum(weighted, axis=1, keepdims=True), 0.0)
        for a in range(3):
            dipole = jnp.sum(weighted * (facets[a : a + 1] - centres_s[a, b]), axis=1, keepdims=True)
            moments += jnp.where(lane == 32 * (a + 1) + slot, dipole, 0.0)
            centres += jnp.where((lane == slot) & (row == a), centres_s[a, b], 0.0)
        return moments, centres

    zeros = jnp.zeros((8, 128), f32)
    moments, centres = lax.fori_loop(0, boxes, one_box, (zeros, zeros), unroll=4)
    _, _, z = lattice(centres_s, 0)
    base_z = (z - (z & 1)).astype(f32) + 0.5
    centres = jnp.where((row == 3) | (row == 4), 1.5, jnp.where(row == 5, base_z, centres))
    half = lax.axis_index("rhs")
    away = pl.multiple_of((1 - half) * 256, 256)
    here = pl.multiple_of(half * 256, 256)
    pieces = jnp.concatenate([*thirds(moments), zeros], axis=0).astype(bf16)
    cross_ref[:512] = charges_v[...].astype(bf16)
    cross_ref[512:] = pieces
    second_ref[:256] = charges_v[pl.ds(here, 256), :].astype(bf16)
    second_ref[256:] = pieces
    first_ref[:256] = charges_v[pl.ds(away, 256), :].astype(bf16).astype(f32)
    for place in range(plane_boxes):
        first_ref[256 + 8 * place : 264 + 8 * place] = local_ref[pl.ds(away + 16 * place, 8), :]
    first_ref[384:392] = moments
    first_ref[392:] = centres
    local_ref[512:520] = moments
    local_ref[520:] = centres


def thirds(x):
    high = x.astype(bf16).astype(f32)
    rest = x - high
    middle = rest.astype(bf16).astype(f32)
    return high, middle, (rest - middle).astype(bf16).astype(f32)


def stacked_rows(parts, width):
    zeros = jnp.zeros((depth - 8 * len(parts), width), f32)
    return jnp.concatenate([*parts, zeros], axis=0)


def padded(rows):
    return jnp.concatenate([rows, jnp.zeros((8 - rows.shape[0], rows.shape[1]), f32)], axis=0)


def wide_charges(ref, place):
    both = ref[pl.ds(pl.multiple_of(place * 16, 16), 16), :].astype(f32)
    return jnp.concatenate([both[:8], both[8:]], axis=1)


def wide_tile(ref, start):
    tile = ref[pl.ds(pl.multiple_of(start, 8), 8), :]
    return jnp.concatenate([tile[0:3], tile[3:6]], axis=1)


def whole_moments(pieces):
    return pieces[:8] + (pieces[8:16] + pieces[16:24])


def store_geometry(local, box, geometry):
    row = lax.broadcasted_iota(jnp.int32, (8, per_box), 0)
    square = jnp.sum(local * local, axis=0, keepdims=True)
    features = jnp.where(row == 3, square, jnp.where(row == 4, 1.0, local))
    high, middle, low = thirds(features)
    rows = stacked_rows((high, high, high, middle, middle, low), per_box)
    geometry[pl.ds(pl.multiple_of(box * depth, depth), depth), :] = rows.astype(bf16)


def store_strengths(local, charges, box, strengths):
    products = jnp.concatenate([charges * local[a : a + 1] for a in range(3)], axis=0)
    rows = jnp.concatenate([charges, *thirds(products)], axis=0)
    strengths[pl.ds(pl.multiple_of(box * 80, 80), 80), :] = rows.astype(bf16)


def feature_kernel(local_ref, sent_ref, geometry, mine, targets, planes, local_out):
    boxes = 2 * plane_boxes
    half = lax.axis_index("rhs")
    origin = local_ref[523:526, 0:1]
    row = lax.broadcasted_iota(jnp.int32, (8, per_box), 0)

    def source(slot, _):
        local = padded(wide_tile(local_ref, slot * 16) - origin)
        store_geometry(local, slot, geometry)
        store_strengths(local, wide_charges(sent_ref, slot), slot, mine)
        return 0

    lax.fori_loop(0, boxes, source, 0, unroll=4)

    def target(place, _):
        start = (half * plane_boxes + place) * 16
        local = padded(wide_tile(local_ref, start) - origin)
        normal = padded(wide_tile(local_ref, start + 8))
        square = jnp.sum(local * local, axis=0, keepdims=True) + soften
        along = jnp.sum(local * normal, axis=0, keepdims=True)
        distance = jnp.where(row == 3, 1.0, jnp.where(row == 4, square, -2.0 * local))
        high, middle, low = thirds(distance)
        rows = stacked_rows((high, middle, low, high, middle, high), per_box)
        start = pl.multiple_of(place * per_box, per_box)
        targets[pl.ds(start, per_box), :] = jnp.transpose(rows).astype(bf16)
        planes[pl.ds(pl.multiple_of(place * 8, 8), 8), :] = jnp.where(row == 3, along, normal)
        return 0

    lax.fori_loop(0, plane_boxes, target, 0, unroll=4)
    local_out[...] = local_ref[...]


def near_planes(sources, targets, total, beside):
    def rows_at(pair, place, number):
        ref, first = pair
        return ref[pl.ds(pl.multiple_of((first + place) * number, number), number), :]

    def target_row(target_y, source_y, rows):
        runs = []
        for near_x in range(4):
            target = target_y * 4 + near_x
            for source in sources:
                for k in range(rows):
                    for x in range(max(near_x - 1, 0), min(near_x + 2, 4)):
                        runs.append((target, source, (source_y + k) * 4 + x))

        def distances(target, source, place):
            facets = targets[pl.ds(pl.multiple_of(target * per_box, per_box), per_box), :]
            return jnp.dot(facets, rows_at(source[0], place, depth), preferred_element_type=f32)

        ahead = distances(*runs[0])
        cubed = []
        given = []
        for i, (target, source, place) in enumerate(runs):
            here = ahead
            if i + 1 < len(runs):
                ahead = distances(*runs[i + 1])
            inverse = lax.rsqrt(here)
            cubed.append((inverse * inverse * inverse).astype(bf16))
            given.append(jnp.concatenate([rows_at(source[1], place, 80), rows_at(source[2], place, 80)], axis=0))
            if i + 1 == len(runs) or runs[i + 1][0] is not target:
                total[pl.ds(pl.multiple_of(target * 160, 160), 160), :] = lax.dot_general(
                    jnp.concatenate(given, axis=1),
                    jnp.concatenate(cubed, axis=1),
                    (((1,), (1,)), ((), ())),
                    preferred_element_type=f32,
                )
                cubed = []
                given = []

    def outer(i, _):
        target_row(3 * i, 2 * i, 2)
        beside(i)
        return 0

    def inner(i, _):
        target_row(i + 1, i, 3)
        beside(i + 2)
        return 0

    lax.fori_loop(0, 2, outer, 0)
    lax.fori_loop(0, 2, inner, 0)


def field_kernel(
    centres_s, local_ref, cross_ref, first_ref, second_ref, geometry, mine, targets, planes, mine_ref, theirs_ref,
    halo_geometry, halo_mine, theirs, total, far, far_centres, far_moments
):
    boxes = 2 * plane_boxes
    half = lax.axis_index("rhs")
    origin = local_ref[523:526, 0:1]

    def source(slot, _):
        local = wide_tile(local_ref, slot * 16) - origin
        store_strengths(local, wide_charges(cross_ref, slot), slot, theirs)
        return 0

    lax.fori_loop(0, boxes, source, 0, unroll=4)

    def halo_source(place, _):
        local = padded(wide_tile(first_ref, 256 + place * 8) - origin)
        store_geometry(local, place, halo_geometry)
        store_strengths(local, wide_charges(first_ref, place), place, halo_mine)
        store_strengths(local, wide_charges(second_ref, place), boxes + place, theirs)
        return 0

    lax.fori_loop(0, plane_boxes, halo_source, 0, unroll=4)

    for group, (centres, ours, others) in enumerate(
        (
            (first_ref[392:400], first_ref[384:392], second_ref[256:288]),
            (local_ref[520:528], local_ref[512:520], cross_ref[512:544]),
        )
    ):
        columns = jnp.transpose(jnp.concatenate([centres[:3] - origin, centres[3:]], axis=0))[:32]
        for a in range(3):
            far_centres[(group * 3 + a) * 32 : (group * 3 + a + 1) * 32, :] = jnp.broadcast_to(
                columns[:, a : a + 1], (32, 128)
            )
        both = jnp.concatenate([ours, whole_moments(others.astype(f32))], axis=0)
        high = both.astype(bf16).astype(f32)
        far_moments[group * 32 : group * 32 + 32, :] = jnp.concatenate([high, both - high], axis=0)
    lane = lax.broadcasted_iota(jnp.int32, (1, 128), 1)
    lane_x = lane & 3
    lane_y = (lane >> 2) & 3
    lane_plane = (lane >> 4) & 1

    def far_field(k):
        group = (k >= boxes).astype(jnp.int32)
        slot = jnp.where(k < boxes, k, half * plane_boxes + k - boxes)
        x, y, plane = slot & 3, (slot >> 2) & 3, slot >> 4
        local = wide_tile(local_ref, slot * 16) - origin
        normal = wide_tile(local_ref, slot * 16 + 8)
        d = []
        for a in range(3):
            centre = far_centres[pl.ds(pl.multiple_of((group * 3 + a) * 32, 32), 32), :]
            d.append(local[a : a + 1] - jnp.concatenate([centre, centre], axis=1))
        q = d[0] * d[0] + d[1] * d[1] + d[2] * d[2] + soften
        inverse = lax.rsqrt(q)
        inverse_2 = inverse * inverse
        inverse_3 = inverse_2 * inverse
        t = d[0] * normal[0:1] + d[1] * normal[1:2] + d[2] * normal[2:3]
        single = t * inverse_3
        steep = 3.0 * single * inverse_2
        coefficients = [single] + [steep * d[a] - normal[a : a + 1] * inverse_3 for a in range(3)]
        whole = jnp.concatenate(coefficients, axis=0)
        upper = whole.astype(bf16)
        lower = (whole - upper.astype(f32)).astype(bf16)
        lane_z = lane_plane + jnp.where(group == 0, 4 * half - 2, 0)
        near = (jnp.abs(lane_x - x) <= 1) & (jnp.abs(lane_y - y) <= 1) & (jnp.abs(lane_z - plane) <= 1)
        picked = jnp.where(near, 0.0, far_moments[pl.ds(pl.multiple_of(group * 32, 32), 32), :]).astype(bf16)
        first = jnp.dot(picked, upper, preferred_element_type=f32)
        second = jnp.dot(picked, lower, preferred_element_type=f32)
        return first[:16] + first[16:] + second[:16]

    def far_boxes(i):
        for k in range(12):
            k = i * 12 + k
            far[pl.ds(pl.multiple_of(k * 16, 16), 16), :] = far_field(k)

    sources = [((geometry, p), (mine, p), (theirs, p)) for p in (0, plane_boxes)]
    sources.append(((halo_geometry, 0), (halo_mine, 0), (theirs, boxes)))
    near_planes(sources, targets, total, far_boxes)

    def near_field(place, _):
        sums = total[pl.ds(pl.multiple_of(place * 160, 160), 160), :]
        side = planes[pl.ds(pl.multiple_of(place * 8, 8), 8), :]
        values = []
        for start in (0, 80):
            value = side[3:4] * sums[start : start + 8]
            for a in range(3):
                high, middle, low = (sums[i : i + 8] for i in range(start + 8 + 8 * a, start + 80, 24))
                value = value - side[a : a + 1] * (high + (middle + low))
            values.append(value)
        value = jnp.concatenate(values, axis=0)
        slot = half * plane_boxes + place
        rows = pl.ds(pl.multiple_of(slot * 16, 16), 16)
        far[rows, :] += value + far[pl.ds(pl.multiple_of((boxes + place) * 16, 16), 16), :]
        return 0

    lax.fori_loop(0, plane_boxes, near_field, 0, unroll=4)

    def given_back(b, _):
        start = pl.multiple_of(slot_of(centres_s, b) * 16, 16)
        rows = pl.ds(pl.multiple_of(b * 8, 8), 8)
        mine_ref[rows, :] = far[pl.ds(start, 8), :]
        theirs_ref[rows, :] = far[pl.ds(start + 8, 8), :]
        return 0

    lax.fori_loop(0, boxes, given_back, 0, unroll=4)


def gram_kernel(counts_s, basis_ref, sums_ref, live_ref):
    krylov = basis_ref.shape[0]
    pairs = [(m, n) for m in range(krylov) for n in range(m + 1)]

    def one_box(b, carry):
        lanes = pl.ds(pl.multiple_of(b * per_box, per_box), per_box)
        live = live_row(counts_s, b)
        live_ref[pl.ds(2 * b, 1), :] = live[:, :128]
        live_ref[pl.ds(2 * b + 1, 1), :] = live[:, 128:]
        rows = [basis_ref[m, :, lanes] * live for m in range(krylov)]
        out = []
        for k, (m, n) in enumerate(pairs):
            product = rows[m] * rows[n]
            out.append(carry[k] + product[:, :128] + product[:, 128:])
        return tuple(out)

    zeros = jnp.zeros((8, 128), f32)
    gram = lax.fori_loop(0, counts_s.shape[0], one_box, (zeros,) * len(pairs))
    lane = lax.broadcasted_iota(jnp.int32, (8, 128), 1)
    total = zeros
    for k, value in enumerate(gram):
        total = jnp.where(lane == krylov + 1 + k, jnp.sum(value, axis=1, keepdims=True), total)
    sums_ref[...] = total


def image_kernel(mine_ref, theirs_ref, gram_ref, live_ref, contrast_ref, basis_ref, image_ref, sums_ref):
    krylov = basis_ref.shape[0]

    def one_box(b, carry):
        lanes = pl.ds(pl.multiple_of(b * per_box, per_box), per_box)
        rows = pl.ds(pl.multiple_of(b * 8, 8), 8)
        live = wide_row(live_ref, b)
        part = mine_ref[rows, :] + theirs_ref[rows, :]
        image = live * (basis_ref[krylov - 1, :, lanes] - 2.0 * wide_row(contrast_ref, b) * part)
        image_ref[:, lanes] = image
        sums = []
        for m in range(krylov + 1):
            product = image * (basis_ref[m, :, lanes] if m < krylov else image)
            sums.append(carry[m] + product[:, :128] + product[:, 128:])
        return tuple(sums)

    zeros = jnp.zeros((8, 128), f32)
    sums = lax.fori_loop(0, live_ref.shape[0] // 2, one_box, (zeros,) * (krylov + 1), unroll=4)
    lane = lax.broadcasted_iota(jnp.int32, (8, 128), 1)
    total = gram_ref[...]
    for k, value in enumerate(sums):
        total = jnp.where(lane == k, jnp.sum(value, axis=1, keepdims=True), total)
    sums_ref[...] = jnp.broadcast_to(total[None], sums_ref.shape)


def two_sum(a, b):
    s = a + b
    c = s - a
    return s, (a - (s - c)) + (b - c)


def halves(a):
    c = a * 4097.0
    high = c - (c - a)
    return high, a - high


def two_product(a, b):
    p = a * b
    a_high, a_low = halves(a)
    b_high, b_low = halves(b)
    return p, ((a_high * b_high - p) + a_high * b_low + a_low * b_high) + a_low * b_low


def finish_kernel(total_facets, tiles_ref, live_ref, image_ref, basis_ref, next_ref, hessenberg_ref):
    boxes = live_ref.shape[0] // 2
    krylov = basis_ref.shape[0]
    lane = lax.broadcasted_iota(jnp.int32, (8, 128), 1)

    sums, rest = tiles_ref[0], jnp.zeros((8, 128), f32)
    for i in range(1, tiles_ref.shape[0]):
        sums, error = two_sum(sums, tiles_ref[i])
        rest = rest + error
    exact = sums + rest
    projections = [exact[:, m : m + 1] / total_facets for m in range(krylov)]
    pairs = [(m, n) for m in range(krylov) for n in range(m + 1)]
    first = jnp.where(lane == krylov, 1.0, 0.0)
    second = jnp.where(lane <= krylov, 1.0, 0.0)
    for m in range(krylov):
        first = jnp.where(lane == m, -2.0 * projections[m], first)
    for k, (m, n) in enumerate(pairs):
        at = lane == krylov + 1 + k
        scale = 1.0 if m == n else 2.0
        first = jnp.where(at, scale * projections[m], first)
        second = jnp.where(at, projections[n], second)
    factor, factor_rest = two_product(first, second)
    value, value_rest = two_product(factor, sums)
    value_rest = value_rest + (factor * rest + factor_rest * sums)
    for shift in (64, 32, 16, 8, 4, 2, 1):
        other = pltpu.roll(value, shift, 1)
        other_rest = pltpu.roll(value_rest, shift, 1)
        value, error = two_sum(value, other)
        value_rest = (value_rest + other_rest) + error
    remaining = jnp.maximum(value + value_rest, 0.0)
    norm = jnp.sqrt(remaining / total_facets + epsilon)
    heads = jnp.where(lane == krylov, norm, 0.0)
    for m in range(krylov):
        heads = jnp.where(lane == m, projections[m], heads)
    hessenberg_ref[...] = heads[:, : krylov + 1]
    wide = [jnp.broadcast_to(p, (8, per_box)) for p in projections]
    scale = jnp.concatenate([1.0 / norm] * (per_box // 128), axis=1)

    def one_box(b, _):
        lanes = pl.ds(pl.multiple_of(b * per_box, per_box), per_box)
        live = wide_row(live_ref, b)
        sent = wide[0] * basis_ref[0, :, lanes]
        for m in range(1, krylov):
            sent += wide[m] * basis_ref[m, :, lanes]
        next_ref[:, lanes] = (image_ref[:, lanes] - sent * live) * scale
        return 0

    lax.fori_loop(0, boxes, one_box, 0, unroll=4)


smem = pl.BlockSpec(memory_space=pltpu.SMEM)
vmem = pl.BlockSpec(memory_space=pltpu.VMEM)


def on_device(
    basis, facet_centres, normals, areas, contrast, facet_counts, box_centres, near_boxes, far_boxes
):
    krylov, rhs_local, facet_local = basis.shape
    boxes = facet_counts.shape[0]
    count = lax.axis_size("box")
    total_facets = count * facet_local
    areas = areas.reshape(-1, 128)
    contrast = contrast.reshape(-1, 128)

    def rows(number, width=128, dtype=f32):
        return jax.ShapeDtypeStruct((number, width), dtype)

    def limit(mebibytes):
        return pltpu.CompilerParams(vmem_limit_bytes=mebibytes * 1024 * 1024)

    sent, first, second, local = pl.pallas_call(
        prep_kernel,
        out_shape=(rows(544, dtype=bf16), rows(400), rows(288, dtype=bf16), rows(528)),
        in_specs=[pl.BlockSpec(memory_space=pl.ANY)] * 6,
        out_specs=(vmem,) * 4,
        scratch_shapes=[
            pltpu.VMEM((512, 128), f32),
            pltpu.SMEM(box_centres.shape, f32),
            pltpu.SMEM(facet_counts.shape, jnp.int32),
            pltpu.VMEM((rhs_local, facet_local), f32),
            pltpu.VMEM(facet_centres.shape, f32),
            pltpu.VMEM(areas.shape, f32),
            pltpu.VMEM(normals.shape, f32),
            pltpu.SemaphoreType.DMA((6,)),
        ],
        name="prepare",
    )(box_centres, facet_counts, basis, facet_centres, areas, normals)
    swap = [(0, 1), (1, 0)]
    ups = range(count - 1)
    cross = lax.ppermute(sent, "rhs", swap)
    first = lax.ppermute(
        first, ("box", "rhs"), [(2 * i, 2 * i + 2) for i in ups] + [(2 * i + 3, 2 * i + 1) for i in ups]
    )
    second = lax.ppermute(
        second, ("box", "rhs"), [(2 * i + 1, 2 * i + 2) for i in ups] + [(2 * i + 2, 2 * i + 1) for i in ups]
    )
    plane_slots = plane_boxes * per_box
    geometry, strengths, targets, planes, local = pl.pallas_call(
        feature_kernel,
        out_shape=(
            rows(boxes * depth, per_box, bf16),
            rows(boxes * 80, per_box, bf16),
            rows(plane_slots, depth, bf16),
            rows(plane_boxes * 8, per_box),
            rows(528),
        ),
        in_specs=[vmem] * 2,
        out_specs=(vmem,) * 5,
        compiler_params=limit(12),
        name="features",
    )(local, sent)
    mine, theirs = pl.pallas_call(
        field_kernel,
        out_shape=(rows(boxes * 8, per_box),) * 2,
        in_specs=[smem] + [vmem] * 8,
        out_specs=(vmem, vmem),
        scratch_shapes=[
            pltpu.VMEM((plane_boxes * depth, per_box), bf16),
            pltpu.VMEM((plane_boxes * 80, per_box), bf16),
            pltpu.VMEM((3 * plane_boxes * 80, per_box), bf16),
            pltpu.VMEM((plane_boxes * 160, per_box), f32),
            pltpu.VMEM((3 * plane_boxes * 16, per_box), f32),
            pltpu.VMEM((6 * 32, 128), f32),
            pltpu.VMEM((2 * 32, 128), f32),
        ],
        compiler_params=limit(32),
        name="fields",
    )(box_centres, local, cross, first, second, geometry, strengths, targets, planes)
    theirs = lax.ppermute(theirs, "rhs", swap)
    gram, live = pl.pallas_call(
        gram_kernel,
        out_shape=(rows(8), rows(2 * boxes)),
        in_specs=[smem, vmem],
        out_specs=(vmem, vmem),
        compiler_params=limit(8),
        name="gram",
    )(facet_counts, basis)
    image, tiles = pl.pallas_call(
        image_kernel,
        out_shape=(rows(rhs_local, facet_local), jax.ShapeDtypeStruct((count, 8, 128), f32)),
        in_specs=[vmem] * 6,
        out_specs=(vmem, vmem),
        compiler_params=limit(8),
        name="image",
    )(mine, theirs, gram, live, contrast, basis)
    tiles = lax.all_to_all(tiles, "box", 0, 0, tiled=True)
    next_vector, hessenberg = pl.pallas_call(
        functools.partial(finish_kernel, total_facets),
        out_shape=(rows(rhs_local, facet_local), rows(rhs_local, krylov + 1)),
        in_specs=[vmem] * 4,
        out_specs=(vmem, vmem),
        compiler_params=limit(16),
        name="finish",
    )(tiles, live, image, basis)
    return next_vector, hessenberg.T


def solution(mesh):
    return jax.shard_map(
        on_device,
        mesh=mesh,
        in_specs=(
            P(None, "rhs", "box"),
            P(None, "box"),
            P(None, "box"),
            P("box"),
            P("box"),
            P("box"),
            P(None, "box"),
            P("box", None),
            P("box", None),
        ),
        out_specs=(P("rhs", "box"), P(None, "rhs")),
        check_vma=False,
    )
```

```python
import functools

import jax
import jax.numpy as jnp
from jax import lax
from jax.experimental import pallas as pl
from jax.experimental.pallas import tpu as pltpu
from jax.sharding import PartitionSpec as P

soften = 0.0025
epsilon = 1e-06
f32 = jnp.float32
bf16 = jnp.bfloat16
plane_boxes = 16
per_box = 256
depth = 64


def lattice(centres_s, b):
    x = (centres_s[0, b] + 0.5).astype(jnp.int32)
    y = (centres_s[1, b] + 0.5).astype(jnp.int32)
    z = (centres_s[2, b] + 0.5).astype(jnp.int32)
    return x, y, z


def slot_of(centres_s, b):
    x, y, z = lattice(centres_s, b)
    return (z & 1) * plane_boxes + y * 4 + x


def wide_row(ref, b):
    return jnp.concatenate([ref[pl.ds(2 * b, 1), :], ref[pl.ds(2 * b + 1, 1), :]], axis=1)


def live_row(counts_s, b):
    slots = lax.broadcasted_iota(jnp.int32, (1, per_box), 1)
    return (slots < counts_s[b]).astype(f32)


def prep_kernel(
    centres_h, counts_h, basis_h, facets_h, areas_h, normals_h, cross_ref, first_ref, second_ref, local_ref,
    charges_v, centres_s, counts_s, current_ref, facets_ref, areas_ref, normals_ref, arrived
):
    boxes = counts_s.shape[0]
    moves = [
        (basis_h.at[basis_h.shape[0] - 1], current_ref),
        (facets_h, facets_ref),
        (areas_h, areas_ref),
        (normals_h, normals_ref),
        (centres_h, centres_s),
        (counts_h, counts_s),
    ]
    copies = [pltpu.make_async_copy(a, b, arrived.at[k]) for k, (a, b) in enumerate(moves)]
    for copy in copies:
        copy.start()
    for copy in copies:
        copy.wait()
    lane = lax.broadcasted_iota(jnp.int32, (8, 128), 1)
    row = lax.broadcasted_iota(jnp.int32, (8, 128), 0)
    empty = jnp.zeros((2, 128), f32)

    def one_box(b, carry):
        moments, centres = carry
        slot = slot_of(centres_s, b)
        lanes = pl.ds(pl.multiple_of(b * per_box, per_box), per_box)
        facets = facets_ref[:, lanes]
        normals = normals_ref[:, lanes]
        live = live_row(counts_s, b)
        weighted = current_ref[:, lanes] * (wide_row(areas_ref, b) * live / per_box)
        start = pl.multiple_of(slot * 16, 16)
        charges_v[pl.ds(start, 16), :] = jnp.concatenate([weighted[:, :128], weighted[:, 128:]], axis=0)
        local_ref[pl.ds(start, 16), :] = jnp.concatenate(
            [facets[:, :128], facets[:, 128:], empty, normals[:, :128], normals[:, 128:], empty], axis=0
        )
        moments += jnp.where(lane == slot, jnp.sum(weighted, axis=1, keepdims=True), 0.0)
        for a in range(3):
            dipole = jnp.sum(weighted * (facets[a : a + 1] - centres_s[a, b]), axis=1, keepdims=True)
            moments += jnp.where(lane == 32 * (a + 1) + slot, dipole, 0.0)
            centres += jnp.where((lane == slot) & (row == a), centres_s[a, b], 0.0)
        return moments, centres

    zeros = jnp.zeros((8, 128), f32)
    moments, centres = lax.fori_loop(0, boxes, one_box, (zeros, zeros), unroll=4)
    _, _, z = lattice(centres_s, 0)
    base_z = (z - (z & 1)).astype(f32) + 0.5
    centres = jnp.where((row == 3) | (row == 4), 1.5, jnp.where(row == 5, base_z, centres))
    half = lax.axis_index("rhs")
    away = pl.multiple_of((1 - half) * 256, 256)
    here = pl.multiple_of(half * 256, 256)
    pieces = jnp.concatenate([*thirds(moments), zeros], axis=0).astype(bf16)
    cross_ref[:512] = charges_v[...].astype(bf16)
    cross_ref[512:] = pieces
    second_ref[:256] = charges_v[pl.ds(here, 256), :].astype(bf16)
    second_ref[256:] = pieces
    first_ref[:256] = charges_v[pl.ds(away, 256), :].astype(bf16).astype(f32)
    for place in range(plane_boxes):
        first_ref[256 + 8 * place : 264 + 8 * place] = local_ref[pl.ds(away + 16 * place, 8), :]
    first_ref[384:392] = moments
    first_ref[392:] = centres
    local_ref[512:520] = moments
    local_ref[520:] = centres


def thirds(x):
    high = x.astype(bf16).astype(f32)
    rest = x - high
    middle = rest.astype(bf16).astype(f32)
    return high, middle, (rest - middle).astype(bf16).astype(f32)


def stacked_rows(parts, width):
    zeros = jnp.zeros((depth - 8 * len(parts), width), f32)
    return jnp.concatenate([*parts, zeros], axis=0)


def padded(rows):
    return jnp.concatenate([rows, jnp.zeros((8 - rows.shape[0], rows.shape[1]), f32)], axis=0)


def wide_charges(ref, place):
    both = ref[pl.ds(pl.multiple_of(place * 16, 16), 16), :].astype(f32)
    return jnp.concatenate([both[:8], both[8:]], axis=1)


def wide_tile(ref, start):
    tile = ref[pl.ds(pl.multiple_of(start, 8), 8), :]
    return jnp.concatenate([tile[0:3], tile[3:6]], axis=1)


def whole_moments(pieces):
    return pieces[:8] + (pieces[8:16] + pieces[16:24])


def store_geometry(local, box, geometry):
    row = lax.broadcasted_iota(jnp.int32, (8, per_box), 0)
    square = jnp.sum(local * local, axis=0, keepdims=True)
    features = jnp.where(row == 3, square, jnp.where(row == 4, 1.0, local))
    high, middle, low = thirds(features)
    rows = stacked_rows((high, high, high, middle, middle, low), per_box)
    start = pl.multiple_of((box // 4) * depth, depth)
    lanes = pl.multiple_of(lax.rem(box, 4) * per_box, per_box)
    geometry[pl.ds(start, depth), pl.ds(lanes, per_box)] = rows.astype(bf16)


def store_strengths(local, charges, box, strengths):
    products = jnp.concatenate([charges * local[a : a + 1] for a in range(3)], axis=0)
    rows = jnp.concatenate([charges, *thirds(products)], axis=0)
    strengths[pl.ds(pl.multiple_of(box * 80, 80), 80), :] = rows.astype(bf16)


def feature_kernel(local_ref, sent_ref, geometry, mine, targets, planes, local_out):
    boxes = 2 * plane_boxes
    half = lax.axis_index("rhs")
    origin = local_ref[523:526, 0:1]
    row = lax.broadcasted_iota(jnp.int32, (8, per_box), 0)

    def source(slot, _):
        local = padded(wide_tile(local_ref, slot * 16) - origin)
        store_geometry(local, slot, geometry)
        store_strengths(local, wide_charges(sent_ref, slot), slot, mine)
        return 0

    lax.fori_loop(0, boxes, source, 0, unroll=4)

    def target(place, _):
        start = (half * plane_boxes + place) * 16
        local = padded(wide_tile(local_ref, start) - origin)
        normal = padded(wide_tile(local_ref, start + 8))
        square = jnp.sum(local * local, axis=0, keepdims=True) + soften
        along = jnp.sum(local * normal, axis=0, keepdims=True)
        distance = jnp.where(row == 3, 1.0, jnp.where(row == 4, square, -2.0 * local))
        high, middle, low = thirds(distance)
        rows = stacked_rows((high, middle, low, high, middle, high), per_box)
        start = pl.multiple_of(place * per_box, per_box)
        targets[pl.ds(start, per_box), :] = jnp.transpose(rows).astype(bf16)
        planes[pl.ds(pl.multiple_of(place * 8, 8), 8), :] = jnp.where(row == 3, along, normal)
        return 0

    lax.fori_loop(0, plane_boxes, target, 0, unroll=4)
    local_out[...] = local_ref[...]


def near_planes(sources, targets, total, beside):
    def rows_at(pair, place, number):
        ref, first = pair
        return ref[pl.ds(pl.multiple_of((first + place) * number, number), number), :]

    def target_row(target_y, source_y, rows):
        runs = []
        for near_x in range(4):
            target = target_y * 4 + near_x
            for source in sources:
                for k in range(rows):
                    runs.append((target, source, source_y + k, max(near_x - 1, 0), min(near_x + 2, 4)))

        def distances(target, source, y, low, high):
            facets = targets[pl.ds(pl.multiple_of(target * per_box, per_box), per_box), :]
            ref, first = source[0]
            start = pl.multiple_of((first // 4 + y) * depth, depth)
            weights = ref[pl.ds(start, depth), low * per_box : high * per_box]
            return jnp.dot(facets, weights, preferred_element_type=f32)

        ahead = distances(*runs[0])
        cubed = []
        given = []
        for i, (target, source, y, low, high) in enumerate(runs):
            here = ahead
            if i + 1 < len(runs):
                ahead = distances(*runs[i + 1])
            inverse = lax.rsqrt(here)
            cubed.append((inverse * inverse * inverse).astype(bf16))
            for x in range(low, high):
                both = [rows_at(half, y * 4 + x, 80) for half in source[1:]]
                given.append(jnp.concatenate(both, axis=0))
            if i + 1 == len(runs) or runs[i + 1][0] is not target:
                total[pl.ds(pl.multiple_of(target * 160, 160), 160), :] = lax.dot_general(
                    jnp.concatenate(given, axis=1),
                    jnp.concatenate(cubed, axis=1),
                    (((1,), (1,)), ((), ())),
                    preferred_element_type=f32,
                )
                cubed = []
                given = []

    def outer(i, _):
        target_row(3 * i, 2 * i, 2)
        beside(i)
        return 0

    def inner(i, _):
        target_row(i + 1, i, 3)
        beside(i + 2)
        return 0

    lax.fori_loop(0, 2, outer, 0)
    lax.fori_loop(0, 2, inner, 0)


def field_kernel(
    centres_s, local_ref, cross_ref, first_ref, second_ref, geometry, mine, targets, planes, mine_ref, theirs_ref,
    halo_geometry, halo_mine, theirs, total, far, far_centres, far_moments
):
    boxes = 2 * plane_boxes
    half = lax.axis_index("rhs")
    origin = local_ref[523:526, 0:1]

    def source(slot, _):
        local = wide_tile(local_ref, slot * 16) - origin
        store_strengths(local, wide_charges(cross_ref, slot), slot, theirs)
        return 0

    lax.fori_loop(0, boxes, source, 0, unroll=4)

    def halo_source(place, _):
        local = padded(wide_tile(first_ref, 256 + place * 8) - origin)
        store_geometry(local, place, halo_geometry)
        store_strengths(local, wide_charges(first_ref, place), place, halo_mine)
        store_strengths(local, wide_charges(second_ref, place), boxes + place, theirs)
        return 0

    lax.fori_loop(0, plane_boxes, halo_source, 0, unroll=4)

    for group, (centres, ours, others) in enumerate(
        (
            (first_ref[392:400], first_ref[384:392], second_ref[256:288]),
            (local_ref[520:528], local_ref[512:520], cross_ref[512:544]),
        )
    ):
        columns = jnp.transpose(jnp.concatenate([centres[:3] - origin, centres[3:]], axis=0))[:32]
        for a in range(3):
            far_centres[(group * 3 + a) * 32 : (group * 3 + a + 1) * 32, :] = jnp.broadcast_to(
                columns[:, a : a + 1], (32, 128)
            )
        both = jnp.concatenate([ours, whole_moments(others.astype(f32))], axis=0)
        high = both.astype(bf16).astype(f32)
        far_moments[group * 32 : group * 32 + 32, :] = jnp.concatenate([high, both - high], axis=0)
    lane = lax.broadcasted_iota(jnp.int32, (1, 128), 1)
    lane_x = lane & 3
    lane_y = (lane >> 2) & 3
    lane_plane = (lane >> 4) & 1

    def far_field(k):
        group = (k >= boxes).astype(jnp.int32)
        slot = jnp.where(k < boxes, k, half * plane_boxes + k - boxes)
        x, y, plane = slot & 3, (slot >> 2) & 3, slot >> 4
        local = wide_tile(local_ref, slot * 16) - origin
        normal = wide_tile(local_ref, slot * 16 + 8)
        d = []
        for a in range(3):
            centre = far_centres[pl.ds(pl.multiple_of((group * 3 + a) * 32, 32), 32), :]
            d.append(local[a : a + 1] - jnp.concatenate([centre, centre], axis=1))
        q = d[0] * d[0] + d[1] * d[1] + d[2] * d[2] + soften
        inverse = lax.rsqrt(q)
        inverse_2 = inverse * inverse
        inverse_3 = inverse_2 * inverse
        t = d[0] * normal[0:1] + d[1] * normal[1:2] + d[2] * normal[2:3]
        single = t * inverse_3
        steep = 3.0 * single * inverse_2
        coefficients = [single] + [steep * d[a] - normal[a : a + 1] * inverse_3 for a in range(3)]
        whole = jnp.concatenate(coefficients, axis=0)
        upper = whole.astype(bf16)
        lower = (whole - upper.astype(f32)).astype(bf16)
        lane_z = lane_plane + jnp.where(group == 0, 4 * half - 2, 0)
        near = (jnp.abs(lane_x - x) <= 1) & (jnp.abs(lane_y - y) <= 1) & (jnp.abs(lane_z - plane) <= 1)
        picked = jnp.where(near, 0.0, far_moments[pl.ds(pl.multiple_of(group * 32, 32), 32), :]).astype(bf16)
        first = jnp.dot(picked, upper, preferred_element_type=f32)
        second = jnp.dot(picked, lower, preferred_element_type=f32)
        return first[:16] + first[16:] + second[:16]

    def far_boxes(i):
        for k in range(12):
            k = i * 12 + k
            far[pl.ds(pl.multiple_of(k * 16, 16), 16), :] = far_field(k)

    sources = [((geometry, p), (mine, p), (theirs, p)) for p in (0, plane_boxes)]
    sources.append(((halo_geometry, 0), (halo_mine, 0), (theirs, boxes)))
    near_planes(sources, targets, total, far_boxes)

    def near_field(place, _):
        sums = total[pl.ds(pl.multiple_of(place * 160, 160), 160), :]
        side = planes[pl.ds(pl.multiple_of(place * 8, 8), 8), :]
        values = []
        for start in (0, 80):
            value = side[3:4] * sums[start : start + 8]
            for a in range(3):
                high, middle, low = (sums[i : i + 8] for i in range(start + 8 + 8 * a, start + 80, 24))
                value = value - side[a : a + 1] * (high + (middle + low))
            values.append(value)
        value = jnp.concatenate(values, axis=0)
        slot = half * plane_boxes + place
        rows = pl.ds(pl.multiple_of(slot * 16, 16), 16)
        far[rows, :] += value + far[pl.ds(pl.multiple_of((boxes + place) * 16, 16), 16), :]
        return 0

    lax.fori_loop(0, plane_boxes, near_field, 0, unroll=4)

    def given_back(b, _):
        start = pl.multiple_of(slot_of(centres_s, b) * 16, 16)
        rows = pl.ds(pl.multiple_of(b * 8, 8), 8)
        mine_ref[rows, :] = far[pl.ds(start, 8), :]
        theirs_ref[rows, :] = far[pl.ds(start + 8, 8), :]
        return 0

    lax.fori_loop(0, boxes, given_back, 0, unroll=4)


def gram_kernel(counts_s, basis_ref, sums_ref, live_ref):
    krylov = basis_ref.shape[0]
    pairs = [(m, n) for m in range(krylov) for n in range(m + 1)]

    def one_box(b, carry):
        lanes = pl.ds(pl.multiple_of(b * per_box, per_box), per_box)
        live = live_row(counts_s, b)
        live_ref[pl.ds(2 * b, 1), :] = live[:, :128]
        live_ref[pl.ds(2 * b + 1, 1), :] = live[:, 128:]
        rows = [basis_ref[m, :, lanes] * live for m in range(krylov)]
        out = []
        for k, (m, n) in enumerate(pairs):
            product = rows[m] * rows[n]
            out.append(carry[k] + product[:, :128] + product[:, 128:])
        return tuple(out)

    zeros = jnp.zeros((8, 128), f32)
    gram = lax.fori_loop(0, counts_s.shape[0], one_box, (zeros,) * len(pairs))
    lane = lax.broadcasted_iota(jnp.int32, (8, 128), 1)
    total = zeros
    for k, value in enumerate(gram):
        total = jnp.where(lane == krylov + 1 + k, jnp.sum(value, axis=1, keepdims=True), total)
    sums_ref[...] = total


def image_kernel(mine_ref, theirs_ref, gram_ref, live_ref, contrast_ref, basis_ref, image_ref, sums_ref):
    krylov = basis_ref.shape[0]

    def one_box(b, carry):
        lanes = pl.ds(pl.multiple_of(b * per_box, per_box), per_box)
        rows = pl.ds(pl.multiple_of(b * 8, 8), 8)
        live = wide_row(live_ref, b)
        part = mine_ref[rows, :] + theirs_ref[rows, :]
        image = live * (basis_ref[krylov - 1, :, lanes] - 2.0 * wide_row(contrast_ref, b) * part)
        image_ref[:, lanes] = image
        sums = []
        for m in range(krylov + 1):
            product = image * (basis_ref[m, :, lanes] if m < krylov else image)
            sums.append(carry[m] + product[:, :128] + product[:, 128:])
        return tuple(sums)

    zeros = jnp.zeros((8, 128), f32)
    sums = lax.fori_loop(0, live_ref.shape[0] // 2, one_box, (zeros,) * (krylov + 1), unroll=4)
    lane = lax.broadcasted_iota(jnp.int32, (8, 128), 1)
    total = gram_ref[...]
    for k, value in enumerate(sums):
        total = jnp.where(lane == k, jnp.sum(value, axis=1, keepdims=True), total)
    sums_ref[...] = jnp.broadcast_to(total[None], sums_ref.shape)


def two_sum(a, b):
    s = a + b
    c = s - a
    return s, (a - (s - c)) + (b - c)


def halves(a):
    c = a * 4097.0
    high = c - (c - a)
    return high, a - high


def two_product(a, b):
    p = a * b
    a_high, a_low = halves(a)
    b_high, b_low = halves(b)
    return p, ((a_high * b_high - p) + a_high * b_low + a_low * b_high) + a_low * b_low


def finish_kernel(total_facets, tiles_ref, live_ref, image_ref, basis_ref, next_ref, hessenberg_ref):
    boxes = live_ref.shape[0] // 2
    krylov = basis_ref.shape[0]
    lane = lax.broadcasted_iota(jnp.int32, (8, 128), 1)

    sums, rest = tiles_ref[0], jnp.zeros((8, 128), f32)
    for i in range(1, tiles_ref.shape[0]):
        sums, error = two_sum(sums, tiles_ref[i])
        rest = rest + error
    exact = sums + rest
    projections = [exact[:, m : m + 1] / total_facets for m in range(krylov)]
    pairs = [(m, n) for m in range(krylov) for n in range(m + 1)]
    first = jnp.where(lane == krylov, 1.0, 0.0)
    second = jnp.where(lane <= krylov, 1.0, 0.0)
    for m in range(krylov):
        first = jnp.where(lane == m, -2.0 * projections[m], first)
    for k, (m, n) in enumerate(pairs):
        at = lane == krylov + 1 + k
        scale = 1.0 if m == n else 2.0
        first = jnp.where(at, scale * projections[m], first)
        second = jnp.where(at, projections[n], second)
    factor, factor_rest = two_product(first, second)
    value, value_rest = two_product(factor, sums)
    value_rest = value_rest + (factor * rest + factor_rest * sums)
    for shift in (64, 32, 16, 8, 4, 2, 1):
        other = pltpu.roll(value, shift, 1)
        other_rest = pltpu.roll(value_rest, shift, 1)
        value, error = two_sum(value, other)
        value_rest = (value_rest + other_rest) + error
    remaining = jnp.maximum(value + value_rest, 0.0)
    norm = jnp.sqrt(remaining / total_facets + epsilon)
    heads = jnp.where(lane == krylov, norm, 0.0)
    for m in range(krylov):
        heads = jnp.where(lane == m, projections[m], heads)
    hessenberg_ref[...] = heads[:, : krylov + 1]
    wide = [jnp.broadcast_to(p, (8, per_box)) for p in projections]
    scale = jnp.concatenate([1.0 / norm] * (per_box // 128), axis=1)

    def one_box(b, _):
        lanes = pl.ds(pl.multiple_of(b * per_box, per_box), per_box)
        live = wide_row(live_ref, b)
        sent = wide[0] * basis_ref[0, :, lanes]
        for m in range(1, krylov):
            sent += wide[m] * basis_ref[m, :, lanes]
        next_ref[:, lanes] = (image_ref[:, lanes] - sent * live) * scale
        return 0

    lax.fori_loop(0, boxes, one_box, 0, unroll=4)


smem = pl.BlockSpec(memory_space=pltpu.SMEM)
vmem = pl.BlockSpec(memory_space=pltpu.VMEM)


def on_device(
    basis, facet_centres, normals, areas, contrast, facet_counts, box_centres, near_boxes, far_boxes
):
    krylov, rhs_local, facet_local = basis.shape
    boxes = facet_counts.shape[0]
    count = lax.axis_size("box")
    total_facets = count * facet_local
    areas = areas.reshape(-1, 128)
    contrast = contrast.reshape(-1, 128)

    def rows(number, width=128, dtype=f32):
        return jax.ShapeDtypeStruct((number, width), dtype)

    def limit(mebibytes):
        return pltpu.CompilerParams(vmem_limit_bytes=mebibytes * 1024 * 1024)

    sent, first, second, local = pl.pallas_call(
        prep_kernel,
        out_shape=(rows(544, dtype=bf16), rows(400), rows(288, dtype=bf16), rows(528)),
        in_specs=[pl.BlockSpec(memory_space=pl.ANY)] * 6,
        out_specs=(vmem,) * 4,
        scratch_shapes=[
            pltpu.VMEM((512, 128), f32),
            pltpu.SMEM(box_centres.shape, f32),
            pltpu.SMEM(facet_counts.shape, jnp.int32),
            pltpu.VMEM((rhs_local, facet_local), f32),
            pltpu.VMEM(facet_centres.shape, f32),
            pltpu.VMEM(areas.shape, f32),
            pltpu.VMEM(normals.shape, f32),
            pltpu.SemaphoreType.DMA((6,)),
        ],
        name="prepare",
    )(box_centres, facet_counts, basis, facet_centres, areas, normals)
    swap = [(0, 1), (1, 0)]
    ups = range(count - 1)
    cross = lax.ppermute(sent, "rhs", swap)
    first = lax.ppermute(
        first, ("box", "rhs"), [(2 * i, 2 * i + 2) for i in ups] + [(2 * i + 3, 2 * i + 1) for i in ups]
    )
    second = lax.ppermute(
        second, ("box", "rhs"), [(2 * i + 1, 2 * i + 2) for i in ups] + [(2 * i + 2, 2 * i + 1) for i in ups]
    )
    plane_slots = plane_boxes * per_box
    geometry, strengths, targets, planes, local = pl.pallas_call(
        feature_kernel,
        out_shape=(
            rows(boxes // 4 * depth, 4 * per_box, bf16),
            rows(boxes * 80, per_box, bf16),
            rows(plane_slots, depth, bf16),
            rows(plane_boxes * 8, per_box),
            rows(528),
        ),
        in_specs=[vmem] * 2,
        out_specs=(vmem,) * 5,
        compiler_params=limit(12),
        name="features",
    )(local, sent)
    mine, theirs = pl.pallas_call(
        field_kernel,
        out_shape=(rows(boxes * 8, per_box),) * 2,
        in_specs=[smem] + [vmem] * 8,
        out_specs=(vmem, vmem),
        scratch_shapes=[
            pltpu.VMEM((plane_boxes // 4 * depth, 4 * per_box), bf16),
            pltpu.VMEM((plane_boxes * 80, per_box), bf16),
            pltpu.VMEM((3 * plane_boxes * 80, per_box), bf16),
            pltpu.VMEM((plane_boxes * 160, per_box), f32),
            pltpu.VMEM((3 * plane_boxes * 16, per_box), f32),
            pltpu.VMEM((6 * 32, 128), f32),
            pltpu.VMEM((2 * 32, 128), f32),
        ],
        compiler_params=limit(32),
        name="fields",
    )(box_centres, local, cross, first, second, geometry, strengths, targets, planes)
    theirs = lax.ppermute(theirs, "rhs", swap)
    gram, live = pl.pallas_call(
        gram_kernel,
        out_shape=(rows(8), rows(2 * boxes)),
        in_specs=[smem, vmem],
        out_specs=(vmem, vmem),
        compiler_params=limit(8),
        name="gram",
    )(facet_counts, basis)
    image, tiles = pl.pallas_call(
        image_kernel,
        out_shape=(rows(rhs_local, facet_local), jax.ShapeDtypeStruct((count, 8, 128), f32)),
        in_specs=[vmem] * 6,
        out_specs=(vmem, vmem),
        compiler_params=limit(8),
        name="image",
    )(mine, theirs, gram, live, contrast, basis)
    tiles = lax.all_to_all(tiles, "box", 0, 0, tiled=True)
    next_vector, hessenberg = pl.pallas_call(
        functools.partial(finish_kernel, total_facets),
        out_shape=(rows(rhs_local, facet_local), rows(rhs_local, krylov + 1)),
        in_specs=[vmem] * 4,
        out_specs=(vmem, vmem),
        compiler_params=limit(16),
        name="finish",
    )(tiles, live, image, basis)
    return next_vector, hessenberg.T


def solution(mesh):
    return jax.shard_map(
        on_device,
        mesh=mesh,
        in_specs=(
            P(None, "rhs", "box"),
            P(None, "box"),
            P(None, "box"),
            P("box"),
            P("box"),
            P("box"),
            P(None, "box"),
            P("box", None),
            P("box", None),
        ),
        out_specs=(P("rhs", "box"), P(None, "rhs")),
        check_vma=False,
    )
```

```python
import functools

import jax
import jax.numpy as jnp
from jax import lax
from jax.experimental import pallas as pl
from jax.experimental.pallas import tpu as pltpu
from jax.sharding import PartitionSpec as P

soften = 0.0025
epsilon = 1e-06
f32 = jnp.float32
bf16 = jnp.bfloat16
plane_boxes = 16
per_box = 256
depth = 64


def lattice(centres_s, b):
    x = (centres_s[0, b] + 0.5).astype(jnp.int32)
    y = (centres_s[1, b] + 0.5).astype(jnp.int32)
    z = (centres_s[2, b] + 0.5).astype(jnp.int32)
    return x, y, z


def slot_of(centres_s, b):
    x, y, z = lattice(centres_s, b)
    return (z & 1) * plane_boxes + y * 4 + x


def wide_row(ref, b):
    return jnp.concatenate([ref[pl.ds(2 * b, 1), :], ref[pl.ds(2 * b + 1, 1), :]], axis=1)


def live_row(counts_s, b):
    slots = lax.broadcasted_iota(jnp.int32, (1, per_box), 1)
    return (slots < counts_s[b]).astype(f32)


def prep_kernel(
    centres_h, counts_h, basis_h, facets_h, areas_h, normals_h, cross_ref, first_ref, second_ref, local_ref,
    charges_v, centres_s, counts_s, current_ref, facets_ref, areas_ref, normals_ref, arrived
):
    boxes = counts_s.shape[0]
    moves = [
        (basis_h.at[basis_h.shape[0] - 1], current_ref),
        (facets_h, facets_ref),
        (areas_h, areas_ref),
        (normals_h, normals_ref),
        (centres_h, centres_s),
        (counts_h, counts_s),
    ]
    copies = [pltpu.make_async_copy(a, b, arrived.at[k]) for k, (a, b) in enumerate(moves)]
    for copy in copies:
        copy.start()
    for copy in copies:
        copy.wait()
    lane = lax.broadcasted_iota(jnp.int32, (8, 128), 1)
    row = lax.broadcasted_iota(jnp.int32, (8, 128), 0)
    empty = jnp.zeros((2, 128), f32)

    def one_box(b, carry):
        moments, centres = carry
        slot = slot_of(centres_s, b)
        lanes = pl.ds(pl.multiple_of(b * per_box, per_box), per_box)
        facets = facets_ref[:, lanes]
        normals = normals_ref[:, lanes]
        live = live_row(counts_s, b)
        weighted = current_ref[:, lanes] * (wide_row(areas_ref, b) * live / per_box)
        start = pl.multiple_of(slot * 16, 16)
        charges_v[pl.ds(start, 16), :] = jnp.concatenate([weighted[:, :128], weighted[:, 128:]], axis=0)
        local_ref[pl.ds(start, 16), :] = jnp.concatenate(
            [facets[:, :128], facets[:, 128:], empty, normals[:, :128], normals[:, 128:], empty], axis=0
        )
        moments += jnp.where(lane == slot, jnp.sum(weighted, axis=1, keepdims=True), 0.0)
        for a in range(3):
            dipole = jnp.sum(weighted * (facets[a : a + 1] - centres_s[a, b]), axis=1, keepdims=True)
            moments += jnp.where(lane == 32 * (a + 1) + slot, dipole, 0.0)
            centres += jnp.where((lane == slot) & (row == a), centres_s[a, b], 0.0)
        return moments, centres

    zeros = jnp.zeros((8, 128), f32)
    moments, centres = lax.fori_loop(0, boxes, one_box, (zeros, zeros), unroll=4)
    _, _, z = lattice(centres_s, 0)
    base_z = (z - (z & 1)).astype(f32) + 0.5
    centres = jnp.where((row == 3) | (row == 4), 1.5, jnp.where(row == 5, base_z, centres))
    half = lax.axis_index("rhs")
    away = pl.multiple_of((1 - half) * 256, 256)
    here = pl.multiple_of(half * 256, 256)
    pieces = jnp.concatenate([*thirds(moments), zeros], axis=0).astype(bf16)
    cross_ref[:512] = charges_v[...].astype(bf16)
    cross_ref[512:] = pieces
    second_ref[:256] = charges_v[pl.ds(here, 256), :].astype(bf16)
    second_ref[256:] = pieces
    first_ref[:256] = charges_v[pl.ds(away, 256), :].astype(bf16).astype(f32)
    for place in range(plane_boxes):
        first_ref[256 + 8 * place : 264 + 8 * place] = local_ref[pl.ds(away + 16 * place, 8), :]
    first_ref[384:392] = moments
    first_ref[392:] = centres
    local_ref[512:520] = moments
    local_ref[520:] = centres


def thirds(x):
    high = x.astype(bf16).astype(f32)
    rest = x - high
    middle = rest.astype(bf16).astype(f32)
    return high, middle, (rest - middle).astype(bf16).astype(f32)


def stacked_rows(parts, width):
    zeros = jnp.zeros((depth - 8 * len(parts), width), f32)
    return jnp.concatenate([*parts, zeros], axis=0)


def padded(rows):
    return jnp.concatenate([rows, jnp.zeros((8 - rows.shape[0], rows.shape[1]), f32)], axis=0)


def wide_charges(ref, place):
    both = ref[pl.ds(pl.multiple_of(place * 16, 16), 16), :].astype(f32)
    return jnp.concatenate([both[:8], both[8:]], axis=1)


def wide_tile(ref, start):
    tile = ref[pl.ds(pl.multiple_of(start, 8), 8), :]
    return jnp.concatenate([tile[0:3], tile[3:6]], axis=1)


def whole_moments(pieces):
    return pieces[:8] + (pieces[8:16] + pieces[16:24])


def store_geometry(local, box, geometry):
    row = lax.broadcasted_iota(jnp.int32, (8, per_box), 0)
    square = jnp.sum(local * local, axis=0, keepdims=True)
    features = jnp.where(row == 3, square, jnp.where(row == 4, 1.0, local))
    high, middle, low = thirds(features)
    rows = stacked_rows((high, high, high, middle, middle, low), per_box)
    geometry[pl.ds(pl.multiple_of(box * depth, depth), depth), :] = rows.astype(bf16)


def store_strengths(local, charges, box, strengths):
    products = jnp.concatenate([charges * local[a : a + 1] for a in range(3)], axis=0)
    rows = jnp.concatenate([charges, *thirds(products)], axis=0)
    strengths[pl.ds(pl.multiple_of(box * 80, 80), 80), :] = rows.astype(bf16)


def feature_kernel(local_ref, sent_ref, geometry, mine, targets, planes, local_out):
    boxes = 2 * plane_boxes
    half = lax.axis_index("rhs")
    origin = local_ref[523:526, 0:1]
    row = lax.broadcasted_iota(jnp.int32, (8, per_box), 0)

    def source(slot, _):
        local = padded(wide_tile(local_ref, slot * 16) - origin)
        store_geometry(local, slot, geometry)
        store_strengths(local, wide_charges(sent_ref, slot), slot, mine)
        return 0

    lax.fori_loop(0, boxes, source, 0, unroll=4)

    def target(place, _):
        start = (half * plane_boxes + place) * 16
        local = padded(wide_tile(local_ref, start) - origin)
        normal = padded(wide_tile(local_ref, start + 8))
        square = jnp.sum(local * local, axis=0, keepdims=True) + soften
        along = jnp.sum(local * normal, axis=0, keepdims=True)
        distance = jnp.where(row == 3, 1.0, jnp.where(row == 4, square, -2.0 * local))
        high, middle, low = thirds(distance)
        rows = stacked_rows((high, middle, low, high, middle, high), per_box)
        start = pl.multiple_of(place * per_box, per_box)
        targets[pl.ds(start, per_box), :] = jnp.transpose(rows).astype(bf16)
        planes[pl.ds(pl.multiple_of(place * 8, 8), 8), :] = jnp.where(row == 3, along, normal)
        return 0

    lax.fori_loop(0, plane_boxes, target, 0, unroll=4)
    local_out[...] = local_ref[...]


def near_planes(sources, targets, total, beside):
    def rows_at(pair, place, number):
        ref, first = pair
        return ref[pl.ds(pl.multiple_of((first + place) * number, number), number), :]

    def target_row(target_y, source_y, rows, step):
        runs = []
        for near_x in range(4):
            target = target_y * 4 + near_x
            for source in sources:
                for k in range(rows):
                    for x in range(max(near_x - 1, 0), min(near_x + 2, 4)):
                        runs.append((target, source, (source_y + k) * 4 + x))

        def distances(target, source, place):
            facets = targets[pl.ds(pl.multiple_of(target * per_box, per_box), per_box), :]
            return jnp.dot(facets, rows_at(source[0], place, depth), preferred_element_type=f32)

        ahead = distances(*runs[0])
        cubed = []
        given = []
        for i, (target, source, place) in enumerate(runs):
            here = ahead
            if i + 1 < len(runs):
                ahead = distances(*runs[i + 1])
            inverse = lax.rsqrt(here)
            cubed.append((inverse * inverse * inverse).astype(bf16))
            given.append(jnp.concatenate([rows_at(source[1], place, 80), rows_at(source[2], place, 80)], axis=0))
            if i + 1 == len(runs) or runs[i + 1][0] is not target:
                total[pl.ds(pl.multiple_of(target * 160, 160), 160), :] = lax.dot_general(
                    jnp.concatenate(given, axis=1),
                    jnp.concatenate(cubed, axis=1),
                    (((1,), (1,)), ((), ())),
                    preferred_element_type=f32,
                )
                cubed = []
                given = []
            turn, rest = divmod(i, len(runs) // 12)
            if turn < 12 and rest == len(runs) // 24:
                beside(step * 12 + turn)

    def outer(i, _):
        target_row(3 * i, 2 * i, 2, i)
        return 0

    def inner(i, _):
        target_row(i + 1, i, 3, i + 2)
        return 0

    lax.fori_loop(0, 2, outer, 0)
    lax.fori_loop(0, 2, inner, 0)


def field_kernel(
    centres_s, local_ref, cross_ref, first_ref, second_ref, geometry, mine, targets, planes, mine_ref, theirs_ref,
    halo_geometry, halo_mine, theirs, total, far, far_centres, far_moments
):
    boxes = 2 * plane_boxes
    half = lax.axis_index("rhs")
    origin = local_ref[523:526, 0:1]

    def source(slot, _):
        local = wide_tile(local_ref, slot * 16) - origin
        store_strengths(local, wide_charges(cross_ref, slot), slot, theirs)
        return 0

    lax.fori_loop(0, boxes, source, 0, unroll=4)

    def halo_source(place, _):
        local = padded(wide_tile(first_ref, 256 + place * 8) - origin)
        store_geometry(local, place, halo_geometry)
        store_strengths(local, wide_charges(first_ref, place), place, halo_mine)
        store_strengths(local, wide_charges(second_ref, place), boxes + place, theirs)
        return 0

    lax.fori_loop(0, plane_boxes, halo_source, 0, unroll=4)

    for group, (centres, ours, others) in enumerate(
        (
            (first_ref[392:400], first_ref[384:392], second_ref[256:288]),
            (local_ref[520:528], local_ref[512:520], cross_ref[512:544]),
        )
    ):
        columns = jnp.transpose(jnp.concatenate([centres[:3] - origin, centres[3:]], axis=0))[:32]
        for a in range(3):
            far_centres[(group * 3 + a) * 32 : (group * 3 + a + 1) * 32, :] = jnp.broadcast_to(
                columns[:, a : a + 1], (32, 128)
            )
        both = jnp.concatenate([ours, whole_moments(others.astype(f32))], axis=0)
        high = both.astype(bf16).astype(f32)
        far_moments[group * 32 : group * 32 + 32, :] = jnp.concatenate([high, both - high], axis=0)
    lane = lax.broadcasted_iota(jnp.int32, (1, 128), 1)
    lane_x = lane & 3
    lane_y = (lane >> 2) & 3
    lane_plane = (lane >> 4) & 1

    def far_field(k):
        group = (k >= boxes).astype(jnp.int32)
        slot = jnp.where(k < boxes, k, half * plane_boxes + k - boxes)
        x, y, plane = slot & 3, (slot >> 2) & 3, slot >> 4
        local = wide_tile(local_ref, slot * 16) - origin
        normal = wide_tile(local_ref, slot * 16 + 8)
        d = []
        for a in range(3):
            centre = far_centres[pl.ds(pl.multiple_of((group * 3 + a) * 32, 32), 32), :]
            d.append(local[a : a + 1] - jnp.concatenate([centre, centre], axis=1))
        q = d[0] * d[0] + d[1] * d[1] + d[2] * d[2] + soften
        inverse = lax.rsqrt(q)
        inverse_2 = inverse * inverse
        inverse_3 = inverse_2 * inverse
        t = d[0] * normal[0:1] + d[1] * normal[1:2] + d[2] * normal[2:3]
        single = t * inverse_3
        steep = 3.0 * single * inverse_2
        coefficients = [single] + [steep * d[a] - normal[a : a + 1] * inverse_3 for a in range(3)]
        whole = jnp.concatenate(coefficients, axis=0)
        upper = whole.astype(bf16)
        lower = (whole - upper.astype(f32)).astype(bf16)
        lane_z = lane_plane + jnp.where(group == 0, 4 * half - 2, 0)
        near = (jnp.abs(lane_x - x) <= 1) & (jnp.abs(lane_y - y) <= 1) & (jnp.abs(lane_z - plane) <= 1)
        picked = jnp.where(near, 0.0, far_moments[pl.ds(pl.multiple_of(group * 32, 32), 32), :]).astype(bf16)
        first = jnp.dot(picked, upper, preferred_element_type=f32)
        second = jnp.dot(picked, lower, preferred_element_type=f32)
        return first[:16] + first[16:] + second[:16]

    def far_boxes(k):
        far[pl.ds(pl.multiple_of(k * 16, 16), 16), :] = far_field(k)

    sources = [((geometry, p), (mine, p), (theirs, p)) for p in (0, plane_boxes)]
    sources.append(((halo_geometry, 0), (halo_mine, 0), (theirs, boxes)))
    near_planes(sources, targets, total, far_boxes)

    def near_field(place, _):
        sums = total[pl.ds(pl.multiple_of(place * 160, 160), 160), :]
        side = planes[pl.ds(pl.multiple_of(place * 8, 8), 8), :]
        values = []
        for start in (0, 80):
            value = side[3:4] * sums[start : start + 8]
            for a in range(3):
                high, middle, low = (sums[i : i + 8] for i in range(start + 8 + 8 * a, start + 80, 24))
                value = value - side[a : a + 1] * (high + (middle + low))
            values.append(value)
        value = jnp.concatenate(values, axis=0)
        slot = half * plane_boxes + place
        rows = pl.ds(pl.multiple_of(slot * 16, 16), 16)
        far[rows, :] += value + far[pl.ds(pl.multiple_of((boxes + place) * 16, 16), 16), :]
        return 0

    lax.fori_loop(0, plane_boxes, near_field, 0, unroll=4)

    def given_back(b, _):
        start = pl.multiple_of(slot_of(centres_s, b) * 16, 16)
        rows = pl.ds(pl.multiple_of(b * 8, 8), 8)
        mine_ref[rows, :] = far[pl.ds(start, 8), :]
        theirs_ref[rows, :] = far[pl.ds(start + 8, 8), :]
        return 0

    lax.fori_loop(0, boxes, given_back, 0, unroll=4)


def gram_kernel(counts_s, basis_ref, sums_ref, live_ref):
    krylov = basis_ref.shape[0]
    pairs = [(m, n) for m in range(krylov) for n in range(m + 1)]

    def one_box(b, carry):
        lanes = pl.ds(pl.multiple_of(b * per_box, per_box), per_box)
        live = live_row(counts_s, b)
        live_ref[pl.ds(2 * b, 1), :] = live[:, :128]
        live_ref[pl.ds(2 * b + 1, 1), :] = live[:, 128:]
        rows = [basis_ref[m, :, lanes] * live for m in range(krylov)]
        out = []
        for k, (m, n) in enumerate(pairs):
            product = rows[m] * rows[n]
            out.append(carry[k] + product[:, :128] + product[:, 128:])
        return tuple(out)

    zeros = jnp.zeros((8, 128), f32)
    gram = lax.fori_loop(0, counts_s.shape[0], one_box, (zeros,) * len(pairs))
    lane = lax.broadcasted_iota(jnp.int32, (8, 128), 1)
    total = zeros
    for k, value in enumerate(gram):
        total = jnp.where(lane == krylov + 1 + k, jnp.sum(value, axis=1, keepdims=True), total)
    sums_ref[...] = total


def image_kernel(mine_ref, theirs_ref, gram_ref, live_ref, contrast_ref, basis_ref, image_ref, sums_ref):
    krylov = basis_ref.shape[0]

    def one_box(b, carry):
        lanes = pl.ds(pl.multiple_of(b * per_box, per_box), per_box)
        rows = pl.ds(pl.multiple_of(b * 8, 8), 8)
        live = wide_row(live_ref, b)
        part = mine_ref[rows, :] + theirs_ref[rows, :]
        image = live * (basis_ref[krylov - 1, :, lanes] - 2.0 * wide_row(contrast_ref, b) * part)
        image_ref[:, lanes] = image
        sums = []
        for m in range(krylov + 1):
            product = image * (basis_ref[m, :, lanes] if m < krylov else image)
            sums.append(carry[m] + product[:, :128] + product[:, 128:])
        return tuple(sums)

    zeros = jnp.zeros((8, 128), f32)
    sums = lax.fori_loop(0, live_ref.shape[0] // 2, one_box, (zeros,) * (krylov + 1), unroll=4)
    lane = lax.broadcasted_iota(jnp.int32, (8, 128), 1)
    total = gram_ref[...]
    for k, value in enumerate(sums):
        total = jnp.where(lane == k, jnp.sum(value, axis=1, keepdims=True), total)
    sums_ref[...] = jnp.broadcast_to(total[None], sums_ref.shape)


def two_sum(a, b):
    s = a + b
    c = s - a
    return s, (a - (s - c)) + (b - c)


def halves(a):
    c = a * 4097.0
    high = c - (c - a)
    return high, a - high


def two_product(a, b):
    p = a * b
    a_high, a_low = halves(a)
    b_high, b_low = halves(b)
    return p, ((a_high * b_high - p) + a_high * b_low + a_low * b_high) + a_low * b_low


def finish_kernel(total_facets, tiles_ref, live_ref, image_ref, basis_ref, next_ref, hessenberg_ref):
    boxes = live_ref.shape[0] // 2
    krylov = basis_ref.shape[0]
    lane = lax.broadcasted_iota(jnp.int32, (8, 128), 1)

    sums, rest = tiles_ref[0], jnp.zeros((8, 128), f32)
    for i in range(1, tiles_ref.shape[0]):
        sums, error = two_sum(sums, tiles_ref[i])
        rest = rest + error
    exact = sums + rest
    projections = [exact[:, m : m + 1] / total_facets for m in range(krylov)]
    pairs = [(m, n) for m in range(krylov) for n in range(m + 1)]
    first = jnp.where(lane == krylov, 1.0, 0.0)
    second = jnp.where(lane <= krylov, 1.0, 0.0)
    for m in range(krylov):
        first = jnp.where(lane == m, -2.0 * projections[m], first)
    for k, (m, n) in enumerate(pairs):
        at = lane == krylov + 1 + k
        scale = 1.0 if m == n else 2.0
        first = jnp.where(at, scale * projections[m], first)
        second = jnp.where(at, projections[n], second)
    factor, factor_rest = two_product(first, second)
    value, value_rest = two_product(factor, sums)
    value_rest = value_rest + (factor * rest + factor_rest * sums)
    for shift in (64, 32, 16, 8, 4, 2, 1):
        other = pltpu.roll(value, shift, 1)
        other_rest = pltpu.roll(value_rest, shift, 1)
        value, error = two_sum(value, other)
        value_rest = (value_rest + other_rest) + error
    remaining = jnp.maximum(value + value_rest, 0.0)
    norm = jnp.sqrt(remaining / total_facets + epsilon)
    heads = jnp.where(lane == krylov, norm, 0.0)
    for m in range(krylov):
        heads = jnp.where(lane == m, projections[m], heads)
    hessenberg_ref[...] = heads[:, : krylov + 1]
    wide = [jnp.broadcast_to(p, (8, per_box)) for p in projections]
    scale = jnp.concatenate([1.0 / norm] * (per_box // 128), axis=1)

    def one_box(b, _):
        lanes = pl.ds(pl.multiple_of(b * per_box, per_box), per_box)
        live = wide_row(live_ref, b)
        sent = wide[0] * basis_ref[0, :, lanes]
        for m in range(1, krylov):
            sent += wide[m] * basis_ref[m, :, lanes]
        next_ref[:, lanes] = (image_ref[:, lanes] - sent * live) * scale
        return 0

    lax.fori_loop(0, boxes, one_box, 0, unroll=4)


smem = pl.BlockSpec(memory_space=pltpu.SMEM)
vmem = pl.BlockSpec(memory_space=pltpu.VMEM)


def on_device(
    basis, facet_centres, normals, areas, contrast, facet_counts, box_centres, near_boxes, far_boxes
):
    krylov, rhs_local, facet_local = basis.shape
    boxes = facet_counts.shape[0]
    count = lax.axis_size("box")
    total_facets = count * facet_local
    areas = areas.reshape(-1, 128)
    contrast = contrast.reshape(-1, 128)

    def rows(number, width=128, dtype=f32):
        return jax.ShapeDtypeStruct((number, width), dtype)

    def limit(mebibytes):
        return pltpu.CompilerParams(vmem_limit_bytes=mebibytes * 1024 * 1024)

    sent, first, second, local = pl.pallas_call(
        prep_kernel,
        out_shape=(rows(544, dtype=bf16), rows(400), rows(288, dtype=bf16), rows(528)),
        in_specs=[pl.BlockSpec(memory_space=pl.ANY)] * 6,
        out_specs=(vmem,) * 4,
        scratch_shapes=[
            pltpu.VMEM((512, 128), f32),
            pltpu.SMEM(box_centres.shape, f32),
            pltpu.SMEM(facet_counts.shape, jnp.int32),
            pltpu.VMEM((rhs_local, facet_local), f32),
            pltpu.VMEM(facet_centres.shape, f32),
            pltpu.VMEM(areas.shape, f32),
            pltpu.VMEM(normals.shape, f32),
            pltpu.SemaphoreType.DMA((6,)),
        ],
        name="prepare",
    )(box_centres, facet_counts, basis, facet_centres, areas, normals)
    swap = [(0, 1), (1, 0)]
    ups = range(count - 1)
    cross = lax.ppermute(sent, "rhs", swap)
    first = lax.ppermute(
        first, ("box", "rhs"), [(2 * i, 2 * i + 2) for i in ups] + [(2 * i + 3, 2 * i + 1) for i in ups]
    )
    second = lax.ppermute(
        second, ("box", "rhs"), [(2 * i + 1, 2 * i + 2) for i in ups] + [(2 * i + 2, 2 * i + 1) for i in ups]
    )
    plane_slots = plane_boxes * per_box
    geometry, strengths, targets, planes, local = pl.pallas_call(
        feature_kernel,
        out_shape=(
            rows(boxes * depth, per_box, bf16),
            rows(boxes * 80, per_box, bf16),
            rows(plane_slots, depth, bf16),
            rows(plane_boxes * 8, per_box),
            rows(528),
        ),
        in_specs=[vmem] * 2,
        out_specs=(vmem,) * 5,
        compiler_params=limit(12),
        name="features",
    )(local, sent)
    mine, theirs = pl.pallas_call(
        field_kernel,
        out_shape=(rows(boxes * 8, per_box),) * 2,
        in_specs=[smem] + [vmem] * 8,
        out_specs=(vmem, vmem),
        scratch_shapes=[
            pltpu.VMEM((plane_boxes * depth, per_box), bf16),
            pltpu.VMEM((plane_boxes * 80, per_box), bf16),
            pltpu.VMEM((3 * plane_boxes * 80, per_box), bf16),
            pltpu.VMEM((plane_boxes * 160, per_box), f32),
            pltpu.VMEM((3 * plane_boxes * 16, per_box), f32),
            pltpu.VMEM((6 * 32, 128), f32),
            pltpu.VMEM((2 * 32, 128), f32),
        ],
        compiler_params=limit(32),
        name="fields",
    )(box_centres, local, cross, first, second, geometry, strengths, targets, planes)
    theirs = lax.ppermute(theirs, "rhs", swap)
    gram, live = pl.pallas_call(
        gram_kernel,
        out_shape=(rows(8), rows(2 * boxes)),
        in_specs=[smem, vmem],
        out_specs=(vmem, vmem),
        compiler_params=limit(8),
        name="gram",
    )(facet_counts, basis)
    image, tiles = pl.pallas_call(
        image_kernel,
        out_shape=(rows(rhs_local, facet_local), jax.ShapeDtypeStruct((count, 8, 128), f32)),
        in_specs=[vmem] * 6,
        out_specs=(vmem, vmem),
        compiler_params=limit(8),
        name="image",
    )(mine, theirs, gram, live, contrast, basis)
    tiles = lax.all_to_all(tiles, "box", 0, 0, tiled=True)
    next_vector, hessenberg = pl.pallas_call(
        functools.partial(finish_kernel, total_facets),
        out_shape=(rows(rhs_local, facet_local), rows(rhs_local, krylov + 1)),
        in_specs=[vmem] * 4,
        out_specs=(vmem, vmem),
        compiler_params=limit(16),
        name="finish",
    )(tiles, live, image, basis)
    return next_vector, hessenberg.T


def solution(mesh):
    return jax.shard_map(
        on_device,
        mesh=mesh,
        in_specs=(
            P(None, "rhs", "box"),
            P(None, "box"),
            P(None, "box"),
            P("box"),
            P("box"),
            P("box"),
            P(None, "box"),
            P("box", None),
            P("box", None),
        ),
        out_specs=(P("rhs", "box"), P(None, "rhs")),
        check_vma=False,
    )
```

```python
import functools

import jax
import jax.numpy as jnp
from jax import lax
from jax.experimental import pallas as pl
from jax.experimental.pallas import tpu as pltpu
from jax.sharding import PartitionSpec as P

soften = 0.0025
epsilon = 1e-06
f32 = jnp.float32
bf16 = jnp.bfloat16
plane_boxes = 16
per_box = 256
depth = 64


def lattice(centres_s, b):
    x = (centres_s[0, b] + 0.5).astype(jnp.int32)
    y = (centres_s[1, b] + 0.5).astype(jnp.int32)
    z = (centres_s[2, b] + 0.5).astype(jnp.int32)
    return x, y, z


def slot_of(centres_s, b):
    x, y, z = lattice(centres_s, b)
    return (z & 1) * plane_boxes + y * 4 + x


def wide_row(ref, b):
    return jnp.concatenate([ref[pl.ds(2 * b, 1), :], ref[pl.ds(2 * b + 1, 1), :]], axis=1)


def live_row(counts_s, b):
    slots = lax.broadcasted_iota(jnp.int32, (1, per_box), 1)
    return (slots < counts_s[b]).astype(f32)


def prep_kernel(
    centres_h, counts_h, basis_h, facets_h, areas_h, normals_h, cross_ref, first_ref, second_ref, local_ref,
    charges_v, centres_s, counts_s, current_ref, facets_ref, areas_ref, normals_ref, arrived
):
    boxes = counts_s.shape[0]
    moves = [
        (basis_h.at[basis_h.shape[0] - 1], current_ref),
        (facets_h, facets_ref),
        (areas_h, areas_ref),
        (normals_h, normals_ref),
        (centres_h, centres_s),
        (counts_h, counts_s),
    ]
    copies = [pltpu.make_async_copy(a, b, arrived.at[k]) for k, (a, b) in enumerate(moves)]
    for copy in copies:
        copy.start()
    for copy in copies:
        copy.wait()
    lane = lax.broadcasted_iota(jnp.int32, (8, 128), 1)
    row = lax.broadcasted_iota(jnp.int32, (8, 128), 0)
    empty = jnp.zeros((2, 128), f32)

    def one_box(b, carry):
        moments, centres = carry
        slot = slot_of(centres_s, b)
        lanes = pl.ds(pl.multiple_of(b * per_box, per_box), per_box)
        facets = facets_ref[:, lanes]
        normals = normals_ref[:, lanes]
        live = live_row(counts_s, b)
        weighted = current_ref[:, lanes] * (wide_row(areas_ref, b) * live / per_box)
        start = pl.multiple_of(slot * 16, 16)
        charges_v[pl.ds(start, 16), :] = jnp.concatenate([weighted[:, :128], weighted[:, 128:]], axis=0)
        local_ref[pl.ds(start, 16), :] = jnp.concatenate(
            [facets[:, :128], facets[:, 128:], empty, normals[:, :128], normals[:, 128:], empty], axis=0
        )
        moments += jnp.where(lane == slot, jnp.sum(weighted, axis=1, keepdims=True), 0.0)
        for a in range(3):
            dipole = jnp.sum(weighted * (facets[a : a + 1] - centres_s[a, b]), axis=1, keepdims=True)
            moments += jnp.where(lane == 32 * (a + 1) + slot, dipole, 0.0)
            centres += jnp.where((lane == slot) & (row == a), centres_s[a, b], 0.0)
        return moments, centres

    zeros = jnp.zeros((8, 128), f32)
    moments, centres = lax.fori_loop(0, boxes, one_box, (zeros, zeros), unroll=4)
    _, _, z = lattice(centres_s, 0)
    base_z = (z - (z & 1)).astype(f32) + 0.5
    centres = jnp.where((row == 3) | (row == 4), 1.5, jnp.where(row == 5, base_z, centres))
    half = lax.axis_index("rhs")
    away = pl.multiple_of((1 - half) * 256, 256)
    here = pl.multiple_of(half * 256, 256)
    pieces = jnp.concatenate([*thirds(moments), zeros], axis=0).astype(bf16)
    cross_ref[:512] = charges_v[...].astype(bf16)
    cross_ref[512:] = pieces
    second_ref[:256] = charges_v[pl.ds(here, 256), :].astype(bf16)
    second_ref[256:] = pieces
    first_ref[:256] = charges_v[pl.ds(away, 256), :].astype(bf16).astype(f32)
    for place in range(plane_boxes):
        first_ref[256 + 8 * place : 264 + 8 * place] = local_ref[pl.ds(away + 16 * place, 8), :]
    first_ref[384:392] = moments
    first_ref[392:] = centres
    local_ref[512:520] = moments
    local_ref[520:] = centres


def thirds(x):
    high = x.astype(bf16).astype(f32)
    rest = x - high
    middle = rest.astype(bf16).astype(f32)
    return high, middle, (rest - middle).astype(bf16).astype(f32)


def stacked_rows(parts, width):
    zeros = jnp.zeros((depth - 8 * len(parts), width), f32)
    return jnp.concatenate([*parts, zeros], axis=0)


def padded(rows):
    return jnp.concatenate([rows, jnp.zeros((8 - rows.shape[0], rows.shape[1]), f32)], axis=0)


def wide_charges(ref, place):
    both = ref[pl.ds(pl.multiple_of(place * 16, 16), 16), :].astype(f32)
    return jnp.concatenate([both[:8], both[8:]], axis=1)


def wide_tile(ref, start):
    tile = ref[pl.ds(pl.multiple_of(start, 8), 8), :]
    return jnp.concatenate([tile[0:3], tile[3:6]], axis=1)


def whole_moments(pieces):
    return pieces[:8] + (pieces[8:16] + pieces[16:24])


def store_geometry(local, box, geometry):
    row = lax.broadcasted_iota(jnp.int32, (8, per_box), 0)
    square = jnp.sum(local * local, axis=0, keepdims=True)
    features = jnp.where(row == 3, square, jnp.where(row == 4, 1.0, local))
    high, middle, low = thirds(features)
    rows = stacked_rows((high, high, high, middle, middle, low), per_box)
    geometry[pl.ds(pl.multiple_of(box * depth, depth), depth), :] = rows.astype(bf16)


def store_strengths(local, charges, box, strengths):
    products = jnp.concatenate([charges * local[a : a + 1] for a in range(3)], axis=0)
    rows = jnp.concatenate([charges, *thirds(products)], axis=0)
    strengths[pl.ds(pl.multiple_of(box * 80, 80), 80), :] = rows.astype(bf16)


def feature_kernel(local_ref, sent_ref, geometry, mine, targets, planes, local_out):
    boxes = 2 * plane_boxes
    half = lax.axis_index("rhs")
    origin = local_ref[523:526, 0:1]
    row = lax.broadcasted_iota(jnp.int32, (8, per_box), 0)

    def source(slot, _):
        local = padded(wide_tile(local_ref, slot * 16) - origin)
        store_geometry(local, slot, geometry)
        store_strengths(local, wide_charges(sent_ref, slot), slot, mine)
        return 0

    lax.fori_loop(0, boxes, source, 0, unroll=4)

    def target(place, _):
        start = (half * plane_boxes + place) * 16
        local = padded(wide_tile(local_ref, start) - origin)
        normal = padded(wide_tile(local_ref, start + 8))
        square = jnp.sum(local * local, axis=0, keepdims=True) + soften
        along = jnp.sum(local * normal, axis=0, keepdims=True)
        distance = jnp.where(row == 3, 1.0, jnp.where(row == 4, square, -2.0 * local))
        high, middle, low = thirds(distance)
        rows = stacked_rows((high, middle, low, high, middle, high), per_box)
        start = pl.multiple_of(place * per_box, per_box)
        targets[pl.ds(start, per_box), :] = jnp.transpose(rows).astype(bf16)
        planes[pl.ds(pl.multiple_of(place * 8, 8), 8), :] = jnp.where(row == 3, along, normal)
        return 0

    lax.fori_loop(0, plane_boxes, target, 0, unroll=4)
    local_out[...] = local_ref[...]


def near_planes(sources, targets, total, beside):
    def rows_at(pair, place, number):
        ref, first = pair
        return ref[pl.ds(pl.multiple_of((first + place) * number, number), number), :]

    def target_row(target_y, source_y, rows):
        runs = []
        for near_x in range(4):
            target = target_y * 4 + near_x
            for source in sources:
                for k in range(rows):
                    for x in range(max(near_x - 1, 0), min(near_x + 2, 4)):
                        runs.append((target, source, (source_y + k) * 4 + x))

        def distances(target, source, place):
            weights = rows_at(source[0], place, depth)
            starts = [pl.multiple_of(target * per_box + k, 128) for k in (0, 128)]
            return [jnp.dot(targets[pl.ds(start, 128), :], weights, preferred_element_type=f32) for start in starts]

        ahead = distances(*runs[0])
        cubed = []
        given = []
        for i, (target, source, place) in enumerate(runs):
            here = ahead
            if i + 1 < len(runs):
                ahead = distances(*runs[i + 1])
            parts = []
            for square in here:
                inverse = lax.rsqrt(square)
                parts.append((inverse * inverse * inverse).astype(bf16))
            cubed.append(jnp.concatenate(parts, axis=0))
            given.append(jnp.concatenate([rows_at(source[1], place, 80), rows_at(source[2], place, 80)], axis=0))
            if i + 1 == len(runs) or runs[i + 1][0] is not target:
                total[pl.ds(pl.multiple_of(target * 160, 160), 160), :] = lax.dot_general(
                    jnp.concatenate(given, axis=1),
                    jnp.concatenate(cubed, axis=1),
                    (((1,), (1,)), ((), ())),
                    preferred_element_type=f32,
                )
                cubed = []
                given = []

    def outer(i, _):
        target_row(3 * i, 2 * i, 2)
        beside(i)
        return 0

    def inner(i, _):
        target_row(i + 1, i, 3)
        beside(i + 2)
        return 0

    lax.fori_loop(0, 2, outer, 0)
    lax.fori_loop(0, 2, inner, 0)


def field_kernel(
    centres_s, local_ref, cross_ref, first_ref, second_ref, geometry, mine, targets, planes, mine_ref, theirs_ref,
    halo_geometry, halo_mine, theirs, total, far, far_centres, far_moments
):
    boxes = 2 * plane_boxes
    half = lax.axis_index("rhs")
    origin = local_ref[523:526, 0:1]

    def source(slot, _):
        local = wide_tile(local_ref, slot * 16) - origin
        store_strengths(local, wide_charges(cross_ref, slot), slot, theirs)
        return 0

    lax.fori_loop(0, boxes, source, 0, unroll=4)

    def halo_source(place, _):
        local = padded(wide_tile(first_ref, 256 + place * 8) - origin)
        store_geometry(local, place, halo_geometry)
        store_strengths(local, wide_charges(first_ref, place), place, halo_mine)
        store_strengths(local, wide_charges(second_ref, place), boxes + place, theirs)
        return 0

    lax.fori_loop(0, plane_boxes, halo_source, 0, unroll=4)

    for group, (centres, ours, others) in enumerate(
        (
            (first_ref[392:400], first_ref[384:392], second_ref[256:288]),
            (local_ref[520:528], local_ref[512:520], cross_ref[512:544]),
        )
    ):
        columns = jnp.transpose(jnp.concatenate([centres[:3] - origin, centres[3:]], axis=0))[:32]
        for a in range(3):
            far_centres[(group * 3 + a) * 32 : (group * 3 + a + 1) * 32, :] = jnp.broadcast_to(
                columns[:, a : a + 1], (32, 128)
            )
        both = jnp.concatenate([ours, whole_moments(others.astype(f32))], axis=0)
        high = both.astype(bf16).astype(f32)
        far_moments[group * 32 : group * 32 + 32, :] = jnp.concatenate([high, both - high], axis=0)
    lane = lax.broadcasted_iota(jnp.int32, (1, 128), 1)
    lane_x = lane & 3
    lane_y = (lane >> 2) & 3
    lane_plane = (lane >> 4) & 1

    def far_field(k):
        group = (k >= boxes).astype(jnp.int32)
        slot = jnp.where(k < boxes, k, half * plane_boxes + k - boxes)
        x, y, plane = slot & 3, (slot >> 2) & 3, slot >> 4
        local = wide_tile(local_ref, slot * 16) - origin
        normal = wide_tile(local_ref, slot * 16 + 8)
        d = []
        for a in range(3):
            centre = far_centres[pl.ds(pl.multiple_of((group * 3 + a) * 32, 32), 32), :]
            d.append(local[a : a + 1] - jnp.concatenate([centre, centre], axis=1))
        q = d[0] * d[0] + d[1] * d[1] + d[2] * d[2] + soften
        inverse = lax.rsqrt(q)
        inverse_2 = inverse * inverse
        inverse_3 = inverse_2 * inverse
        t = d[0] * normal[0:1] + d[1] * normal[1:2] + d[2] * normal[2:3]
        single = t * inverse_3
        steep = 3.0 * single * inverse_2
        coefficients = [single] + [steep * d[a] - normal[a : a + 1] * inverse_3 for a in range(3)]
        whole = jnp.concatenate(coefficients, axis=0)
        upper = whole.astype(bf16)
        lower = (whole - upper.astype(f32)).astype(bf16)
        lane_z = lane_plane + jnp.where(group == 0, 4 * half - 2, 0)
        near = (jnp.abs(lane_x - x) <= 1) & (jnp.abs(lane_y - y) <= 1) & (jnp.abs(lane_z - plane) <= 1)
        picked = jnp.where(near, 0.0, far_moments[pl.ds(pl.multiple_of(group * 32, 32), 32), :]).astype(bf16)
        first = jnp.dot(picked, upper, preferred_element_type=f32)
        second = jnp.dot(picked, lower, preferred_element_type=f32)
        return first[:16] + first[16:] + second[:16]

    def far_boxes(i):
        for k in range(12):
            k = i * 12 + k
            far[pl.ds(pl.multiple_of(k * 16, 16), 16), :] = far_field(k)

    sources = [((geometry, p), (mine, p), (theirs, p)) for p in (0, plane_boxes)]
    sources.append(((halo_geometry, 0), (halo_mine, 0), (theirs, boxes)))
    near_planes(sources, targets, total, far_boxes)

    def near_field(place, _):
        sums = total[pl.ds(pl.multiple_of(place * 160, 160), 160), :]
        side = planes[pl.ds(pl.multiple_of(place * 8, 8), 8), :]
        values = []
        for start in (0, 80):
            value = side[3:4] * sums[start : start + 8]
            for a in range(3):
                high, middle, low = (sums[i : i + 8] for i in range(start + 8 + 8 * a, start + 80, 24))
                value = value - side[a : a + 1] * (high + (middle + low))
            values.append(value)
        value = jnp.concatenate(values, axis=0)
        slot = half * plane_boxes + place
        rows = pl.ds(pl.multiple_of(slot * 16, 16), 16)
        far[rows, :] += value + far[pl.ds(pl.multiple_of((boxes + place) * 16, 16), 16), :]
        return 0

    lax.fori_loop(0, plane_boxes, near_field, 0, unroll=4)

    def given_back(b, _):
        start = pl.multiple_of(slot_of(centres_s, b) * 16, 16)
        rows = pl.ds(pl.multiple_of(b * 8, 8), 8)
        mine_ref[rows, :] = far[pl.ds(start, 8), :]
        theirs_ref[rows, :] = far[pl.ds(start + 8, 8), :]
        return 0

    lax.fori_loop(0, boxes, given_back, 0, unroll=4)


def gram_kernel(counts_s, basis_ref, sums_ref, live_ref):
    krylov = basis_ref.shape[0]
    pairs = [(m, n) for m in range(krylov) for n in range(m + 1)]

    def one_box(b, carry):
        lanes = pl.ds(pl.multiple_of(b * per_box, per_box), per_box)
        live = live_row(counts_s, b)
        live_ref[pl.ds(2 * b, 1), :] = live[:, :128]
        live_ref[pl.ds(2 * b + 1, 1), :] = live[:, 128:]
        rows = [basis_ref[m, :, lanes] * live for m in range(krylov)]
        out = []
        for k, (m, n) in enumerate(pairs):
            product = rows[m] * rows[n]
            out.append(carry[k] + product[:, :128] + product[:, 128:])
        return tuple(out)

    zeros = jnp.zeros((8, 128), f32)
    gram = lax.fori_loop(0, counts_s.shape[0], one_box, (zeros,) * len(pairs))
    lane = lax.broadcasted_iota(jnp.int32, (8, 128), 1)
    total = zeros
    for k, value in enumerate(gram):
        total = jnp.where(lane == krylov + 1 + k, jnp.sum(value, axis=1, keepdims=True), total)
    sums_ref[...] = total


def image_kernel(mine_ref, theirs_ref, gram_ref, live_ref, contrast_ref, basis_ref, image_ref, sums_ref):
    krylov = basis_ref.shape[0]

    def one_box(b, carry):
        lanes = pl.ds(pl.multiple_of(b * per_box, per_box), per_box)
        rows = pl.ds(pl.multiple_of(b * 8, 8), 8)
        live = wide_row(live_ref, b)
        part = mine_ref[rows, :] + theirs_ref[rows, :]
        image = live * (basis_ref[krylov - 1, :, lanes] - 2.0 * wide_row(contrast_ref, b) * part)
        image_ref[:, lanes] = image
        sums = []
        for m in range(krylov + 1):
            product = image * (basis_ref[m, :, lanes] if m < krylov else image)
            sums.append(carry[m] + product[:, :128] + product[:, 128:])
        return tuple(sums)

    zeros = jnp.zeros((8, 128), f32)
    sums = lax.fori_loop(0, live_ref.shape[0] // 2, one_box, (zeros,) * (krylov + 1), unroll=4)
    lane = lax.broadcasted_iota(jnp.int32, (8, 128), 1)
    total = gram_ref[...]
    for k, value in enumerate(sums):
        total = jnp.where(lane == k, jnp.sum(value, axis=1, keepdims=True), total)
    sums_ref[...] = jnp.broadcast_to(total[None], sums_ref.shape)


def two_sum(a, b):
    s = a + b
    c = s - a
    return s, (a - (s - c)) + (b - c)


def halves(a):
    c = a * 4097.0
    high = c - (c - a)
    return high, a - high


def two_product(a, b):
    p = a * b
    a_high, a_low = halves(a)
    b_high, b_low = halves(b)
    return p, ((a_high * b_high - p) + a_high * b_low + a_low * b_high) + a_low * b_low


def finish_kernel(total_facets, tiles_ref, live_ref, image_ref, basis_ref, next_ref, hessenberg_ref):
    boxes = live_ref.shape[0] // 2
    krylov = basis_ref.shape[0]
    lane = lax.broadcasted_iota(jnp.int32, (8, 128), 1)

    sums, rest = tiles_ref[0], jnp.zeros((8, 128), f32)
    for i in range(1, tiles_ref.shape[0]):
        sums, error = two_sum(sums, tiles_ref[i])
        rest = rest + error
    exact = sums + rest
    projections = [exact[:, m : m + 1] / total_facets for m in range(krylov)]
    pairs = [(m, n) for m in range(krylov) for n in range(m + 1)]
    first = jnp.where(lane == krylov, 1.0, 0.0)
    second = jnp.where(lane <= krylov, 1.0, 0.0)
    for m in range(krylov):
        first = jnp.where(lane == m, -2.0 * projections[m], first)
    for k, (m, n) in enumerate(pairs):
        at = lane == krylov + 1 + k
        scale = 1.0 if m == n else 2.0
        first = jnp.where(at, scale * projections[m], first)
        second = jnp.where(at, projections[n], second)
    factor, factor_rest = two_product(first, second)
    value, value_rest = two_product(factor, sums)
    value_rest = value_rest + (factor * rest + factor_rest * sums)
    for shift in (64, 32, 16, 8, 4, 2, 1):
        other = pltpu.roll(value, shift, 1)
        other_rest = pltpu.roll(value_rest, shift, 1)
        value, error = two_sum(value, other)
        value_rest = (value_rest + other_rest) + error
    remaining = jnp.maximum(value + value_rest, 0.0)
    norm = jnp.sqrt(remaining / total_facets + epsilon)
    heads = jnp.where(lane == krylov, norm, 0.0)
    for m in range(krylov):
        heads = jnp.where(lane == m, projections[m], heads)
    hessenberg_ref[...] = heads[:, : krylov + 1]
    wide = [jnp.broadcast_to(p, (8, per_box)) for p in projections]
    scale = jnp.concatenate([1.0 / norm] * (per_box // 128), axis=1)

    def one_box(b, _):
        lanes = pl.ds(pl.multiple_of(b * per_box, per_box), per_box)
        live = wide_row(live_ref, b)
        sent = wide[0] * basis_ref[0, :, lanes]
        for m in range(1, krylov):
            sent += wide[m] * basis_ref[m, :, lanes]
        next_ref[:, lanes] = (image_ref[:, lanes] - sent * live) * scale
        return 0

    lax.fori_loop(0, boxes, one_box, 0, unroll=4)


smem = pl.BlockSpec(memory_space=pltpu.SMEM)
vmem = pl.BlockSpec(memory_space=pltpu.VMEM)


def on_device(
    basis, facet_centres, normals, areas, contrast, facet_counts, box_centres, near_boxes, far_boxes
):
    krylov, rhs_local, facet_local = basis.shape
    boxes = facet_counts.shape[0]
    count = lax.axis_size("box")
    total_facets = count * facet_local
    areas = areas.reshape(-1, 128)
    contrast = contrast.reshape(-1, 128)

    def rows(number, width=128, dtype=f32):
        return jax.ShapeDtypeStruct((number, width), dtype)

    def limit(mebibytes):
        return pltpu.CompilerParams(vmem_limit_bytes=mebibytes * 1024 * 1024)

    sent, first, second, local = pl.pallas_call(
        prep_kernel,
        out_shape=(rows(544, dtype=bf16), rows(400), rows(288, dtype=bf16), rows(528)),
        in_specs=[pl.BlockSpec(memory_space=pl.ANY)] * 6,
        out_specs=(vmem,) * 4,
        scratch_shapes=[
            pltpu.VMEM((512, 128), f32),
            pltpu.SMEM(box_centres.shape, f32),
            pltpu.SMEM(facet_counts.shape, jnp.int32),
            pltpu.VMEM((rhs_local, facet_local), f32),
            pltpu.VMEM(facet_centres.shape, f32),
            pltpu.VMEM(areas.shape, f32),
            pltpu.VMEM(normals.shape, f32),
            pltpu.SemaphoreType.DMA((6,)),
        ],
        name="prepare",
    )(box_centres, facet_counts, basis, facet_centres, areas, normals)
    swap = [(0, 1), (1, 0)]
    ups = range(count - 1)
    cross = lax.ppermute(sent, "rhs", swap)
    first = lax.ppermute(
        first, ("box", "rhs"), [(2 * i, 2 * i + 2) for i in ups] + [(2 * i + 3, 2 * i + 1) for i in ups]
    )
    second = lax.ppermute(
        second, ("box", "rhs"), [(2 * i + 1, 2 * i + 2) for i in ups] + [(2 * i + 2, 2 * i + 1) for i in ups]
    )
    plane_slots = plane_boxes * per_box
    geometry, strengths, targets, planes, local = pl.pallas_call(
        feature_kernel,
        out_shape=(
            rows(boxes * depth, per_box, bf16),
            rows(boxes * 80, per_box, bf16),
            rows(plane_slots, depth, bf16),
            rows(plane_boxes * 8, per_box),
            rows(528),
        ),
        in_specs=[vmem] * 2,
        out_specs=(vmem,) * 5,
        compiler_params=limit(12),
        name="features",
    )(local, sent)
    mine, theirs = pl.pallas_call(
        field_kernel,
        out_shape=(rows(boxes * 8, per_box),) * 2,
        in_specs=[smem] + [vmem] * 8,
        out_specs=(vmem, vmem),
        scratch_shapes=[
            pltpu.VMEM((plane_boxes * depth, per_box), bf16),
            pltpu.VMEM((plane_boxes * 80, per_box), bf16),
            pltpu.VMEM((3 * plane_boxes * 80, per_box), bf16),
            pltpu.VMEM((plane_boxes * 160, per_box), f32),
            pltpu.VMEM((3 * plane_boxes * 16, per_box), f32),
            pltpu.VMEM((6 * 32, 128), f32),
            pltpu.VMEM((2 * 32, 128), f32),
        ],
        compiler_params=limit(32),
        name="fields",
    )(box_centres, local, cross, first, second, geometry, strengths, targets, planes)
    theirs = lax.ppermute(theirs, "rhs", swap)
    gram, live = pl.pallas_call(
        gram_kernel,
        out_shape=(rows(8), rows(2 * boxes)),
        in_specs=[smem, vmem],
        out_specs=(vmem, vmem),
        compiler_params=limit(8),
        name="gram",
    )(facet_counts, basis)
    image, tiles = pl.pallas_call(
        image_kernel,
        out_shape=(rows(rhs_local, facet_local), jax.ShapeDtypeStruct((count, 8, 128), f32)),
        in_specs=[vmem] * 6,
        out_specs=(vmem, vmem),
        compiler_params=limit(8),
        name="image",
    )(mine, theirs, gram, live, contrast, basis)
    tiles = lax.all_to_all(tiles, "box", 0, 0, tiled=True)
    next_vector, hessenberg = pl.pallas_call(
        functools.partial(finish_kernel, total_facets),
        out_shape=(rows(rhs_local, facet_local), rows(rhs_local, krylov + 1)),
        in_specs=[vmem] * 4,
        out_specs=(vmem, vmem),
        compiler_params=limit(16),
        name="finish",
    )(tiles, live, image, basis)
    return next_vector, hessenberg.T


def solution(mesh):
    return jax.shard_map(
        on_device,
        mesh=mesh,
        in_specs=(
            P(None, "rhs", "box"),
            P(None, "box"),
            P(None, "box"),
            P("box"),
            P("box"),
            P("box"),
            P(None, "box"),
            P("box", None),
            P("box", None),
        ),
        out_specs=(P("rhs", "box"), P(None, "rhs")),
        check_vma=False,
    )
```

```python
import functools

import jax
import jax.numpy as jnp
from jax import lax
from jax.experimental import pallas as pl
from jax.experimental.pallas import tpu as pltpu
from jax.sharding import PartitionSpec as P

soften = 0.0025
epsilon = 1e-06
f32 = jnp.float32
bf16 = jnp.bfloat16
plane_boxes = 16
per_box = 256
depth = 64


def lattice(centres_s, b):
    x = (centres_s[0, b] + 0.5).astype(jnp.int32)
    y = (centres_s[1, b] + 0.5).astype(jnp.int32)
    z = (centres_s[2, b] + 0.5).astype(jnp.int32)
    return x, y, z


def slot_of(centres_s, b):
    x, y, z = lattice(centres_s, b)
    return (z & 1) * plane_boxes + y * 4 + x


def wide_row(ref, b):
    return jnp.concatenate([ref[pl.ds(2 * b, 1), :], ref[pl.ds(2 * b + 1, 1), :]], axis=1)


def live_row(counts_s, b):
    slots = lax.broadcasted_iota(jnp.int32, (1, per_box), 1)
    return (slots < counts_s[b]).astype(f32)


def prep_kernel(
    centres_h, counts_h, basis_h, facets_h, areas_h, normals_h, cross_ref, first_ref, second_ref, local_ref,
    charges_v, centres_s, counts_s, current_ref, facets_ref, areas_ref, normals_ref, arrived
):
    boxes = counts_s.shape[0]
    moves = [
        (basis_h.at[basis_h.shape[0] - 1], current_ref),
        (facets_h, facets_ref),
        (areas_h, areas_ref),
        (normals_h, normals_ref),
        (centres_h, centres_s),
        (counts_h, counts_s),
    ]
    copies = [pltpu.make_async_copy(a, b, arrived.at[k]) for k, (a, b) in enumerate(moves)]
    for copy in copies:
        copy.start()
    for copy in copies:
        copy.wait()
    lane = lax.broadcasted_iota(jnp.int32, (8, 128), 1)
    row = lax.broadcasted_iota(jnp.int32, (8, 128), 0)
    empty = jnp.zeros((2, 128), f32)

    def one_box(b, carry):
        moments, centres = carry
        slot = slot_of(centres_s, b)
        lanes = pl.ds(pl.multiple_of(b * per_box, per_box), per_box)
        facets = facets_ref[:, lanes]
        normals = normals_ref[:, lanes]
        live = live_row(counts_s, b)
        weighted = current_ref[:, lanes] * (wide_row(areas_ref, b) * live / per_box)
        start = pl.multiple_of(slot * 16, 16)
        charges_v[pl.ds(start, 16), :] = jnp.concatenate([weighted[:, :128], weighted[:, 128:]], axis=0)
        local_ref[pl.ds(start, 16), :] = jnp.concatenate(
            [facets[:, :128], facets[:, 128:], empty, normals[:, :128], normals[:, 128:], empty], axis=0
        )
        moments += jnp.where(lane == slot, jnp.sum(weighted, axis=1, keepdims=True), 0.0)
        for a in range(3):
            dipole = jnp.sum(weighted * (facets[a : a + 1] - centres_s[a, b]), axis=1, keepdims=True)
            moments += jnp.where(lane == 32 * (a + 1) + slot, dipole, 0.0)
            centres += jnp.where((lane == slot) & (row == a), centres_s[a, b], 0.0)
        return moments, centres

    zeros = jnp.zeros((8, 128), f32)
    moments, centres = lax.fori_loop(0, boxes, one_box, (zeros, zeros), unroll=8)
    _, _, z = lattice(centres_s, 0)
    base_z = (z - (z & 1)).astype(f32) + 0.5
    centres = jnp.where((row == 3) | (row == 4), 1.5, jnp.where(row == 5, base_z, centres))
    half = lax.axis_index("rhs")
    away = pl.multiple_of((1 - half) * 256, 256)
    here = pl.multiple_of(half * 256, 256)
    pieces = jnp.concatenate([*thirds(moments), zeros], axis=0).astype(bf16)
    cross_ref[:512] = charges_v[...].astype(bf16)
    cross_ref[512:] = pieces
    second_ref[:256] = charges_v[pl.ds(here, 256), :].astype(bf16)
    second_ref[256:] = pieces
    first_ref[:256] = charges_v[pl.ds(away, 256), :].astype(bf16).astype(f32)
    for place in range(plane_boxes):
        first_ref[256 + 8 * place : 264 + 8 * place] = local_ref[pl.ds(away + 16 * place, 8), :]
    first_ref[384:392] = moments
    first_ref[392:] = centres
    local_ref[512:520] = moments
    local_ref[520:528] = centres
    local_ref[528:] = charges_v[...].astype(bf16).astype(f32)


def thirds(x):
    high = x.astype(bf16).astype(f32)
    rest = x - high
    middle = rest.astype(bf16).astype(f32)
    return high, middle, (rest - middle).astype(bf16).astype(f32)


def stacked_rows(parts, width):
    zeros = jnp.zeros((depth - 8 * len(parts), width), f32)
    return jnp.concatenate([*parts, zeros], axis=0)


def padded(rows):
    return jnp.concatenate([rows, jnp.zeros((8 - rows.shape[0], rows.shape[1]), f32)], axis=0)


def wide_charges(ref, place):
    both = ref[pl.ds(pl.multiple_of(place * 16, 16), 16), :].astype(f32)
    return jnp.concatenate([both[:8], both[8:]], axis=1)


def wide_tile(ref, start):
    tile = ref[pl.ds(pl.multiple_of(start, 8), 8), :]
    return jnp.concatenate([tile[0:3], tile[3:6]], axis=1)


def whole_moments(pieces):
    return pieces[:8] + (pieces[8:16] + pieces[16:24])


def store_geometry(local, box, geometry):
    row = lax.broadcasted_iota(jnp.int32, (8, per_box), 0)
    square = jnp.sum(local * local, axis=0, keepdims=True)
    features = jnp.where(row == 3, square, jnp.where(row == 4, 1.0, local))
    high, middle, low = thirds(features)
    rows = stacked_rows((high, high, high, middle, middle, low), per_box)
    geometry[pl.ds(pl.multiple_of(box * depth, depth), depth), :] = rows.astype(bf16)


def store_strengths(local, charges, box, strengths):
    products = jnp.concatenate([charges * local[a : a + 1] for a in range(3)], axis=0)
    rows = jnp.concatenate([charges, *thirds(products)], axis=0)
    strengths[pl.ds(pl.multiple_of(box * 80, 80), 80), :] = rows.astype(bf16)


def feature_kernel(local_ref, geometry, mine, targets, planes, local_out):
    boxes = 2 * plane_boxes
    half = lax.axis_index("rhs")
    origin = local_ref[523:526, 0:1]
    row = lax.broadcasted_iota(jnp.int32, (8, per_box), 0)

    def source(slot, _):
        local = padded(wide_tile(local_ref, slot * 16) - origin)
        store_geometry(local, slot, geometry)
        store_strengths(local, wide_charges(local_ref, 33 + slot), slot, mine)
        return 0

    lax.fori_loop(0, boxes, source, 0, unroll=4)

    def target(place, _):
        start = (half * plane_boxes + place) * 16
        local = padded(wide_tile(local_ref, start) - origin)
        normal = padded(wide_tile(local_ref, start + 8))
        square = jnp.sum(local * local, axis=0, keepdims=True) + soften
        along = jnp.sum(local * normal, axis=0, keepdims=True)
        distance = jnp.where(row == 3, 1.0, jnp.where(row == 4, square, -2.0 * local))
        high, middle, low = thirds(distance)
        rows = stacked_rows((high, middle, low, high, middle, high), per_box)
        start = pl.multiple_of(place * per_box, per_box)
        targets[pl.ds(start, per_box), :] = jnp.transpose(rows).astype(bf16)
        planes[pl.ds(pl.multiple_of(place * 8, 8), 8), :] = jnp.where(row == 3, along, normal)
        return 0

    lax.fori_loop(0, plane_boxes, target, 0, unroll=4)
    local_out[...] = local_ref[:528]


def near_planes(sources, targets, total, beside):
    def rows_at(pair, place, number):
        ref, first = pair
        return ref[pl.ds(pl.multiple_of((first + place) * number, number), number), :]

    def target_row(target_y, source_y, rows):
        runs = []
        for near_x in range(4):
            target = target_y * 4 + near_x
            for source in sources:
                for k in range(rows):
                    for x in range(max(near_x - 1, 0), min(near_x + 2, 4)):
                        runs.append((target, source, (source_y + k) * 4 + x))

        def distances(target, source, place):
            facets = targets[pl.ds(pl.multiple_of(target * per_box, per_box), per_box), :]
            return jnp.dot(facets, rows_at(source[0], place, depth), preferred_element_type=f32)

        ahead = distances(*runs[0])
        cubed = []
        given = []
        for i, (target, source, place) in enumerate(runs):
            here = ahead
            if i + 1 < len(runs):
                ahead = distances(*runs[i + 1])
            inverse = lax.rsqrt(here)
            cubed.append((inverse * inverse * inverse).astype(bf16))
            given.append(jnp.concatenate([rows_at(source[1], place, 80), rows_at(source[2], place, 80)], axis=0))
            if i + 1 == len(runs) or runs[i + 1][0] is not target:
                total[pl.ds(pl.multiple_of(target * 160, 160), 160), :] = lax.dot_general(
                    jnp.concatenate(given, axis=1),
                    jnp.concatenate(cubed, axis=1),
                    (((1,), (1,)), ((), ())),
                    preferred_element_type=f32,
                )
                cubed = []
                given = []

    def outer(i, _):
        target_row(3 * i, 2 * i, 2)
        beside(i)
        return 0

    def inner(i, _):
        target_row(i + 1, i, 3)
        beside(i + 2)
        return 0

    lax.fori_loop(0, 2, outer, 0)
    lax.fori_loop(0, 2, inner, 0)


def field_kernel(
    centres_s, local_ref, cross_ref, first_ref, second_ref, geometry, mine, targets, planes, mine_ref, theirs_ref,
    halo_geometry, halo_mine, theirs, total, far, far_centres, far_moments
):
    boxes = 2 * plane_boxes
    half = lax.axis_index("rhs")
    origin = local_ref[523:526, 0:1]

    def source(slot, _):
        local = wide_tile(local_ref, slot * 16) - origin
        store_strengths(local, wide_charges(cross_ref, slot), slot, theirs)
        return 0

    lax.fori_loop(0, boxes, source, 0, unroll=4)

    def halo_source(place, _):
        local = padded(wide_tile(first_ref, 256 + place * 8) - origin)
        store_geometry(local, place, halo_geometry)
        store_strengths(local, wide_charges(first_ref, place), place, halo_mine)
        store_strengths(local, wide_charges(second_ref, place), boxes + place, theirs)
        return 0

    lax.fori_loop(0, plane_boxes, halo_source, 0, unroll=4)

    for group, (centres, ours, others) in enumerate(
        (
            (first_ref[392:400], first_ref[384:392], second_ref[256:288]),
            (local_ref[520:528], local_ref[512:520], cross_ref[512:544]),
        )
    ):
        columns = jnp.transpose(jnp.concatenate([centres[:3] - origin, centres[3:]], axis=0))[:32]
        for a in range(3):
            far_centres[(group * 3 + a) * 32 : (group * 3 + a + 1) * 32, :] = jnp.broadcast_to(
                columns[:, a : a + 1], (32, 128)
            )
        both = jnp.concatenate([ours, whole_moments(others.astype(f32))], axis=0)
        high = both.astype(bf16).astype(f32)
        far_moments[group * 32 : group * 32 + 32, :] = jnp.concatenate([high, both - high], axis=0)
    lane = lax.broadcasted_iota(jnp.int32, (1, 128), 1)
    lane_x = lane & 3
    lane_y = (lane >> 2) & 3
    lane_plane = (lane >> 4) & 1

    def far_field(k):
        group = (k >= boxes).astype(jnp.int32)
        slot = jnp.where(k < boxes, k, half * plane_boxes + k - boxes)
        x, y, plane = slot & 3, (slot >> 2) & 3, slot >> 4
        local = wide_tile(local_ref, slot * 16) - origin
        normal = wide_tile(local_ref, slot * 16 + 8)
        d = []
        for a in range(3):
            centre = far_centres[pl.ds(pl.multiple_of((group * 3 + a) * 32, 32), 32), :]
            d.append(local[a : a + 1] - jnp.concatenate([centre, centre], axis=1))
        q = d[0] * d[0] + d[1] * d[1] + d[2] * d[2] + soften
        inverse = lax.rsqrt(q)
        inverse_2 = inverse * inverse
        inverse_3 = inverse_2 * inverse
        t = d[0] * normal[0:1] + d[1] * normal[1:2] + d[2] * normal[2:3]
        single = t * inverse_3
        steep = 3.0 * single * inverse_2
        coefficients = [single] + [steep * d[a] - normal[a : a + 1] * inverse_3 for a in range(3)]
        whole = jnp.concatenate(coefficients, axis=0)
        upper = whole.astype(bf16)
        lower = (whole - upper.astype(f32)).astype(bf16)
        lane_z = lane_plane + jnp.where(group == 0, 4 * half - 2, 0)
        near = (jnp.abs(lane_x - x) <= 1) & (jnp.abs(lane_y - y) <= 1) & (jnp.abs(lane_z - plane) <= 1)
        picked = jnp.where(near, 0.0, far_moments[pl.ds(pl.multiple_of(group * 32, 32), 32), :]).astype(bf16)
        first = jnp.dot(picked, upper, preferred_element_type=f32)
        second = jnp.dot(picked, lower, preferred_element_type=f32)
        return first[:16] + first[16:] + second[:16]

    def far_boxes(i):
        for k in range(12):
            k = i * 12 + k
            far[pl.ds(pl.multiple_of(k * 16, 16), 16), :] = far_field(k)

    sources = [((geometry, p), (mine, p), (theirs, p)) for p in (0, plane_boxes)]
    sources.append(((halo_geometry, 0), (halo_mine, 0), (theirs, boxes)))
    near_planes(sources, targets, total, far_boxes)

    def near_field(place, _):
        sums = total[pl.ds(pl.multiple_of(place * 160, 160), 160), :]
        side = planes[pl.ds(pl.multiple_of(place * 8, 8), 8), :]
        values = []
        for start in (0, 80):
            value = side[3:4] * sums[start : start + 8]
            for a in range(3):
                high, middle, low = (sums[i : i + 8] for i in range(start + 8 + 8 * a, start + 80, 24))
                value = value - side[a : a + 1] * (high + (middle + low))
            values.append(value)
        value = jnp.concatenate(values, axis=0)
        slot = half * plane_boxes + place
        rows = pl.ds(pl.multiple_of(slot * 16, 16), 16)
        far[rows, :] += value + far[pl.ds(pl.multiple_of((boxes + place) * 16, 16), 16), :]
        return 0

    lax.fori_loop(0, plane_boxes, near_field, 0, unroll=4)

    def given_back(b, _):
        start = pl.multiple_of(slot_of(centres_s, b) * 16, 16)
        rows = pl.ds(pl.multiple_of(b * 8, 8), 8)
        mine_ref[rows, :] = far[pl.ds(start, 8), :]
        theirs_ref[rows, :] = far[pl.ds(start + 8, 8), :]
        return 0

    lax.fori_loop(0, boxes, given_back, 0, unroll=4)


def gram_kernel(counts_s, basis_ref, sums_ref, live_ref):
    krylov = basis_ref.shape[0]
    pairs = [(m, n) for m in range(krylov) for n in range(m + 1)]

    def one_box(b, carry):
        lanes = pl.ds(pl.multiple_of(b * per_box, per_box), per_box)
        live = live_row(counts_s, b)
        live_ref[pl.ds(2 * b, 1), :] = live[:, :128]
        live_ref[pl.ds(2 * b + 1, 1), :] = live[:, 128:]
        rows = [basis_ref[m, :, lanes] * live for m in range(krylov)]
        out = []
        for k, (m, n) in enumerate(pairs):
            product = rows[m] * rows[n]
            out.append(carry[k] + product[:, :128] + product[:, 128:])
        return tuple(out)

    zeros = jnp.zeros((8, 128), f32)
    gram = lax.fori_loop(0, counts_s.shape[0], one_box, (zeros,) * len(pairs))
    lane = lax.broadcasted_iota(jnp.int32, (8, 128), 1)
    total = zeros
    for k, value in enumerate(gram):
        total = jnp.where(lane == krylov + 1 + k, jnp.sum(value, axis=1, keepdims=True), total)
    sums_ref[...] = total


def image_kernel(mine_ref, theirs_ref, gram_ref, live_ref, contrast_ref, basis_ref, image_ref, sums_ref):
    krylov = basis_ref.shape[0]

    def one_box(b, carry):
        lanes = pl.ds(pl.multiple_of(b * per_box, per_box), per_box)
        rows = pl.ds(pl.multiple_of(b * 8, 8), 8)
        live = wide_row(live_ref, b)
        part = mine_ref[rows, :] + theirs_ref[rows, :]
        image = live * (basis_ref[krylov - 1, :, lanes] - 2.0 * wide_row(contrast_ref, b) * part)
        image_ref[:, lanes] = image
        sums = []
        for m in range(krylov + 1):
            product = image * (basis_ref[m, :, lanes] if m < krylov else image)
            sums.append(carry[m] + product[:, :128] + product[:, 128:])
        return tuple(sums)

    zeros = jnp.zeros((8, 128), f32)
    sums = lax.fori_loop(0, live_ref.shape[0] // 2, one_box, (zeros,) * (krylov + 1), unroll=4)
    lane = lax.broadcasted_iota(jnp.int32, (8, 128), 1)
    total = gram_ref[...]
    for k, value in enumerate(sums):
        total = jnp.where(lane == k, jnp.sum(value, axis=1, keepdims=True), total)
    sums_ref[...] = jnp.broadcast_to(total[None], sums_ref.shape)


def two_sum(a, b):
    s = a + b
    c = s - a
    return s, (a - (s - c)) + (b - c)


def halves(a):
    c = a * 4097.0
    high = c - (c - a)
    return high, a - high


def two_product(a, b):
    p = a * b
    a_high, a_low = halves(a)
    b_high, b_low = halves(b)
    return p, ((a_high * b_high - p) + a_high * b_low + a_low * b_high) + a_low * b_low


def finish_kernel(total_facets, tiles_ref, live_ref, image_ref, basis_ref, next_ref, hessenberg_ref):
    boxes = live_ref.shape[0] // 2
    krylov = basis_ref.shape[0]
    lane = lax.broadcasted_iota(jnp.int32, (8, 128), 1)

    sums, rest = tiles_ref[0], jnp.zeros((8, 128), f32)
    for i in range(1, tiles_ref.shape[0]):
        sums, error = two_sum(sums, tiles_ref[i])
        rest = rest + error
    exact = sums + rest
    projections = [exact[:, m : m + 1] / total_facets for m in range(krylov)]
    pairs = [(m, n) for m in range(krylov) for n in range(m + 1)]
    first = jnp.where(lane == krylov, 1.0, 0.0)
    second = jnp.where(lane <= krylov, 1.0, 0.0)
    for m in range(krylov):
        first = jnp.where(lane == m, -2.0 * projections[m], first)
    for k, (m, n) in enumerate(pairs):
        at = lane == krylov + 1 + k
        scale = 1.0 if m == n else 2.0
        first = jnp.where(at, scale * projections[m], first)
        second = jnp.where(at, projections[n], second)
    factor, factor_rest = two_product(first, second)
    value, value_rest = two_product(factor, sums)
    value_rest = value_rest + (factor * rest + factor_rest * sums)
    for shift in (64, 32, 16, 8, 4, 2, 1):
        other = pltpu.roll(value, shift, 1)
        other_rest = pltpu.roll(value_rest, shift, 1)
        value, error = two_sum(value, other)
        value_rest = (value_rest + other_rest) + error
    remaining = jnp.maximum(value + value_rest, 0.0)
    norm = jnp.sqrt(remaining / total_facets + epsilon)
    heads = jnp.where(lane == krylov, norm, 0.0)
    for m in range(krylov):
        heads = jnp.where(lane == m, projections[m], heads)
    hessenberg_ref[...] = heads[:, : krylov + 1]
    wide = [jnp.broadcast_to(p, (8, per_box)) for p in projections]
    scale = jnp.concatenate([1.0 / norm] * (per_box // 128), axis=1)

    def one_box(b, _):
        lanes = pl.ds(pl.multiple_of(b * per_box, per_box), per_box)
        live = wide_row(live_ref, b)
        sent = wide[0] * basis_ref[0, :, lanes]
        for m in range(1, krylov):
            sent += wide[m] * basis_ref[m, :, lanes]
        next_ref[:, lanes] = (image_ref[:, lanes] - sent * live) * scale
        return 0

    lax.fori_loop(0, boxes, one_box, 0, unroll=4)


smem = pl.BlockSpec(memory_space=pltpu.SMEM)
vmem = pl.BlockSpec(memory_space=pltpu.VMEM)


def on_device(
    basis, facet_centres, normals, areas, contrast, facet_counts, box_centres, near_boxes, far_boxes
):
    krylov, rhs_local, facet_local = basis.shape
    boxes = facet_counts.shape[0]
    count = lax.axis_size("box")
    total_facets = count * facet_local
    areas = areas.reshape(-1, 128)
    contrast = contrast.reshape(-1, 128)

    def rows(number, width=128, dtype=f32):
        return jax.ShapeDtypeStruct((number, width), dtype)

    def limit(mebibytes):
        return pltpu.CompilerParams(vmem_limit_bytes=mebibytes * 1024 * 1024)

    sent, first, second, local = pl.pallas_call(
        prep_kernel,
        out_shape=(rows(544, dtype=bf16), rows(400), rows(288, dtype=bf16), rows(1040)),
        in_specs=[pl.BlockSpec(memory_space=pl.ANY)] * 6,
        out_specs=(vmem,) * 4,
        scratch_shapes=[
            pltpu.VMEM((512, 128), f32),
            pltpu.SMEM(box_centres.shape, f32),
            pltpu.SMEM(facet_counts.shape, jnp.int32),
            pltpu.VMEM((rhs_local, facet_local), f32),
            pltpu.VMEM(facet_centres.shape, f32),
            pltpu.VMEM(areas.shape, f32),
            pltpu.VMEM(normals.shape, f32),
            pltpu.SemaphoreType.DMA((6,)),
        ],
        name="prepare",
    )(box_centres, facet_counts, basis, facet_centres, areas, normals)
    swap = [(0, 1), (1, 0)]
    ups = range(count - 1)
    cross = lax.ppermute(sent, "rhs", swap)
    first = lax.ppermute(
        first, ("box", "rhs"), [(2 * i, 2 * i + 2) for i in ups] + [(2 * i + 3, 2 * i + 1) for i in ups]
    )
    second = lax.ppermute(
        second, ("box", "rhs"), [(2 * i + 1, 2 * i + 2) for i in ups] + [(2 * i + 2, 2 * i + 1) for i in ups]
    )
    plane_slots = plane_boxes * per_box
    geometry, strengths, targets, planes, local = pl.pallas_call(
        feature_kernel,
        out_shape=(
            rows(boxes * depth, per_box, bf16),
            rows(boxes * 80, per_box, bf16),
            rows(plane_slots, depth, bf16),
            rows(plane_boxes * 8, per_box),
            rows(528),
        ),
        in_specs=[vmem],
        out_specs=(vmem,) * 5,
        compiler_params=limit(12),
        name="features",
    )(local)
    mine, theirs = pl.pallas_call(
        field_kernel,
        out_shape=(rows(boxes * 8, per_box),) * 2,
        in_specs=[smem] + [vmem] * 8,
        out_specs=(vmem, vmem),
        scratch_shapes=[
            pltpu.VMEM((plane_boxes * depth, per_box), bf16),
            pltpu.VMEM((plane_boxes * 80, per_box), bf16),
            pltpu.VMEM((3 * plane_boxes * 80, per_box), bf16),
            pltpu.VMEM((plane_boxes * 160, per_box), f32),
            pltpu.VMEM((3 * plane_boxes * 16, per_box), f32),
            pltpu.VMEM((6 * 32, 128), f32),
            pltpu.VMEM((2 * 32, 128), f32),
        ],
        compiler_params=limit(32),
        name="fields",
    )(box_centres, local, cross, first, second, geometry, strengths, targets, planes)
    theirs = lax.ppermute(theirs, "rhs", swap)
    gram, live = pl.pallas_call(
        gram_kernel,
        out_shape=(rows(8), rows(2 * boxes)),
        in_specs=[smem, vmem],
        out_specs=(vmem, vmem),
        compiler_params=limit(8),
        name="gram",
    )(facet_counts, basis)
    image, tiles = pl.pallas_call(
        image_kernel,
        out_shape=(rows(rhs_local, facet_local), jax.ShapeDtypeStruct((count, 8, 128), f32)),
        in_specs=[vmem] * 6,
        out_specs=(vmem, vmem),
        compiler_params=limit(8),
        name="image",
    )(mine, theirs, gram, live, contrast, basis)
    tiles = lax.all_to_all(tiles, "box", 0, 0, tiled=True)
    next_vector, hessenberg = pl.pallas_call(
        functools.partial(finish_kernel, total_facets),
        out_shape=(rows(rhs_local, facet_local), rows(rhs_local, krylov + 1)),
        in_specs=[vmem] * 4,
        out_specs=(vmem, vmem),
        compiler_params=limit(16),
        name="finish",
    )(tiles, live, image, basis)
    return next_vector, hessenberg.T


def solution(mesh):
    return jax.shard_map(
        on_device,
        mesh=mesh,
        in_specs=(
            P(None, "rhs", "box"),
            P(None, "box"),
            P(None, "box"),
            P("box"),
            P("box"),
            P("box"),
            P(None, "box"),
            P("box", None),
            P("box", None),
        ),
        out_specs=(P("rhs", "box"), P(None, "rhs")),
        check_vma=False,
    )
```

```python
import functools

import jax
import jax.numpy as jnp
from jax import lax
from jax.experimental import pallas as pl
from jax.experimental.pallas import tpu as pltpu
from jax.sharding import PartitionSpec as P

soften = 0.0025
epsilon = 1e-06
f32 = jnp.float32
bf16 = jnp.bfloat16
plane_boxes = 16
per_box = 256
depth = 64


def lattice(centres_s, b):
    x = (centres_s[0, b] + 0.5).astype(jnp.int32)
    y = (centres_s[1, b] + 0.5).astype(jnp.int32)
    z = (centres_s[2, b] + 0.5).astype(jnp.int32)
    return x, y, z


def slot_of(centres_s, b):
    x, y, z = lattice(centres_s, b)
    return (z & 1) * plane_boxes + y * 4 + x


def wide_row(ref, b):
    return jnp.concatenate([ref[pl.ds(2 * b, 1), :], ref[pl.ds(2 * b + 1, 1), :]], axis=1)


def live_row(counts_s, b):
    slots = lax.broadcasted_iota(jnp.int32, (1, per_box), 1)
    return (slots < counts_s[b]).astype(f32)


def prep_kernel(
    centres_h, counts_h, basis_h, facets_h, areas_h, normals_h, cross_ref, first_ref, second_ref, local_ref,
    charges_v, centres_s, counts_s, current_ref, facets_ref, areas_ref, normals_ref, arrived
):
    boxes = counts_s.shape[0]
    moves = [
        (basis_h.at[basis_h.shape[0] - 1], current_ref),
        (facets_h, facets_ref),
        (areas_h, areas_ref),
        (normals_h, normals_ref),
        (centres_h, centres_s),
        (counts_h, counts_s),
    ]
    copies = [pltpu.make_async_copy(a, b, arrived.at[k]) for k, (a, b) in enumerate(moves)]
    for copy in copies:
        copy.start()
    for copy in copies:
        copy.wait()
    lane = lax.broadcasted_iota(jnp.int32, (8, 128), 1)
    row = lax.broadcasted_iota(jnp.int32, (8, 128), 0)
    empty = jnp.zeros((2, 128), f32)

    def one_box(b, carry):
        moments, centres = carry
        slot = slot_of(centres_s, b)
        lanes = pl.ds(pl.multiple_of(b * per_box, per_box), per_box)
        facets = facets_ref[:, lanes]
        normals = normals_ref[:, lanes]
        live = live_row(counts_s, b)
        weighted = current_ref[:, lanes] * (wide_row(areas_ref, b) * live / per_box)
        start = pl.multiple_of(slot * 16, 16)
        charges_v[pl.ds(start, 16), :] = jnp.concatenate([weighted[:, :128], weighted[:, 128:]], axis=0)
        local_ref[pl.ds(start, 16), :] = jnp.concatenate(
            [facets[:, :128], facets[:, 128:], empty, normals[:, :128], normals[:, 128:], empty], axis=0
        )
        moments += jnp.where(lane == slot, jnp.sum(weighted, axis=1, keepdims=True), 0.0)
        for a in range(3):
            dipole = jnp.sum(weighted * (facets[a : a + 1] - centres_s[a, b]), axis=1, keepdims=True)
            moments += jnp.where(lane == 32 * (a + 1) + slot, dipole, 0.0)
            centres += jnp.where((lane == slot) & (row == a), centres_s[a, b], 0.0)
        return moments, centres

    zeros = jnp.zeros((8, 128), f32)
    moments, centres = lax.fori_loop(0, boxes, one_box, (zeros, zeros), unroll=8)
    _, _, z = lattice(centres_s, 0)
    base_z = (z - (z & 1)).astype(f32) + 0.5
    centres = jnp.where((row == 3) | (row == 4), 1.5, jnp.where(row == 5, base_z, centres))
    half = lax.axis_index("rhs")
    away = pl.multiple_of((1 - half) * 256, 256)
    here = pl.multiple_of(half * 256, 256)
    pieces = jnp.concatenate([*thirds(moments), zeros], axis=0).astype(bf16)
    cross_ref[:512] = charges_v[...].astype(bf16)
    cross_ref[512:] = pieces
    second_ref[:256] = charges_v[pl.ds(here, 256), :].astype(bf16)
    second_ref[256:] = pieces
    first_ref[:256] = charges_v[pl.ds(away, 256), :].astype(bf16).astype(f32)
    for place in range(plane_boxes):
        first_ref[256 + 8 * place : 264 + 8 * place] = local_ref[pl.ds(away + 16 * place, 8), :]
    first_ref[384:392] = moments
    first_ref[392:] = centres
    local_ref[512:520] = moments
    local_ref[520:528] = centres
    local_ref[528:] = charges_v[...].astype(bf16).astype(f32)


def thirds(x):
    high = x.astype(bf16).astype(f32)
    rest = x - high
    middle = rest.astype(bf16).astype(f32)
    return high, middle, (rest - middle).astype(bf16).astype(f32)


def stacked_rows(parts, width):
    zeros = jnp.zeros((depth - 8 * len(parts), width), f32)
    return jnp.concatenate([*parts, zeros], axis=0)


def padded(rows):
    return jnp.concatenate([rows, jnp.zeros((8 - rows.shape[0], rows.shape[1]), f32)], axis=0)


def wide_charges(ref, place):
    both = ref[pl.ds(pl.multiple_of(place * 16, 16), 16), :].astype(f32)
    return jnp.concatenate([both[:8], both[8:]], axis=1)


def wide_tile(ref, start):
    tile = ref[pl.ds(pl.multiple_of(start, 8), 8), :]
    return jnp.concatenate([tile[0:3], tile[3:6]], axis=1)


def whole_moments(pieces):
    return pieces[:8] + (pieces[8:16] + pieces[16:24])


def store_geometry(local, box, geometry):
    row = lax.broadcasted_iota(jnp.int32, (8, per_box), 0)
    square = jnp.sum(local * local, axis=0, keepdims=True)
    features = jnp.where(row == 3, square, jnp.where(row == 4, 1.0, local))
    high, middle, low = thirds(features)
    rows = stacked_rows((high, high, high, middle, middle, low), per_box)
    geometry[pl.ds(pl.multiple_of(box * depth, depth), depth), :] = rows.astype(bf16)


def store_strengths(local, charges, box, strengths):
    products = jnp.concatenate([charges * local[a : a + 1] for a in range(3)], axis=0)
    rows = jnp.concatenate([charges, *thirds(products)], axis=0)
    strengths[pl.ds(pl.multiple_of(box * 80, 80), 80), :] = rows.astype(bf16)


def feature_kernel(local_ref, geometry, mine, targets, planes, local_out):
    boxes = 2 * plane_boxes
    half = lax.axis_index("rhs")
    origin = local_ref[523:526, 0:1]
    row = lax.broadcasted_iota(jnp.int32, (8, per_box), 0)

    def source(slot, _):
        local = padded(wide_tile(local_ref, slot * 16) - origin)
        store_geometry(local, slot, geometry)
        store_strengths(local, wide_charges(local_ref, 33 + slot), slot, mine)
        return 0

    lax.fori_loop(0, boxes, source, 0, unroll=8)

    def target(place, _):
        start = (half * plane_boxes + place) * 16
        local = padded(wide_tile(local_ref, start) - origin)
        normal = padded(wide_tile(local_ref, start + 8))
        square = jnp.sum(local * local, axis=0, keepdims=True) + soften
        along = jnp.sum(local * normal, axis=0, keepdims=True)
        distance = jnp.where(row == 3, 1.0, jnp.where(row == 4, square, -2.0 * local))
        high, middle, low = thirds(distance)
        rows = stacked_rows((high, middle, low, high, middle, high), per_box)
        start = pl.multiple_of(place * per_box, per_box)
        targets[pl.ds(start, per_box), :] = jnp.transpose(rows).astype(bf16)
        planes[pl.ds(pl.multiple_of(place * 8, 8), 8), :] = jnp.where(row == 3, along, normal)
        return 0

    lax.fori_loop(0, plane_boxes, target, 0, unroll=4)
    local_out[...] = local_ref[:528]


def near_planes(sources, targets, planes, near, beside):
    def rows_at(pair, place, number):
        ref, first = pair
        return ref[pl.ds(pl.multiple_of((first + place) * number, number), number), :]

    def target_row(target_y, source_y, rows):
        runs = []
        for near_x in range(4):
            target = target_y * 4 + near_x
            for source in sources:
                for k in range(rows):
                    for x in range(max(near_x - 1, 0), min(near_x + 2, 4)):
                        runs.append((target, source, (source_y + k) * 4 + x))

        def distances(target, source, place):
            facets = targets[pl.ds(pl.multiple_of(target * per_box, per_box), per_box), :]
            return jnp.dot(facets, rows_at(source[0], place, depth), preferred_element_type=f32)

        ahead = distances(*runs[0])
        cubed = []
        given = []
        for i, (target, source, place) in enumerate(runs):
            here = ahead
            if i + 1 < len(runs):
                ahead = distances(*runs[i + 1])
            inverse = lax.rsqrt(here)
            cubed.append((inverse * inverse * inverse).astype(bf16))
            given.append(jnp.concatenate([rows_at(source[1], place, 80), rows_at(source[2], place, 80)], axis=0))
            if i + 1 == len(runs) or runs[i + 1][0] is not target:
                sums = lax.dot_general(
                    jnp.concatenate(given, axis=1),
                    jnp.concatenate(cubed, axis=1),
                    (((1,), (1,)), ((), ())),
                    preferred_element_type=f32,
                )
                side = planes[pl.ds(pl.multiple_of(target * 8, 8), 8), :]
                values = []
                for start in (0, 80):
                    value = side[3:4] * sums[start : start + 8]
                    for a in range(3):
                        high, middle, low = (sums[j : j + 8] for j in range(start + 8 + 8 * a, start + 80, 24))
                        value = value - side[a : a + 1] * (high + (middle + low))
                    values.append(value)
                near[pl.ds(pl.multiple_of(target * 16, 16), 16), :] = jnp.concatenate(values, axis=0)
                cubed = []
                given = []

    def outer(i, _):
        target_row(3 * i, 2 * i, 2)
        beside(i)
        return 0

    def inner(i, _):
        target_row(i + 1, i, 3)
        beside(i + 2)
        return 0

    lax.fori_loop(0, 2, outer, 0)
    lax.fori_loop(0, 2, inner, 0)


def field_kernel(
    centres_s, local_ref, cross_ref, first_ref, second_ref, geometry, mine, targets, planes, mine_ref, theirs_ref,
    halo_geometry, halo_mine, theirs, near, far, far_centres, far_moments
):
    boxes = 2 * plane_boxes
    half = lax.axis_index("rhs")
    origin = local_ref[523:526, 0:1]

    def source(slot, _):
        local = wide_tile(local_ref, slot * 16) - origin
        store_strengths(local, wide_charges(cross_ref, slot), slot, theirs)
        return 0

    lax.fori_loop(0, boxes, source, 0, unroll=8)

    def halo_source(place, _):
        local = padded(wide_tile(first_ref, 256 + place * 8) - origin)
        store_geometry(local, place, halo_geometry)
        store_strengths(local, wide_charges(first_ref, place), place, halo_mine)
        store_strengths(local, wide_charges(second_ref, place), boxes + place, theirs)
        return 0

    lax.fori_loop(0, plane_boxes, halo_source, 0, unroll=8)

    for group, (centres, ours, others) in enumerate(
        (
            (first_ref[392:400], first_ref[384:392], second_ref[256:288]),
            (local_ref[520:528], local_ref[512:520], cross_ref[512:544]),
        )
    ):
        columns = jnp.transpose(jnp.concatenate([centres[:3] - origin, centres[3:]], axis=0))[:32]
        for a in range(3):
            far_centres[(group * 3 + a) * 32 : (group * 3 + a + 1) * 32, :] = jnp.broadcast_to(
                columns[:, a : a + 1], (32, 128)
            )
        both = jnp.concatenate([ours, whole_moments(others.astype(f32))], axis=0)
        high = both.astype(bf16).astype(f32)
        far_moments[group * 32 : group * 32 + 32, :] = jnp.concatenate([high, both - high], axis=0)
    lane = lax.broadcasted_iota(jnp.int32, (1, 128), 1)
    lane_x = lane & 3
    lane_y = (lane >> 2) & 3
    lane_plane = (lane >> 4) & 1

    def far_field(k):
        group = (k >= boxes).astype(jnp.int32)
        slot = jnp.where(k < boxes, k, half * plane_boxes + k - boxes)
        x, y, plane = slot & 3, (slot >> 2) & 3, slot >> 4
        local = wide_tile(local_ref, slot * 16) - origin
        normal = wide_tile(local_ref, slot * 16 + 8)
        d = []
        for a in range(3):
            centre = far_centres[pl.ds(pl.multiple_of((group * 3 + a) * 32, 32), 32), :]
            d.append(local[a : a + 1] - jnp.concatenate([centre, centre], axis=1))
        q = d[0] * d[0] + d[1] * d[1] + d[2] * d[2] + soften
        inverse = lax.rsqrt(q)
        inverse_2 = inverse * inverse
        inverse_3 = inverse_2 * inverse
        t = d[0] * normal[0:1] + d[1] * normal[1:2] + d[2] * normal[2:3]
        single = t * inverse_3
        steep = 3.0 * single * inverse_2
        coefficients = [single] + [steep * d[a] - normal[a : a + 1] * inverse_3 for a in range(3)]
        whole = jnp.concatenate(coefficients, axis=0)
        upper = whole.astype(bf16)
        lower = (whole - upper.astype(f32)).astype(bf16)
        lane_z = lane_plane + jnp.where(group == 0, 4 * half - 2, 0)
        near = (jnp.abs(lane_x - x) <= 1) & (jnp.abs(lane_y - y) <= 1) & (jnp.abs(lane_z - plane) <= 1)
        picked = jnp.where(near, 0.0, far_moments[pl.ds(pl.multiple_of(group * 32, 32), 32), :]).astype(bf16)
        first = jnp.dot(picked, upper, preferred_element_type=f32)
        second = jnp.dot(picked, lower, preferred_element_type=f32)
        return first[:16] + first[16:] + second[:16]

    def far_boxes(i):
        for k in range(12):
            k = i * 12 + k
            far[pl.ds(pl.multiple_of(k * 16, 16), 16), :] = far_field(k)

    sources = [((geometry, p), (mine, p), (theirs, p)) for p in (0, plane_boxes)]
    sources.append(((halo_geometry, 0), (halo_mine, 0), (theirs, boxes)))
    near_planes(sources, targets, planes, near, far_boxes)

    def near_field(place, _):
        value = near[pl.ds(pl.multiple_of(place * 16, 16), 16), :]
        slot = half * plane_boxes + place
        rows = pl.ds(pl.multiple_of(slot * 16, 16), 16)
        far[rows, :] += value + far[pl.ds(pl.multiple_of((boxes + place) * 16, 16), 16), :]
        return 0

    lax.fori_loop(0, plane_boxes, near_field, 0, unroll=4)

    def given_back(b, _):
        start = pl.multiple_of(slot_of(centres_s, b) * 16, 16)
        rows = pl.ds(pl.multiple_of(b * 8, 8), 8)
        mine_ref[rows, :] = far[pl.ds(start, 8), :]
        theirs_ref[rows, :] = far[pl.ds(start + 8, 8), :]
        return 0

    lax.fori_loop(0, boxes, given_back, 0, unroll=4)


def gram_kernel(counts_s, basis_ref, sums_ref, live_ref):
    krylov = basis_ref.shape[0]
    pairs = [(m, n) for m in range(krylov) for n in range(m + 1)]

    def one_box(b, carry):
        lanes = pl.ds(pl.multiple_of(b * per_box, per_box), per_box)
        live = live_row(counts_s, b)
        live_ref[pl.ds(2 * b, 1), :] = live[:, :128]
        live_ref[pl.ds(2 * b + 1, 1), :] = live[:, 128:]
        rows = [basis_ref[m, :, lanes] * live for m in range(krylov)]
        out = []
        for k, (m, n) in enumerate(pairs):
            product = rows[m] * rows[n]
            out.append(carry[k] + product[:, :128] + product[:, 128:])
        return tuple(out)

    zeros = jnp.zeros((8, 128), f32)
    gram = lax.fori_loop(0, counts_s.shape[0], one_box, (zeros,) * len(pairs))
    lane = lax.broadcasted_iota(jnp.int32, (8, 128), 1)
    total = zeros
    for k, value in enumerate(gram):
        total = jnp.where(lane == krylov + 1 + k, jnp.sum(value, axis=1, keepdims=True), total)
    sums_ref[...] = total


def image_kernel(mine_ref, theirs_ref, gram_ref, live_ref, contrast_ref, basis_ref, image_ref, sums_ref):
    krylov = basis_ref.shape[0]

    def one_box(b, carry):
        lanes = pl.ds(pl.multiple_of(b * per_box, per_box), per_box)
        rows = pl.ds(pl.multiple_of(b * 8, 8), 8)
        live = wide_row(live_ref, b)
        part = mine_ref[rows, :] + theirs_ref[rows, :]
        image = live * (basis_ref[krylov - 1, :, lanes] - 2.0 * wide_row(contrast_ref, b) * part)
        image_ref[:, lanes] = image
        sums = []
        for m in range(krylov + 1):
            product = image * (basis_ref[m, :, lanes] if m < krylov else image)
            sums.append(carry[m] + product[:, :128] + product[:, 128:])
        return tuple(sums)

    zeros = jnp.zeros((8, 128), f32)
    sums = lax.fori_loop(0, live_ref.shape[0] // 2, one_box, (zeros,) * (krylov + 1), unroll=4)
    lane = lax.broadcasted_iota(jnp.int32, (8, 128), 1)
    total = gram_ref[...]
    for k, value in enumerate(sums):
        total = jnp.where(lane == k, jnp.sum(value, axis=1, keepdims=True), total)
    sums_ref[...] = jnp.broadcast_to(total[None], sums_ref.shape)


def two_sum(a, b):
    s = a + b
    c = s - a
    return s, (a - (s - c)) + (b - c)


def halves(a):
    c = a * 4097.0
    high = c - (c - a)
    return high, a - high


def two_product(a, b):
    p = a * b
    a_high, a_low = halves(a)
    b_high, b_low = halves(b)
    return p, ((a_high * b_high - p) + a_high * b_low + a_low * b_high) + a_low * b_low


def finish_kernel(total_facets, tiles_ref, live_ref, image_ref, basis_ref, next_ref, hessenberg_ref):
    boxes = live_ref.shape[0] // 2
    krylov = basis_ref.shape[0]
    lane = lax.broadcasted_iota(jnp.int32, (8, 128), 1)

    sums, rest = tiles_ref[0], jnp.zeros((8, 128), f32)
    for i in range(1, tiles_ref.shape[0]):
        sums, error = two_sum(sums, tiles_ref[i])
        rest = rest + error
    exact = sums + rest
    projections = [exact[:, m : m + 1] / total_facets for m in range(krylov)]
    pairs = [(m, n) for m in range(krylov) for n in range(m + 1)]
    first = jnp.where(lane == krylov, 1.0, 0.0)
    second = jnp.where(lane <= krylov, 1.0, 0.0)
    for m in range(krylov):
        first = jnp.where(lane == m, -2.0 * projections[m], first)
    for k, (m, n) in enumerate(pairs):
        at = lane == krylov + 1 + k
        scale = 1.0 if m == n else 2.0
        first = jnp.where(at, scale * projections[m], first)
        second = jnp.where(at, projections[n], second)
    factor, factor_rest = two_product(first, second)
    value, value_rest = two_product(factor, sums)
    value_rest = value_rest + (factor * rest + factor_rest * sums)
    for shift in (64, 32, 16, 8, 4, 2, 1):
        other = pltpu.roll(value, shift, 1)
        other_rest = pltpu.roll(value_rest, shift, 1)
        value, error = two_sum(value, other)
        value_rest = (value_rest + other_rest) + error
    remaining = jnp.maximum(value + value_rest, 0.0)
    norm = jnp.sqrt(remaining / total_facets + epsilon)
    heads = jnp.where(lane == krylov, norm, 0.0)
    for m in range(krylov):
        heads = jnp.where(lane == m, projections[m], heads)
    hessenberg_ref[...] = heads[:, : krylov + 1]
    wide = [jnp.broadcast_to(p, (8, per_box)) for p in projections]
    scale = jnp.concatenate([1.0 / norm] * (per_box // 128), axis=1)

    def one_box(b, _):
        lanes = pl.ds(pl.multiple_of(b * per_box, per_box), per_box)
        live = wide_row(live_ref, b)
        sent = wide[0] * basis_ref[0, :, lanes]
        for m in range(1, krylov):
            sent += wide[m] * basis_ref[m, :, lanes]
        next_ref[:, lanes] = (image_ref[:, lanes] - sent * live) * scale
        return 0

    lax.fori_loop(0, boxes, one_box, 0, unroll=4)


smem = pl.BlockSpec(memory_space=pltpu.SMEM)
vmem = pl.BlockSpec(memory_space=pltpu.VMEM)


def on_device(
    basis, facet_centres, normals, areas, contrast, facet_counts, box_centres, near_boxes, far_boxes
):
    krylov, rhs_local, facet_local = basis.shape
    boxes = facet_counts.shape[0]
    count = lax.axis_size("box")
    total_facets = count * facet_local
    areas = areas.reshape(-1, 128)
    contrast = contrast.reshape(-1, 128)

    def rows(number, width=128, dtype=f32):
        return jax.ShapeDtypeStruct((number, width), dtype)

    def limit(mebibytes):
        return pltpu.CompilerParams(vmem_limit_bytes=mebibytes * 1024 * 1024)

    sent, first, second, local = pl.pallas_call(
        prep_kernel,
        out_shape=(rows(544, dtype=bf16), rows(400), rows(288, dtype=bf16), rows(1040)),
        in_specs=[pl.BlockSpec(memory_space=pl.ANY)] * 6,
        out_specs=(vmem,) * 4,
        scratch_shapes=[
            pltpu.VMEM((512, 128), f32),
            pltpu.SMEM(box_centres.shape, f32),
            pltpu.SMEM(facet_counts.shape, jnp.int32),
            pltpu.VMEM((rhs_local, facet_local), f32),
            pltpu.VMEM(facet_centres.shape, f32),
            pltpu.VMEM(areas.shape, f32),
            pltpu.VMEM(normals.shape, f32),
            pltpu.SemaphoreType.DMA((6,)),
        ],
        name="prepare",
    )(box_centres, facet_counts, basis, facet_centres, areas, normals)
    swap = [(0, 1), (1, 0)]
    ups = range(count - 1)
    cross = lax.ppermute(sent, "rhs", swap)
    first = lax.ppermute(
        first, ("box", "rhs"), [(2 * i, 2 * i + 2) for i in ups] + [(2 * i + 3, 2 * i + 1) for i in ups]
    )
    second = lax.ppermute(
        second, ("box", "rhs"), [(2 * i + 1, 2 * i + 2) for i in ups] + [(2 * i + 2, 2 * i + 1) for i in ups]
    )
    plane_slots = plane_boxes * per_box
    geometry, strengths, targets, planes, local = pl.pallas_call(
        feature_kernel,
        out_shape=(
            rows(boxes * depth, per_box, bf16),
            rows(boxes * 80, per_box, bf16),
            rows(plane_slots, depth, bf16),
            rows(plane_boxes * 8, per_box),
            rows(528),
        ),
        in_specs=[vmem],
        out_specs=(vmem,) * 5,
        compiler_params=limit(12),
        name="features",
    )(local)
    mine, theirs = pl.pallas_call(
        field_kernel,
        out_shape=(rows(boxes * 8, per_box),) * 2,
        in_specs=[smem] + [vmem] * 8,
        out_specs=(vmem, vmem),
        scratch_shapes=[
            pltpu.VMEM((plane_boxes * depth, per_box), bf16),
            pltpu.VMEM((plane_boxes * 80, per_box), bf16),
            pltpu.VMEM((3 * plane_boxes * 80, per_box), bf16),
            pltpu.VMEM((plane_boxes * 16, per_box), f32),
            pltpu.VMEM((3 * plane_boxes * 16, per_box), f32),
            pltpu.VMEM((6 * 32, 128), f32),
            pltpu.VMEM((2 * 32, 128), f32),
        ],
        compiler_params=limit(32),
        name="fields",
    )(box_centres, local, cross, first, second, geometry, strengths, targets, planes)
    theirs = lax.ppermute(theirs, "rhs", swap)
    gram, live = pl.pallas_call(
        gram_kernel,
        out_shape=(rows(8), rows(2 * boxes)),
        in_specs=[smem, vmem],
        out_specs=(vmem, vmem),
        compiler_params=limit(8),
        name="gram",
    )(facet_counts, basis)
    image, tiles = pl.pallas_call(
        image_kernel,
        out_shape=(rows(rhs_local, facet_local), jax.ShapeDtypeStruct((count, 8, 128), f32)),
        in_specs=[vmem] * 6,
        out_specs=(vmem, vmem),
        compiler_params=limit(8),
        name="image",
    )(mine, theirs, gram, live, contrast, basis)
    tiles = lax.all_to_all(tiles, "box", 0, 0, tiled=True)
    next_vector, hessenberg = pl.pallas_call(
        functools.partial(finish_kernel, total_facets),
        out_shape=(rows(rhs_local, facet_local), rows(rhs_local, krylov + 1)),
        in_specs=[vmem] * 4,
        out_specs=(vmem, vmem),
        compiler_params=limit(16),
        name="finish",
    )(tiles, live, image, basis)
    return next_vector, hessenberg.T


def solution(mesh):
    return jax.shard_map(
        on_device,
        mesh=mesh,
        in_specs=(
            P(None, "rhs", "box"),
            P(None, "box"),
            P(None, "box"),
            P("box"),
            P("box"),
            P("box"),
            P(None, "box"),
            P("box", None),
            P("box", None),
        ),
        out_specs=(P("rhs", "box"), P(None, "rhs")),
        check_vma=False,
    )
```

```python
import functools

import jax
import jax.numpy as jnp
from jax import lax
from jax.experimental import pallas as pl
from jax.experimental.pallas import tpu as pltpu
from jax.sharding import PartitionSpec as P

soften = 0.0025
epsilon = 1e-06
f32 = jnp.float32
bf16 = jnp.bfloat16
plane_boxes = 16
per_box = 256
depth = 64


def lattice(centres_s, b):
    x = (centres_s[0, b] + 0.5).astype(jnp.int32)
    y = (centres_s[1, b] + 0.5).astype(jnp.int32)
    z = (centres_s[2, b] + 0.5).astype(jnp.int32)
    return x, y, z


def slot_of(centres_s, b):
    x, y, z = lattice(centres_s, b)
    return (z & 1) * plane_boxes + y * 4 + x


def wide_row(ref, b):
    return jnp.concatenate([ref[pl.ds(2 * b, 1), :], ref[pl.ds(2 * b + 1, 1), :]], axis=1)


def live_row(counts_s, b):
    slots = lax.broadcasted_iota(jnp.int32, (1, per_box), 1)
    return (slots < counts_s[b]).astype(f32)


def prep_kernel(
    centres_h, counts_h, basis_h, facets_h, areas_h, normals_h, cross_ref, first_ref, second_ref, local_ref,
    charges_v, centres_s, counts_s, current_ref, facets_ref, areas_ref, normals_ref, arrived
):
    boxes = counts_s.shape[0]
    moves = [
        (basis_h.at[basis_h.shape[0] - 1], current_ref),
        (facets_h, facets_ref),
        (areas_h, areas_ref),
        (normals_h, normals_ref),
        (centres_h, centres_s),
        (counts_h, counts_s),
    ]
    copies = [pltpu.make_async_copy(a, b, arrived.at[k]) for k, (a, b) in enumerate(moves)]
    for copy in copies:
        copy.start()
    for copy in copies:
        copy.wait()
    lane = lax.broadcasted_iota(jnp.int32, (8, 128), 1)
    row = lax.broadcasted_iota(jnp.int32, (8, 128), 0)
    empty = jnp.zeros((2, 128), f32)

    def one_box(b, carry):
        moments, centres = carry
        slot = slot_of(centres_s, b)
        lanes = pl.ds(pl.multiple_of(b * per_box, per_box), per_box)
        facets = facets_ref[:, lanes]
        normals = normals_ref[:, lanes]
        live = live_row(counts_s, b)
        weighted = current_ref[:, lanes] * (wide_row(areas_ref, b) * live / per_box)
        start = pl.multiple_of(slot * 16, 16)
        charges_v[pl.ds(start, 16), :] = jnp.concatenate([weighted[:, :128], weighted[:, 128:]], axis=0)
        local_ref[pl.ds(start, 16), :] = jnp.concatenate(
            [facets[:, :128], facets[:, 128:], empty, normals[:, :128], normals[:, 128:], empty], axis=0
        )
        moments += jnp.where(lane == slot, jnp.sum(weighted, axis=1, keepdims=True), 0.0)
        for a in range(3):
            dipole = jnp.sum(weighted * (facets[a : a + 1] - centres_s[a, b]), axis=1, keepdims=True)
            moments += jnp.where(lane == 32 * (a + 1) + slot, dipole, 0.0)
            centres += jnp.where((lane == slot) & (row == a), centres_s[a, b], 0.0)
        return moments, centres

    zeros = jnp.zeros((8, 128), f32)
    moments, centres = lax.fori_loop(0, boxes, one_box, (zeros, zeros), unroll=8)
    _, _, z = lattice(centres_s, 0)
    base_z = (z - (z & 1)).astype(f32) + 0.5
    centres = jnp.where((row == 3) | (row == 4), 1.5, jnp.where(row == 5, base_z, centres))
    half = lax.axis_index("rhs")
    away = pl.multiple_of((1 - half) * 256, 256)
    here = pl.multiple_of(half * 256, 256)
    pieces = jnp.concatenate([*thirds(moments), zeros], axis=0).astype(bf16)
    cross_ref[:512] = charges_v[...].astype(bf16)
    cross_ref[512:] = pieces
    second_ref[:256] = charges_v[pl.ds(here, 256), :].astype(bf16)
    second_ref[256:] = pieces
    first_ref[:256] = charges_v[pl.ds(away, 256), :].astype(bf16).astype(f32)
    for place in range(plane_boxes):
        first_ref[256 + 8 * place : 264 + 8 * place] = local_ref[pl.ds(away + 16 * place, 8), :]
    first_ref[384:392] = moments
    first_ref[392:] = centres
    local_ref[512:520] = moments
    local_ref[520:528] = centres
    local_ref[528:] = charges_v[...].astype(bf16).astype(f32)


def thirds(x):
    high = x.astype(bf16).astype(f32)
    rest = x - high
    middle = rest.astype(bf16).astype(f32)
    return high, middle, (rest - middle).astype(bf16).astype(f32)


def stacked_rows(parts, width):
    zeros = jnp.zeros((depth - 8 * len(parts), width), f32)
    return jnp.concatenate([*parts, zeros], axis=0)


def padded(rows):
    return jnp.concatenate([rows, jnp.zeros((8 - rows.shape[0], rows.shape[1]), f32)], axis=0)


def wide_charges(ref, place):
    both = ref[pl.ds(pl.multiple_of(place * 16, 16), 16), :].astype(f32)
    return jnp.concatenate([both[:8], both[8:]], axis=1)


def wide_tile(ref, start):
    tile = ref[pl.ds(pl.multiple_of(start, 8), 8), :]
    return jnp.concatenate([tile[0:3], tile[3:6]], axis=1)


def whole_moments(pieces):
    return pieces[:8] + (pieces[8:16] + pieces[16:24])


def store_geometry(local, box, geometry):
    row = lax.broadcasted_iota(jnp.int32, (8, per_box), 0)
    square = jnp.sum(local * local, axis=0, keepdims=True)
    features = jnp.where(row == 3, square, jnp.where(row == 4, 1.0, local))
    high, middle, low = thirds(features)
    rows = stacked_rows((high, high, high, middle, middle, low), per_box)
    geometry[pl.ds(pl.multiple_of(box * depth, depth), depth), :] = rows.astype(bf16)


def store_strengths(local, charges, box, strengths):
    products = jnp.concatenate([charges * local[a : a + 1] for a in range(3)], axis=0)
    rows = jnp.concatenate([charges, *thirds(products)], axis=0)
    strengths[pl.ds(pl.multiple_of(box * 80, 80), 80), :] = rows.astype(bf16)


def feature_kernel(local_ref, geometry, mine, targets, planes, local_out):
    boxes = 2 * plane_boxes
    half = lax.axis_index("rhs")
    origin = local_ref[523:526, 0:1]
    row = lax.broadcasted_iota(jnp.int32, (8, per_box), 0)

    def source(slot, _):
        local = padded(wide_tile(local_ref, slot * 16) - origin)
        store_geometry(local, slot, geometry)
        store_strengths(local, wide_charges(local_ref, 33 + slot), slot, mine)
        return 0

    lax.fori_loop(0, boxes, source, 0, unroll=8)

    def target(place, _):
        start = (half * plane_boxes + place) * 16
        local = padded(wide_tile(local_ref, start) - origin)
        normal = padded(wide_tile(local_ref, start + 8))
        square = jnp.sum(local * local, axis=0, keepdims=True) + soften
        along = jnp.sum(local * normal, axis=0, keepdims=True)
        distance = jnp.where(row == 3, 1.0, jnp.where(row == 4, square, -2.0 * local))
        high, middle, low = thirds(distance)
        rows = stacked_rows((high, middle, low, high, middle, high), per_box)
        start = pl.multiple_of(place * per_box, per_box)
        targets[pl.ds(start, per_box), :] = jnp.transpose(rows).astype(bf16)
        planes[pl.ds(pl.multiple_of(place * 8, 8), 8), :] = jnp.where(row == 3, along, normal)
        return 0

    lax.fori_loop(0, plane_boxes, target, 0, unroll=4)
    local_out[...] = local_ref[:528]


def near_planes(sources, targets, planes, near, beside):
    def rows_at(pair, place, number):
        ref, first = pair
        return ref[pl.ds(pl.multiple_of((first + place) * number, number), number), :]

    def target_row(target_y, source_y, rows):
        runs = []
        for near_x in range(4):
            target = target_y * 4 + near_x
            for source in sources:
                for k in range(rows):
                    for x in range(max(near_x - 1, 0), min(near_x + 2, 4)):
                        runs.append((target, source, (source_y + k) * 4 + x))

        def distances(target, source, place):
            facets = targets[pl.ds(pl.multiple_of(target * per_box, per_box), per_box), :]
            return jnp.dot(facets, rows_at(source[0], place, depth), preferred_element_type=f32)

        ahead = distances(*runs[0])
        cubed = []
        given = []
        for i, (target, source, place) in enumerate(runs):
            here = ahead
            if i + 1 < len(runs):
                ahead = distances(*runs[i + 1])
            inverse = lax.rsqrt(here)
            cubed.append((inverse * inverse * inverse).astype(bf16))
            given.append(jnp.concatenate([rows_at(source[1], place, 80), rows_at(source[2], place, 80)], axis=0))
            if i + 1 == len(runs) or runs[i + 1][0] is not target:
                sums = lax.dot_general(
                    jnp.concatenate(given, axis=1),
                    jnp.concatenate(cubed, axis=1),
                    (((1,), (1,)), ((), ())),
                    preferred_element_type=f32,
                )
                side = planes[pl.ds(pl.multiple_of(target * 8, 8), 8), :]
                values = []
                for start in (0, 80):
                    value = side[3:4] * sums[start : start + 8]
                    for a in range(3):
                        high, middle, low = (sums[j : j + 8] for j in range(start + 8 + 8 * a, start + 80, 24))
                        value = value - side[a : a + 1] * (high + (middle + low))
                    values.append(value)
                near[pl.ds(pl.multiple_of(target * 16, 16), 16), :] = jnp.concatenate(values, axis=0)
                cubed = []
                given = []

    def outer(i, _):
        target_row(3 * i, 2 * i, 2)
        beside(i)
        return 0

    def inner(i, _):
        target_row(i + 1, i, 3)
        beside(i + 2)
        return 0

    lax.fori_loop(0, 2, outer, 0)
    lax.fori_loop(0, 2, inner, 0)


def field_kernel(
    centres_s, local_ref, cross_ref, first_ref, second_ref, geometry, mine, targets, planes, mine_ref, theirs_ref,
    halo_geometry, halo_mine, theirs, near, far, far_centres, far_moments
):
    boxes = 2 * plane_boxes
    half = lax.axis_index("rhs")
    origin = local_ref[523:526, 0:1]

    def source(slot, _):
        local = wide_tile(local_ref, slot * 16) - origin
        store_strengths(local, wide_charges(cross_ref, slot), slot, theirs)
        return 0

    lax.fori_loop(0, boxes, source, 0, unroll=8)

    def halo_source(place, _):
        local = padded(wide_tile(first_ref, 256 + place * 8) - origin)
        store_geometry(local, place, halo_geometry)
        store_strengths(local, wide_charges(first_ref, place), place, halo_mine)
        store_strengths(local, wide_charges(second_ref, place), boxes + place, theirs)
        return 0

    lax.fori_loop(0, plane_boxes, halo_source, 0, unroll=8)

    for group, (centres, ours, others) in enumerate(
        (
            (first_ref[392:400], first_ref[384:392], second_ref[256:288]),
            (local_ref[520:528], local_ref[512:520], cross_ref[512:544]),
        )
    ):
        columns = jnp.transpose(jnp.concatenate([centres[:3] - origin, centres[3:]], axis=0))[:32]
        for a in range(3):
            far_centres[(group * 3 + a) * 32 : (group * 3 + a + 1) * 32, :] = jnp.broadcast_to(
                columns[:, a : a + 1], (32, 128)
            )
        both = jnp.concatenate([ours, whole_moments(others.astype(f32))], axis=0)
        high = both.astype(bf16).astype(f32)
        far_moments[group * 32 : group * 32 + 32, :] = jnp.concatenate([high, both - high], axis=0)
    lane = lax.broadcasted_iota(jnp.int32, (1, 128), 1)
    lane_x = lane & 3
    lane_y = (lane >> 2) & 3
    lane_plane = (lane >> 4) & 1

    def far_field(k):
        group = (k >= boxes).astype(jnp.int32)
        slot = jnp.where(k < boxes, k, half * plane_boxes + k - boxes)
        x, y, plane = slot & 3, (slot >> 2) & 3, slot >> 4
        local = wide_tile(local_ref, slot * 16) - origin
        normal = wide_tile(local_ref, slot * 16 + 8)
        d = []
        for a in range(3):
            centre = far_centres[pl.ds(pl.multiple_of((group * 3 + a) * 32, 32), 32), :]
            d.append(local[a : a + 1] - jnp.concatenate([centre, centre], axis=1))
        q = d[0] * d[0] + d[1] * d[1] + d[2] * d[2] + soften
        inverse = lax.rsqrt(q)
        inverse_2 = inverse * inverse
        inverse_3 = inverse_2 * inverse
        t = d[0] * normal[0:1] + d[1] * normal[1:2] + d[2] * normal[2:3]
        single = t * inverse_3
        steep = 3.0 * single * inverse_2
        coefficients = [single] + [steep * d[a] - normal[a : a + 1] * inverse_3 for a in range(3)]
        whole = jnp.concatenate(coefficients, axis=0)
        upper = whole.astype(bf16)
        lower = (whole - upper.astype(f32)).astype(bf16)
        lane_z = lane_plane + jnp.where(group == 0, 4 * half - 2, 0)
        near = (jnp.abs(lane_x - x) <= 1) & (jnp.abs(lane_y - y) <= 1) & (jnp.abs(lane_z - plane) <= 1)
        picked = jnp.where(near, 0.0, far_moments[pl.ds(pl.multiple_of(group * 32, 32), 32), :]).astype(bf16)
        first = jnp.dot(picked, upper, preferred_element_type=f32)
        second = jnp.dot(picked, lower, preferred_element_type=f32)
        return first[:16] + first[16:] + second[:16]

    def far_boxes(i):
        for k in range(12):
            k = i * 12 + k
            far[pl.ds(pl.multiple_of(k * 16, 16), 16), :] = far_field(k)

    sources = [((geometry, p), (mine, p), (theirs, p)) for p in (0, plane_boxes)]
    sources.append(((halo_geometry, 0), (halo_mine, 0), (theirs, boxes)))
    near_planes(sources, targets, planes, near, far_boxes)

    def near_field(place, _):
        value = near[pl.ds(pl.multiple_of(place * 16, 16), 16), :]
        slot = half * plane_boxes + place
        rows = pl.ds(pl.multiple_of(slot * 16, 16), 16)
        far[rows, :] += value + far[pl.ds(pl.multiple_of((boxes + place) * 16, 16), 16), :]
        return 0

    lax.fori_loop(0, plane_boxes, near_field, 0, unroll=4)

    def given_back(b, _):
        start = pl.multiple_of(slot_of(centres_s, b) * 16, 16)
        rows = pl.ds(pl.multiple_of(b * 8, 8), 8)
        mine_ref[rows, :] = far[pl.ds(start, 8), :]
        theirs_ref[rows, :] = far[pl.ds(start + 8, 8), :]
        return 0

    lax.fori_loop(0, boxes, given_back, 0, unroll=4)


def gram_kernel(counts_s, basis_ref, sums_ref, live_ref):
    krylov = basis_ref.shape[0]
    pairs = [(m, n) for m in range(krylov) for n in range(m + 1)]

    def one_box(b, carry):
        lanes = pl.ds(pl.multiple_of(b * per_box, per_box), per_box)
        live = live_row(counts_s, b)
        live_ref[pl.ds(2 * b, 1), :] = live[:, :128]
        live_ref[pl.ds(2 * b + 1, 1), :] = live[:, 128:]
        rows = [basis_ref[m, :, lanes] * live for m in range(krylov)]
        out = []
        for k, (m, n) in enumerate(pairs):
            product = rows[m] * rows[n]
            out.append(carry[k] + product[:, :128] + product[:, 128:])
        return tuple(out)

    zeros = jnp.zeros((8, 128), f32)
    gram = lax.fori_loop(0, counts_s.shape[0], one_box, (zeros,) * len(pairs))
    lane = lax.broadcasted_iota(jnp.int32, (8, 128), 1)
    total = zeros
    for k, value in enumerate(gram):
        total = jnp.where(lane == krylov + 1 + k, jnp.sum(value, axis=1, keepdims=True), total)
    sums_ref[...] = total


def image_kernel(mine_ref, theirs_ref, gram_ref, live_ref, contrast_ref, basis_ref, image_ref, sums_ref):
    krylov = basis_ref.shape[0]

    def one_box(b, carry):
        lanes = pl.ds(pl.multiple_of(b * per_box, per_box), per_box)
        rows = pl.ds(pl.multiple_of(b * 8, 8), 8)
        live = wide_row(live_ref, b)
        part = mine_ref[rows, :] + theirs_ref[rows, :]
        image = live * (basis_ref[krylov - 1, :, lanes] - 2.0 * wide_row(contrast_ref, b) * part)
        image_ref[:, lanes] = image
        sums = []
        for m in range(krylov + 1):
            product = image * (basis_ref[m, :, lanes] if m < krylov else image)
            sums.append(carry[m] + product[:, :128] + product[:, 128:])
        return tuple(sums)

    zeros = jnp.zeros((8, 128), f32)
    sums = lax.fori_loop(0, live_ref.shape[0] // 2, one_box, (zeros,) * (krylov + 1), unroll=4)
    lane = lax.broadcasted_iota(jnp.int32, (8, 128), 1)
    total = gram_ref[...]
    for k, value in enumerate(sums):
        total = jnp.where(lane == k, jnp.sum(value, axis=1, keepdims=True), total)
    sums_ref[...] = jnp.broadcast_to(total[None], sums_ref.shape)


def two_sum(a, b):
    s = a + b
    c = s - a
    return s, (a - (s - c)) + (b - c)


def halves(a):
    c = a * 4097.0
    high = c - (c - a)
    return high, a - high


def two_product(a, b):
    p = a * b
    a_high, a_low = halves(a)
    b_high, b_low = halves(b)
    return p, ((a_high * b_high - p) + a_high * b_low + a_low * b_high) + a_low * b_low


def finish_kernel(total_facets, tiles_ref, live_ref, image_ref, basis_ref, next_ref, hessenberg_ref):
    boxes = live_ref.shape[0] // 2
    krylov = basis_ref.shape[0]
    lane = lax.broadcasted_iota(jnp.int32, (8, 128), 1)

    tiles = [(tiles_ref[i], jnp.zeros((8, 128), f32)) for i in range(tiles_ref.shape[0])]
    while len(tiles) > 1:
        merged = []
        for (one, one_rest), (two, two_rest) in zip(tiles[::2], tiles[1::2]):
            value, error = two_sum(one, two)
            merged.append((value, (one_rest + two_rest) + error))
        tiles = merged + tiles[len(tiles) // 2 * 2 :]
    sums, rest = tiles[0]
    exact = sums + rest
    projections = [exact[:, m : m + 1] / total_facets for m in range(krylov)]
    pairs = [(m, n) for m in range(krylov) for n in range(m + 1)]
    first = jnp.where(lane == krylov, 1.0, 0.0)
    second = jnp.where(lane <= krylov, 1.0, 0.0)
    for m in range(krylov):
        first = jnp.where(lane == m, -2.0 * projections[m], first)
    for k, (m, n) in enumerate(pairs):
        at = lane == krylov + 1 + k
        scale = 1.0 if m == n else 2.0
        first = jnp.where(at, scale * projections[m], first)
        second = jnp.where(at, projections[n], second)
    factor, factor_rest = two_product(first, second)
    value, value_rest = two_product(factor, sums)
    value_rest = value_rest + (factor * rest + factor_rest * sums)
    for shift in (64, 32, 16, 8, 4, 2, 1):
        other = pltpu.roll(value, shift, 1)
        other_rest = pltpu.roll(value_rest, shift, 1)
        value, error = two_sum(value, other)
        value_rest = (value_rest + other_rest) + error
    remaining = jnp.maximum(value + value_rest, 0.0)
    norm = jnp.sqrt(remaining / total_facets + epsilon)
    heads = jnp.where(lane == krylov, norm, 0.0)
    for m in range(krylov):
        heads = jnp.where(lane == m, projections[m], heads)
    hessenberg_ref[...] = heads[:, : krylov + 1]
    wide = [jnp.broadcast_to(p, (8, per_box)) for p in projections]
    scale = jnp.concatenate([1.0 / norm] * (per_box // 128), axis=1)

    def one_box(b, _):
        lanes = pl.ds(pl.multiple_of(b * per_box, per_box), per_box)
        live = wide_row(live_ref, b)
        sent = wide[0] * basis_ref[0, :, lanes]
        for m in range(1, krylov):
            sent += wide[m] * basis_ref[m, :, lanes]
        next_ref[:, lanes] = (image_ref[:, lanes] - sent * live) * scale
        return 0

    lax.fori_loop(0, boxes, one_box, 0, unroll=8)


smem = pl.BlockSpec(memory_space=pltpu.SMEM)
vmem = pl.BlockSpec(memory_space=pltpu.VMEM)


def on_device(
    basis, facet_centres, normals, areas, contrast, facet_counts, box_centres, near_boxes, far_boxes
):
    krylov, rhs_local, facet_local = basis.shape
    boxes = facet_counts.shape[0]
    count = lax.axis_size("box")
    total_facets = count * facet_local
    areas = areas.reshape(-1, 128)
    contrast = contrast.reshape(-1, 128)

    def rows(number, width=128, dtype=f32):
        return jax.ShapeDtypeStruct((number, width), dtype)

    def limit(mebibytes):
        return pltpu.CompilerParams(vmem_limit_bytes=mebibytes * 1024 * 1024)

    sent, first, second, local = pl.pallas_call(
        prep_kernel,
        out_shape=(rows(544, dtype=bf16), rows(400), rows(288, dtype=bf16), rows(1040)),
        in_specs=[pl.BlockSpec(memory_space=pl.ANY)] * 6,
        out_specs=(vmem,) * 4,
        scratch_shapes=[
            pltpu.VMEM((512, 128), f32),
            pltpu.SMEM(box_centres.shape, f32),
            pltpu.SMEM(facet_counts.shape, jnp.int32),
            pltpu.VMEM((rhs_local, facet_local), f32),
            pltpu.VMEM(facet_centres.shape, f32),
            pltpu.VMEM(areas.shape, f32),
            pltpu.VMEM(normals.shape, f32),
            pltpu.SemaphoreType.DMA((6,)),
        ],
        name="prepare",
    )(box_centres, facet_counts, basis, facet_centres, areas, normals)
    swap = [(0, 1), (1, 0)]
    ups = range(count - 1)
    cross = lax.ppermute(sent, "rhs", swap)
    first = lax.ppermute(
        first, ("box", "rhs"), [(2 * i, 2 * i + 2) for i in ups] + [(2 * i + 3, 2 * i + 1) for i in ups]
    )
    second = lax.ppermute(
        second, ("box", "rhs"), [(2 * i + 1, 2 * i + 2) for i in ups] + [(2 * i + 2, 2 * i + 1) for i in ups]
    )
    plane_slots = plane_boxes * per_box
    geometry, strengths, targets, planes, local = pl.pallas_call(
        feature_kernel,
        out_shape=(
            rows(boxes * depth, per_box, bf16),
            rows(boxes * 80, per_box, bf16),
            rows(plane_slots, depth, bf16),
            rows(plane_boxes * 8, per_box),
            rows(528),
        ),
        in_specs=[vmem],
        out_specs=(vmem,) * 5,
        compiler_params=limit(12),
        name="features",
    )(local)
    mine, theirs = pl.pallas_call(
        field_kernel,
        out_shape=(rows(boxes * 8, per_box),) * 2,
        in_specs=[smem] + [vmem] * 8,
        out_specs=(vmem, vmem),
        scratch_shapes=[
            pltpu.VMEM((plane_boxes * depth, per_box), bf16),
            pltpu.VMEM((plane_boxes * 80, per_box), bf16),
            pltpu.VMEM((3 * plane_boxes * 80, per_box), bf16),
            pltpu.VMEM((plane_boxes * 16, per_box), f32),
            pltpu.VMEM((3 * plane_boxes * 16, per_box), f32),
            pltpu.VMEM((6 * 32, 128), f32),
            pltpu.VMEM((2 * 32, 128), f32),
        ],
        compiler_params=limit(32),
        name="fields",
    )(box_centres, local, cross, first, second, geometry, strengths, targets, planes)
    theirs = lax.ppermute(theirs, "rhs", swap)
    gram, live = pl.pallas_call(
        gram_kernel,
        out_shape=(rows(8), rows(2 * boxes)),
        in_specs=[smem, vmem],
        out_specs=(vmem, vmem),
        compiler_params=limit(8),
        name="gram",
    )(facet_counts, basis)
    image, tiles = pl.pallas_call(
        image_kernel,
        out_shape=(rows(rhs_local, facet_local), jax.ShapeDtypeStruct((count, 8, 128), f32)),
        in_specs=[vmem] * 6,
        out_specs=(vmem, vmem),
        compiler_params=limit(8),
        name="image",
    )(mine, theirs, gram, live, contrast, basis)
    tiles = lax.all_to_all(tiles, "box", 0, 0, tiled=True)
    next_vector, hessenberg = pl.pallas_call(
        functools.partial(finish_kernel, total_facets),
        out_shape=(rows(rhs_local, facet_local), rows(rhs_local, krylov + 1)),
        in_specs=[vmem] * 4,
        out_specs=(vmem, vmem),
        compiler_params=limit(16),
        name="finish",
    )(tiles, live, image, basis)
    return next_vector, hessenberg.T


def solution(mesh):
    return jax.shard_map(
        on_device,
        mesh=mesh,
        in_specs=(
            P(None, "rhs", "box"),
            P(None, "box"),
            P(None, "box"),
            P("box"),
            P("box"),
            P("box"),
            P(None, "box"),
            P("box", None),
            P("box", None),
        ),
        out_specs=(P("rhs", "box"), P(None, "rhs")),
        check_vma=False,
    )
```
